32 devices in a mesh: groups: 2 (over y), seg: 4 (over z), sta: 2 (over x), pol: 2 (over core).
Axes of the slice: x: 2, y: 2, z: 4, core: 2. Of those that a mesh axis runs over, the one named last changes fastest.
Arguments:
- raw_spectra: bfloat16 [8, 16, 2, 2048], P(('groups', 'seg'), 'sta', None, 'pol'), parts along dimension 0
- owner_plan: int32 [6], P('groups'), parts along dimension 0, may hold values from 0 to 1
- pair_valid: int32 [8, 16, 16], P(('groups', 'seg'), None, 'sta'), parts along dimension 0, may hold values 0 or 1
- quality: int32 [8, 16], P(('groups', 'seg')), parts along dimension 0, may hold values 0 or 1
Outputs:
- pair_functions: float32 [6, 8, 16, 4096], P('groups', None, 'sta', ('seg', 'pol')), parts along dimension 0
The draws below stay inside these ranges and needn't reach their ends.
There are 2 independent parts, one for each index of `groups`. The reference program is written for one: setup_inputs(seed, part) draws one part's arguments, and reference() takes and returns one part's arrays. A program takes and returns all parts, laid end to end along the dimension named above; each array names one. Nothing has to cross between parts.
All inputs are finite; a program needn't handle non-finite values. No bound on the sum of `pair_valid` or of `quality` on one device may be relied on, other than what follows from the above.
Results may differ from the reference program's by a relative error of at most 0.0041.
Values may be sent and summed in bfloat16 or wider, within the bound.
No kernel may reach another device: no remote copies, remote signals or barrier semaphores. Data moves between devices by JAX's collectives and lax.ppermute only.
A program may use at most 64 MiB of HBM per device.

```python
import jax
import jax.numpy as jnp
from jax import lax

S_DEV = 8
STEPS = 3
FREQ = 2048
BAND = 128
LAGS = 4096
STATIONS = 16
SEGMENTS = 4


def draw_raw_spectra(key, part):
    key = jax.random.fold_in(key, 7)
    first_key, second_key = jax.random.split(key)
    shape_full = (SEGMENTS, STATIONS, 2, FREQ // BAND, BAND)
    base = jnp.clip(jax.random.normal(first_key, shape_full, jnp.float32), -5.5, 5.5)
    level = jax.random.uniform(second_key, (SEGMENTS, STATIONS, 1, FREQ // BAND, 1), jnp.float32, -2.3, 2.3)
    return (base * jnp.exp(level)).reshape(SEGMENTS, STATIONS, 2, FREQ).astype(jnp.bfloat16)


def draw_owner_plan(key, part):
    key = jax.random.fold_in(key, 11)
    end_key, rest_key = jax.random.split(key)
    block_count = STATIONS // S_DEV
    first_owner = jax.random.randint(end_key, (1,), 0, 2, jnp.int32) * (block_count - 1)
    second_owner = block_count - 1 - first_owner
    others = jax.random.randint(rest_key, (STEPS,), 0, block_count, jnp.int32)
    return jnp.concatenate([first_owner, second_owner, others[2:]]).astype(jnp.int32)


def set_ends(array, rng, smallest, top_value):
    spot = [jax.random.randint(jax.random.fold_in(rng, axis), (), 0, length) for axis, length in enumerate(array.shape)]
    main_axis = array.shape.index(max(array.shape))
    next_to = spot[:main_axis] + [(spot[main_axis] + 1) % array.shape[main_axis]] + spot[main_axis + 1:]
    return array.at[tuple(spot)].set(smallest).at[tuple(next_to)].set(top_value)


def setup_inputs(seed: int = 0, part: int = 0) -> dict:
    streams_of = jax.random.split(jax.random.key(seed), 5)
    own_keys = jax.random.split(jax.random.fold_in(streams_of[4], part), 5)
    raw_spectra = draw_raw_spectra(jax.random.fold_in(jax.random.fold_in(streams_of[4], part), 71), part)
    owner_plan = draw_owner_plan(jax.random.fold_in(jax.random.fold_in(streams_of[4], part), 71), part)
    pair_valid = set_ends((jax.random.randint(own_keys[2], (SEGMENTS, STATIONS, STATIONS), 0, 4) < 3).astype(jnp.int32), jax.random.fold_in(own_keys[2], 1), 0, 1)
    quality = set_ends((jax.random.randint(own_keys[3], (SEGMENTS, STATIONS), 0, 8) < 7).astype(jnp.int32), jax.random.fold_in(own_keys[3], 1), 0, 1)
    return {"raw_spectra": raw_spectra, "owner_plan": owner_plan, "pair_valid": pair_valid, "quality": quality}


def whiten(raw_values, band_len):
    values = raw_values.astype(jnp.float32)
    dims_all = values.shape
    blocks = values.reshape(dims_all[0], dims_all[1], 2, dims_all[3] // band_len, band_len)
    power = lax.optimization_barrier(jnp.mean(blocks * blocks, axis=(2, 4), keepdims=True))
    return (blocks / jnp.sqrt(power + 1e-06)).reshape(dims_all).astype(jnp.bfloat16)

def reference(raw_spectra, owner_plan, pair_valid, quality):
    white = whiten(raw_spectra, BAND).astype(jnp.float32)
    flags = quality.astype(jnp.float32)
    high = lax.Precision.HIGHEST
    results = []
    for step in range(STEPS):
        first = (owner_plan[step] * S_DEV).astype(jnp.int32)
        source = lax.dynamic_slice_in_dim(white, first, S_DEV, 1)
        valid = lax.dynamic_slice_in_dim(pair_valid, first, S_DEV, 1).astype(jnp.float32)
        source_flags = lax.dynamic_slice_in_dim(flags, first, S_DEV, 1)
        weight = valid * source_flags[:, :, None] * flags[:, None, :]
        real_src, imag_src = (source[:, :, 0], source[:, :, 1])
        real_loc, imag_loc = (white[:, :, 0], white[:, :, 1])
        real_part = jnp.einsum('gij,gif,gjf->ijf', weight, real_src, real_loc, precision=high) + jnp.einsum('gij,gif,gjf->ijf', weight, imag_src, imag_loc, precision=high)
        imag_part = jnp.einsum('gij,gif,gjf->ijf', weight, imag_src, real_loc, precision=high) - jnp.einsum('gij,gif,gjf->ijf', weight, real_src, imag_loc, precision=high)
        spectrum = real_part + 1j * imag_part
        lagged = jnp.fft.irfft(spectrum, n=LAGS, axis=-1)
        results.append(lagged * (LAGS / jnp.sqrt(jnp.float32(FREQ * SEGMENTS))))
    return jnp.stack(results).astype(jnp.float32)
```

```python
import functools
import math

import jax
import jax.numpy as jnp
import numpy as np
from jax import lax
from jax.experimental import pallas as pl
from jax.experimental.pallas import tpu as pltpu
from jax.sharding import PartitionSpec as P

STEPS = 3
BAND = 128
LANES = 128


def lag_table(lags, bins, scale):
    bin_index = np.arange(bins, dtype=np.int64)
    phase = (bin_index[:, None] * np.arange(lags, dtype=np.int64)[None, :]) % (2 * bins)
    angle = phase * (2.0 * math.pi / (2 * bins))
    factor = np.where(bin_index == 0, 1.0, 2.0)[:, None] * scale
    parts = np.stack([np.cos(angle) * factor, -np.sin(angle) * factor])
    parts = parts.reshape(2, bins // LANES, LANES, lags).transpose(1, 0, 2, 3)
    return parts.reshape(2 * bins, lags).astype(jnp.bfloat16)


def phase_table(blocks):
    phase = (np.arange(blocks)[:, None] * np.arange(LANES)[None, :]) % blocks
    angle = phase * (2.0 * math.pi / blocks)
    parts = np.stack([np.cos(angle), np.sin(angle)], axis=1).astype(np.float32)
    return np.repeat(parts[:, :, None, :], 8, axis=2)


def prepare_kernel(sizes, plan_ref, raw_ref, valid_ref, quality_ref, out_ref, wide):
    stations, bands, sta, blocks, weight_rows = sizes
    total = stations * sta
    me = lax.axis_index("sta")
    wide[...] = raw_ref[...].astype(jnp.float32)
    count = stations * bands
    real = wide[pl.ds(0, count, stride=2), :]
    imag = wide[pl.ds(1, count, stride=2), :]
    power = jnp.sum(real * real + imag * imag, axis=1, keepdims=True) * (1.0 / (2 * BAND))
    inverse = 1.0 / jnp.sqrt(power + 1e-06)
    real = (real * inverse).reshape(stations, bands, LANES)
    imag = (imag * inverse).reshape(stations, bands, LANES)
    white = jnp.concatenate([real, imag], axis=1).reshape(2 * count, LANES)
    out_ref[pl.ds(0, 2 * count), :] = white.astype(jnp.bfloat16)

    valid = valid_ref[...].astype(jnp.float32).astype(jnp.bfloat16)
    quality = jnp.broadcast_to(quality_ref[...].astype(jnp.float32), (8, total)).astype(jnp.bfloat16)
    rows = []
    for row in range(weight_rows):
        pair = row * LANES + lax.broadcasted_iota(jnp.int32, (total, LANES), 1)
        station = lax.broadcasted_iota(jnp.int32, (total, LANES), 0)
        block = pair // (stations * stations)
        first = jnp.zeros_like(pair)
        for k in range(blocks):
            owner = k if sta == blocks else plan_ref[k]
            first = jnp.where(block == k, owner * stations, first)
        source = first + pair // stations % stations
        local = me * stations + pair % stations
        pick_source = (station == source).astype(jnp.float32).astype(jnp.bfloat16)
        pick_local = (station == local).astype(jnp.float32).astype(jnp.bfloat16)
        dot = functools.partial(jnp.dot, preferred_element_type=jnp.float32)
        valid_pairs = dot(valid, pick_source)
        mine = lax.broadcasted_iota(jnp.int32, (stations, LANES), 0) == (
            lax.broadcasted_iota(jnp.int32, (stations, LANES), 1) % stations
        )
        valid_row = jnp.sum(jnp.where(mine, valid_pairs, 0.0), axis=0, keepdims=True)
        flags = dot(quality, pick_source) * dot(quality, pick_local)
        rows.append(valid_row * flags[:1])
    rows.append(jnp.zeros((16 - weight_rows, LANES), jnp.float32))
    out_ref[pl.ds(2 * count, 16), :] = jnp.concatenate(rows, axis=0).astype(jnp.bfloat16)


def stack_kernel(
    sizes, plan_ref, spectra_ref, table_ref, phase_ref, out_ref, wide_weight, local, real_x, imag_x, packed, lags_x
):
    stations, bands, seg, sta, pol, blocks, weight_rows = sizes
    pairs = blocks * stations * stations
    me = lax.axis_index("sta")
    lag_block = lax.axis_index("seg") * pol + lax.axis_index("pol")

    diagonal = lax.broadcasted_iota(jnp.int32, (LANES, LANES), 0) == lax.broadcasted_iota(
        jnp.int32, (LANES, LANES), 1
    )
    ones = jnp.ones((LANES, LANES), jnp.bfloat16)
    for g in range(seg):
        rows = spectra_ref[(g * sta + me) * pol, pl.ds(2 * stations * bands, 16), :].astype(jnp.float32)
        for row in range(weight_rows):
            spread = jnp.where(diagonal, rows[row : row + 1], 0.0).astype(jnp.bfloat16)
            wide_weight[g, pl.ds(row * LANES, LANES), :] = jnp.dot(
                spread, ones, preferred_element_type=jnp.float32
            )

    cosine = phase_ref[lag_block, 0]
    sine = phase_ref[lag_block, 1]
    for p in range(pol):
        for g in range(seg):
            for j in range(stations):
                tile = spectra_ref[(g * sta + me) * pol + p, pl.ds(j * 16, 16), :].astype(jnp.float32)
                local[g, j, 0] = tile[:8] * cosine + tile[8:] * sine
                local[g, j, 1] = tile[8:] * cosine - tile[:8] * sine
        for k in range(blocks):
            owner = k if sta == blocks else plan_ref[k]

            def one_source(a, carry):
                start = pl.multiple_of(a * 16, 16)
                tiles = [
                    spectra_ref[(g * sta + owner) * pol + p, pl.ds(start, 16), :].astype(jnp.float32)
                    for g in range(seg)
                ]
                for j in range(stations):
                    pair = (k * stations + a) * stations + j
                    real_sum = imag_sum = None
                    for g in range(seg):
                        weight = jnp.broadcast_to(wide_weight[g, pl.ds(pair, 1), :], (8, LANES))
                        real_src = tiles[g][:8] * weight
                        imag_src = tiles[g][8:] * weight
                        real_loc = local[g, j, 0]
                        imag_loc = local[g, j, 1]
                        real_term = real_src * real_loc + imag_src * imag_loc
                        imag_term = imag_src * real_loc - real_src * imag_loc
                        real_sum = real_term if g == 0 else real_sum + real_term
                        imag_sum = imag_term if g == 0 else imag_sum + imag_term
                    at = pl.ds(pl.multiple_of(pair * 8, 8), 8)
                    real_x[at, :] = real_sum
                    imag_x[at, :] = imag_sum
                return carry

            lax.fori_loop(0, stations, one_source, 0)
        for band in range(bands):
            column = (p * bands + band) * 2 * LANES
            packed[:, pl.ds(column, LANES)] = real_x[pl.ds(band, pairs, stride=8), :].astype(jnp.bfloat16)
            packed[:, pl.ds(column + LANES, LANES)] = imag_x[pl.ds(band, pairs, stride=8), :].astype(jnp.bfloat16)
    lags_x[...] = jnp.dot(packed[...], table_ref[...], preferred_element_type=jnp.float32)
    block_pairs = stations * stations
    for step in range(STEPS):
        first = (plan_ref[step] if sta == blocks else step) * block_pairs
        out_ref[step] = lags_x[pl.ds(pl.multiple_of(first, block_pairs), block_pairs), :]


def shards(table, phases, raw_spectra, owner_plan, pair_valid, quality):
    seg, sta, pol = (lax.axis_size(name) for name in ("seg", "sta", "pol"))
    _, stations, _, bins = raw_spectra.shape
    bands = bins // BAND
    blocks = min(sta, STEPS)
    pairs = blocks * stations * stations
    weight_rows = -(-pairs // LANES)
    lags = table.shape[1]
    rows = 2 * stations * bands + 16

    raw = raw_spectra.reshape(stations, 2, bands, BAND).transpose(0, 2, 1, 3).reshape(-1, BAND)
    vmem = pl.BlockSpec(memory_space=pltpu.VMEM)
    smem = pl.BlockSpec(memory_space=pltpu.SMEM)
    payload = pl.pallas_call(
        functools.partial(prepare_kernel, (stations, bands, sta, blocks, weight_rows)),
        out_shape=jax.ShapeDtypeStruct((rows, LANES), jnp.bfloat16),
        in_specs=[smem, vmem, vmem, vmem],
        out_specs=vmem,
        scratch_shapes=[pltpu.VMEM((2 * stations * bands, LANES), jnp.float32)],
        name="prepare",
    )(owner_plan, raw, jnp.transpose(pair_valid[0]), quality)

    spectra = lax.all_gather(payload, ("seg", "sta", "pol"))

    out = pl.pallas_call(
        functools.partial(stack_kernel, (stations, bands, seg, sta, pol, blocks, weight_rows)),
        out_shape=jax.ShapeDtypeStruct((STEPS, stations * stations, lags), jnp.float32),
        in_specs=[smem, vmem, vmem, vmem],
        out_specs=vmem,
        scratch_shapes=[
            pltpu.VMEM((seg, weight_rows * LANES, LANES), jnp.float32),
            pltpu.VMEM((seg, stations, 2, 8, LANES), jnp.float32),
            pltpu.VMEM((pairs * 8, LANES), jnp.float32),
            pltpu.VMEM((pairs * 8, LANES), jnp.float32),
            pltpu.VMEM((pairs, table.shape[0]), jnp.bfloat16),
            pltpu.VMEM((pairs, lags), jnp.float32),
        ],
        compiler_params=pltpu.CompilerParams(vmem_limit_bytes=48 * 1024 * 1024),
        name="stack",
    )(owner_plan, spectra, table, phases)
    return out.reshape(STEPS, stations, stations, lags)


def solution(mesh):
    placed = (
        P(("groups", "seg"), "sta", None, "pol"),
        P("groups"),
        P(("groups", "seg"), None, "sta"),
        P(("groups", "seg"), None),
    )

    def whole(raw_spectra, owner_plan, pair_valid, quality):
        seg, pol = mesh.shape["seg"], mesh.shape["pol"]
        bins = raw_spectra.shape[3]
        segments = raw_spectra.shape[0] // mesh.shape["groups"]
        lag_blocks = seg * pol
        table = lag_table(2 * bins // lag_blocks, bins, 1.0 / math.sqrt(bins * segments))
        phases = phase_table(lag_blocks)
        return jax.shard_map(
            shards,
            mesh=mesh,
            in_specs=(P(), P()) + placed,
            out_specs=P("groups", None, "sta", ("seg", "pol")),
            check_vma=False,
        )(jnp.asarray(table), jnp.asarray(phases), raw_spectra, owner_plan, pair_valid, quality)

    return whole
```

```python
import functools
import math

import jax
import jax.numpy as jnp
import numpy as np
from jax import lax
from jax.experimental import pallas as pl
from jax.experimental.pallas import tpu as pltpu
from jax.sharding import PartitionSpec as P

STEPS = 3
BAND = 128
LANES = 128


def lag_table(lags, bins, scale):
    bin_index = np.arange(bins, dtype=np.int64)
    phase = (bin_index[:, None] * np.arange(lags, dtype=np.int64)[None, :]) % (2 * bins)
    angle = phase * (2.0 * math.pi / (2 * bins))
    factor = np.where(bin_index == 0, 1.0, 2.0)[:, None] * scale
    parts = np.stack([np.cos(angle) * factor, -np.sin(angle) * factor])
    parts = parts.reshape(2, bins // LANES, LANES, lags).transpose(1, 0, 2, 3)
    return parts.reshape(2 * bins, lags).astype(jnp.bfloat16)


def phase_table(blocks):
    phase = (np.arange(blocks)[:, None] * np.arange(LANES)[None, :]) % blocks
    angle = phase * (2.0 * math.pi / blocks)
    parts = np.stack([np.cos(angle), np.sin(angle)], axis=1).astype(np.float32)
    return np.repeat(parts[:, :, None, :], 8, axis=2)


def prepare_kernel(sizes, plan_ref, raw_ref, valid_ref, quality_ref, out_ref, wide):
    stations, bands, sta, blocks, weight_rows = sizes
    total = stations * sta
    me = lax.axis_index("sta")
    wide[...] = raw_ref[...].astype(jnp.float32)
    count = stations * bands
    real = wide[pl.ds(0, count, stride=2), :]
    imag = wide[pl.ds(1, count, stride=2), :]
    power = jnp.sum(real * real + imag * imag, axis=1, keepdims=True) * (1.0 / (2 * BAND))
    inverse = 1.0 / jnp.sqrt(power + 1e-06)
    real = (real * inverse).reshape(stations, bands, LANES)
    imag = (imag * inverse).reshape(stations, bands, LANES)
    white = jnp.concatenate([real, imag], axis=1).reshape(2 * count, LANES)
    out_ref[pl.ds(0, 2 * count), :] = white.astype(jnp.bfloat16)

    valid = valid_ref[...].astype(jnp.float32).astype(jnp.bfloat16)
    quality = jnp.broadcast_to(quality_ref[...].astype(jnp.float32), (8, total)).astype(jnp.bfloat16)
    rows = []
    for row in range(weight_rows):
        pair = row * LANES + lax.broadcasted_iota(jnp.int32, (total, LANES), 1)
        station = lax.broadcasted_iota(jnp.int32, (total, LANES), 0)
        block = pair // (stations * stations)
        first = jnp.zeros_like(pair)
        for k in range(blocks):
            owner = k if sta == blocks else plan_ref[k]
            first = jnp.where(block == k, owner * stations, first)
        source = first + pair // stations % stations
        local = me * stations + pair % stations
        pick_source = (station == source).astype(jnp.float32).astype(jnp.bfloat16)
        pick_local = (station == local).astype(jnp.float32).astype(jnp.bfloat16)
        dot = functools.partial(jnp.dot, preferred_element_type=jnp.float32)
        valid_pairs = dot(valid, pick_source)
        mine = lax.broadcasted_iota(jnp.int32, (stations, LANES), 0) == (
            lax.broadcasted_iota(jnp.int32, (stations, LANES), 1) % stations
        )
        valid_row = jnp.sum(jnp.where(mine, valid_pairs, 0.0), axis=0, keepdims=True)
        flags = dot(quality, pick_source) * dot(quality, pick_local)
        rows.append(valid_row * flags[:1])
    rows.append(jnp.zeros((16 - weight_rows, LANES), jnp.float32))
    out_ref[pl.ds(2 * count, 16), :] = jnp.concatenate(rows, axis=0).astype(jnp.bfloat16)


def partner(index, step, size):
    return index ^ step if size & (size - 1) == 0 else (index + step) % size


def half_kernel(sizes, distance, *refs):
    stations, bands, seg, sta, pol, blocks, weight_rows = sizes
    held = seg * sta
    plan_ref, table_hbm, phase_hbm = refs[:3]
    spectra_hbm = refs[3 : 3 + held]
    rest = refs[3 + held :]
    if distance:
        before_hbm, rest = rest[0], rest[1:]
    out_ref, table, phase, spectra, before, wide_weight, local, real_x, imag_x, packed, sems = rest
    last = distance == pol - 1
    pairs = blocks * stations * stations
    me = lax.axis_index("sta")
    lag_block = lax.axis_index("seg") * pol + lax.axis_index("pol")
    half = partner(lax.axis_index("pol"), distance, pol)
    rows = 2 * bands * LANES

    copies = [pltpu.make_async_copy(spectra_hbm[n], spectra.at[n], sems.at[n]) for n in range(held)]
    copies.append(pltpu.make_async_copy(phase_hbm.at[lag_block], phase, sems.at[held]))
    late = [
        pltpu.make_async_copy(
            table_hbm.at[pl.ds(pl.multiple_of(half * rows, rows), rows)], table, sems.at[held + 1]
        )
    ]
    if distance:
        late.append(pltpu.make_async_copy(before_hbm, before, sems.at[held + 2]))
    for copy in copies + late:
        copy.start()
    for copy in copies:
        copy.wait()

    diagonal = lax.broadcasted_iota(jnp.int32, (LANES, LANES), 0) == lax.broadcasted_iota(
        jnp.int32, (LANES, LANES), 1
    )
    ones = jnp.ones((LANES, LANES), jnp.bfloat16)
    for g in range(seg):
        flags = spectra[g * sta, pl.ds(2 * stations * bands, 16), :].astype(jnp.float32)
        for row in range(weight_rows):
            spread = jnp.where(diagonal, flags[row : row + 1], 0.0).astype(jnp.bfloat16)
            wide_weight[g, pl.ds(row * LANES, LANES), :] = jnp.dot(
                spread, ones, preferred_element_type=jnp.float32
            )

    cosine = phase[0]
    sine = phase[1]
    for g in range(seg):
        for j in range(stations):
            tile = spectra[g * sta, pl.ds(j * 16, 16), :].astype(jnp.float32)
            local[g, j, 0] = tile[:8] * cosine + tile[8:] * sine
            local[g, j, 1] = tile[8:] * cosine - tile[:8] * sine
    for k in range(blocks):
        owner = partner(k if sta == blocks else plan_ref[k], me, sta)

        def one_source(a, carry):
            start = pl.multiple_of(a * 16, 16)
            tiles = [
                spectra[g * sta + owner, pl.ds(start, 16), :].astype(jnp.float32) for g in range(seg)
            ]
            for j in range(stations):
                pair = (k * stations + a) * stations + j
                real_sum = imag_sum = None
                for g in range(seg):
                    weight = jnp.broadcast_to(wide_weight[g, pl.ds(pair, 1), :], (8, LANES))
                    real_src = tiles[g][:8] * weight
                    imag_src = tiles[g][8:] * weight
                    real_loc = local[g, j, 0]
                    imag_loc = local[g, j, 1]
                    real_term = real_src * real_loc + imag_src * imag_loc
                    imag_term = imag_src * real_loc - real_src * imag_loc
                    real_sum = real_term if g == 0 else real_sum + real_term
                    imag_sum = imag_term if g == 0 else imag_sum + imag_term
                at = pl.ds(pl.multiple_of(pair * 8, 8), 8)
                real_x[at, :] = real_sum
                imag_x[at, :] = imag_sum
            return carry

        lax.fori_loop(0, stations, one_source, 0)
    for band in range(bands):
        column = band * 2 * LANES
        packed[:, pl.ds(column, LANES)] = real_x[pl.ds(band, pairs, stride=8), :].astype(jnp.bfloat16)
        packed[:, pl.ds(column + LANES, LANES)] = imag_x[pl.ds(band, pairs, stride=8), :].astype(jnp.bfloat16)
    for copy in late:
        copy.wait()
    part = jnp.dot(packed[...], table[...], preferred_element_type=jnp.float32)
    if distance:
        part = before[...] + part
    if not last:
        out_ref[...] = part
        return
    before[...] = part
    block_pairs = stations * stations
    for step in range(STEPS):
        first = (plan_ref[step] if sta == blocks else step) * block_pairs
        out_ref[step] = before[pl.ds(pl.multiple_of(first, block_pairs), block_pairs), :]


def swap(value, axes, sizes, steps):
    pairs = []
    for index in np.ndindex(*sizes):
        source = tuple(partner(i, d, n) for i, d, n in zip(index, steps, sizes))
        pairs.append((int(np.ravel_multi_index(source, sizes)), int(np.ravel_multi_index(index, sizes))))
    return lax.ppermute(value, axes, pairs)


def shards(table, phases, raw_spectra, owner_plan, pair_valid, quality):
    seg, sta, pol = (lax.axis_size(name) for name in ("seg", "sta", "pol"))
    _, stations, _, bins = raw_spectra.shape
    bands = bins // BAND
    blocks = min(sta, STEPS)
    pairs = blocks * stations * stations
    weight_rows = -(-pairs // LANES)
    lags = table.shape[1]
    rows = 2 * stations * bands + 16

    raw = raw_spectra.reshape(stations, 2, bands, BAND).transpose(0, 2, 1, 3).reshape(-1, BAND)
    vmem = pl.BlockSpec(memory_space=pltpu.VMEM)
    smem = pl.BlockSpec(memory_space=pltpu.SMEM)
    anywhere = pl.BlockSpec(memory_space=pl.ANY)
    payload = pl.pallas_call(
        functools.partial(prepare_kernel, (stations, bands, sta, blocks, weight_rows)),
        out_shape=jax.ShapeDtypeStruct((rows, LANES), jnp.bfloat16),
        in_specs=[smem, vmem, vmem, vmem],
        out_specs=vmem,
        scratch_shapes=[pltpu.VMEM((2 * stations * bands, LANES), jnp.float32)],
        name="prepare",
    )(owner_plan, raw, jnp.transpose(pair_valid[0]), quality)

    spectra = [
        swap(payload, ("seg", "sta"), (seg, sta), (g, q)) if g or q else payload
        for g in range(seg)
        for q in range(sta)
    ]
    held = len(spectra)
    sizes = (stations, bands, seg, sta, pol, blocks, weight_rows)
    out = None
    for distance in range(pol):
        last = distance == pol - 1
        theirs = [swap(x, ("pol",), (pol,), (distance,)) for x in spectra] if distance else spectra
        out_shape = (STEPS, stations * stations, lags) if last else (pairs, lags)
        flops = 2 * pairs * 2 * bins * lags
        out = pl.pallas_call(
            functools.partial(half_kernel, sizes, distance),
            out_shape=jax.ShapeDtypeStruct(out_shape, jnp.float32),
            in_specs=[smem] + [anywhere] * (2 + held + (1 if distance else 0)),
            out_specs=vmem,
            scratch_shapes=[
                pltpu.VMEM((2 * bins, lags), jnp.bfloat16),
                pltpu.VMEM((2, 8, LANES), jnp.float32),
                pltpu.VMEM((held, rows, LANES), jnp.bfloat16),
                pltpu.VMEM((pairs, lags), jnp.float32),
                pltpu.VMEM((seg, weight_rows * LANES, LANES), jnp.float32),
                pltpu.VMEM((seg, stations, 2, 8, LANES), jnp.float32),
                pltpu.VMEM((pairs * 8, LANES), jnp.float32),
                pltpu.VMEM((pairs * 8, LANES), jnp.float32),
                pltpu.VMEM((pairs, 2 * bins), jnp.bfloat16),
                pltpu.SemaphoreType.DMA((held + 3,)),
            ],
            compiler_params=pltpu.CompilerParams(vmem_limit_bytes=48 * 1024 * 1024),
            cost_estimate=pl.CostEstimate(flops=8 * flops, bytes_accessed=4 * 1024 * 1024, transcendentals=0),
            name="stack_first" if distance == 0 else "stack_rest",
        )(owner_plan, table, phases, *theirs, *([out] if distance else []))
    return out.reshape(STEPS, stations, stations, lags)


def solution(mesh):
    placed = (
        P(("groups", "seg"), "sta", None, "pol"),
        P("groups"),
        P(("groups", "seg"), None, "sta"),
        P(("groups", "seg"), None),
    )

    def whole(raw_spectra, owner_plan, pair_valid, quality):
        seg, pol = mesh.shape["seg"], mesh.shape["pol"]
        bins = raw_spectra.shape[3]
        segments = raw_spectra.shape[0] // mesh.shape["groups"]
        lag_blocks = seg * pol
        table = lag_table(2 * bins // lag_blocks, bins, 1.0 / math.sqrt(bins * segments))
        phases = phase_table(lag_blocks)
        return jax.shard_map(
            shards,
            mesh=mesh,
            in_specs=(P(), P()) + placed,
            out_specs=P("groups", None, "sta", ("seg", "pol")),
            check_vma=False,
        )(jnp.asarray(table), jnp.asarray(phases), raw_spectra, owner_plan, pair_valid, quality)

    return whole
```

```python
import functools
import math

import jax
import jax.numpy as jnp
import numpy as np
from jax import lax
from jax.experimental import pallas as pl
from jax.experimental.pallas import tpu as pltpu
from jax.sharding import PartitionSpec as P

STEPS = 3
BAND = 128
LANES = 128


def lag_table(lags, bins, scale):
    bin_index = np.arange(bins, dtype=np.int64)
    phase = (bin_index[:, None] * np.arange(lags, dtype=np.int64)[None, :]) % (2 * bins)
    angle = phase * (2.0 * math.pi / (2 * bins))
    factor = np.where(bin_index == 0, 1.0, 2.0)[:, None] * scale
    parts = np.stack([np.cos(angle) * factor, -np.sin(angle) * factor])
    parts = parts.reshape(2, bins // LANES, LANES, lags).transpose(1, 0, 2, 3)
    return parts.reshape(2 * bins, lags).astype(jnp.bfloat16)


def phases_of(block, blocks):
    turn = lax.broadcasted_iota(jnp.int32, (8, LANES), 1) * block % blocks
    cosine = sine = jnp.zeros((8, LANES), jnp.float32)
    for part in range(blocks):
        angle = 2.0 * math.pi * part / blocks
        cosine = jnp.where(turn == part, math.cos(angle), cosine)
        sine = jnp.where(turn == part, math.sin(angle), sine)
    return cosine, sine


def prepare_kernel(sizes, *refs):
    stations, bands, sta, blocks, weight_rows = sizes
    *plan, raw_ref, valid_ref, quality_ref, out_ref, wide = refs
    total = stations * sta
    me = lax.axis_index("sta")
    wide[...] = raw_ref[...].astype(jnp.float32)
    count = stations * bands
    real = wide[pl.ds(0, count, stride=2), :]
    imag = wide[pl.ds(1, count, stride=2), :]
    power = jnp.sum(real * real + imag * imag, axis=1, keepdims=True) * (1.0 / (2 * BAND))
    inverse = 1.0 / jnp.sqrt(power + 1e-06)
    real = (real * inverse).reshape(stations, bands, LANES)
    imag = (imag * inverse).reshape(stations, bands, LANES)
    white = jnp.concatenate([real, imag], axis=1).reshape(2 * count, LANES)
    white = white.astype(jnp.bfloat16)

    valid = valid_ref[...].astype(jnp.float32).astype(jnp.bfloat16)
    quality = jnp.broadcast_to(quality_ref[...].astype(jnp.float32), (8, total)).astype(jnp.bfloat16)
    rows = []
    for row in range(weight_rows):
        pair = row * LANES + lax.broadcasted_iota(jnp.int32, (total, LANES), 1)
        station = lax.broadcasted_iota(jnp.int32, (total, LANES), 0)
        block = pair // (stations * stations)
        first = jnp.zeros_like(pair)
        for k in range(blocks):
            owner = plan[0][k] if plan else k
            first = jnp.where(block == k, owner * stations, first)
        source = first + pair // stations % stations
        local = me * stations + pair % stations
        pick_source = (station == source).astype(jnp.float32).astype(jnp.bfloat16)
        pick_local = (station == local).astype(jnp.float32).astype(jnp.bfloat16)
        dot = functools.partial(jnp.dot, preferred_element_type=jnp.float32)
        valid_pairs = dot(valid, pick_source)
        mine = lax.broadcasted_iota(jnp.int32, (stations, LANES), 0) == (
            lax.broadcasted_iota(jnp.int32, (stations, LANES), 1) % stations
        )
        valid_row = jnp.sum(jnp.where(mine, valid_pairs, 0.0), axis=0, keepdims=True)
        flags = dot(quality, pick_source) * dot(quality, pick_local)
        rows.append(valid_row * flags[:1])
    rows.append(jnp.zeros((16 - weight_rows, LANES), jnp.float32))
    weights = jnp.concatenate(rows, axis=0).astype(jnp.bfloat16)
    for target in range(out_ref.shape[0]):
        out_ref[target, pl.ds(0, 2 * count), :] = white
        out_ref[target, pl.ds(2 * count, 16), :] = weights


def partner(index, step, size):
    return index ^ step if size & (size - 1) == 0 else (index + step) % size


def half_kernel(sizes, distance, *refs):
    stations, bands, seg, sta, pol, blocks, weight_rows = sizes
    all_blocks = sta == blocks
    last = distance == pol - 1
    if last or not all_blocks:
        plan_ref, refs = refs[0], refs[1:]
    table_hbm, spectra, *rest = refs
    if distance:
        before_hbm, rest = rest[0], rest[1:]
    out_ref, table, before, wide_weight, local, real_x, imag_x, packed, sems = rest
    pairs = blocks * stations * stations
    me = lax.axis_index("sta")
    lag_block = lax.axis_index("seg") * pol + lax.axis_index("pol")
    half = partner(lax.axis_index("pol"), distance, pol)
    rows = 2 * bands * LANES

    late = [
        pltpu.make_async_copy(
            table_hbm.at[pl.ds(pl.multiple_of(half * rows, rows), rows)], table, sems.at[0]
        )
    ]
    if distance:
        late.append(pltpu.make_async_copy(before_hbm, before, sems.at[1]))
    for copy in late:
        copy.start()

    diagonal = lax.broadcasted_iota(jnp.int32, (LANES, LANES), 0) == lax.broadcasted_iota(
        jnp.int32, (LANES, LANES), 1
    )
    ones = jnp.ones((LANES, LANES), jnp.bfloat16)
    for g in range(seg):
        flags = spectra[g * sta + me, pl.ds(2 * stations * bands, 16), :].astype(jnp.float32)
        for row in range(weight_rows):
            spread = jnp.where(diagonal, flags[row : row + 1], 0.0).astype(jnp.bfloat16)
            wide_weight[g, pl.ds(row * LANES, LANES), :] = jnp.dot(
                spread, ones, preferred_element_type=jnp.float32
            )

    cosine, sine = phases_of(lag_block, seg * pol)
    for g in range(seg):
        for j in range(stations):
            tile = spectra[g * sta + me, pl.ds(j * 16, 16), :].astype(jnp.float32)
            local[g, j, 0] = tile[:8] * cosine + tile[8:] * sine
            local[g, j, 1] = tile[8:] * cosine - tile[:8] * sine
    for k in range(blocks):
        owner = k if all_blocks else plan_ref[k]

        def one_source(a, carry):
            start = pl.multiple_of(a * 16, 16)
            tiles = [
                spectra[g * sta + owner, pl.ds(start, 16), :].astype(jnp.float32) for g in range(seg)
            ]
            for j in range(stations):
                pair = (k * stations + a) * stations + j
                real_sum = imag_sum = None
                for g in range(seg):
                    weight = jnp.broadcast_to(wide_weight[g, pl.ds(pair, 1), :], (8, LANES))
                    real_src = tiles[g][:8] * weight
                    imag_src = tiles[g][8:] * weight
                    real_loc = local[g, j, 0]
                    imag_loc = local[g, j, 1]
                    real_term = real_src * real_loc + imag_src * imag_loc
                    imag_term = imag_src * real_loc - real_src * imag_loc
                    real_sum = real_term if g == 0 else real_sum + real_term
                    imag_sum = imag_term if g == 0 else imag_sum + imag_term
                at = pl.ds(pl.multiple_of(pair * 8, 8), 8)
                real_x[at, :] = real_sum
                imag_x[at, :] = imag_sum
            return carry

        lax.fori_loop(0, stations, one_source, 0)
    for band in range(bands):
        column = band * 2 * LANES
        packed[:, pl.ds(column, LANES)] = real_x[pl.ds(band, pairs, stride=8), :].astype(jnp.bfloat16)
        packed[:, pl.ds(column + LANES, LANES)] = imag_x[pl.ds(band, pairs, stride=8), :].astype(jnp.bfloat16)
    for copy in late:
        copy.wait()
    part = jnp.dot(packed[...], table[...], preferred_element_type=jnp.float32)
    if distance:
        part = before[...] + part
    if not last:
        out_ref[...] = part
        return
    before[...] = part
    block_pairs = stations * stations
    for step in range(STEPS):
        first = (plan_ref[step] if all_blocks else step) * block_pairs
        out_ref[step] = before[pl.ds(pl.multiple_of(first, block_pairs), block_pairs), :]


def shards(table, raw_spectra, owner_plan, pair_valid, quality):
    seg, sta, pol = (lax.axis_size(name) for name in ("seg", "sta", "pol"))
    _, stations, _, bins = raw_spectra.shape
    bands = bins // BAND
    blocks = min(sta, STEPS)
    pairs = blocks * stations * stations
    weight_rows = -(-pairs // LANES)
    lags = table.shape[1]
    rows = 2 * stations * bands + 16

    raw = raw_spectra.reshape(stations, 2, bands, BAND).transpose(0, 2, 1, 3).reshape(-1, BAND)
    vmem = pl.BlockSpec(memory_space=pltpu.VMEM)
    smem = pl.BlockSpec(memory_space=pltpu.SMEM)
    hbm = pl.BlockSpec(memory_space=pltpu.HBM)
    plan, plan_specs = ([], []) if sta == blocks else ([owner_plan], [smem])
    payload = pl.pallas_call(
        functools.partial(prepare_kernel, (stations, bands, sta, blocks, weight_rows)),
        out_shape=jax.ShapeDtypeStruct((seg * sta, rows, LANES), jnp.bfloat16),
        in_specs=plan_specs + [vmem, vmem, vmem],
        out_specs=vmem,
        scratch_shapes=[pltpu.VMEM((2 * stations * bands, LANES), jnp.float32)],
        name="prepare",
    )(*plan, raw, jnp.transpose(pair_valid[0]), quality)

    spectra = lax.all_to_all(payload, ("seg", "sta"), split_axis=0, concat_axis=0)
    sizes = (stations, bands, seg, sta, pol, blocks, weight_rows)
    out = None
    for distance in range(pol):
        last = distance == pol - 1
        pairs_of = [(partner(i, distance, pol), i) for i in range(pol)]
        if last:
            plan, plan_specs = [owner_plan], [smem]
        theirs = lax.ppermute(spectra, "pol", pairs_of) if distance else spectra
        out_shape = (STEPS, stations * stations, lags) if last else (pairs, lags)
        flops = 2 * pairs * 2 * bins * lags
        out = pl.pallas_call(
            functools.partial(half_kernel, sizes, distance),
            out_shape=jax.ShapeDtypeStruct(out_shape, jnp.float32),
            in_specs=plan_specs + [hbm, vmem] + [hbm] * (1 if distance else 0),
            out_specs=vmem,
            scratch_shapes=[
                pltpu.VMEM((2 * bins, lags), jnp.bfloat16),
                pltpu.VMEM((pairs, lags), jnp.float32),
                pltpu.VMEM((seg, weight_rows * LANES, LANES), jnp.float32),
                pltpu.VMEM((seg, stations, 2, 8, LANES), jnp.float32),
                pltpu.VMEM((pairs * 8, LANES), jnp.float32),
                pltpu.VMEM((pairs * 8, LANES), jnp.float32),
                pltpu.VMEM((pairs, 2 * bins), jnp.bfloat16),
                pltpu.SemaphoreType.DMA((2,)),
            ],
            compiler_params=pltpu.CompilerParams(vmem_limit_bytes=52 * 1024 * 1024),
            cost_estimate=pl.CostEstimate(flops=8 * flops, bytes_accessed=4 * 1024 * 1024, transcendentals=0),
            name="stack_first" if distance == 0 else "stack_rest",
        )(*plan, table, theirs, *([out] if distance else []))
    return out.reshape(STEPS, stations, stations, lags)


def solution(mesh):
    placed = (
        P(("groups", "seg"), "sta", None, "pol"),
        P("groups"),
        P(("groups", "seg"), None, "sta"),
        P(("groups", "seg"), None),
    )

    def whole(raw_spectra, owner_plan, pair_valid, quality):
        seg, pol = mesh.shape["seg"], mesh.shape["pol"]
        bins = raw_spectra.shape[3]
        segments = raw_spectra.shape[0] // mesh.shape["groups"]
        lag_blocks = seg * pol
        table = lag_table(2 * bins // lag_blocks, bins, 1.0 / math.sqrt(bins * segments))
        return jax.shard_map(
            shards,
            mesh=mesh,
            in_specs=(P(),) + placed,
            out_specs=P("groups", None, "sta", ("seg", "pol")),
            check_vma=False,
        )(jnp.asarray(table), raw_spectra, owner_plan, pair_valid, quality)

    return whole
```

```python
import functools
import math

import jax
import jax.numpy as jnp
import numpy as np
from jax import lax
from jax.experimental import pallas as pl
from jax.experimental.pallas import tpu as pltpu
from jax.sharding import PartitionSpec as P

STEPS = 3
BAND = 128
LANES = 128


def lag_table(lags, bins, scale):
    bin_index = np.arange(bins, dtype=np.int64)
    phase = (bin_index[:, None] * np.arange(lags, dtype=np.int64)[None, :]) % (2 * bins)
    angle = phase * (2.0 * math.pi / (2 * bins))
    factor = np.where(bin_index == 0, 1.0, 2.0)[:, None] * scale
    parts = np.stack([np.cos(angle) * factor, -np.sin(angle) * factor])
    parts = parts.reshape(2, bins // LANES, LANES, lags).transpose(1, 0, 2, 3)
    return parts.reshape(2 * bins, lags).astype(jnp.bfloat16)


def phases_of(block, blocks):
    turn = lax.broadcasted_iota(jnp.int32, (8, LANES), 1) * block % blocks
    cosine = sine = jnp.zeros((8, LANES), jnp.float32)
    for part in range(blocks):
        angle = 2.0 * math.pi * part / blocks
        cosine = jnp.where(turn == part, math.cos(angle), cosine)
        sine = jnp.where(turn == part, math.sin(angle), sine)
    return cosine, sine


def prepare_kernel(sizes, *refs):
    stations, bands, sta, blocks = sizes
    *plan, raw_ref, valid_ref, quality_ref, out_ref, wide = refs
    total = stations * sta
    me = lax.axis_index("sta")
    wide[...] = raw_ref[...].astype(jnp.float32)
    count = stations * bands
    real = wide[pl.ds(0, count, stride=2), :]
    imag = wide[pl.ds(1, count, stride=2), :]
    power = jnp.sum(real * real + imag * imag, axis=1, keepdims=True) * (1.0 / (2 * BAND))
    inverse = 1.0 / jnp.sqrt(power + 1e-06)
    real = (real * inverse).reshape(stations, bands, LANES)
    imag = (imag * inverse).reshape(stations, bands, LANES)
    white = jnp.concatenate([real, imag], axis=1).reshape(2 * count, LANES).astype(jnp.bfloat16)

    valid = valid_ref[...].astype(jnp.float32).astype(jnp.bfloat16)
    quality = jnp.broadcast_to(quality_ref[...].astype(jnp.float32), (8, total)).astype(jnp.bfloat16)
    pair = lax.broadcasted_iota(jnp.int32, (total, LANES), 1)
    station = lax.broadcasted_iota(jnp.int32, (total, LANES), 0)
    mine = lax.broadcasted_iota(jnp.int32, (stations, LANES), 0) == (
        lax.broadcasted_iota(jnp.int32, (stations, LANES), 1) % stations
    )
    dot = functools.partial(jnp.dot, preferred_element_type=jnp.float32)
    pick_local = (station == me * stations + pair % stations).astype(jnp.float32).astype(jnp.bfloat16)
    local_flags = dot(quality, pick_local)
    rows = []
    for k in range(blocks):
        source = (plan[0][k] if plan else k) * stations + pair // stations
        pick_source = (station == source).astype(jnp.float32).astype(jnp.bfloat16)
        valid_row = jnp.sum(jnp.where(mine, dot(valid, pick_source), 0.0), axis=0, keepdims=True)
        rows.append(valid_row * (dot(quality, pick_source) * local_flags)[:1])
    rows.append(jnp.zeros((16 - blocks, LANES), jnp.float32))
    weights = jnp.concatenate(rows, axis=0).astype(jnp.bfloat16)
    for target in range(out_ref.shape[0]):
        out_ref[target, pl.ds(0, 2 * count), :] = white
        out_ref[target, pl.ds(2 * count, 16), :] = weights


def stack(sizes, block, locals_ref, source_ref, wide_weight, local, real_x, imag_x, packed):
    stations, bands, seg, lag_blocks = sizes
    pairs = stations * stations
    row_index = lax.broadcasted_iota(jnp.int32, (16, LANES), 0)
    diagonal = lax.broadcasted_iota(jnp.int32, (pairs, LANES), 0) == lax.broadcasted_iota(
        jnp.int32, (pairs, LANES), 1
    )
    ones = jnp.ones((LANES, LANES), jnp.bfloat16)
    for g in range(seg):
        flags = locals_ref[g, pl.ds(2 * stations * bands, 16), :].astype(jnp.float32)
        flags = jnp.sum(jnp.where(row_index == block, flags, 0.0), axis=0, keepdims=True)
        spread = jnp.where(diagonal, flags, 0.0).astype(jnp.bfloat16)
        wide_weight[g] = jnp.dot(spread, ones, preferred_element_type=jnp.float32)

    lag_block = lax.axis_index("seg") * lax.axis_size("pol") + lax.axis_index("pol")
    cosine, sine = phases_of(lag_block, lag_blocks)
    for g in range(seg):
        for j in range(stations):
            tile = locals_ref[g, pl.ds(j * 16, 16), :].astype(jnp.float32)
            local[g, j, 0] = tile[:8] * cosine + tile[8:] * sine
            local[g, j, 1] = tile[8:] * cosine - tile[:8] * sine

    def one_source(a, carry):
        start = pl.multiple_of(a * 16, 16)
        tiles = [source_ref[g, pl.ds(start, 16), :].astype(jnp.float32) for g in range(seg)]
        for j in range(stations):
            pair = a * stations + j
            real_sum = imag_sum = None
            for g in range(seg):
                weight = jnp.broadcast_to(wide_weight[g, pl.ds(pair, 1), :], (8, LANES))
                real_src = tiles[g][:8] * weight
                imag_src = tiles[g][8:] * weight
                real_loc = local[g, j, 0]
                imag_loc = local[g, j, 1]
                real_term = real_src * real_loc + imag_src * imag_loc
                imag_term = imag_src * real_loc - real_src * imag_loc
                real_sum = real_term if g == 0 else real_sum + real_term
                imag_sum = imag_term if g == 0 else imag_sum + imag_term
            at = pl.ds(pl.multiple_of(pair * 8, 8), 8)
            real_x[at, :] = real_sum
            imag_x[at, :] = imag_sum
        return carry

    lax.fori_loop(0, stations, one_source, 0)
    for band in range(bands):
        column = band * 2 * LANES
        packed[:, pl.ds(column, LANES)] = real_x[pl.ds(band, pairs, stride=8), :].astype(jnp.bfloat16)
        packed[:, pl.ds(column + LANES, LANES)] = imag_x[pl.ds(band, pairs, stride=8), :].astype(jnp.bfloat16)


def stack_kernel(sizes, piece, halves, pieces, *refs):
    stations, bands, seg, sta, pol, blocks = sizes
    own_first = sta == blocks
    final = piece == pieces - 1 and halves[-1] == pol - 1
    refs = list(refs)
    plan_ref = refs.pop(0) if final else None
    table_hbm = refs.pop(0)
    spectra = [(refs.pop(0), refs.pop(0)) for _ in halves]
    others = [refs.pop(0) for _ in range(piece if final else 0)]
    before = refs.pop(0) if halves[0] else None
    out_ref = refs.pop(0)
    tables, total, wide_weight, local, real_x, imag_x, packed, sems = refs
    me = lax.axis_index("sta")
    block = me ^ piece if own_first else piece
    rows = 2 * bands * LANES

    copies = []
    for n, half in enumerate(halves):
        start = pl.multiple_of((lax.axis_index("pol") ^ half) * rows, rows)
        copies.append(pltpu.make_async_copy(table_hbm.at[pl.ds(start, rows)], tables.at[n], sems.at[n]))
    for n, other in enumerate(others):
        copies.append(pltpu.make_async_copy(other, total.at[n], sems.at[len(halves) + n]))
    for copy in copies:
        copy.start()

    part = None
    for n, (locals_ref, source_ref) in enumerate(spectra):
        stack(
            (stations, bands, seg, seg * pol), block, locals_ref, source_ref,
            wide_weight, local, real_x, imag_x, packed,
        )
        copies[n].wait()
        term = jnp.dot(packed[...], tables[n], preferred_element_type=jnp.float32)
        part = term if part is None else part + term
    if before is not None:
        part = part + before[...]
    if not final:
        out_ref[...] = part
        return
    total[piece] = part
    for copy in copies[len(halves) :]:
        copy.wait()
    for step in range(STEPS):
        out_ref[step] = total[plan_ref[step] ^ me] if own_first else total[step]


def exchange(value, axis, distance):
    size = lax.axis_size(axis)
    return lax.ppermute(value, axis, [(i ^ distance, i) for i in range(size)]) if distance else value


def shards(table, raw_spectra, owner_plan, pair_valid, quality):
    seg, sta, pol = (lax.axis_size(name) for name in ("seg", "sta", "pol"))
    _, stations, _, bins = raw_spectra.shape
    bands = bins // BAND
    blocks = min(sta, STEPS)
    pairs = stations * stations
    lags = table.shape[1]
    rows = 2 * stations * bands + 16
    sizes = (stations, bands, seg, sta, pol, blocks)

    raw = raw_spectra.reshape(stations, 2, bands, BAND).transpose(0, 2, 1, 3).reshape(-1, BAND)
    vmem = pl.BlockSpec(memory_space=pltpu.VMEM)
    smem = pl.BlockSpec(memory_space=pltpu.SMEM)
    hbm = pl.BlockSpec(memory_space=pltpu.HBM)
    plan = [] if sta == blocks else [owner_plan]
    payload = pl.pallas_call(
        functools.partial(prepare_kernel, (stations, bands, sta, blocks)),
        out_shape=jax.ShapeDtypeStruct((seg, rows, LANES), jnp.bfloat16),
        in_specs=[smem] * len(plan) + [vmem, vmem, vmem],
        out_specs=vmem,
        scratch_shapes=[pltpu.VMEM((2 * stations * bands, LANES), jnp.float32)],
        name="prepare",
    )(*plan, raw, jnp.transpose(pair_valid[0]), quality)

    mine = lax.all_to_all(payload, "seg", split_axis=0, concat_axis=0)
    if sta == blocks:
        sources = [exchange(mine, "sta", distance) for distance in range(sta)]
    else:
        gathered = lax.all_gather(mine, "sta")
        sources = [gathered[owner_plan[k]] for k in range(blocks)]

    done = []
    for piece in range(blocks):
        last = piece == blocks - 1
        before = []
        for halves in [(h,) for h in range(pol)] if last else [tuple(range(pol))]:
            final = last and halves[-1] == pol - 1
            spectra = [x for h in halves for x in (exchange(mine, "pol", h), exchange(sources[piece], "pol", h))]
            others = done if final else []
            flops = 2 * pairs * 2 * bins * lags * len(halves)
            result = pl.pallas_call(
                functools.partial(stack_kernel, sizes, piece, halves, blocks),
                out_shape=jax.ShapeDtypeStruct((STEPS, pairs, lags) if final else (pairs, lags), jnp.float32),
                in_specs=[smem] * final + [hbm] + [vmem] * len(spectra) + [hbm] * len(others) + [vmem] * len(before),
                out_specs=vmem,
                scratch_shapes=[
                    pltpu.VMEM((len(halves), 2 * bins, lags), jnp.bfloat16),
                    pltpu.VMEM((blocks, pairs, lags), jnp.float32),
                    pltpu.VMEM((seg, pairs, LANES), jnp.float32),
                    pltpu.VMEM((seg, stations, 2, 8, LANES), jnp.float32),
                    pltpu.VMEM((pairs * 8, LANES), jnp.float32),
                    pltpu.VMEM((pairs * 8, LANES), jnp.float32),
                    pltpu.VMEM((pairs, 2 * bins), jnp.bfloat16),
                    pltpu.SemaphoreType.DMA((len(halves) + blocks,)),
                ],
                compiler_params=pltpu.CompilerParams(vmem_limit_bytes=52 * 1024 * 1024),
                cost_estimate=pl.CostEstimate(
                    flops=16 * flops, bytes_accessed=2 * 1024 * 1024 * len(halves), transcendentals=0
                ),
                name="stack",
            )(*([owner_plan] if final else []), table, *spectra, *others, *before)
            before = [result]
        done.append(result)
        if not last:
            sources[piece + 1], done[-1] = lax.optimization_barrier((sources[piece + 1], result))
    return result.reshape(STEPS, stations, stations, lags)


def solution(mesh):
    placed = (
        P(("groups", "seg"), "sta", None, "pol"),
        P("groups"),
        P(("groups", "seg"), None, "sta"),
        P(("groups", "seg"), None),
    )

    def whole(raw_spectra, owner_plan, pair_valid, quality):
        seg, pol = mesh.shape["seg"], mesh.shape["pol"]
        bins = raw_spectra.shape[3]
        segments = raw_spectra.shape[0] // mesh.shape["groups"]
        lag_blocks = seg * pol
        table = lag_table(2 * bins // lag_blocks, bins, 1.0 / math.sqrt(bins * segments))
        return jax.shard_map(
            shards,
            mesh=mesh,
            in_specs=(P(),) + placed,
            out_specs=P("groups", None, "sta", ("seg", "pol")),
            check_vma=False,
        )(jnp.asarray(table), raw_spectra, owner_plan, pair_valid, quality)

    return whole
```

```python
import functools
import math

import jax
import jax.numpy as jnp
import numpy as np
from jax import lax
from jax.experimental import pallas as pl
from jax.experimental.pallas import tpu as pltpu
from jax.sharding import PartitionSpec as P

STEPS = 3
BAND = 128
LANES = 128


def lag_table(lags, bins, halves, scale):
    bin_index = np.arange(bins, dtype=np.int64)
    lag = 2 * np.arange(lags // 2, dtype=np.int64) + 1
    phase = (bin_index[:, None] * lag[None, :]) % (4 * bins)
    angle = phase * (2.0 * math.pi / (4 * bins))
    factor = np.where(bin_index == 0, 1.0, 2.0)[:, None] * scale
    parts = np.stack([np.cos(angle) * factor, np.sin(angle) * factor])
    parts = parts.reshape(2, halves, bins // halves, lags // 2).transpose(1, 0, 2, 3)
    return parts.astype(jnp.bfloat16)


def turn(count, period):
    count = count % period
    quarter = (count + period // 8) // (period // 4)
    x = (count - quarter * (period // 4)).astype(jnp.float32) * (2.0 * math.pi / period)
    y = x * x
    sine = x * (1.0 + y * (-1 / 6 + y * (1 / 120 + y * (-1 / 5040 + y * (1 / 362880)))))
    cosine = 1.0 + y * (-1 / 2 + y * (1 / 24 + y * (-1 / 720 + y * (1 / 40320))))
    quarter = quarter % 4
    odd = quarter % 2 == 1
    real = jnp.where(odd, sine, cosine)
    imag = jnp.where(odd, cosine, sine)
    real = jnp.where((quarter == 1) | (quarter == 2), -real, real)
    imag = jnp.where(quarter >= 2, -imag, imag)
    return real, imag


def prepare_kernel(sizes, *refs):
    stations, bands, sta, blocks = sizes
    *plan, raw_ref, valid_ref, quality_ref, out_ref, wide = refs
    total = stations * sta
    me = lax.axis_index("sta")
    wide[...] = raw_ref[...].astype(jnp.float32)
    count = stations * bands
    real = wide[pl.ds(0, count, stride=2), :]
    imag = wide[pl.ds(1, count, stride=2), :]
    power = jnp.sum(real * real + imag * imag, axis=1, keepdims=True) * (1.0 / (2 * BAND))
    inverse = 1.0 / jnp.sqrt(power + 1e-06)
    real = (real * inverse).reshape(stations, bands, LANES)
    imag = (imag * inverse).reshape(stations, bands, LANES)
    white = jnp.concatenate([real, imag], axis=1).reshape(2 * count, LANES).astype(jnp.bfloat16)

    valid = valid_ref[...].astype(jnp.float32).astype(jnp.bfloat16)
    quality = jnp.broadcast_to(quality_ref[...].astype(jnp.float32), (8, total)).astype(jnp.bfloat16)
    pair = lax.broadcasted_iota(jnp.int32, (total, LANES), 1)
    station = lax.broadcasted_iota(jnp.int32, (total, LANES), 0)
    mine = lax.broadcasted_iota(jnp.int32, (stations, LANES), 0) == (
        lax.broadcasted_iota(jnp.int32, (stations, LANES), 1) % stations
    )
    dot = functools.partial(jnp.dot, preferred_element_type=jnp.float32)
    pick_local = (station == me * stations + pair % stations).astype(jnp.float32).astype(jnp.bfloat16)
    local_flags = dot(quality, pick_local)
    rows = []
    for k in range(blocks):
        source = (plan[0][k] if plan else k) * stations + pair // stations
        pick_source = (station == source).astype(jnp.float32).astype(jnp.bfloat16)
        valid_row = jnp.sum(jnp.where(mine, dot(valid, pick_source), 0.0), axis=0, keepdims=True)
        rows.append(valid_row * (dot(quality, pick_source) * local_flags)[:1])
    rows.append(jnp.zeros((16 - blocks, LANES), jnp.float32))
    weights = jnp.concatenate(rows, axis=0).astype(jnp.bfloat16)
    out_ref[pl.ds(0, 2 * count), :] = white
    out_ref[pl.ds(2 * count, 16), :] = weights


def stack(sizes, block, half, locals_refs, source_refs, wide_weight, local, real_x, imag_x, packed):
    stations, bands, seg, pol, lags = sizes
    pairs = stations * stations
    row_index = lax.broadcasted_iota(jnp.int32, (16, LANES), 0)
    diagonal = lax.broadcasted_iota(jnp.int32, (pairs, LANES), 0) == lax.broadcasted_iota(
        jnp.int32, (pairs, LANES), 1
    )
    ones = jnp.ones((LANES, LANES), jnp.bfloat16)
    for g in range(seg):
        flags = locals_refs[g][pl.ds(2 * stations * bands, 16), :].astype(jnp.float32)
        flags = jnp.sum(jnp.where(row_index == block, flags, 0.0), axis=0, keepdims=True)
        spread = jnp.where(diagonal, flags, 0.0).astype(jnp.bfloat16)
        wide_weight[g] = jnp.dot(spread, ones, preferred_element_type=jnp.float32)

    lag_block = lax.axis_index("seg") * pol + lax.axis_index("pol")
    row = half * bands + lax.broadcasted_iota(jnp.int32, (bands, LANES), 0)
    bin_index = row * LANES + lax.broadcasted_iota(jnp.int32, (bands, LANES), 1)
    cosine, sine = turn(bin_index * (2 * lags * lag_block + lags - 1), 2 * lags * seg * pol)
    for g in range(seg):
        for j in range(stations):
            tile = locals_refs[g][pl.ds(j * 16, 16), :].astype(jnp.float32)
            local[g, j, 0] = tile[:8] * cosine + tile[8:] * sine
            local[g, j, 1] = tile[8:] * cosine - tile[:8] * sine

    def one_source(a, carry):
        start = pl.multiple_of(a * 16, 16)
        tiles = [source_refs[g][pl.ds(start, 16), :].astype(jnp.float32) for g in range(seg)]
        for j in range(stations):
            pair = a * stations + j
            real_sum = imag_sum = None
            for g in range(seg):
                weight = jnp.broadcast_to(wide_weight[g, pl.ds(pair, 1), :], (8, LANES))
                real_src = tiles[g][:8] * weight
                imag_src = tiles[g][8:] * weight
                real_loc = local[g, j, 0]
                imag_loc = local[g, j, 1]
                real_term = real_src * real_loc + imag_src * imag_loc
                imag_term = imag_src * real_loc - real_src * imag_loc
                real_sum = real_term if g == 0 else real_sum + real_term
                imag_sum = imag_term if g == 0 else imag_sum + imag_term
            at = pl.ds(pl.multiple_of(pair * 8, 8), 8)
            real_x[at, :] = real_sum
            imag_x[at, :] = imag_sum
        return carry

    lax.fori_loop(0, stations, one_source, 0)
    for band in range(bands):
        at = pl.ds(band * LANES, LANES)
        packed[0, :, at] = real_x[pl.ds(band, pairs, stride=8), :].astype(jnp.bfloat16)
        packed[1, :, at] = imag_x[pl.ds(band, pairs, stride=8), :].astype(jnp.bfloat16)


def unfold(even, odd):
    half = even.shape[1]
    after = even - odd
    before = even + odd
    if half % LANES:
        flip = lax.broadcasted_iota(jnp.int32, (half, half), 0) + lax.broadcasted_iota(
            jnp.int32, (half, half), 1
        )
        flip = (flip == half - 1).astype(jnp.float32)
        before = jnp.dot(before, flip, precision=lax.Precision.HIGHEST, preferred_element_type=jnp.float32)
        return jnp.concatenate([before, after], axis=1)
    index = LANES - 1 - lax.broadcasted_iota(jnp.int32, (even.shape[0], LANES), 1)
    runs = [before[:, n * LANES : (n + 1) * LANES] for n in reversed(range(half // LANES))]
    runs = [jnp.take_along_axis(run, index, axis=1, mode="promise_in_bounds") for run in runs]
    return jnp.concatenate(runs + [after], axis=1)


def stack_kernel(sizes, piece, halves, pieces, *refs):
    stations, bands, seg, sta, pol, blocks, lags = sizes
    own_first = sta == blocks
    complete = halves[-1] == pol - 1
    final = complete and piece == pieces - 1
    refs = list(refs)
    plan_ref = refs.pop(0) if final else None
    table_hbm = refs.pop(0)
    spectra = [([refs.pop(0) for _ in range(seg)], [refs.pop(0) for _ in range(seg)]) for _ in halves]
    others = [refs.pop(0) for _ in range(piece if final else 0)]
    sums = refs.pop(0) if halves[0] else None
    out_ref = refs.pop(0)
    tables, result, wide_weight, local, real_x, imag_x, packed, sems, out_sems = refs
    me = lax.axis_index("sta")
    block = me ^ piece if own_first else piece

    copies = []
    for n, distance in enumerate(halves):
        half = lax.axis_index("pol") ^ distance
        copies.append(pltpu.make_async_copy(table_hbm.at[half], tables.at[n], sems.at[n]))
        copies[-1].start()
    if final:
        chosen = [plan_ref[step] ^ me if own_first else step for step in range(STEPS)]
        for step in range(STEPS):
            for n, other in enumerate(others):

                @pl.when(chosen[step] == n)
                def _():
                    pltpu.make_async_copy(other, out_ref.at[step], out_sems.at[step]).start()

    even = odd = None
    for n, (locals_refs, source_refs) in enumerate(spectra):
        half = lax.axis_index("pol") ^ halves[n]
        stack(
            (stations, bands, seg, pol, lags), block, half, locals_refs, source_refs,
            wide_weight, local, real_x, imag_x, packed,
        )
        copies[n].wait()
        even_term = jnp.dot(packed[0], tables[n, 0], preferred_element_type=jnp.float32)
        odd_term = jnp.dot(packed[1], tables[n, 1], preferred_element_type=jnp.float32)
        even = even_term if even is None else even + even_term
        odd = odd_term if odd is None else odd + odd_term
    if sums is not None:
        even = even + sums[0]
        odd = odd + sums[1]
    if not complete:
        out_ref[0] = even
        out_ref[1] = odd
    elif not final:
        out_ref[...] = unfold(even, odd)
    else:
        result[...] = unfold(even, odd)
        for step in range(STEPS):

            @pl.when(chosen[step] == piece)
            def _():
                pltpu.make_async_copy(result, out_ref.at[step], out_sems.at[step]).start()

        for step in range(STEPS):
            pltpu.make_async_copy(result, out_ref.at[step], out_sems.at[step]).wait()


def exchange(value, axis, distance):
    size = lax.axis_size(axis)
    return lax.ppermute(value, axis, [(i ^ distance, i) for i in range(size)]) if distance else value


def shards(table, raw_spectra, owner_plan, pair_valid, quality):
    seg, sta, pol = (lax.axis_size(name) for name in ("seg", "sta", "pol"))
    _, stations, _, bins = raw_spectra.shape
    bands = bins // BAND
    blocks = min(sta, STEPS)
    pairs = stations * stations
    half_lags = table.shape[3]
    lags = 2 * half_lags
    rows = 2 * stations * bands + 16
    sizes = (stations, bands, seg, sta, pol, blocks, lags)

    raw = raw_spectra.reshape(stations, 2, bands, BAND).transpose(0, 2, 1, 3).reshape(-1, BAND)
    vmem = pl.BlockSpec(memory_space=pltpu.VMEM)
    smem = pl.BlockSpec(memory_space=pltpu.SMEM)
    hbm = pl.BlockSpec(memory_space=pltpu.HBM)
    plan = [] if sta == blocks else [owner_plan]
    payload = pl.pallas_call(
        functools.partial(prepare_kernel, (stations, bands, sta, blocks)),
        out_shape=jax.ShapeDtypeStruct((rows, LANES), jnp.bfloat16),
        in_specs=[smem] * len(plan) + [vmem, vmem, vmem],
        out_specs=vmem,
        scratch_shapes=[pltpu.VMEM((2 * stations * bands, LANES), jnp.float32)],
        name="prepare",
    )(*plan, raw, jnp.transpose(pair_valid[0]), quality)

    mine = [exchange(payload, "seg", g) for g in range(seg)]
    if sta == blocks:
        sources = [[exchange(x, "sta", distance) for x in mine] for distance in range(sta)]
    else:
        gathered = lax.all_gather(jnp.stack(mine), "sta")
        chosen = [gathered[owner_plan[k]] for k in range(blocks)]
        sources = [[x[g] for g in range(seg)] for x in chosen]

    done = []
    for piece in range(blocks):
        last = piece == blocks - 1
        sums = []
        for halves in [(h,) for h in range(pol)] if last else [tuple(range(pol))]:
            complete = halves[-1] == pol - 1
            final = last and complete
            spectra = []
            for h in halves:
                spectra += [exchange(x, "pol", h) for x in mine]
                spectra += [exchange(x, "pol", h) for x in sources[piece]]
            others = done if final else []
            if final:
                out_shape = (STEPS, pairs, lags)
            else:
                out_shape = (pairs, lags) if complete else (2, pairs, half_lags)
            flops = 2 * pairs * 2 * bins * lags * len(halves)
            result = pl.pallas_call(
                functools.partial(stack_kernel, sizes, piece, halves, blocks),
                out_shape=jax.ShapeDtypeStruct(out_shape, jnp.float32),
                in_specs=[smem] * final + [hbm] + [vmem] * len(spectra) + [hbm] * len(others) + [vmem] * len(sums),
                out_specs=hbm if final else vmem,
                scratch_shapes=[
                    pltpu.VMEM((len(halves), 2, bins, half_lags), jnp.bfloat16),
                    pltpu.VMEM((pairs, lags), jnp.float32),
                    pltpu.VMEM((seg, pairs, LANES), jnp.float32),
                    pltpu.VMEM((seg, stations, 2, 8, LANES), jnp.float32),
                    pltpu.VMEM((pairs * 8, LANES), jnp.float32),
                    pltpu.VMEM((pairs * 8, LANES), jnp.float32),
                    pltpu.VMEM((2, pairs, bins), jnp.bfloat16),
                    pltpu.SemaphoreType.DMA((len(halves),)),
                    pltpu.SemaphoreType.DMA((STEPS,)),
                ],
                compiler_params=pltpu.CompilerParams(vmem_limit_bytes=52 * 1024 * 1024),
                cost_estimate=pl.CostEstimate(
                    flops=16 * flops, bytes_accessed=1024 * 1024 * len(halves), transcendentals=0
                ),
                name="stack",
            )(*([owner_plan] if final else []), table, *spectra, *others, *sums)
            sums = [result]
        done.append(result)
        if not last:
            sources[piece + 1], done[-1] = lax.optimization_barrier((sources[piece + 1], result))
    return result.reshape(STEPS, stations, stations, lags)


def solution(mesh):
    placed = (
        P(("groups", "seg"), "sta", None, "pol"),
        P("groups"),
        P(("groups", "seg"), None, "sta"),
        P(("groups", "seg"), None),
    )

    def whole(raw_spectra, owner_plan, pair_valid, quality):
        seg, pol = mesh.shape["seg"], mesh.shape["pol"]
        bins = raw_spectra.shape[3]
        segments = raw_spectra.shape[0] // mesh.shape["groups"]
        lag_blocks = seg * pol
        table = lag_table(2 * bins // lag_blocks, bins, pol, 1.0 / math.sqrt(bins * segments))
        return jax.shard_map(
            shards,
            mesh=mesh,
            in_specs=(P(),) + placed,
            out_specs=P("groups", None, "sta", ("seg", "pol")),
            check_vma=False,
        )(jnp.asarray(table), raw_spectra, owner_plan, pair_valid, quality)

    return whole
```

```python
import functools
import math

import jax
import jax.numpy as jnp
import numpy as np
from jax import lax
from jax.experimental import pallas as pl
from jax.experimental.pallas import tpu as pltpu
from jax.sharding import PartitionSpec as P

STEPS = 3
BAND = 128
LANES = 128
VMEM_BYTES = 32 * 1024 * 1024


def lag_table(lags, bins, halves, scale):
    bin_index = np.arange(bins, dtype=np.int64)
    lag = 2 * np.arange(lags // 2, dtype=np.int64) + 1
    phase = (bin_index[:, None] * lag[None, :]) % (4 * bins)
    angle = phase * (2.0 * math.pi / (4 * bins))
    factor = np.where(bin_index == 0, 1.0, 2.0)[:, None] * scale
    parts = np.stack([np.cos(angle) * factor, np.sin(angle) * factor])
    parts = parts.reshape(2, halves, bins // halves, lags // 2).transpose(1, 0, 2, 3)
    return parts.astype(jnp.bfloat16)


def turn(count, period):
    count = count % period
    quarter = (count + period // 8) // (period // 4)
    x = (count - quarter * (period // 4)).astype(jnp.float32) * (2.0 * math.pi / period)
    y = x * x
    sine = x * (1.0 + y * (-1 / 6 + y * (1 / 120 + y * (-1 / 5040 + y * (1 / 362880)))))
    cosine = 1.0 + y * (-1 / 2 + y * (1 / 24 + y * (-1 / 720 + y * (1 / 40320))))
    quarter = quarter % 4
    odd = quarter % 2 == 1
    real = jnp.where(odd, sine, cosine)
    imag = jnp.where(odd, cosine, sine)
    real = jnp.where((quarter == 1) | (quarter == 2), -real, real)
    imag = jnp.where(quarter >= 2, -imag, imag)
    return real, imag


def prepare_kernel(sizes, *refs):
    stations, bands, sta, blocks = sizes
    *plan, raw_ref, valid_ref, quality_ref, out_ref, wide = refs
    total = stations * sta
    me = lax.axis_index("sta")
    wide[...] = raw_ref[...].astype(jnp.float32)
    count = stations * bands
    real = wide[pl.ds(0, count, stride=2), :]
    imag = wide[pl.ds(1, count, stride=2), :]
    power = jnp.sum(real * real + imag * imag, axis=1, keepdims=True) * (1.0 / (2 * BAND))
    inverse = 1.0 / jnp.sqrt(power + 1e-06)
    real = (real * inverse).reshape(stations, bands, LANES)
    imag = (imag * inverse).reshape(stations, bands, LANES)
    white = jnp.concatenate([real, imag], axis=1).reshape(2 * count, LANES).astype(jnp.bfloat16)

    valid = valid_ref[...].astype(jnp.float32).astype(jnp.bfloat16)
    quality = jnp.broadcast_to(quality_ref[...].astype(jnp.float32), (8, total)).astype(jnp.bfloat16)
    pair = lax.broadcasted_iota(jnp.int32, (total, LANES), 1)
    station = lax.broadcasted_iota(jnp.int32, (total, LANES), 0)
    mine = lax.broadcasted_iota(jnp.int32, (stations, LANES), 0) == (
        lax.broadcasted_iota(jnp.int32, (stations, LANES), 1) % stations
    )
    dot = functools.partial(jnp.dot, preferred_element_type=jnp.float32)
    pick_local = (station == me * stations + pair % stations).astype(jnp.float32).astype(jnp.bfloat16)
    local_flags = dot(quality, pick_local)
    rows = []
    for k in range(blocks):
        source = (plan[0][k] if plan else k) * stations + pair // stations
        pick_source = (station == source).astype(jnp.float32).astype(jnp.bfloat16)
        valid_row = jnp.sum(jnp.where(mine, dot(valid, pick_source), 0.0), axis=0, keepdims=True)
        rows.append(valid_row * (dot(quality, pick_source) * local_flags)[:1])
    rows.append(jnp.zeros((16 - blocks, LANES), jnp.float32))
    weights = jnp.concatenate(rows, axis=0).astype(jnp.bfloat16)
    out_ref[pl.ds(0, 2 * count), :] = white
    out_ref[pl.ds(2 * count, 16), :] = weights


def stack(sizes, block, half, locals_ref, source_ref, wide_weight, local, real_x, imag_x, packed):
    stations, bands, seg, pol, lags = sizes
    pairs = stations * stations
    row_index = lax.broadcasted_iota(jnp.int32, (16, LANES), 0)
    diagonal = lax.broadcasted_iota(jnp.int32, (pairs, LANES), 0) == lax.broadcasted_iota(
        jnp.int32, (pairs, LANES), 1
    )
    ones = jnp.ones((LANES, LANES), jnp.bfloat16)
    for g in range(seg):
        flags = locals_ref[g, pl.ds(2 * stations * bands, 16), :].astype(jnp.float32)
        flags = jnp.sum(jnp.where(row_index == block, flags, 0.0), axis=0, keepdims=True)
        spread = jnp.where(diagonal, flags, 0.0).astype(jnp.bfloat16)
        wide_weight[g] = jnp.dot(spread, ones, preferred_element_type=jnp.float32)

    lag_block = lax.axis_index("seg") * pol + lax.axis_index("pol")
    row = half * bands + lax.broadcasted_iota(jnp.int32, (bands, LANES), 0)
    bin_index = row * LANES + lax.broadcasted_iota(jnp.int32, (bands, LANES), 1)
    cosine, sine = turn(bin_index * (2 * lags * lag_block + lags - 1), 2 * lags * seg * pol)
    for g in range(seg):
        for j in range(stations):
            tile = locals_ref[g, pl.ds(j * 16, 16), :].astype(jnp.float32)
            local[g, j, 0] = tile[:8] * cosine + tile[8:] * sine
            local[g, j, 1] = tile[8:] * cosine - tile[:8] * sine

    def one_source(a, carry):
        start = pl.multiple_of(a * 16, 16)
        tiles = [source_ref[g, pl.ds(start, 16), :].astype(jnp.float32) for g in range(seg)]
        for j in range(stations):
            pair = a * stations + j
            real_sum = imag_sum = None
            for g in range(seg):
                weight = jnp.broadcast_to(wide_weight[g, pl.ds(pair, 1), :], (8, LANES))
                real_src = tiles[g][:8] * weight
                imag_src = tiles[g][8:] * weight
                real_loc = local[g, j, 0]
                imag_loc = local[g, j, 1]
                real_term = real_src * real_loc + imag_src * imag_loc
                imag_term = imag_src * real_loc - real_src * imag_loc
                real_sum = real_term if g == 0 else real_sum + real_term
                imag_sum = imag_term if g == 0 else imag_sum + imag_term
            at = pl.ds(pl.multiple_of(pair * 8, 8), 8)
            real_x[at, :] = real_sum
            imag_x[at, :] = imag_sum
        return carry

    lax.fori_loop(0, stations, one_source, 0)
    for band in range(bands):
        at = pl.ds(band * LANES, LANES)
        packed[0, :, at] = real_x[pl.ds(band, pairs, stride=8), :].astype(jnp.bfloat16)
        packed[1, :, at] = imag_x[pl.ds(band, pairs, stride=8), :].astype(jnp.bfloat16)


def unfold(even, odd):
    half = even.shape[1]
    after = even - odd
    before = even + odd
    if half % LANES:
        flip = lax.broadcasted_iota(jnp.int32, (half, half), 0) + lax.broadcasted_iota(
            jnp.int32, (half, half), 1
        )
        flip = (flip == half - 1).astype(jnp.float32)
        before = jnp.dot(before, flip, precision=lax.Precision.HIGHEST, preferred_element_type=jnp.float32)
        return jnp.concatenate([before, after], axis=1)
    index = LANES - 1 - lax.broadcasted_iota(jnp.int32, (even.shape[0], LANES), 1)
    runs = [before[:, n * LANES : (n + 1) * LANES] for n in reversed(range(half // LANES))]
    runs = [jnp.take_along_axis(run, index, axis=1, mode="promise_in_bounds") for run in runs]
    return jnp.concatenate(runs + [after], axis=1)


def stack_kernel(sizes, piece, halves, pieces, *refs):
    stations, bands, seg, sta, pol, blocks, lags = sizes
    own_first = sta == blocks
    complete = halves[-1] == pol - 1
    final = complete and piece == pieces - 1
    refs = list(refs)
    plan_ref = refs.pop(0) if final else None
    table = refs.pop(0)
    spectra = [(refs.pop(0), refs.pop(0)) for _ in halves]
    others = [refs.pop(0) for _ in range(piece if final else 0)]
    sums = refs.pop(0) if halves[0] else None
    out_ref = refs.pop(0)
    result, wide_weight, local, real_x, imag_x, packed, out_sems = refs
    me = lax.axis_index("sta")
    block = me ^ piece if own_first else piece

    if final:
        chosen = [plan_ref[step] ^ me if own_first else step for step in range(STEPS)]
        for step in range(STEPS):
            for n, other in enumerate(others):

                @pl.when(chosen[step] == n)
                def _():
                    pltpu.make_async_copy(other, out_ref.at[step], out_sems.at[step]).start()

    even = odd = None
    for n, (locals_ref, source_ref) in enumerate(spectra):
        half = lax.axis_index("pol") ^ halves[n]
        stack(
            (stations, bands, seg, pol, lags), block, half, locals_ref, source_ref,
            wide_weight, local, real_x, imag_x, packed,
        )
        even_term = jnp.dot(packed[0], table[half, 0], preferred_element_type=jnp.float32)
        odd_term = jnp.dot(packed[1], table[half, 1], preferred_element_type=jnp.float32)
        even = even_term if even is None else even + even_term
        odd = odd_term if odd is None else odd + odd_term
    if sums is not None:
        even = even + sums[0]
        odd = odd + sums[1]
    if not complete:
        out_ref[0] = even
        out_ref[1] = odd
    elif not final:
        out_ref[...] = unfold(even, odd)
    else:
        result[...] = unfold(even, odd)
        for step in range(STEPS):

            @pl.when(chosen[step] == piece)
            def _():
                pltpu.make_async_copy(result, out_ref.at[step], out_sems.at[step]).start()

        for step in range(STEPS):
            pltpu.make_async_copy(result, out_ref.at[step], out_sems.at[step]).wait()


def fetch_kernel(table_hbm, payload_hbm, table_ref, payload_ref, sems):
    copies = [
        pltpu.make_async_copy(table_hbm, table_ref, sems.at[0]),
        pltpu.make_async_copy(payload_hbm, payload_ref, sems.at[1]),
    ]
    for copy in copies:
        copy.start()
    for copy in copies:
        copy.wait()


def join_kernel(*refs):
    *pieces, out_ref = refs
    for n, piece in enumerate(pieces):
        out_ref[n] = piece[...]


def exchange(value, axis, distance):
    size = lax.axis_size(axis)
    return lax.ppermute(value, axis, [(i ^ distance, i) for i in range(size)]) if distance else value


def shards(table, raw_spectra, owner_plan, pair_valid, quality):
    seg, sta, pol = (lax.axis_size(name) for name in ("seg", "sta", "pol"))
    _, stations, _, bins = raw_spectra.shape
    bands = bins // BAND
    blocks = min(sta, STEPS)
    pairs = stations * stations
    half_lags = table.shape[3]
    lags = 2 * half_lags
    rows = 2 * stations * bands + 16
    sizes = (stations, bands, seg, sta, pol, blocks, lags)

    raw = raw_spectra.reshape(stations, 2, bands, BAND).transpose(0, 2, 1, 3).reshape(-1, BAND)
    vmem = pl.BlockSpec(memory_space=pltpu.VMEM)
    smem = pl.BlockSpec(memory_space=pltpu.SMEM)
    hbm = pl.BlockSpec(memory_space=pltpu.HBM)
    plan = [] if sta == blocks else [owner_plan]
    payload = pl.pallas_call(
        functools.partial(prepare_kernel, (stations, bands, sta, blocks)),
        out_shape=jax.ShapeDtypeStruct((rows, LANES), jnp.bfloat16),
        in_specs=[smem] * len(plan) + [vmem, vmem, vmem],
        out_specs=vmem,
        scratch_shapes=[pltpu.VMEM((2 * stations * bands, LANES), jnp.float32)],
        name="prepare",
    )(*plan, raw, jnp.transpose(pair_valid[0]), quality)

    table, near = pl.pallas_call(
        fetch_kernel,
        out_shape=[jax.ShapeDtypeStruct(x.shape, x.dtype) for x in (table, payload)],
        in_specs=[hbm, hbm],
        out_specs=[vmem, vmem],
        scratch_shapes=[pltpu.SemaphoreType.DMA((2,))],
        compiler_params=pltpu.CompilerParams(vmem_limit_bytes=VMEM_BYTES),
        cost_estimate=pl.CostEstimate(flops=0, bytes_accessed=2 * table.size * 2, transcendentals=0),
        name="fetch",
    )(table, payload)

    held = {0: payload}
    distance = seg // 2
    while distance:
        held.update({g ^ distance: exchange(x, "seg", distance) for g, x in held.items()})
        distance //= 2
    mine = pl.pallas_call(
        join_kernel,
        out_shape=jax.ShapeDtypeStruct((seg, rows, LANES), jnp.bfloat16),
        in_specs=[vmem] * seg,
        out_specs=vmem,
        compiler_params=pltpu.CompilerParams(vmem_limit_bytes=VMEM_BYTES),
        name="join",
    )(near, *(held[g] for g in range(1, seg)))
    if sta == blocks:
        sources = [exchange(mine, "sta", distance) for distance in range(sta)]
    else:
        gathered = lax.all_gather(mine, "sta")
        sources = [gathered[owner_plan[k]] for k in range(blocks)]

    done = []
    for piece in range(blocks):
        last = piece == blocks - 1
        sums = []
        for halves in [(h,) for h in range(pol)] if last else [tuple(range(pol))]:
            complete = halves[-1] == pol - 1
            final = last and complete
            spectra = []
            for h in halves:
                spectra += [exchange(mine, "pol", h), exchange(sources[piece], "pol", h)]
            others = done if final else []
            if final:
                out_shape = (STEPS, pairs, lags)
            else:
                out_shape = (pairs, lags) if complete else (2, pairs, half_lags)
            flops = 2 * pairs * 2 * bins * lags * len(halves)
            result = pl.pallas_call(
                functools.partial(stack_kernel, sizes, piece, halves, blocks),
                out_shape=jax.ShapeDtypeStruct(out_shape, jnp.float32),
                in_specs=[smem] * final + [vmem] * (1 + len(spectra)) + [hbm] * len(others) + [vmem] * len(sums),
                out_specs=hbm if final else vmem,
                scratch_shapes=[
                    pltpu.VMEM((pairs, lags), jnp.float32),
                    pltpu.VMEM((seg, pairs, LANES), jnp.float32),
                    pltpu.VMEM((seg, stations, 2, 8, LANES), jnp.float32),
                    pltpu.VMEM((pairs * 8, LANES), jnp.float32),
                    pltpu.VMEM((pairs * 8, LANES), jnp.float32),
                    pltpu.VMEM((2, pairs, bins), jnp.bfloat16),
                    pltpu.SemaphoreType.DMA((STEPS,)),
                ],
                compiler_params=pltpu.CompilerParams(vmem_limit_bytes=VMEM_BYTES),
                cost_estimate=pl.CostEstimate(
                    flops=16 * flops, bytes_accessed=1024 * 1024 * len(halves), transcendentals=0
                ),
                name="stack",
            )(*([owner_plan] if final else []), table, *spectra, *others, *sums)
            sums = [result]
        done.append(result)
        if not last:
            sources[piece + 1], done[-1] = lax.optimization_barrier((sources[piece + 1], result))
    return result.reshape(STEPS, stations, stations, lags)


def solution(mesh):
    placed = (
        P(("groups", "seg"), "sta", None, "pol"),
        P("groups"),
        P(("groups", "seg"), None, "sta"),
        P(("groups", "seg"), None),
    )

    def whole(raw_spectra, owner_plan, pair_valid, quality):
        seg, pol = mesh.shape["seg"], mesh.shape["pol"]
        bins = raw_spectra.shape[3]
        segments = raw_spectra.shape[0] // mesh.shape["groups"]
        lag_blocks = seg * pol
        table = lag_table(2 * bins // lag_blocks, bins, pol, 1.0 / math.sqrt(bins * segments))
        return jax.shard_map(
            shards,
            mesh=mesh,
            in_specs=(P(),) + placed,
            out_specs=P("groups", None, "sta", ("seg", "pol")),
            check_vma=False,
        )(jnp.asarray(table), raw_spectra, owner_plan, pair_valid, quality)

    return whole
```

```python
import functools
import math

import jax
import jax.numpy as jnp
import numpy as np
from jax import lax
from jax.experimental import pallas as pl
from jax.experimental.pallas import tpu as pltpu
from jax.sharding import PartitionSpec as P

STEPS = 3
BAND = 128
LANES = 128
VMEM_BYTES = 32 * 1024 * 1024


def lag_table(lags, bins, halves, scale):
    bin_index = np.arange(bins, dtype=np.int64)
    lag = 2 * np.arange(lags // 2, dtype=np.int64) + 1
    phase = (bin_index[:, None] * lag[None, :]) % (4 * bins)
    angle = phase * (2.0 * math.pi / (4 * bins))
    factor = np.where(bin_index == 0, 1.0, 2.0)[:, None] * scale
    parts = np.stack([np.cos(angle) * factor, np.sin(angle) * factor])
    parts = parts.reshape(2, halves, bins // halves, lags // 2).transpose(1, 0, 2, 3)
    return parts.astype(jnp.bfloat16)


def turn(count, period):
    count = count % period
    quarter = (count + period // 8) // (period // 4)
    x = (count - quarter * (period // 4)).astype(jnp.float32) * (2.0 * math.pi / period)
    y = x * x
    sine = x * (1.0 + y * (-1 / 6 + y * (1 / 120 + y * (-1 / 5040 + y * (1 / 362880)))))
    cosine = 1.0 + y * (-1 / 2 + y * (1 / 24 + y * (-1 / 720 + y * (1 / 40320))))
    quarter = quarter % 4
    odd = quarter % 2 == 1
    real = jnp.where(odd, sine, cosine)
    imag = jnp.where(odd, cosine, sine)
    real = jnp.where((quarter == 1) | (quarter == 2), -real, real)
    imag = jnp.where(quarter >= 2, -imag, imag)
    return real, imag


def prepare_kernel(sizes, *refs):
    stations, bands, sta, blocks = sizes
    *plan, raw_ref, valid_ref, quality_ref, out_ref, wide = refs
    total = stations * sta
    me = lax.axis_index("sta")
    wide[...] = raw_ref[...].astype(jnp.float32)
    count = stations * bands
    real = wide[pl.ds(0, count, stride=2), :]
    imag = wide[pl.ds(1, count, stride=2), :]
    power = jnp.sum(real * real + imag * imag, axis=1, keepdims=True) * (1.0 / (2 * BAND))
    inverse = 1.0 / jnp.sqrt(power + 1e-06)
    real = (real * inverse).reshape(stations, bands, LANES)
    imag = (imag * inverse).reshape(stations, bands, LANES)
    white = jnp.concatenate([real, imag], axis=1).reshape(2 * count, LANES).astype(jnp.bfloat16)

    valid = valid_ref[...].astype(jnp.float32).astype(jnp.bfloat16)
    quality = jnp.broadcast_to(quality_ref[...].astype(jnp.float32), (8, total)).astype(jnp.bfloat16)
    pair = lax.broadcasted_iota(jnp.int32, (total, LANES), 1)
    station = lax.broadcasted_iota(jnp.int32, (total, LANES), 0)
    mine = lax.broadcasted_iota(jnp.int32, (stations, LANES), 0) == (
        lax.broadcasted_iota(jnp.int32, (stations, LANES), 1) % stations
    )
    dot = functools.partial(jnp.dot, preferred_element_type=jnp.float32)
    pick_local = (station == me * stations + pair % stations).astype(jnp.float32).astype(jnp.bfloat16)
    local_flags = dot(quality, pick_local)
    rows = []
    for k in range(blocks):
        source = (plan[0][k] if plan else k) * stations + pair // stations
        pick_source = (station == source).astype(jnp.float32).astype(jnp.bfloat16)
        valid_row = jnp.sum(jnp.where(mine, dot(valid, pick_source), 0.0), axis=0, keepdims=True)
        rows.append(valid_row * (dot(quality, pick_source) * local_flags)[:1])
    rows.append(jnp.zeros((16 - blocks, LANES), jnp.float32))
    weights = jnp.concatenate(rows, axis=0).astype(jnp.bfloat16)
    out_ref[pl.ds(0, 2 * count), :] = white
    out_ref[pl.ds(2 * count, 16), :] = weights


def stack(sizes, half, spectra, wide_weight, local, real_x, imag_x, packed):
    stations, bands, seg, sta, pol, blocks, lags = sizes
    own_first = sta == blocks
    pairs = stations * stations
    me = lax.axis_index("sta")
    row_index = lax.broadcasted_iota(jnp.int32, (16, LANES), 0)
    diagonal = lax.broadcasted_iota(jnp.int32, (pairs, LANES), 0) == lax.broadcasted_iota(
        jnp.int32, (pairs, LANES), 1
    )
    ones = jnp.ones((LANES, LANES), jnp.bfloat16)
    for g in range(seg):
        flags = spectra[g, pl.ds(2 * stations * bands, 16), :].astype(jnp.float32)
        spread = []
        for n in range(blocks):
            block = me ^ n if own_first else n
            row = jnp.sum(jnp.where(row_index == block, flags, 0.0), axis=0, keepdims=True)
            spread.append(jnp.where(diagonal, row, 0.0))
        spread = jnp.concatenate(spread, axis=0).astype(jnp.bfloat16)
        wide_weight[g] = jnp.dot(spread, ones, preferred_element_type=jnp.float32)

    lag_block = lax.axis_index("seg") * pol + lax.axis_index("pol")
    row = half * bands + lax.broadcasted_iota(jnp.int32, (bands, LANES), 0)
    bin_index = row * LANES + lax.broadcasted_iota(jnp.int32, (bands, LANES), 1)
    cosine, sine = turn(bin_index * (2 * lags * lag_block + lags - 1), 2 * lags * seg * pol)
    for g in range(seg):
        for j in range(stations):
            tile = spectra[g, pl.ds(j * 16, 16), :].astype(jnp.float32)
            local[g, j, 0] = tile[:8] * cosine + tile[8:] * sine
            local[g, j, 1] = tile[8:] * cosine - tile[:8] * sine

    def one_source(a, carry):
        start = pl.multiple_of(a % stations * 16, 16)
        held = (a // stations + (0 if own_first else 1)) * seg
        tiles = [spectra[held + g, pl.ds(start, 16), :].astype(jnp.float32) for g in range(seg)]
        for j in range(stations):
            pair = a * stations + j
            real_sum = imag_sum = None
            for g in range(seg):
                weight = jnp.broadcast_to(wide_weight[g, pl.ds(pair, 1), :], (8, LANES))
                real_src = tiles[g][:8] * weight
                imag_src = tiles[g][8:] * weight
                real_loc = local[g, j, 0]
                imag_loc = local[g, j, 1]
                real_term = real_src * real_loc + imag_src * imag_loc
                imag_term = imag_src * real_loc - real_src * imag_loc
                real_sum = real_term if g == 0 else real_sum + real_term
                imag_sum = imag_term if g == 0 else imag_sum + imag_term
            at = pl.ds(pl.multiple_of(pair * 8, 8), 8)
            real_x[at, :] = real_sum
            imag_x[at, :] = imag_sum
        return carry

    lax.fori_loop(0, blocks * stations, one_source, 0)
    for band in range(bands):
        at = pl.ds(band * LANES, LANES)
        rows = pl.ds(band, blocks * pairs, stride=8)
        packed[0, :, at] = real_x[rows, :].astype(jnp.bfloat16)
        packed[1, :, at] = imag_x[rows, :].astype(jnp.bfloat16)


def unfold(even, odd):
    half = even.shape[1]
    after = even - odd
    before = even + odd
    if half % LANES:
        flip = lax.broadcasted_iota(jnp.int32, (half, half), 0) + lax.broadcasted_iota(
            jnp.int32, (half, half), 1
        )
        flip = (flip == half - 1).astype(jnp.float32)
        before = jnp.dot(before, flip, precision=lax.Precision.HIGHEST, preferred_element_type=jnp.float32)
        return jnp.concatenate([before, after], axis=1)
    index = LANES - 1 - lax.broadcasted_iota(jnp.int32, (even.shape[0], LANES), 1)
    runs = [before[:, n * LANES : (n + 1) * LANES] for n in reversed(range(half // LANES))]
    runs = [jnp.take_along_axis(run, index, axis=1, mode="promise_in_bounds") for run in runs]
    return jnp.concatenate(runs + [after], axis=1)


def stack_kernel(sizes, distance, *refs):
    stations, bands, seg, sta, pol, blocks, lags = sizes
    first, last = distance == 0, distance == pol - 1
    refs = list(refs)
    plan_ref = refs.pop(0) if last else None
    table, spectra = refs.pop(0), refs.pop(0)
    sums = None if first else refs.pop(0)
    out_ref, result, wide_weight, local, real_x, imag_x, packed, sems = refs
    half = lax.axis_index("pol") ^ distance
    stack(sizes, half, spectra, wide_weight, local, real_x, imag_x, packed)
    even = jnp.dot(packed[0], table[half, 0], preferred_element_type=jnp.float32)
    odd = jnp.dot(packed[1], table[half, 1], preferred_element_type=jnp.float32)
    if not first:
        even = even + sums[0]
        odd = odd + sums[1]
    if not last:
        out_ref[0] = even
        out_ref[1] = odd
        return
    pairs = stations * stations
    result[...] = unfold(even, odd).reshape(blocks, pairs, lags)
    copies = []
    for step in range(STEPS):
        block = plan_ref[step] ^ lax.axis_index("sta") if sta == blocks else step
        copies.append(pltpu.make_async_copy(result.at[block], out_ref.at[step], sems.at[step]))
        copies[-1].start()
    for copy in copies:
        copy.wait()


def fetch_kernel(table_hbm, payload_hbm, table_ref, payload_ref, sems):
    copies = [
        pltpu.make_async_copy(table_hbm, table_ref, sems.at[0]),
        pltpu.make_async_copy(payload_hbm, payload_ref, sems.at[1]),
    ]
    for copy in copies:
        copy.start()
    for copy in copies:
        copy.wait()


def join_kernel(*refs):
    *pieces, out_ref = refs
    first = 0
    for piece in pieces:
        out_ref[pl.ds(first, piece.shape[0])] = piece[...]
        first += piece.shape[0]


def join(*pieces):
    vmem = pl.BlockSpec(memory_space=pltpu.VMEM)
    shape = (sum(piece.shape[0] for piece in pieces),) + pieces[0].shape[1:]
    return pl.pallas_call(
        join_kernel,
        out_shape=jax.ShapeDtypeStruct(shape, pieces[0].dtype),
        in_specs=[vmem] * len(pieces),
        out_specs=vmem,
        compiler_params=pltpu.CompilerParams(vmem_limit_bytes=VMEM_BYTES),
        name="join",
    )(*pieces)


def exchange(value, axes, steps):
    if isinstance(axes, str):
        axes, steps = (axes,), (steps,)
    if not any(steps):
        return value
    sizes = tuple(lax.axis_size(axis) for axis in axes)
    pairs = []
    for index in np.ndindex(*sizes):
        source = tuple(i ^ step for i, step in zip(index, steps))
        pairs.append((int(np.ravel_multi_index(source, sizes)), int(np.ravel_multi_index(index, sizes))))
    return lax.ppermute(value, axes, pairs)


def shards(table, raw_spectra, owner_plan, pair_valid, quality):
    seg, sta, pol = (lax.axis_size(name) for name in ("seg", "sta", "pol"))
    _, stations, _, bins = raw_spectra.shape
    bands = bins // BAND
    blocks = min(sta, STEPS)
    pairs = stations * stations
    half_lags = table.shape[3]
    lags = 2 * half_lags
    rows = 2 * stations * bands + 16
    sizes = (stations, bands, seg, sta, pol, blocks, lags)

    raw = raw_spectra.reshape(stations, 2, bands, BAND).transpose(0, 2, 1, 3).reshape(-1, BAND)
    vmem = pl.BlockSpec(memory_space=pltpu.VMEM)
    smem = pl.BlockSpec(memory_space=pltpu.SMEM)
    hbm = pl.BlockSpec(memory_space=pltpu.HBM)
    plan = [] if sta == blocks else [owner_plan]
    payload = pl.pallas_call(
        functools.partial(prepare_kernel, (stations, bands, sta, blocks)),
        out_shape=jax.ShapeDtypeStruct((rows, LANES), jnp.bfloat16),
        in_specs=[smem] * len(plan) + [vmem, vmem, vmem],
        out_specs=vmem,
        scratch_shapes=[pltpu.VMEM((2 * stations * bands, LANES), jnp.float32)],
        name="prepare",
    )(*plan, raw, jnp.transpose(pair_valid[0]), quality)

    table, near = pl.pallas_call(
        fetch_kernel,
        out_shape=[jax.ShapeDtypeStruct(x.shape, x.dtype) for x in (table, payload)],
        in_specs=[hbm, hbm],
        out_specs=[vmem, vmem],
        scratch_shapes=[pltpu.SemaphoreType.DMA((2,))],
        compiler_params=pltpu.CompilerParams(vmem_limit_bytes=VMEM_BYTES),
        cost_estimate=pl.CostEstimate(flops=0, bytes_accessed=2 * table.size * 2, transcendentals=0),
        name="fetch",
    )(table, payload)

    held = near[None]
    distance = seg // 2
    while distance > 1:
        arrived = exchange(payload[None] if held.shape[0] == 1 else held, "seg", distance)
        held = join(held, arrived)
        distance //= 2
    if sta == 2 and seg > 1:
        steps = [(1, 0), (0, 1), (1, 1)]
        spectra = join(held, *(exchange(held, ("seg", "sta"), step) for step in steps))
    else:
        mine = join(held, exchange(held, "seg", 1)) if seg > 1 else held
        gathered = lax.all_gather(mine, "sta")
        if sta == blocks:
            spectra = join(*(gathered[lax.axis_index("sta") ^ k] for k in range(blocks)))
        else:
            spectra = join(mine, *(gathered[owner_plan[k]] for k in range(blocks)))

    result = None
    for distance in range(pol):
        last = distance == pol - 1
        out_shape = (STEPS, pairs, lags) if last else (2, blocks * pairs, half_lags)
        flops = 2 * blocks * pairs * 2 * bins * lags
        sums = [] if result is None else [result]
        result = pl.pallas_call(
            functools.partial(stack_kernel, sizes, distance),
            out_shape=jax.ShapeDtypeStruct(out_shape, jnp.float32),
            in_specs=[smem] * last + [vmem] * (2 + len(sums)),
            out_specs=hbm if last else vmem,
            scratch_shapes=[
                pltpu.VMEM((blocks, pairs, lags), jnp.float32),
                pltpu.VMEM((seg, blocks * pairs, LANES), jnp.float32),
                pltpu.VMEM((seg, stations, 2, 8, LANES), jnp.float32),
                pltpu.VMEM((blocks * pairs * 8, LANES), jnp.float32),
                pltpu.VMEM((blocks * pairs * 8, LANES), jnp.float32),
                pltpu.VMEM((2, blocks * pairs, bins), jnp.bfloat16),
                pltpu.SemaphoreType.DMA((STEPS,)),
            ],
            compiler_params=pltpu.CompilerParams(vmem_limit_bytes=VMEM_BYTES),
            cost_estimate=pl.CostEstimate(flops=16 * flops, bytes_accessed=1024 * 1024, transcendentals=0),
            name="stack",
        )(*([owner_plan] if last else []), table, exchange(spectra, "pol", distance), *sums)
    return result.reshape(STEPS, stations, stations, lags)


def solution(mesh):
    placed = (
        P(("groups", "seg"), "sta", None, "pol"),
        P("groups"),
        P(("groups", "seg"), None, "sta"),
        P(("groups", "seg"), None),
    )

    def whole(raw_spectra, owner_plan, pair_valid, quality):
        seg, pol = mesh.shape["seg"], mesh.shape["pol"]
        bins = raw_spectra.shape[3]
        segments = raw_spectra.shape[0] // mesh.shape["groups"]
        lag_blocks = seg * pol
        table = lag_table(2 * bins // lag_blocks, bins, pol, 1.0 / math.sqrt(bins * segments))
        return jax.shard_map(
            shards,
            mesh=mesh,
            in_specs=(P(),) + placed,
            out_specs=P("groups", None, "sta", ("seg", "pol")),
            check_vma=False,
        )(jnp.asarray(table), raw_spectra, owner_plan, pair_valid, quality)

    return whole
```

```python
import functools
import math

import jax
import jax.numpy as jnp
import numpy as np
from jax import lax
from jax.experimental import pallas as pl
from jax.experimental.pallas import tpu as pltpu
from jax.sharding import PartitionSpec as P

STEPS = 3
BAND = 128
LANES = 128
VMEM_BYTES = 32 * 1024 * 1024


def lag_table(lags, bins, halves, scale):
    bin_index = np.arange(bins, dtype=np.int64)
    lag = 2 * np.arange(lags // 2, dtype=np.int64) + 1
    phase = (bin_index[:, None] * lag[None, :]) % (4 * bins)
    angle = phase * (2.0 * math.pi / (4 * bins))
    factor = np.where(bin_index == 0, 1.0, 2.0)[:, None] * scale
    parts = np.stack([np.cos(angle) * factor, np.sin(angle) * factor])
    parts = parts.reshape(2, halves, bins // halves, lags // 2).transpose(1, 0, 2, 3)
    return parts.astype(jnp.bfloat16)


def turn(count, period):
    count = count % period
    quarter = (count + period // 8) // (period // 4)
    x = (count - quarter * (period // 4)).astype(jnp.float32) * (2.0 * math.pi / period)
    y = x * x
    sine = x * (1.0 + y * (-1 / 6 + y * (1 / 120 + y * (-1 / 5040 + y * (1 / 362880)))))
    cosine = 1.0 + y * (-1 / 2 + y * (1 / 24 + y * (-1 / 720 + y * (1 / 40320))))
    quarter = quarter % 4
    odd = quarter % 2 == 1
    real = jnp.where(odd, sine, cosine)
    imag = jnp.where(odd, cosine, sine)
    real = jnp.where((quarter == 1) | (quarter == 2), -real, real)
    imag = jnp.where(quarter >= 2, -imag, imag)
    return real, imag


def prepare_kernel(sizes, *refs):
    stations, bands, sta, blocks = sizes
    *plan, raw_ref, valid_ref, quality_ref, out_ref, wide = refs
    total = stations * sta
    me = lax.axis_index("sta")
    wide[...] = raw_ref[...].astype(jnp.float32)
    count = stations * bands
    real = wide[pl.ds(0, count, stride=2), :]
    imag = wide[pl.ds(1, count, stride=2), :]
    power = jnp.sum(real * real + imag * imag, axis=1, keepdims=True) * (1.0 / (2 * BAND))
    inverse = 1.0 / jnp.sqrt(power + 1e-06)
    real = (real * inverse).reshape(stations, bands, LANES)
    imag = (imag * inverse).reshape(stations, bands, LANES)
    white = jnp.concatenate([real, imag], axis=1).reshape(2 * count, LANES).astype(jnp.bfloat16)

    valid = valid_ref[...].astype(jnp.float32).astype(jnp.bfloat16)
    quality = jnp.broadcast_to(quality_ref[...].astype(jnp.float32), (8, total)).astype(jnp.bfloat16)
    pair = lax.broadcasted_iota(jnp.int32, (total, LANES), 1)
    station = lax.broadcasted_iota(jnp.int32, (total, LANES), 0)
    mine = lax.broadcasted_iota(jnp.int32, (stations, LANES), 0) == (
        lax.broadcasted_iota(jnp.int32, (stations, LANES), 1) % stations
    )
    dot = functools.partial(jnp.dot, preferred_element_type=jnp.float32)
    pick_local = (station == me * stations + pair % stations).astype(jnp.float32).astype(jnp.bfloat16)
    local_flags = dot(quality, pick_local)
    rows = []
    for k in range(blocks):
        source = (plan[0][k] if plan else k) * stations + pair // stations
        pick_source = (station == source).astype(jnp.float32).astype(jnp.bfloat16)
        valid_row = jnp.sum(jnp.where(mine, dot(valid, pick_source), 0.0), axis=0, keepdims=True)
        rows.append(valid_row * (dot(quality, pick_source) * local_flags)[:1])
    rows.append(jnp.zeros((16 - blocks, LANES), jnp.float32))
    weights = jnp.concatenate(rows, axis=0).astype(jnp.bfloat16)
    out_ref[pl.ds(0, 2 * count), :] = white
    out_ref[pl.ds(2 * count, 16), :] = weights


def stack(sizes, half, held, locals_ref, sources_ref, wide_weight, local, real_x, imag_x, packed):
    first_block, count, base = held
    stations, bands, seg, sta, pol, blocks, lags = sizes
    own_first = sta == blocks
    pairs = stations * stations
    me = lax.axis_index("sta")
    row_index = lax.broadcasted_iota(jnp.int32, (16, LANES), 0)
    diagonal = lax.broadcasted_iota(jnp.int32, (pairs, LANES), 0) == lax.broadcasted_iota(
        jnp.int32, (pairs, LANES), 1
    )
    ones = jnp.ones((LANES, LANES), jnp.bfloat16)
    for g in range(seg):
        flags = locals_ref[g, pl.ds(2 * stations * bands, 16), :].astype(jnp.float32)
        spread = []
        for n in range(first_block, first_block + count):
            block = me ^ n if own_first else n
            row = jnp.sum(jnp.where(row_index == block, flags, 0.0), axis=0, keepdims=True)
            spread.append(jnp.where(diagonal, row, 0.0))
        spread = jnp.concatenate(spread, axis=0).astype(jnp.bfloat16)
        wide_weight[g] = jnp.dot(spread, ones, preferred_element_type=jnp.float32)

    lag_block = lax.axis_index("seg") * pol + lax.axis_index("pol")
    row = half * bands + lax.broadcasted_iota(jnp.int32, (bands, LANES), 0)
    bin_index = row * LANES + lax.broadcasted_iota(jnp.int32, (bands, LANES), 1)
    cosine, sine = turn(bin_index * (2 * lags * lag_block + lags - 1), 2 * lags * seg * pol)
    for g in range(seg):
        for j in range(stations):
            tile = locals_ref[g, pl.ds(j * 16, 16), :].astype(jnp.float32)
            local[g, j, 0] = tile[:8] * cosine + tile[8:] * sine
            local[g, j, 1] = tile[8:] * cosine - tile[:8] * sine

    def one_source(a, carry):
        start = pl.multiple_of(a % stations * 16, 16)
        begin = base + a // stations * seg
        tiles = [sources_ref[begin + g, pl.ds(start, 16), :].astype(jnp.float32) for g in range(seg)]
        for j in range(stations):
            pair = a * stations + j
            real_sum = imag_sum = None
            for g in range(seg):
                weight = jnp.broadcast_to(wide_weight[g, pl.ds(pair, 1), :], (8, LANES))
                real_src = tiles[g][:8] * weight
                imag_src = tiles[g][8:] * weight
                real_loc = local[g, j, 0]
                imag_loc = local[g, j, 1]
                real_term = real_src * real_loc + imag_src * imag_loc
                imag_term = imag_src * real_loc - real_src * imag_loc
                real_sum = real_term if g == 0 else real_sum + real_term
                imag_sum = imag_term if g == 0 else imag_sum + imag_term
            at = pl.ds(pl.multiple_of(pair * 8, 8), 8)
            real_x[at, :] = real_sum
            imag_x[at, :] = imag_sum
        return carry

    lax.fori_loop(0, count * stations, one_source, 0, unroll=2)
    for band in range(bands):
        at = pl.ds(band * LANES, LANES)
        rows = pl.ds(band, count * pairs, stride=8)
        packed[0, :, at] = real_x[rows, :].astype(jnp.bfloat16)
        packed[1, :, at] = imag_x[rows, :].astype(jnp.bfloat16)


def unfold(even, odd):
    half = even.shape[1]
    after = even - odd
    before = even + odd
    if half % LANES:
        flip = lax.broadcasted_iota(jnp.int32, (half, half), 0) + lax.broadcasted_iota(
            jnp.int32, (half, half), 1
        )
        flip = (flip == half - 1).astype(jnp.float32)
        before = jnp.dot(before, flip, precision=lax.Precision.HIGHEST, preferred_element_type=jnp.float32)
        return jnp.concatenate([before, after], axis=1)
    index = LANES - 1 - lax.broadcasted_iota(jnp.int32, (even.shape[0], LANES), 1)
    runs = [before[:, n * LANES : (n + 1) * LANES] for n in reversed(range(half // LANES))]
    runs = [jnp.take_along_axis(run, index, axis=1, mode="promise_in_bounds") for run in runs]
    return jnp.concatenate(runs + [after], axis=1)


def stack_kernel(sizes, distance, held, before, *refs):
    stations, bands, seg, sta, pol, blocks, lags = sizes
    refs = list(refs)
    plan_any = refs.pop(0) if before else None
    table, locals_ref, sources_ref = refs.pop(0), refs.pop(0), refs.pop(0)
    sums = [refs.pop(0) for _ in range(before)]
    out_ref, result, wide_weight, local, real_x, imag_x, packed, plan_ref, sems = refs
    if before:
        plan_copy = pltpu.make_async_copy(plan_any, plan_ref, sems.at[STEPS])
        plan_copy.start()
    half = lax.axis_index("pol") ^ distance
    stack(sizes, half, held, locals_ref, sources_ref, wide_weight, local, real_x, imag_x, packed)
    even = jnp.dot(packed[0], table[half, 0], preferred_element_type=jnp.float32)
    odd = jnp.dot(packed[1], table[half, 1], preferred_element_type=jnp.float32)
    if not before:
        out_ref[0] = even
        out_ref[1] = odd
        return
    even = even + jnp.concatenate([part[0] for part in sums], axis=0)
    odd = odd + jnp.concatenate([part[1] for part in sums], axis=0)
    result[...] = unfold(even, odd).reshape(blocks, stations * stations, lags)
    plan_copy.wait()
    copies = []
    for step in range(STEPS):
        block = plan_ref[step] ^ lax.axis_index("sta") if sta == blocks else step
        copies.append(pltpu.make_async_copy(result.at[block], out_ref.at[step], sems.at[step]))
        copies[-1].start()
    for copy in copies:
        copy.wait()


def fetch_kernel(table_hbm, payload_hbm, table_ref, payload_ref, sems):
    copies = [
        pltpu.make_async_copy(table_hbm, table_ref, sems.at[0]),
        pltpu.make_async_copy(payload_hbm, payload_ref, sems.at[1]),
    ]
    for copy in copies:
        copy.start()
    for copy in copies:
        copy.wait()


def join_kernel(*refs):
    *pieces, out_ref = refs
    first = 0
    for piece in pieces:
        out_ref[pl.ds(first, piece.shape[0])] = piece[...]
        first += piece.shape[0]


def join(*pieces):
    vmem = pl.BlockSpec(memory_space=pltpu.VMEM)
    shape = (sum(piece.shape[0] for piece in pieces),) + pieces[0].shape[1:]
    return pl.pallas_call(
        join_kernel,
        out_shape=jax.ShapeDtypeStruct(shape, pieces[0].dtype),
        in_specs=[vmem] * len(pieces),
        out_specs=vmem,
        compiler_params=pltpu.CompilerParams(vmem_limit_bytes=VMEM_BYTES),
        name="join",
    )(*pieces)


def exchange(value, axes, steps):
    if isinstance(axes, str):
        axes, steps = (axes,), (steps,)
    if not any(steps):
        return value
    sizes = tuple(lax.axis_size(axis) for axis in axes)
    pairs = []
    for index in np.ndindex(*sizes):
        source = tuple(i ^ step for i, step in zip(index, steps))
        pairs.append((int(np.ravel_multi_index(source, sizes)), int(np.ravel_multi_index(index, sizes))))
    return lax.ppermute(value, axes, pairs)


def shards(table, raw_spectra, owner_plan, pair_valid, quality):
    seg, sta, pol = (lax.axis_size(name) for name in ("seg", "sta", "pol"))
    _, stations, _, bins = raw_spectra.shape
    bands = bins // BAND
    blocks = min(sta, STEPS)
    pairs = stations * stations
    half_lags = table.shape[3]
    lags = 2 * half_lags
    rows = 2 * stations * bands + 16
    sizes = (stations, bands, seg, sta, pol, blocks, lags)

    raw = raw_spectra.reshape(stations, 2, bands, BAND).transpose(0, 2, 1, 3).reshape(-1, BAND)
    vmem = pl.BlockSpec(memory_space=pltpu.VMEM)
    smem = pl.BlockSpec(memory_space=pltpu.SMEM)
    hbm = pl.BlockSpec(memory_space=pltpu.HBM)
    plan = [] if sta == blocks else [owner_plan]
    payload = pl.pallas_call(
        functools.partial(prepare_kernel, (stations, bands, sta, blocks)),
        out_shape=jax.ShapeDtypeStruct((rows, LANES), jnp.bfloat16),
        in_specs=[smem] * len(plan) + [vmem, vmem, vmem],
        out_specs=vmem,
        scratch_shapes=[pltpu.VMEM((2 * stations * bands, LANES), jnp.float32)],
        name="prepare",
    )(*plan, raw, jnp.transpose(pair_valid[0]), quality)

    table, near = pl.pallas_call(
        fetch_kernel,
        out_shape=[jax.ShapeDtypeStruct(x.shape, x.dtype) for x in (table, payload)],
        in_specs=[hbm, hbm],
        out_specs=[vmem, vmem],
        scratch_shapes=[pltpu.SemaphoreType.DMA((2,))],
        compiler_params=pltpu.CompilerParams(vmem_limit_bytes=VMEM_BYTES),
        cost_estimate=pl.CostEstimate(flops=0, bytes_accessed=2 * table.size * 2, transcendentals=0),
        name="fetch",
    )(table, payload)

    held = near[None]
    distance = seg // 2
    while distance > 1:
        arrived = exchange(payload[None] if held.shape[0] == 1 else held, "seg", distance)
        held = join(held, arrived)
        distance //= 2
    def run(distance, held, locals_, sources, sums):
        count = held[1]
        out_shape = (STEPS, pairs, lags) if sums else (2, count * pairs, half_lags)
        return pl.pallas_call(
            functools.partial(stack_kernel, sizes, distance, held, len(sums)),
            out_shape=jax.ShapeDtypeStruct(out_shape, jnp.float32),
            in_specs=([hbm] if sums else []) + [vmem] * (3 + len(sums)),
            out_specs=hbm if sums else vmem,
            scratch_shapes=[
                pltpu.VMEM((count, pairs, lags), jnp.float32),
                pltpu.VMEM((seg, count * pairs, LANES), jnp.float32),
                pltpu.VMEM((seg, stations, 2, 8, LANES), jnp.float32),
                pltpu.VMEM((count * pairs * 8, LANES), jnp.float32),
                pltpu.VMEM((count * pairs * 8, LANES), jnp.float32),
                pltpu.VMEM((2, count * pairs, bins), jnp.bfloat16),
                pltpu.SMEM((STEPS,), jnp.int32),
                pltpu.SemaphoreType.DMA((STEPS + 1,)),
            ],
            compiler_params=pltpu.CompilerParams(vmem_limit_bytes=VMEM_BYTES),
            cost_estimate=pl.CostEstimate(
                flops=32 * count * pairs * 2 * bins * lags, bytes_accessed=1024 * 1024, transcendentals=0
            ),
            name="stack",
        )(*([owner_plan] if sums else []), table, locals_, sources, *sums)

    if sta == 2 and seg > 1:
        next_held, partner_held, across_held = (
            exchange(held, ("seg", "sta"), step) for step in ((1, 0), (0, 1), (1, 1))
        )
        mine = join(held, next_held)
        first = run(0, (0, 1, 0), mine, mine, [])
        first, partner_held, across_held = lax.optimization_barrier((first, partner_held, across_held))
        others = join(partner_held, across_held)
        sums = [first, run(0, (1, 1, 0), mine, others, [])]
        base = 0
    else:
        mine = join(held, exchange(held, "seg", 1)) if seg > 1 else held
        gathered = lax.all_gather(mine, "sta")
        others = join(*(gathered[lax.axis_index("sta") ^ k if sta == blocks else owner_plan[k]] for k in range(blocks)))
        sums = [run(0, (0, blocks, 0), mine, others, [])]
        base = seg
    theirs = exchange(join(mine, others), "pol", 1)
    result = run(1, (0, blocks, base), theirs, theirs, sums)
    return result.reshape(STEPS, stations, stations, lags)


def solution(mesh):
    placed = (
        P(("groups", "seg"), "sta", None, "pol"),
        P("groups"),
        P(("groups", "seg"), None, "sta"),
        P(("groups", "seg"), None),
    )

    def whole(raw_spectra, owner_plan, pair_valid, quality):
        seg, pol = mesh.shape["seg"], mesh.shape["pol"]
        bins = raw_spectra.shape[3]
        segments = raw_spectra.shape[0] // mesh.shape["groups"]
        lag_blocks = seg * pol
        table = lag_table(2 * bins // lag_blocks, bins, pol, 1.0 / math.sqrt(bins * segments))
        return jax.shard_map(
            shards,
            mesh=mesh,
            in_specs=(P(),) + placed,
            out_specs=P("groups", None, "sta", ("seg", "pol")),
            check_vma=False,
        )(jnp.asarray(table), raw_spectra, owner_plan, pair_valid, quality)

    return whole
```

```python
import functools
import math

import jax
import jax.numpy as jnp
import numpy as np
from jax import lax
from jax.experimental import pallas as pl
from jax.experimental.pallas import tpu as pltpu
from jax.sharding import PartitionSpec as P

STEPS = 3
BAND = 128
LANES = 128
VMEM_BYTES = 32 * 1024 * 1024


def lag_table(lags, bins, halves, scale):
    bin_index = np.arange(bins, dtype=np.int64)
    lag = 2 * np.arange(lags // 2, dtype=np.int64) + 1
    phase = (bin_index[:, None] * lag[None, :]) % (4 * bins)
    angle = phase * (2.0 * math.pi / (4 * bins))
    factor = np.where(bin_index == 0, 1.0, 2.0)[:, None] * scale
    parts = np.stack([np.cos(angle) * factor, np.sin(angle) * factor])
    parts = parts.reshape(2, halves, bins // halves, lags // 2).transpose(1, 0, 2, 3)
    return parts.astype(jnp.bfloat16)


def turn(count, period):
    count = count % period
    quarter = (count + period // 8) // (period // 4)
    x = (count - quarter * (period // 4)).astype(jnp.float32) * (2.0 * math.pi / period)
    y = x * x
    sine = x * (1.0 + y * (-1 / 6 + y * (1 / 120 + y * (-1 / 5040 + y * (1 / 362880)))))
    cosine = 1.0 + y * (-1 / 2 + y * (1 / 24 + y * (-1 / 720 + y * (1 / 40320))))
    quarter = quarter % 4
    odd = quarter % 2 == 1
    real = jnp.where(odd, sine, cosine)
    imag = jnp.where(odd, cosine, sine)
    real = jnp.where((quarter == 1) | (quarter == 2), -real, real)
    imag = jnp.where(quarter >= 2, -imag, imag)
    return real, imag


def prepare_kernel(sizes, *refs):
    stations, bands, sta, blocks = sizes
    *plan, raw_ref, valid_ref, quality_ref, out_ref, wide = refs
    total = stations * sta
    me = lax.axis_index("sta")
    wide[...] = raw_ref[...].astype(jnp.float32)
    count = stations * bands
    real = wide[pl.ds(0, count, stride=2), :]
    imag = wide[pl.ds(1, count, stride=2), :]
    power = jnp.sum(real * real + imag * imag, axis=1, keepdims=True) * (1.0 / (2 * BAND))
    inverse = 1.0 / jnp.sqrt(power + 1e-06)
    real = (real * inverse).reshape(stations, bands, LANES)
    imag = (imag * inverse).reshape(stations, bands, LANES)
    white = jnp.concatenate([real, imag], axis=1).reshape(2 * count, LANES).astype(jnp.bfloat16)

    valid = valid_ref[...].astype(jnp.float32).astype(jnp.bfloat16)
    quality = jnp.broadcast_to(quality_ref[...].astype(jnp.float32), (8, total)).astype(jnp.bfloat16)
    pair = lax.broadcasted_iota(jnp.int32, (total, LANES), 1)
    station = lax.broadcasted_iota(jnp.int32, (total, LANES), 0)
    mine = lax.broadcasted_iota(jnp.int32, (stations, LANES), 0) == (
        lax.broadcasted_iota(jnp.int32, (stations, LANES), 1) % stations
    )
    dot = functools.partial(jnp.dot, preferred_element_type=jnp.float32)
    pick_local = (station == me * stations + pair % stations).astype(jnp.float32).astype(jnp.bfloat16)
    local_flags = dot(quality, pick_local)
    rows = []
    for k in range(blocks):
        source = (plan[0][k] if plan else k) * stations + pair // stations
        pick_source = (station == source).astype(jnp.float32).astype(jnp.bfloat16)
        valid_row = jnp.sum(jnp.where(mine, dot(valid, pick_source), 0.0), axis=0, keepdims=True)
        rows.append(valid_row * (dot(quality, pick_source) * local_flags)[:1])
    rows.append(jnp.zeros((16 - blocks, LANES), jnp.float32))
    weights = jnp.concatenate(rows, axis=0).astype(jnp.bfloat16)
    out_ref[0, pl.ds(0, 2 * count), :] = white
    out_ref[0, pl.ds(2 * count, 16), :] = weights


def stack(sizes, half, held, locals_ref, sources_ref, wide_weight, local, real_x, imag_x, packed):
    first_block, count, base = held
    stations, bands, seg, sta, pol, blocks, lags = sizes
    own_first = sta == blocks
    pairs = stations * stations
    me = lax.axis_index("sta")
    row_index = lax.broadcasted_iota(jnp.int32, (16, LANES), 0)
    diagonal = lax.broadcasted_iota(jnp.int32, (pairs, LANES), 0) == lax.broadcasted_iota(
        jnp.int32, (pairs, LANES), 1
    )
    ones = jnp.ones((LANES, LANES), jnp.bfloat16)
    for g in range(seg):
        flags = locals_ref[g, pl.ds(2 * stations * bands, 16), :].astype(jnp.float32)
        spread = []
        for n in range(first_block, first_block + count):
            block = me ^ n if own_first else n
            row = jnp.sum(jnp.where(row_index == block, flags, 0.0), axis=0, keepdims=True)
            spread.append(jnp.where(diagonal, row, 0.0))
        spread = jnp.concatenate(spread, axis=0).astype(jnp.bfloat16)
        wide_weight[g] = jnp.dot(spread, ones, preferred_element_type=jnp.float32)

    lag_block = lax.axis_index("seg") * pol + lax.axis_index("pol")
    row = half * bands + lax.broadcasted_iota(jnp.int32, (bands, LANES), 0)
    bin_index = row * LANES + lax.broadcasted_iota(jnp.int32, (bands, LANES), 1)
    cosine, sine = turn(bin_index * (2 * lags * lag_block + lags - 1), 2 * lags * seg * pol)
    for g in range(seg):
        for j in range(stations):
            tile = locals_ref[g, pl.ds(j * 16, 16), :].astype(jnp.float32)
            local[g, j, 0] = tile[:8] * cosine + tile[8:] * sine
            local[g, j, 1] = tile[8:] * cosine - tile[:8] * sine

    def one_source(a, carry):
        start = pl.multiple_of(a % stations * 16, 16)
        begin = base + a // stations * seg
        tiles = [sources_ref[begin + g, pl.ds(start, 16), :].astype(jnp.float32) for g in range(seg)]
        for j in range(stations):
            pair = a * stations + j
            real_sum = imag_sum = None
            for g in range(seg):
                weight = jnp.broadcast_to(wide_weight[g, pl.ds(pair, 1), :], (8, LANES))
                real_src = tiles[g][:8] * weight
                imag_src = tiles[g][8:] * weight
                real_loc = local[g, j, 0]
                imag_loc = local[g, j, 1]
                real_term = real_src * real_loc + imag_src * imag_loc
                imag_term = imag_src * real_loc - real_src * imag_loc
                real_sum = real_term if g == 0 else real_sum + real_term
                imag_sum = imag_term if g == 0 else imag_sum + imag_term
            at = pl.ds(pl.multiple_of(pair * 8, 8), 8)
            real_x[at, :] = real_sum
            imag_x[at, :] = imag_sum
        return carry

    lax.fori_loop(0, count * stations, one_source, 0, unroll=2)
    for band in range(bands):
        at = pl.ds(band * LANES, LANES)
        rows = pl.ds(band, count * pairs, stride=8)
        packed[0, :, at] = real_x[rows, :].astype(jnp.bfloat16)
        packed[1, :, at] = imag_x[rows, :].astype(jnp.bfloat16)


def unfold(even, odd):
    half = even.shape[1]
    after = even - odd
    before = even + odd
    if half % LANES:
        flip = lax.broadcasted_iota(jnp.int32, (half, half), 0) + lax.broadcasted_iota(
            jnp.int32, (half, half), 1
        )
        flip = (flip == half - 1).astype(jnp.float32)
        before = jnp.dot(before, flip, precision=lax.Precision.HIGHEST, preferred_element_type=jnp.float32)
        return jnp.concatenate([before, after], axis=1)
    index = LANES - 1 - lax.broadcasted_iota(jnp.int32, (even.shape[0], LANES), 1)
    runs = [before[:, n * LANES : (n + 1) * LANES] for n in reversed(range(half // LANES))]
    runs = [jnp.take_along_axis(run, index, axis=1, mode="promise_in_bounds") for run in runs]
    return jnp.concatenate(runs + [after], axis=1)


def stack_kernel(sizes, distance, held, before, *refs):
    stations, bands, seg, sta, pol, blocks, lags = sizes
    refs = list(refs)
    plan_any = refs.pop(0) if before else None
    table, locals_ref, sources_ref = refs.pop(0), refs.pop(0), refs.pop(0)
    sums = [refs.pop(0) for _ in range(before)]
    out_ref, result, wide_weight, local, real_x, imag_x, packed, plan_ref, sems = refs
    if before:
        plan_copy = pltpu.make_async_copy(plan_any, plan_ref, sems.at[STEPS])
        plan_copy.start()
    half = lax.axis_index("pol") ^ distance
    stack(sizes, half, held, locals_ref, sources_ref, wide_weight, local, real_x, imag_x, packed)
    even = jnp.dot(packed[0], table[half, 0], preferred_element_type=jnp.float32)
    odd = jnp.dot(packed[1], table[half, 1], preferred_element_type=jnp.float32)
    if not before:
        out_ref[0] = even
        out_ref[1] = odd
        return
    even = even + jnp.concatenate([part[0] for part in sums], axis=0)
    odd = odd + jnp.concatenate([part[1] for part in sums], axis=0)
    result[...] = unfold(even, odd).reshape(blocks, stations * stations, lags)
    plan_copy.wait()
    copies = []
    for step in range(STEPS):
        block = plan_ref[step] ^ lax.axis_index("sta") if sta == blocks else step
        copies.append(pltpu.make_async_copy(result.at[block], out_ref.at[step], sems.at[step]))
        copies[-1].start()
    for copy in copies:
        copy.wait()


def fetch_kernel(table_hbm, table_ref, sem):
    copy = pltpu.make_async_copy(table_hbm, table_ref, sem)
    copy.start()
    copy.wait()


def join_kernel(ranges, *refs):
    *pieces, out_ref = refs
    at = 0
    for piece, (first, count) in zip(pieces, ranges):
        out_ref[pl.ds(at, count)] = piece[pl.ds(first, count)]
        at += count


def join(*pieces):
    pieces = [piece if isinstance(piece, tuple) else (piece, 0, piece.shape[0]) for piece in pieces]
    arrays = [piece[0] for piece in pieces]
    ranges = [piece[1:] for piece in pieces]
    vmem = pl.BlockSpec(memory_space=pltpu.VMEM)
    return pl.pallas_call(
        functools.partial(join_kernel, ranges),
        out_shape=pltpu.VMEM((sum(count for _, count in ranges),) + arrays[0].shape[1:], arrays[0].dtype),
        in_specs=[vmem] * len(arrays),
        out_specs=vmem,
        compiler_params=pltpu.CompilerParams(vmem_limit_bytes=VMEM_BYTES),
        name="join",
    )(*arrays)


def exchange(value, axes, steps):
    if isinstance(axes, str):
        axes, steps = (axes,), (steps,)
    if not any(steps):
        return value
    sizes = tuple(lax.axis_size(axis) for axis in axes)
    pairs = []
    for index in np.ndindex(*sizes):
        source = tuple(i ^ step for i, step in zip(index, steps))
        pairs.append((int(np.ravel_multi_index(source, sizes)), int(np.ravel_multi_index(index, sizes))))
    return lax.ppermute(value, axes, pairs)


def shards(table, raw_spectra, owner_plan, pair_valid, quality):
    seg, sta, pol = (lax.axis_size(name) for name in ("seg", "sta", "pol"))
    _, stations, _, bins = raw_spectra.shape
    bands = bins // BAND
    blocks = min(sta, STEPS)
    pairs = stations * stations
    half_lags = table.shape[3]
    lags = 2 * half_lags
    rows = 2 * stations * bands + 16
    sizes = (stations, bands, seg, sta, pol, blocks, lags)

    raw = raw_spectra.reshape(stations, 2, bands, BAND).transpose(0, 2, 1, 3).reshape(-1, BAND)
    vmem = pl.BlockSpec(memory_space=pltpu.VMEM)
    smem = pl.BlockSpec(memory_space=pltpu.SMEM)
    hbm = pl.BlockSpec(memory_space=pltpu.HBM)
    plan = [] if sta == blocks else [owner_plan]
    in_hbm = functools.partial(pltpu.with_memory_space_constraint, memory_space=pltpu.HBM)
    own = pl.pallas_call(
        functools.partial(prepare_kernel, (stations, bands, sta, blocks)),
        out_shape=pltpu.VMEM((1, rows, LANES), jnp.bfloat16),
        in_specs=[smem] * len(plan) + [vmem, vmem, vmem],
        out_specs=vmem,
        scratch_shapes=[pltpu.VMEM((2 * stations * bands, LANES), jnp.float32)],
        compiler_params=pltpu.CompilerParams(vmem_limit_bytes=VMEM_BYTES),
        name="prepare",
    )(*plan, in_hbm(raw), in_hbm(jnp.transpose(pair_valid[0])), in_hbm(quality))

    table = pl.pallas_call(
        fetch_kernel,
        out_shape=pltpu.VMEM(table.shape, table.dtype),
        in_specs=[hbm],
        out_specs=vmem,
        scratch_shapes=[pltpu.SemaphoreType.DMA(())],
        compiler_params=pltpu.CompilerParams(vmem_limit_bytes=VMEM_BYTES),
        cost_estimate=pl.CostEstimate(flops=0, bytes_accessed=2 * table.size * 2, transcendentals=0),
        name="fetch",
    )(in_hbm(table))

    def run(table, distance, held, locals_, sources, sums):
        count = held[1]
        out_shape = (STEPS, pairs, lags) if sums else (2, count * pairs, half_lags)
        return pl.pallas_call(
            functools.partial(stack_kernel, sizes, distance, held, len(sums)),
            out_shape=jax.ShapeDtypeStruct(out_shape, jnp.float32),
            in_specs=([hbm] if sums else []) + [vmem] * (3 + len(sums)),
            out_specs=hbm if sums else vmem,
            scratch_shapes=[
                pltpu.VMEM((count, pairs, lags), jnp.float32),
                pltpu.VMEM((seg, count * pairs, LANES), jnp.float32),
                pltpu.VMEM((seg, stations, 2, 8, LANES), jnp.float32),
                pltpu.VMEM((count * pairs * 8, LANES), jnp.float32),
                pltpu.VMEM((count * pairs * 8, LANES), jnp.float32),
                pltpu.VMEM((2, count * pairs, bins), jnp.bfloat16),
                pltpu.SMEM((STEPS,), jnp.int32),
                pltpu.SemaphoreType.DMA((STEPS + 1,)),
            ],
            compiler_params=pltpu.CompilerParams(vmem_limit_bytes=VMEM_BYTES),
            cost_estimate=pl.CostEstimate(
                flops=32 * count * pairs * 2 * bins * lags, bytes_accessed=1024 * 1024, transcendentals=0
            ),
            name="stack",
        )(*([owner_plan] if sums else []), table, locals_, sources, *sums)

    both = ("seg", "sta")
    if sta == 2 and seg == 4:
        far = exchange(own, "seg", 2)
        partner = exchange(own, "sta", 1)
        far, table = lax.optimization_barrier((far, table))
        near = exchange(join(own, partner, far), "seg", 1)
        far_partner = exchange(far, "sta", 1)
        far_across = exchange(far, both, (1, 1))
        mine = join(own, far, (near, 0, 1), (near, 2, 1))
        first = run(table, 0, (0, 1, 0), mine, mine, [])
        first, far_partner, far_across = lax.optimization_barrier((first, far_partner, far_across))
        others = join(partner, far_partner, (near, 1, 1), far_across)
        sums = [first, run(table, 0, (1, 1, 0), mine, others, [])]
        base = 0
    else:
        mine, distance = own, seg // 2
        while distance:
            mine = join(mine, exchange(mine, "seg", distance))
            distance //= 2
        gathered = lax.all_gather(mine, "sta")
        others = join(*(gathered[lax.axis_index("sta") ^ k if sta == blocks else owner_plan[k]] for k in range(blocks)))
        sums = [run(table, 0, (0, blocks, 0), mine, others, [])]
        base = seg
    theirs = exchange(join(mine, others), "pol", 1)
    result = run(table, 1, (0, blocks, base), theirs, theirs, sums)
    return result.reshape(STEPS, stations, stations, lags)


def solution(mesh):
    placed = (
        P(("groups", "seg"), "sta", None, "pol"),
        P("groups"),
        P(("groups", "seg"), None, "sta"),
        P(("groups", "seg"), None),
    )

    def whole(raw_spectra, owner_plan, pair_valid, quality):
        seg, pol = mesh.shape["seg"], mesh.shape["pol"]
        bins = raw_spectra.shape[3]
        segments = raw_spectra.shape[0] // mesh.shape["groups"]
        lag_blocks = seg * pol
        table = lag_table(2 * bins // lag_blocks, bins, pol, 1.0 / math.sqrt(bins * segments))
        return jax.shard_map(
            shards,
            mesh=mesh,
            in_specs=(P(),) + placed,
            out_specs=P("groups", None, "sta", ("seg", "pol")),
            check_vma=False,
        )(jnp.asarray(table), raw_spectra, owner_plan, pair_valid, quality)

    return whole
```

```python
import functools
import math

import jax
import jax.numpy as jnp
import numpy as np
from jax import lax
from jax.experimental import pallas as pl
from jax.experimental.pallas import tpu as pltpu
from jax.sharding import PartitionSpec as P

STEPS = 3
BAND = 128
LANES = 128
VMEM_BYTES = 32 * 1024 * 1024


def lag_table(lags, bins, halves, scale):
    bin_index = np.arange(bins, dtype=np.int64)
    lag = 2 * np.arange(lags // 2, dtype=np.int64) + 1
    phase = (bin_index[:, None] * lag[None, :]) % (4 * bins)
    angle = phase * (2.0 * math.pi / (4 * bins))
    factor = np.where(bin_index == 0, 1.0, 2.0)[:, None] * scale
    parts = np.stack([np.cos(angle) * factor, np.sin(angle) * factor])
    parts = parts.reshape(2, halves, bins // halves, lags // 2).transpose(1, 0, 2, 3)
    return parts.astype(jnp.bfloat16)


def turn(count, period):
    count = count % period
    quarter = (count + period // 8) // (period // 4)
    x = (count - quarter * (period // 4)).astype(jnp.float32) * (2.0 * math.pi / period)
    y = x * x
    sine = x * (1.0 + y * (-1 / 6 + y * (1 / 120 + y * (-1 / 5040 + y * (1 / 362880)))))
    cosine = 1.0 + y * (-1 / 2 + y * (1 / 24 + y * (-1 / 720 + y * (1 / 40320))))
    quarter = quarter % 4
    odd = quarter % 2 == 1
    real = jnp.where(odd, sine, cosine)
    imag = jnp.where(odd, cosine, sine)
    real = jnp.where((quarter == 1) | (quarter == 2), -real, real)
    imag = jnp.where(quarter >= 2, -imag, imag)
    return real, imag


def prepare_kernel(sizes, *refs):
    stations, bands, sta, blocks = sizes
    *plan, raw_ref, valid_ref, quality_ref, out_ref, wide = refs
    total = stations * sta
    me = lax.axis_index("sta")
    wide[...] = raw_ref[...].astype(jnp.float32)
    count = stations * bands
    real = wide[pl.ds(0, count, stride=2), :]
    imag = wide[pl.ds(1, count, stride=2), :]
    power = jnp.sum(real * real + imag * imag, axis=1, keepdims=True) * (1.0 / (2 * BAND))
    inverse = 1.0 / jnp.sqrt(power + 1e-06)
    real = (real * inverse).reshape(stations, bands, LANES)
    imag = (imag * inverse).reshape(stations, bands, LANES)
    white = jnp.concatenate([real, imag], axis=1).reshape(2 * count, LANES).astype(jnp.bfloat16)

    valid = valid_ref[...].astype(jnp.float32).astype(jnp.bfloat16)
    quality = jnp.broadcast_to(quality_ref[...].astype(jnp.float32), (8, total)).astype(jnp.bfloat16)
    pair = lax.broadcasted_iota(jnp.int32, (total, LANES), 1)
    station = lax.broadcasted_iota(jnp.int32, (total, LANES), 0)
    mine = lax.broadcasted_iota(jnp.int32, (stations, LANES), 0) == (
        lax.broadcasted_iota(jnp.int32, (stations, LANES), 1) % stations
    )
    dot = functools.partial(jnp.dot, preferred_element_type=jnp.float32)
    pick_local = (station == me * stations + pair % stations).astype(jnp.float32).astype(jnp.bfloat16)
    local_flags = dot(quality, pick_local)
    rows = []
    for k in range(blocks):
        source = (plan[0][k] if plan else k) * stations + pair // stations
        pick_source = (station == source).astype(jnp.float32).astype(jnp.bfloat16)
        valid_row = jnp.sum(jnp.where(mine, dot(valid, pick_source), 0.0), axis=0, keepdims=True)
        rows.append(valid_row * (dot(quality, pick_source) * local_flags)[:1])
    rows.append(jnp.zeros((16 - blocks, LANES), jnp.float32))
    weights = jnp.concatenate(rows, axis=0).astype(jnp.bfloat16)
    out_ref[0, pl.ds(0, 2 * count), :] = white
    out_ref[0, pl.ds(2 * count, 16), :] = weights


def stack(sizes, half, held, locals_ref, sources_ref, wide_weight, local, real_x, imag_x, packed):
    first_block, count, base = held
    stations, bands, seg, sta, pol, blocks, lags = sizes
    own_first = sta == blocks
    pairs = stations * stations
    me = lax.axis_index("sta")
    row_index = lax.broadcasted_iota(jnp.int32, (16, LANES), 0)
    diagonal = lax.broadcasted_iota(jnp.int32, (pairs, LANES), 0) == lax.broadcasted_iota(
        jnp.int32, (pairs, LANES), 1
    )
    ones = jnp.ones((LANES, LANES), jnp.bfloat16)
    for g in range(seg):
        flags = locals_ref[g, pl.ds(2 * stations * bands, 16), :].astype(jnp.float32)
        spread = []
        for n in range(first_block, first_block + count):
            block = me ^ n if own_first else n
            row = jnp.sum(jnp.where(row_index == block, flags, 0.0), axis=0, keepdims=True)
            spread.append(jnp.where(diagonal, row, 0.0))
        spread = jnp.concatenate(spread, axis=0).astype(jnp.bfloat16)
        wide_weight[g] = jnp.dot(spread, ones, preferred_element_type=jnp.float32)

    lag_block = lax.axis_index("seg") * pol + lax.axis_index("pol")
    row = half * bands + lax.broadcasted_iota(jnp.int32, (bands, LANES), 0)
    bin_index = row * LANES + lax.broadcasted_iota(jnp.int32, (bands, LANES), 1)
    cosine, sine = turn(bin_index * (2 * lags * lag_block + lags - 1), 2 * lags * seg * pol)
    for g in range(seg):
        for j in range(stations):
            tile = locals_ref[g, pl.ds(j * 16, 16), :].astype(jnp.float32)
            local[g, j, 0] = tile[:8] * cosine + tile[8:] * sine
            local[g, j, 1] = tile[8:] * cosine - tile[:8] * sine

    def one_source(a, carry):
        start = pl.multiple_of(a % stations * 16, 16)
        begin = base + a // stations * seg
        tiles = [sources_ref[begin + g, pl.ds(start, 16), :].astype(jnp.float32) for g in range(seg)]
        for j in range(stations):
            pair = a * stations + j
            real_sum = imag_sum = None
            for g in range(seg):
                weight = jnp.broadcast_to(wide_weight[g, pl.ds(pair, 1), :], (8, LANES))
                real_src = tiles[g][:8] * weight
                imag_src = tiles[g][8:] * weight
                real_loc = local[g, j, 0]
                imag_loc = local[g, j, 1]
                real_term = real_src * real_loc + imag_src * imag_loc
                imag_term = imag_src * real_loc - real_src * imag_loc
                real_sum = real_term if g == 0 else real_sum + real_term
                imag_sum = imag_term if g == 0 else imag_sum + imag_term
            at = pl.ds(pl.multiple_of(pair * 8, 8), 8)
            real_x[at, :] = real_sum
            imag_x[at, :] = imag_sum
        return carry

    lax.fori_loop(0, count * stations, one_source, 0, unroll=2)
    for band in range(bands):
        at = pl.ds(band * LANES, LANES)
        rows = pl.ds(band, count * pairs, stride=8)
        packed[0, :, at] = real_x[rows, :].astype(jnp.bfloat16)
        packed[1, :, at] = imag_x[rows, :].astype(jnp.bfloat16)


def unfold(even, odd):
    half = even.shape[1]
    after = even - odd
    before = even + odd
    if half % LANES:
        flip = lax.broadcasted_iota(jnp.int32, (half, half), 0) + lax.broadcasted_iota(
            jnp.int32, (half, half), 1
        )
        flip = (flip == half - 1).astype(jnp.float32)
        before = jnp.dot(before, flip, precision=lax.Precision.HIGHEST, preferred_element_type=jnp.float32)
        return jnp.concatenate([before, after], axis=1)
    index = LANES - 1 - lax.broadcasted_iota(jnp.int32, (even.shape[0], LANES), 1)
    runs = [before[:, n * LANES : (n + 1) * LANES] for n in reversed(range(half // LANES))]
    runs = [jnp.take_along_axis(run, index, axis=1, mode="promise_in_bounds") for run in runs]
    return jnp.concatenate(runs + [after], axis=1)


def stack_kernel(sizes, distance, held, mode, others, *refs):
    stations, bands, seg, sta, pol, blocks, lags = sizes
    refs = list(refs)
    place = mode == "place"
    plan_any = refs.pop(0) if place else None
    table, locals_ref, sources_ref = refs.pop(0), refs.pop(0), refs.pop(0)
    sums = None if mode == "sum" else refs.pop(0)
    others_ref = refs.pop(0) if others else None
    out_ref, result, wide_weight, local, real_x, imag_x, packed, plan_ref, sems = refs
    if place:
        plan_copy = pltpu.make_async_copy(plan_any, plan_ref, sems.at[STEPS])
        plan_copy.start()
    half = lax.axis_index("pol") ^ distance
    stack(sizes, half, held, locals_ref, sources_ref, wide_weight, local, real_x, imag_x, packed)

    first_block = held[0]
    if place:
        plan_copy.wait()
        chosen = [plan_ref[step] ^ lax.axis_index("sta") if sta == blocks else step for step in range(STEPS)]

        def copy_out(step, source):
            return pltpu.make_async_copy(source, out_ref.at[step], sems.at[step])

        for step in range(STEPS if others else 0):

            @pl.when(chosen[step] < first_block)
            def _():
                copy_out(step, others_ref.at[chosen[step]]).start()

    even = jnp.dot(packed[0], table[half, 0], preferred_element_type=jnp.float32)
    odd = jnp.dot(packed[1], table[half, 1], preferred_element_type=jnp.float32)
    if mode == "sum":
        out_ref[0] = even
        out_ref[1] = odd
        return
    lag_sums = unfold(even + sums[0], odd + sums[1]).reshape(held[1], stations * stations, lags)
    if not place:
        out_ref[...] = lag_sums
        return
    result[...] = lag_sums
    for step in range(STEPS):

        @pl.when(chosen[step] >= first_block)
        def _():
            copy_out(step, result.at[chosen[step] - first_block]).start()

    for step in range(STEPS):
        copy_out(step, result.at[0]).wait()


def fetch_kernel(table_hbm, table_ref, sem):
    copy = pltpu.make_async_copy(table_hbm, table_ref, sem)
    copy.start()
    copy.wait()


def join_kernel(ranges, *refs):
    *pieces, out_ref = refs
    at = 0
    for piece, (first, count) in zip(pieces, ranges):
        out_ref[pl.ds(at, count)] = piece[pl.ds(first, count)]
        at += count


def join(*pieces):
    pieces = [piece if isinstance(piece, tuple) else (piece, 0, piece.shape[0]) for piece in pieces]
    arrays = [piece[0] for piece in pieces]
    ranges = [piece[1:] for piece in pieces]
    vmem = pl.BlockSpec(memory_space=pltpu.VMEM)
    return pl.pallas_call(
        functools.partial(join_kernel, ranges),
        out_shape=pltpu.VMEM((sum(count for _, count in ranges),) + arrays[0].shape[1:], arrays[0].dtype),
        in_specs=[vmem] * len(arrays),
        out_specs=vmem,
        compiler_params=pltpu.CompilerParams(vmem_limit_bytes=VMEM_BYTES),
        name="join",
    )(*arrays)


def exchange(value, axes, steps):
    if isinstance(axes, str):
        axes, steps = (axes,), (steps,)
    if not any(steps):
        return value
    sizes = tuple(lax.axis_size(axis) for axis in axes)
    pairs = []
    for index in np.ndindex(*sizes):
        source = tuple(i ^ step for i, step in zip(index, steps))
        pairs.append((int(np.ravel_multi_index(source, sizes)), int(np.ravel_multi_index(index, sizes))))
    return lax.ppermute(value, axes, pairs)


def shards(table, raw_spectra, owner_plan, pair_valid, quality):
    seg, sta, pol = (lax.axis_size(name) for name in ("seg", "sta", "pol"))
    _, stations, _, bins = raw_spectra.shape
    bands = bins // BAND
    blocks = min(sta, STEPS)
    pairs = stations * stations
    half_lags = table.shape[3]
    lags = 2 * half_lags
    rows = 2 * stations * bands + 16
    sizes = (stations, bands, seg, sta, pol, blocks, lags)

    raw = raw_spectra.reshape(stations, 2, bands, BAND).transpose(0, 2, 1, 3).reshape(-1, BAND)
    vmem = pl.BlockSpec(memory_space=pltpu.VMEM)
    smem = pl.BlockSpec(memory_space=pltpu.SMEM)
    hbm = pl.BlockSpec(memory_space=pltpu.HBM)
    plan = [] if sta == blocks else [owner_plan]
    in_hbm = functools.partial(pltpu.with_memory_space_constraint, memory_space=pltpu.HBM)
    own = pl.pallas_call(
        functools.partial(prepare_kernel, (stations, bands, sta, blocks)),
        out_shape=pltpu.VMEM((1, rows, LANES), jnp.bfloat16),
        in_specs=[smem] * len(plan) + [vmem, vmem, vmem],
        out_specs=vmem,
        scratch_shapes=[pltpu.VMEM((2 * stations * bands, LANES), jnp.float32)],
        compiler_params=pltpu.CompilerParams(vmem_limit_bytes=VMEM_BYTES),
        name="prepare",
    )(*plan, in_hbm(raw), in_hbm(jnp.transpose(pair_valid[0])), in_hbm(quality))

    table = pl.pallas_call(
        fetch_kernel,
        out_shape=pltpu.VMEM(table.shape, table.dtype),
        in_specs=[hbm],
        out_specs=vmem,
        scratch_shapes=[pltpu.SemaphoreType.DMA(())],
        compiler_params=pltpu.CompilerParams(vmem_limit_bytes=VMEM_BYTES),
        cost_estimate=pl.CostEstimate(flops=0, bytes_accessed=2 * table.size * 2, transcendentals=0),
        name="fetch",
    )(in_hbm(table))

    def run(mode, distance, held, locals_, sources, sums=None, others=None):
        count = held[1]
        place = mode == "place"
        if place:
            out_shape = jax.ShapeDtypeStruct((STEPS, pairs, lags), jnp.float32)
        else:
            shape = (2, count * pairs, half_lags) if mode == "sum" else (count, pairs, lags)
            out_shape = pltpu.VMEM(shape, jnp.float32)
        before = [x for x in (sums, others) if x is not None]
        return pl.pallas_call(
            functools.partial(stack_kernel, sizes, distance, held, mode, others is not None),
            out_shape=out_shape,
            in_specs=([hbm] if place else []) + [vmem] * (3 + len(before)),
            out_specs=hbm if place else vmem,
            scratch_shapes=[
                pltpu.VMEM((count, pairs, lags), jnp.float32),
                pltpu.VMEM((seg, count * pairs, LANES), jnp.float32),
                pltpu.VMEM((seg, stations, 2, 8, LANES), jnp.float32),
                pltpu.VMEM((count * pairs * 8, LANES), jnp.float32),
                pltpu.VMEM((count * pairs * 8, LANES), jnp.float32),
                pltpu.VMEM((2, count * pairs, bins), jnp.bfloat16),
                pltpu.SMEM((STEPS,), jnp.int32),
                pltpu.SemaphoreType.DMA((STEPS + 1,)),
            ],
            compiler_params=pltpu.CompilerParams(vmem_limit_bytes=VMEM_BYTES),
            cost_estimate=pl.CostEstimate(
                flops=32 * count * pairs * 2 * bins * lags, bytes_accessed=1024 * 1024, transcendentals=0
            ),
            name="stack_" + mode,
        )(*([in_hbm(owner_plan)] if place else []), table, locals_, sources, *before)

    if sta == 2 and seg > 1:
        far, distance = own, seg // 2
        while distance > 1:
            far = join(far, exchange(far, "seg", distance))
            distance //= 2
        far, table = lax.optimization_barrier((far, table))
        near, partner, across = (exchange(far, ("seg", "sta"), step) for step in ((1, 0), (0, 1), (1, 1)))
        mine = join(far, near)
        mine_too = exchange(mine, "pol", 1)
        sums = run("sum", 0, (0, 1, 0), mine, mine)
        first = run("fold", 1, (0, 1, 0), mine_too, mine_too, sums)
        first, partner, across = lax.optimization_barrier((first, partner, across))
        others = join(partner, across)
        others_too = exchange(others, "pol", 1)
        sums = run("sum", 0, (1, 1, 0), mine, others)
        result = run("place", 1, (1, 1, 0), mine_too, others_too, sums, first)
    else:
        mine, distance = own, seg // 2
        while distance:
            mine = join(mine, exchange(mine, "seg", distance))
            distance //= 2
        gathered = lax.all_gather(mine, "sta")
        others = join(*(gathered[lax.axis_index("sta") ^ k if sta == blocks else owner_plan[k]] for k in range(blocks)))
        sums = run("sum", 0, (0, blocks, 0), mine, others)
        theirs = exchange(join(mine, others), "pol", 1)
        result = run("place", 1, (0, blocks, seg), theirs, theirs, sums)
    return result.reshape(STEPS, stations, stations, lags)


def solution(mesh):
    placed = (
        P(("groups", "seg"), "sta", None, "pol"),
        P("groups"),
        P(("groups", "seg"), None, "sta"),
        P(("groups", "seg"), None),
    )

    def whole(raw_spectra, owner_plan, pair_valid, quality):
        seg, pol = mesh.shape["seg"], mesh.shape["pol"]
        bins = raw_spectra.shape[3]
        segments = raw_spectra.shape[0] // mesh.shape["groups"]
        lag_blocks = seg * pol
        table = lag_table(2 * bins // lag_blocks, bins, pol, 1.0 / math.sqrt(bins * segments))
        return jax.shard_map(
            shards,
            mesh=mesh,
            in_specs=(P(),) + placed,
            out_specs=P("groups", None, "sta", ("seg", "pol")),
            check_vma=False,
        )(jnp.asarray(table), raw_spectra, owner_plan, pair_valid, quality)

    return whole
```

```python
import functools
import math

import jax
import jax.numpy as jnp
import numpy as np
from jax import lax
from jax.experimental import pallas as pl
from jax.experimental.pallas import tpu as pltpu
from jax.sharding import PartitionSpec as P

STEPS = 3
BAND = 128
LANES = 128
VMEM_BYTES = 32 * 1024 * 1024


def lag_table(lags, bins, halves, scale):
    bin_index = np.arange(bins, dtype=np.int64)
    lag = 2 * np.arange(lags // 2, dtype=np.int64) + 1
    phase = (bin_index[:, None] * lag[None, :]) % (4 * bins)
    angle = phase * (2.0 * math.pi / (4 * bins))
    factor = np.where(bin_index == 0, 1.0, 2.0)[:, None] * scale
    parts = np.stack([np.cos(angle) * factor, np.sin(angle) * factor])
    parts = parts.reshape(2, halves, bins // halves, lags // 2).transpose(1, 0, 2, 3)
    return parts.astype(jnp.bfloat16)


def turn(count, period):
    count = count % period
    quarter = (count + period // 8) // (period // 4)
    x = (count - quarter * (period // 4)).astype(jnp.float32) * (2.0 * math.pi / period)
    y = x * x
    sine = x * (1.0 + y * (-1 / 6 + y * (1 / 120 + y * (-1 / 5040 + y * (1 / 362880)))))
    cosine = 1.0 + y * (-1 / 2 + y * (1 / 24 + y * (-1 / 720 + y * (1 / 40320))))
    quarter = quarter % 4
    odd = quarter % 2 == 1
    real = jnp.where(odd, sine, cosine)
    imag = jnp.where(odd, cosine, sine)
    real = jnp.where((quarter == 1) | (quarter == 2), -real, real)
    imag = jnp.where(quarter >= 2, -imag, imag)
    return real, imag


def prepare_kernel(sizes, *refs):
    stations, bands, sta, blocks = sizes
    *plan, raw_ref, valid_ref, quality_ref, out_ref, wide = refs
    total = stations * sta
    me = lax.axis_index("sta")
    wide[...] = raw_ref[...].astype(jnp.float32)
    count = stations * bands
    real = wide[pl.ds(0, count, stride=2), :]
    imag = wide[pl.ds(1, count, stride=2), :]
    power = jnp.sum(real * real + imag * imag, axis=1, keepdims=True) * (1.0 / (2 * BAND))
    inverse = 1.0 / jnp.sqrt(power + 1e-06)
    real = (real * inverse).reshape(stations, bands, LANES)
    imag = (imag * inverse).reshape(stations, bands, LANES)
    white = jnp.concatenate([real, imag], axis=1).reshape(2 * count, LANES).astype(jnp.bfloat16)

    valid = valid_ref[...].astype(jnp.float32).astype(jnp.bfloat16)
    quality = jnp.broadcast_to(quality_ref[...].astype(jnp.float32), (8, total)).astype(jnp.bfloat16)
    pair = lax.broadcasted_iota(jnp.int32, (total, LANES), 1)
    station = lax.broadcasted_iota(jnp.int32, (total, LANES), 0)
    mine = lax.broadcasted_iota(jnp.int32, (stations, LANES), 0) == (
        lax.broadcasted_iota(jnp.int32, (stations, LANES), 1) % stations
    )
    dot = functools.partial(jnp.dot, preferred_element_type=jnp.float32)
    pick_local = (station == me * stations + pair % stations).astype(jnp.float32).astype(jnp.bfloat16)
    local_flags = dot(quality, pick_local)
    rows = []
    for k in range(blocks):
        source = (plan[0][k] if plan else k) * stations + pair // stations
        pick_source = (station == source).astype(jnp.float32).astype(jnp.bfloat16)
        valid_row = jnp.sum(jnp.where(mine, dot(valid, pick_source), 0.0), axis=0, keepdims=True)
        rows.append(valid_row * (dot(quality, pick_source) * local_flags)[:1])
    rows.append(jnp.zeros((16 - blocks, LANES), jnp.float32))
    weights = jnp.concatenate(rows, axis=0).astype(jnp.bfloat16)
    out_ref[0, pl.ds(0, 2 * count), :] = white
    out_ref[0, pl.ds(2 * count, 16), :] = weights


def spread_weights(sizes, first_block, locals_ref, wide):
    stations, bands, seg, sta, pol, blocks, lags = sizes
    pairs = stations * stations
    row_index = lax.broadcasted_iota(jnp.int32, (16, LANES), 0)
    diagonal = lax.broadcasted_iota(jnp.int32, (pairs, LANES), 0) == lax.broadcasted_iota(
        jnp.int32, (pairs, LANES), 1
    )
    ones = jnp.ones((LANES, LANES), jnp.bfloat16)
    for g in range(seg):
        flags = locals_ref[g, pl.ds(2 * stations * bands, 16), :].astype(jnp.float32)
        spread = []
        for n in range(first_block, blocks):
            block = lax.axis_index("sta") ^ n if sta == blocks else n
            row = jnp.sum(jnp.where(row_index == block, flags, 0.0), axis=0, keepdims=True)
            spread.append(jnp.where(diagonal, row, 0.0))
        spread = jnp.concatenate(spread, axis=0).astype(jnp.bfloat16)
        wide[g] = jnp.dot(spread, ones, preferred_element_type=jnp.float32)


def middle_phase(sizes, distance):
    stations, bands, seg, sta, pol, blocks, lags = sizes
    lag_block = lax.axis_index("seg") * pol + lax.axis_index("pol")
    half = lax.axis_index("pol") ^ distance
    row = half * bands + lax.broadcasted_iota(jnp.int32, (bands, LANES), 0)
    bin_index = row * LANES + lax.broadcasted_iota(jnp.int32, (bands, LANES), 1)
    return turn(bin_index * (2 * lags * lag_block + lags - 1), 2 * lags * seg * pol)


def turn_locals(sizes, cosine, sine, locals_ref, local):
    stations, bands, seg = sizes[:3]
    for g in range(seg):
        for j in range(stations):
            tile = locals_ref[g, pl.ds(j * 16, 16), :].astype(jnp.float32)
            local[g, j, 0] = tile[:bands] * cosine + tile[bands:] * sine
            local[g, j, 1] = tile[bands:] * cosine - tile[:bands] * sine


def add_products(stations, count, segments, tile_of, weight_of, local_of, before, real_x, imag_x):
    def one_source(a, carry):
        tiles = [tile_of(n, a).astype(jnp.float32) for n in range(segments)]
        for j in range(stations):
            pair = a * stations + j
            at = pl.ds(pair * 8 if isinstance(pair, int) else pl.multiple_of(pair * 8, 8), 8)
            real_sum = imag_sum = None
            if before is not None:
                real_sum, imag_sum = before[0, at, :], before[1, at, :]
            for n in range(segments):
                weight = jnp.broadcast_to(weight_of(n, pair), (8, LANES))
                real_src = tiles[n][:8] * weight
                imag_src = tiles[n][8:] * weight
                real_loc, imag_loc = local_of(n, j)
                real_term = real_src * real_loc + imag_src * imag_loc
                imag_term = imag_src * real_loc - real_src * imag_loc
                real_sum = real_term if real_sum is None else real_sum + real_term
                imag_sum = imag_term if imag_sum is None else imag_sum + imag_term
            real_x[at, :] = real_sum
            imag_x[at, :] = imag_sum
        return carry

    if count <= 8:
        for a in range(count):
            one_source(a, 0)
    else:
        lax.fori_loop(0, count, one_source, 0, unroll=2)


def pack(rows, bands, real_x, imag_x, packed):
    for band in range(bands):
        at = pl.ds(band * LANES, LANES)
        strided = pl.ds(band, rows, stride=8)
        packed[0, :, at] = real_x[strided, :].astype(jnp.bfloat16)
        packed[1, :, at] = imag_x[strided, :].astype(jnp.bfloat16)


def transform(packed, table):
    dot = functools.partial(jnp.dot, preferred_element_type=jnp.float32)
    return dot(packed[0], table[0]), dot(packed[1], table[1])


def source_tile(sources_ref, base, count, stations):
    def tile_of(n, a):
        start = a % stations * 16
        start = start if isinstance(a, int) else pl.multiple_of(start, 16)
        return sources_ref[base + a // stations * count + n, pl.ds(start, 16), :]

    return tile_of


def place(sizes, plan_copy, plan_ref, others_ref, result, out_ref, sems):
    stations, bands, seg, sta, pol, blocks, lags = sizes
    first_block = others_ref.shape[0] if others_ref is not None else 0
    plan_copy.wait()
    chosen = [plan_ref[step] ^ lax.axis_index("sta") if sta == blocks else step for step in range(STEPS)]

    def copy_out(step, source):
        return pltpu.make_async_copy(source, out_ref.at[step], sems.at[step])

    for step in range(STEPS if first_block else 0):

        @pl.when(chosen[step] < first_block)
        def _():
            copy_out(step, others_ref.at[chosen[step]]).start()

    def finish():
        for step in range(STEPS):

            @pl.when(chosen[step] >= first_block)
            def _():
                copy_out(step, result.at[chosen[step] - first_block]).start()

        for step in range(STEPS):
            copy_out(step, result.at[0]).wait()

    return finish


def own_first_kernel(
    sizes, table, phase, mine_ref, sums_ref, local_ref, wide_ref, real_x, imag_x, packed
):
    stations, bands, seg, sta, pol, blocks, lags = sizes
    spread_weights(sizes, 0, mine_ref, wide_ref)
    turn_locals(sizes, phase[0, 0], phase[0, 1], mine_ref, local_ref)
    add_products(
        stations, stations, seg, source_tile(mine_ref, 0, seg, stations),
        lambda n, pair: wide_ref[n, pl.ds(pair, 1), :],
        lambda n, j: (local_ref[n, j, 0], local_ref[n, j, 1]),
        None, real_x, imag_x,
    )
    pack(stations * stations, bands, real_x, imag_x, packed)
    sums_ref[0], sums_ref[1] = transform(packed, table.at[lax.axis_index("pol")])


def own_second_kernel(
    sizes, table, phase, wide_ref, mine_ref, sums_ref, lags_ref, local_ref, real_x, imag_x, packed
):
    stations, bands, seg, sta, pol, blocks, lags = sizes
    turn_locals(sizes, phase[1, 0], phase[1, 1], mine_ref, local_ref)
    add_products(
        stations, stations, seg, source_tile(mine_ref, 0, seg, stations),
        lambda n, pair: wide_ref[n, pl.ds(pair, 1), :],
        lambda n, j: (local_ref[n, j, 0], local_ref[n, j, 1]),
        None, real_x, imag_x,
    )
    pack(stations * stations, bands, real_x, imag_x, packed)
    even, odd = transform(packed, table.at[lax.axis_index("pol") ^ 1])
    lags_ref[0] = unfold(even + sums_ref[0], odd + sums_ref[1])


def other_products(sizes, first_segment, flip, wide_ref, local_refs, received, half, before, real_x, imag_x):
    stations, seg = sizes[0], sizes[2]
    pairs = stations * stations
    count = seg // 2
    add_products(
        stations, stations, count, source_tile(received, (half ^ flip) * count, count, stations),
        lambda n, pair: wide_ref[first_segment + n, pl.ds(pairs + pair, 1), :],
        lambda n, j: (local_refs[half][first_segment + n, j, 0], local_refs[half][first_segment + n, j, 1]),
        before, real_x, imag_x,
    )


def other_first_kernel(sizes, wide_ref, local_ref, local_too_ref, received, partial_ref):
    first_segment = lax.axis_index("pol") * (sizes[2] // 2)
    for half in range(2):
        other_products(
            sizes, first_segment, 0, wide_ref, (local_ref, local_too_ref), received, half,
            None, partial_ref.at[half, 0], partial_ref.at[half, 1],
        )


def other_second_kernel(
    sizes, plan_any, table, wide_ref, local_ref, local_too_ref, received, partial_ref, others_ref,
    out_ref, result, real_x, imag_x, packed, plan_ref, sems,
):
    stations, bands, seg, sta, pol, blocks, lags = sizes
    plan_copy = pltpu.make_async_copy(plan_any, plan_ref, sems.at[STEPS])
    plan_copy.start()
    first_segment = (1 - lax.axis_index("pol")) * (seg // 2)
    even = odd = 0.0
    for half in range(2):
        other_products(
            sizes, first_segment, 1, wide_ref, (local_ref, local_too_ref), received, half,
            partial_ref.at[half], real_x.at[half], imag_x.at[half],
        )
        pack(stations * stations, bands, real_x.at[half], imag_x.at[half], packed.at[half])
        even_term, odd_term = transform(packed.at[half], table.at[lax.axis_index("pol") ^ half])
        even, odd = even + even_term, odd + odd_term
    finish = place(sizes, plan_copy, plan_ref, others_ref, result, out_ref, sems)
    result[0] = unfold(even, odd)
    finish()


def unfold(even, odd):
    half = even.shape[1]
    after = even - odd
    before = even + odd
    if half % LANES:
        flip = lax.broadcasted_iota(jnp.int32, (half, half), 0) + lax.broadcasted_iota(
            jnp.int32, (half, half), 1
        )
        flip = (flip == half - 1).astype(jnp.float32)
        before = jnp.dot(before, flip, precision=lax.Precision.HIGHEST, preferred_element_type=jnp.float32)
        return jnp.concatenate([before, after], axis=1)
    index = LANES - 1 - lax.broadcasted_iota(jnp.int32, (even.shape[0], LANES), 1)
    runs = [before[:, n * LANES : (n + 1) * LANES] for n in reversed(range(half // LANES))]
    runs = [jnp.take_along_axis(run, index, axis=1, mode="promise_in_bounds") for run in runs]
    return jnp.concatenate(runs + [after], axis=1)


def half_kernel(sizes, distance, *refs):
    stations, bands, seg, sta, pol, blocks, lags = sizes
    pairs = stations * stations
    if distance:
        plan_any, table, mine_ref, sources_ref, sums_ref, out_ref, *rest = refs
        plan_ref, sems = rest[-2:]
        plan_copy = pltpu.make_async_copy(plan_any, plan_ref, sems.at[STEPS])
        plan_copy.start()
    else:
        table, mine_ref, sources_ref, out_ref, *rest = refs
    result, wide, local, real_x, imag_x, packed = rest[:6]
    spread_weights(sizes, 0, mine_ref, wide)
    turn_locals(sizes, *middle_phase(sizes, distance), mine_ref, local)
    add_products(
        stations, blocks * stations, seg, source_tile(sources_ref, 0, seg, stations),
        lambda n, pair: wide[n, pl.ds(pair, 1), :],
        lambda n, j: (local[n, j, 0], local[n, j, 1]),
        None, real_x, imag_x,
    )
    pack(blocks * pairs, bands, real_x, imag_x, packed)
    even, odd = transform(packed, table.at[lax.axis_index("pol") ^ distance])
    if not distance:
        out_ref[0], out_ref[1] = even, odd
        return
    finish = place(sizes, plan_copy, plan_ref, None, result, out_ref, sems)
    result[...] = unfold(even + sums_ref[0], odd + sums_ref[1]).reshape(blocks, pairs, lags)
    finish()


def first_half(sizes, *refs):
    half_kernel(sizes, 0, *refs)


def second_half(sizes, *refs):
    half_kernel(sizes, 1, *refs)


def fetch_kernel(sizes, table_hbm, table_ref, phase_ref, sem):
    copy = pltpu.make_async_copy(table_hbm, table_ref, sem)
    copy.start()
    for distance in range(2):
        phase_ref[distance, 0], phase_ref[distance, 1] = middle_phase(sizes, distance)
    copy.wait()


def join_kernel(ranges, *refs):
    *pieces, out_ref = refs
    at = 0
    for piece, (first, count) in zip(pieces, ranges):
        out_ref[pl.ds(at, count)] = piece[pl.ds(first, count)]
        at += count


def join(*pieces):
    pieces = [piece if isinstance(piece, tuple) else (piece, 0, piece.shape[0]) for piece in pieces]
    arrays = [piece[0] for piece in pieces]
    ranges = [piece[1:] for piece in pieces]
    vmem = pl.BlockSpec(memory_space=pltpu.VMEM)
    return pl.pallas_call(
        functools.partial(join_kernel, ranges),
        out_shape=pltpu.VMEM((sum(count for _, count in ranges),) + arrays[0].shape[1:], arrays[0].dtype),
        in_specs=[vmem] * len(arrays),
        out_specs=vmem,
        compiler_params=pltpu.CompilerParams(vmem_limit_bytes=VMEM_BYTES),
        name="join",
    )(*arrays)


def fetch_from(value, axes, source_of):
    sizes = tuple(lax.axis_size(axis) for axis in axes)
    pairs = []
    for index in np.ndindex(*sizes):
        source = source_of(*index)
        pairs.append((int(np.ravel_multi_index(source, sizes)), int(np.ravel_multi_index(index, sizes))))
    return lax.ppermute(value, axes, pairs)


def exchange(value, axis, distance):
    return fetch_from(value, (axis,), lambda i: (i ^ distance,))


def shards(table, raw_spectra, owner_plan, pair_valid, quality):
    seg, sta, pol = (lax.axis_size(name) for name in ("seg", "sta", "pol"))
    _, stations, _, bins = raw_spectra.shape
    bands = bins // BAND
    blocks = min(sta, STEPS)
    pairs = stations * stations
    half_lags = table.shape[3]
    lags = 2 * half_lags
    rows = 2 * stations * bands + 16
    sizes = (stations, bands, seg, sta, pol, blocks, lags)

    raw = raw_spectra.reshape(stations, 2, bands, BAND).transpose(0, 2, 1, 3).reshape(-1, BAND)
    vmem = pl.BlockSpec(memory_space=pltpu.VMEM)
    smem = pl.BlockSpec(memory_space=pltpu.SMEM)
    hbm = pl.BlockSpec(memory_space=pltpu.HBM)
    plan = [] if sta == blocks else [owner_plan]
    in_hbm = functools.partial(pltpu.with_memory_space_constraint, memory_space=pltpu.HBM)
    own = pl.pallas_call(
        functools.partial(prepare_kernel, (stations, bands, sta, blocks)),
        out_shape=pltpu.VMEM((1, rows, LANES), jnp.bfloat16),
        in_specs=[smem] * len(plan) + [vmem, vmem, vmem],
        out_specs=vmem,
        scratch_shapes=[pltpu.VMEM((2 * stations * bands, LANES), jnp.float32)],
        compiler_params=pltpu.CompilerParams(vmem_limit_bytes=VMEM_BYTES),
        name="prepare",
    )(*plan, in_hbm(raw), in_hbm(jnp.transpose(pair_valid[0])), in_hbm(quality))

    def call(kernel, out_shape, *args, out_specs=None, scratch=(), flops=0, moved=0, name=None):
        many = isinstance(out_shape, (list, tuple))
        return pl.pallas_call(
            functools.partial(kernel, sizes),
            out_shape=out_shape,
            in_specs=[hbm if x is table_const or x is plan_const else vmem for x in args],
            out_specs=out_specs or ([vmem] * len(out_shape) if many else vmem),
            scratch_shapes=list(scratch),
            compiler_params=pltpu.CompilerParams(vmem_limit_bytes=VMEM_BYTES),
            cost_estimate=pl.CostEstimate(flops=flops, bytes_accessed=moved, transcendentals=0),
            name=name,
        )(*args)

    f32 = jnp.float32
    table_const, plan_const = in_hbm(table), in_hbm(owner_plan)
    table, phase = call(
        fetch_kernel,
        [pltpu.VMEM(table.shape, table.dtype), pltpu.VMEM((2, 2, bands, LANES), f32)],
        table_const,
        scratch=[pltpu.SemaphoreType.DMA(())],
        moved=4 * table.size,
        name="fetch",
    )

    def products(count):
        return [pltpu.VMEM((count * pairs * 8, LANES), f32)] * 2 + [pltpu.VMEM((2, count * pairs, bins), jnp.bfloat16)]

    plan_scratch = [pltpu.SMEM((STEPS,), jnp.int32), pltpu.SemaphoreType.DMA((STEPS + 1,))]
    quarter = 32 * pairs * 2 * bins * lags
    placed_shape = jax.ShapeDtypeStruct((STEPS, pairs, lags), f32)
    local_shape = pltpu.VMEM((seg, stations, 2, bands, LANES), f32)

    if sta == 2 and pol == 2 and seg > 1:
        far, distance = own, seg // 2
        while distance > 1:
            far = join(far, exchange(far, "seg", distance))
            distance //= 2
        far, table = lax.optimization_barrier((far, table))
        far_too = exchange(far, "pol", 1)
        near = exchange(far, "seg", 1)
        received = fetch_from(
            join(far, far_too), ("seg", "sta", "pol"), lambda z, x, core: (z ^ core, x ^ 1, core)
        )
        near_too = exchange(near, "pol", 1)
        mine, mine_too = join(far, near), join(far_too, near_too)
        sums, local, wide = call(
            own_first_kernel,
            [pltpu.VMEM((2, pairs, half_lags), f32), local_shape, pltpu.VMEM((seg, blocks * pairs, LANES), f32)],
            table, phase, mine,
            scratch=products(1), flops=quarter, name="own_first",
        )
        own_lags, local_too = call(
            own_second_kernel,
            [pltpu.VMEM((1, pairs, lags), f32), local_shape],
            table, phase, wide, mine_too, sums,
            scratch=products(1), flops=quarter, name="own_second",
        )
        own_lags, received = lax.optimization_barrier((own_lags, received))
        received_too = exchange(received, "pol", 1)
        partial = call(
            other_first_kernel,
            pltpu.VMEM((2, 2, pairs * 8, LANES), f32),
            wide, local, local_too, received,
            flops=quarter, name="other_first",
        )
        result = call(
            other_second_kernel, placed_shape,
            plan_const, table, wide, local, local_too, received_too, partial, own_lags,
            out_specs=hbm,
            scratch=[pltpu.VMEM((1, pairs, lags), f32)]
            + [pltpu.VMEM((2, pairs * 8, LANES), f32)] * 2
            + [pltpu.VMEM((2, 2, pairs, bins), jnp.bfloat16)]
            + plan_scratch,
            flops=quarter, name="other_second",
        )
    else:
        mine, distance = own, seg // 2
        while distance:
            mine = join(mine, exchange(mine, "seg", distance))
            distance //= 2
        gathered = lax.all_gather(mine, "sta")
        sources = join(*(gathered[lax.axis_index("sta") ^ k if sta == blocks else owner_plan[k]] for k in range(blocks)))
        scratch = [
            pltpu.VMEM((blocks, pairs, lags), f32),
            pltpu.VMEM((seg, blocks * pairs, LANES), f32),
            pltpu.VMEM((seg, stations, 2, bands, LANES), f32),
            *products(blocks),
        ]
        sums = call(
            first_half, pltpu.VMEM((2, blocks * pairs, half_lags), f32),
            table, mine, sources,
            scratch=scratch, flops=blocks * quarter, name="first_half",
        )
        result = call(
            second_half, placed_shape,
            plan_const, table, exchange(mine, "pol", 1), exchange(sources, "pol", 1), sums,
            out_specs=hbm, scratch=scratch + plan_scratch, flops=blocks * quarter, name="second_half",
        )
    return result.reshape(STEPS, stations, stations, lags)


def solution(mesh):
    placed = (
        P(("groups", "seg"), "sta", None, "pol"),
        P("groups"),
        P(("groups", "seg"), None, "sta"),
        P(("groups", "seg"), None),
    )

    def whole(raw_spectra, owner_plan, pair_valid, quality):
        seg, pol = mesh.shape["seg"], mesh.shape["pol"]
        bins = raw_spectra.shape[3]
        segments = raw_spectra.shape[0] // mesh.shape["groups"]
        lag_blocks = seg * pol
        table = lag_table(2 * bins // lag_blocks, bins, pol, 1.0 / math.sqrt(bins * segments))
        return jax.shard_map(
            shards,
            mesh=mesh,
            in_specs=(P(),) + placed,
            out_specs=P("groups", None, "sta", ("seg", "pol")),
            check_vma=False,
        )(jnp.asarray(table), raw_spectra, owner_plan, pair_valid, quality)

    return whole
```

```python
import functools
import math

import jax
import jax.numpy as jnp
import numpy as np
from jax import lax
from jax.experimental import pallas as pl
from jax.experimental.pallas import tpu as pltpu
from jax.sharding import PartitionSpec as P

STEPS = 3
BAND = 128
LANES = 128
VMEM_BYTES = 32 * 1024 * 1024


def lag_table(lags, bins, halves, scale):
    bin_index = np.arange(bins, dtype=np.int64)
    lag = 2 * np.arange(lags // 2, dtype=np.int64) + 1
    phase = (bin_index[:, None] * lag[None, :]) % (4 * bins)
    angle = phase * (2.0 * math.pi / (4 * bins))
    factor = np.where(bin_index == 0, 1.0, 2.0)[:, None] * scale
    parts = np.stack([np.cos(angle) * factor, np.sin(angle) * factor])
    parts = parts.reshape(2, halves, bins // halves, lags // 2).transpose(1, 0, 2, 3)
    return parts.astype(jnp.bfloat16)


def turn(count, period):
    count = count % period
    quarter = (count + period // 8) // (period // 4)
    x = (count - quarter * (period // 4)).astype(jnp.float32) * (2.0 * math.pi / period)
    y = x * x
    sine = x * (1.0 + y * (-1 / 6 + y * (1 / 120 + y * (-1 / 5040 + y * (1 / 362880)))))
    cosine = 1.0 + y * (-1 / 2 + y * (1 / 24 + y * (-1 / 720 + y * (1 / 40320))))
    quarter = quarter % 4
    odd = quarter % 2 == 1
    real = jnp.where(odd, sine, cosine)
    imag = jnp.where(odd, cosine, sine)
    real = jnp.where((quarter == 1) | (quarter == 2), -real, real)
    imag = jnp.where(quarter >= 2, -imag, imag)
    return real, imag


def prepare_kernel(sizes, *refs):
    stations, bands, sta, blocks = sizes
    *plan, raw_ref, valid_ref, quality_ref, out_ref, wide = refs
    total = stations * sta
    me = lax.axis_index("sta")
    wide[...] = raw_ref[...].astype(jnp.float32)
    count = stations * bands
    real = wide[pl.ds(0, count, stride=2), :]
    imag = wide[pl.ds(1, count, stride=2), :]
    power = jnp.sum(real * real + imag * imag, axis=1, keepdims=True) * (1.0 / (2 * BAND))
    inverse = 1.0 / jnp.sqrt(power + 1e-06)
    real = (real * inverse).reshape(stations, bands, LANES)
    imag = (imag * inverse).reshape(stations, bands, LANES)
    white = jnp.concatenate([real, imag], axis=1).reshape(2 * count, LANES).astype(jnp.bfloat16)

    valid = valid_ref[...].astype(jnp.float32).astype(jnp.bfloat16)
    quality = jnp.broadcast_to(quality_ref[...].astype(jnp.float32), (8, total)).astype(jnp.bfloat16)
    pair = lax.broadcasted_iota(jnp.int32, (total, LANES), 1)
    station = lax.broadcasted_iota(jnp.int32, (total, LANES), 0)
    mine = lax.broadcasted_iota(jnp.int32, (stations, LANES), 0) == (
        lax.broadcasted_iota(jnp.int32, (stations, LANES), 1) % stations
    )
    dot = functools.partial(jnp.dot, preferred_element_type=jnp.float32)
    pick_local = (station == me * stations + pair % stations).astype(jnp.float32).astype(jnp.bfloat16)
    local_flags = dot(quality, pick_local)
    rows = []
    for k in range(blocks):
        source = (plan[0][k] if plan else k) * stations + pair // stations
        pick_source = (station == source).astype(jnp.float32).astype(jnp.bfloat16)
        valid_row = jnp.sum(jnp.where(mine, dot(valid, pick_source), 0.0), axis=0, keepdims=True)
        rows.append(valid_row * (dot(quality, pick_source) * local_flags)[:1])
    rows.append(jnp.zeros((16 - blocks, LANES), jnp.float32))
    weights = jnp.concatenate(rows, axis=0).astype(jnp.bfloat16)
    out_ref[0, pl.ds(0, 2 * count), :] = white
    out_ref[0, pl.ds(2 * count, 16), :] = weights


def spread_weights(sizes, first_block, locals_ref, wide):
    stations, bands, seg, sta, pol, blocks, lags = sizes
    pairs = stations * stations
    row_index = lax.broadcasted_iota(jnp.int32, (16, LANES), 0)
    diagonal = lax.broadcasted_iota(jnp.int32, (pairs, LANES), 0) == lax.broadcasted_iota(
        jnp.int32, (pairs, LANES), 1
    )
    ones = jnp.ones((LANES, LANES), jnp.bfloat16)
    for g in range(seg):
        flags = locals_ref[g, pl.ds(2 * stations * bands, 16), :].astype(jnp.float32)
        spread = []
        for n in range(first_block, blocks):
            block = lax.axis_index("sta") ^ n if sta == blocks else n
            row = jnp.sum(jnp.where(row_index == block, flags, 0.0), axis=0, keepdims=True)
            spread.append(jnp.where(diagonal, row, 0.0))
        spread = jnp.concatenate(spread, axis=0).astype(jnp.bfloat16)
        wide[g] = jnp.dot(spread, ones, preferred_element_type=jnp.float32)


def middle_phase(sizes, distance):
    stations, bands, seg, sta, pol, blocks, lags = sizes
    lag_block = lax.axis_index("seg") * pol + lax.axis_index("pol")
    half = lax.axis_index("pol") ^ distance
    row = half * bands + lax.broadcasted_iota(jnp.int32, (bands, LANES), 0)
    bin_index = row * LANES + lax.broadcasted_iota(jnp.int32, (bands, LANES), 1)
    return turn(bin_index * (2 * lags * lag_block + lags - 1), 2 * lags * seg * pol)


def turn_locals(sizes, cosine, sine, locals_ref, local):
    stations, bands, seg = sizes[:3]
    for g in range(seg):
        for j in range(stations):
            tile = locals_ref[g, pl.ds(j * 16, 16), :].astype(jnp.float32)
            local[g, j, 0] = tile[:bands] * cosine + tile[bands:] * sine
            local[g, j, 1] = tile[bands:] * cosine - tile[:bands] * sine


def add_products(stations, count, segments, tile_of, weight_of, local_of, before, real_x, imag_x):
    def one_source(a, carry):
        tiles = [tile_of(n, a).astype(jnp.float32) for n in range(segments)]
        for j in range(stations):
            pair = a * stations + j
            at = pl.ds(pair * 8 if isinstance(pair, int) else pl.multiple_of(pair * 8, 8), 8)
            real_sum = imag_sum = None
            if before is not None:
                real_sum, imag_sum = before[0, at, :], before[1, at, :]
            for n in range(segments):
                weight = jnp.broadcast_to(weight_of(n, pair), (8, LANES))
                real_src = tiles[n][:8] * weight
                imag_src = tiles[n][8:] * weight
                real_loc, imag_loc = local_of(n, j)
                real_term = real_src * real_loc + imag_src * imag_loc
                imag_term = imag_src * real_loc - real_src * imag_loc
                real_sum = real_term if real_sum is None else real_sum + real_term
                imag_sum = imag_term if imag_sum is None else imag_sum + imag_term
            real_x[at, :] = real_sum
            imag_x[at, :] = imag_sum
        return carry

    if count <= 8:
        for a in range(count):
            one_source(a, 0)
    else:
        lax.fori_loop(0, count, one_source, 0, unroll=2)


def pack(rows, bands, real_x, imag_x, packed):
    for band in range(bands):
        at = pl.ds(band * LANES, LANES)
        strided = pl.ds(band, rows, stride=8)
        packed[0, :, at] = real_x[strided, :].astype(jnp.bfloat16)
        packed[1, :, at] = imag_x[strided, :].astype(jnp.bfloat16)


def transform(packed, table):
    dot = functools.partial(jnp.dot, preferred_element_type=jnp.float32)
    return dot(packed[0], table[0]), dot(packed[1], table[1])


def source_tile(sources_ref, base, count, stations):
    def tile_of(n, a):
        start = a % stations * 16
        start = start if isinstance(a, int) else pl.multiple_of(start, 16)
        return sources_ref[base + a // stations * count + n, pl.ds(start, 16), :]

    return tile_of


def unfold(even, odd):
    half = even.shape[1]
    after = even - odd
    before = even + odd
    if half % LANES:
        flip = lax.broadcasted_iota(jnp.int32, (half, half), 0) + lax.broadcasted_iota(
            jnp.int32, (half, half), 1
        )
        flip = (flip == half - 1).astype(jnp.float32)
        before = jnp.dot(before, flip, precision=lax.Precision.HIGHEST, preferred_element_type=jnp.float32)
        return jnp.concatenate([before, after], axis=1)
    index = LANES - 1 - lax.broadcasted_iota(jnp.int32, (even.shape[0], LANES), 1)
    runs = [before[:, n * LANES : (n + 1) * LANES] for n in reversed(range(half // LANES))]
    runs = [jnp.take_along_axis(run, index, axis=1, mode="promise_in_bounds") for run in runs]
    return jnp.concatenate(runs + [after], axis=1)


def place(sizes, plan_copy, plan_ref, others_ref, result, out_ref, sems):
    stations, bands, seg, sta, pol, blocks, lags = sizes
    first_block = others_ref.shape[0] if others_ref is not None else 0
    plan_copy.wait()
    chosen = [plan_ref[step] ^ lax.axis_index("sta") if sta == blocks else step for step in range(STEPS)]

    def copy_out(step, source):
        return pltpu.make_async_copy(source, out_ref.at[step], sems.at[step])

    for step in range(STEPS if first_block else 0):

        @pl.when(chosen[step] < first_block)
        def _():
            copy_out(step, others_ref.at[chosen[step]]).start()

    def finish():
        for step in range(STEPS):

            @pl.when(chosen[step] >= first_block)
            def _():
                copy_out(step, result.at[chosen[step] - first_block]).start()

        for step in range(STEPS):
            copy_out(step, result.at[0]).wait()

    return finish


def own_first_kernel(
    sizes, table, phase, mine_ref, sums_ref, local_ref, wide_ref, real_x, imag_x, packed
):
    stations, bands, seg, sta, pol, blocks, lags = sizes
    spread_weights(sizes, 0, mine_ref, wide_ref)
    turn_locals(sizes, phase[0, 0], phase[0, 1], mine_ref, local_ref)
    add_products(
        stations, stations, seg, source_tile(mine_ref, 0, seg, stations),
        lambda n, pair: wide_ref[n, pl.ds(pair, 1), :],
        lambda n, j: (local_ref[n, j, 0], local_ref[n, j, 1]),
        None, real_x, imag_x,
    )
    pack(stations * stations, bands, real_x, imag_x, packed)
    sums_ref[0], sums_ref[1] = transform(packed, table.at[lax.axis_index("pol")])


def own_second_kernel(
    sizes, table, phase, wide_ref, mine_ref, sums_ref, lags_ref, local_ref, real_x, imag_x, packed
):
    stations, bands, seg, sta, pol, blocks, lags = sizes
    turn_locals(sizes, phase[1, 0], phase[1, 1], mine_ref, local_ref)
    add_products(
        stations, stations, seg, source_tile(mine_ref, 0, seg, stations),
        lambda n, pair: wide_ref[n, pl.ds(pair, 1), :],
        lambda n, j: (local_ref[n, j, 0], local_ref[n, j, 1]),
        None, real_x, imag_x,
    )
    pack(stations * stations, bands, real_x, imag_x, packed)
    even, odd = transform(packed, table.at[lax.axis_index("pol") ^ 1])
    lags_ref[0] = unfold(even + sums_ref[0], odd + sums_ref[1])


def other_products(sizes, sources_ref, wide_ref, local_ref, real_x, imag_x, packed):
    stations, bands, seg = sizes[:3]
    pairs = stations * stations
    add_products(
        stations, stations, seg, source_tile(sources_ref, 0, seg, stations),
        lambda n, pair: wide_ref[n, pl.ds(pairs + pair, 1), :],
        lambda n, j: (local_ref[n, j, 0], local_ref[n, j, 1]),
        None, real_x, imag_x,
    )
    pack(pairs, bands, real_x, imag_x, packed)


def other_first_kernel(sizes, table, wide_ref, local_ref, sources_ref, sums_ref, real_x, imag_x, packed):
    other_products(sizes, sources_ref, wide_ref, local_ref, real_x, imag_x, packed)
    sums_ref[0], sums_ref[1] = transform(packed, table.at[lax.axis_index("pol")])


def other_second_kernel(
    sizes, plan_any, table, wide_ref, local_ref, sources_ref, sums_ref, others_ref,
    out_ref, result, real_x, imag_x, packed, plan_ref, sems,
):
    plan_copy = pltpu.make_async_copy(plan_any, plan_ref, sems.at[STEPS])
    plan_copy.start()
    other_products(sizes, sources_ref, wide_ref, local_ref, real_x, imag_x, packed)
    finish = place(sizes, plan_copy, plan_ref, others_ref, result, out_ref, sems)
    even, odd = transform(packed, table.at[lax.axis_index("pol") ^ 1])
    result[0] = unfold(even + sums_ref[0], odd + sums_ref[1])
    finish()


def half_kernel(sizes, distance, *refs):
    stations, bands, seg, sta, pol, blocks, lags = sizes
    pairs = stations * stations
    if distance:
        plan_any, table, mine_ref, sources_ref, sums_ref, out_ref, *rest = refs
        plan_ref, sems = rest[-2:]
        plan_copy = pltpu.make_async_copy(plan_any, plan_ref, sems.at[STEPS])
        plan_copy.start()
    else:
        table, mine_ref, sources_ref, out_ref, *rest = refs
    result, wide, local, real_x, imag_x, packed = rest[:6]
    spread_weights(sizes, 0, mine_ref, wide)
    turn_locals(sizes, *middle_phase(sizes, distance), mine_ref, local)
    add_products(
        stations, blocks * stations, seg, source_tile(sources_ref, 0, seg, stations),
        lambda n, pair: wide[n, pl.ds(pair, 1), :],
        lambda n, j: (local[n, j, 0], local[n, j, 1]),
        None, real_x, imag_x,
    )
    pack(blocks * pairs, bands, real_x, imag_x, packed)
    even, odd = transform(packed, table.at[lax.axis_index("pol") ^ distance])
    if not distance:
        out_ref[0], out_ref[1] = even, odd
        return
    finish = place(sizes, plan_copy, plan_ref, None, result, out_ref, sems)
    result[...] = unfold(even + sums_ref[0], odd + sums_ref[1]).reshape(blocks, pairs, lags)
    finish()


def first_half(sizes, *refs):
    half_kernel(sizes, 0, *refs)


def second_half(sizes, *refs):
    half_kernel(sizes, 1, *refs)


def fetch_kernel(sizes, table_hbm, table_ref, phase_ref, sem):
    copy = pltpu.make_async_copy(table_hbm, table_ref, sem)
    copy.start()
    for distance in range(2):
        phase_ref[distance, 0], phase_ref[distance, 1] = middle_phase(sizes, distance)
    copy.wait()


def join_kernel(ranges, *refs):
    *pieces, out_ref = refs
    at = 0
    for piece, (first, count) in zip(pieces, ranges):
        out_ref[pl.ds(at, count)] = piece[pl.ds(first, count), pl.ds(0, out_ref.shape[1]), :]
        at += count


def join(*pieces, rows=None):
    pieces = [piece if isinstance(piece, tuple) else (piece, 0, piece.shape[0]) for piece in pieces]
    arrays = [piece[0] for piece in pieces]
    ranges = [piece[1:] for piece in pieces]
    vmem = pl.BlockSpec(memory_space=pltpu.VMEM)
    return pl.pallas_call(
        functools.partial(join_kernel, ranges),
        out_shape=pltpu.VMEM(
            (sum(count for _, count in ranges), rows or arrays[0].shape[1], LANES), arrays[0].dtype
        ),
        in_specs=[vmem] * len(arrays),
        out_specs=vmem,
        compiler_params=pltpu.CompilerParams(vmem_limit_bytes=VMEM_BYTES),
        name="join",
    )(*arrays)


def fetch_from(value, axes, source_of):
    sizes = tuple(lax.axis_size(axis) for axis in axes)
    pairs = []
    for index in np.ndindex(*sizes):
        source = source_of(*index)
        pairs.append((int(np.ravel_multi_index(source, sizes)), int(np.ravel_multi_index(index, sizes))))
    return lax.ppermute(value, axes, pairs)


def exchange(value, axis, distance):
    return fetch_from(value, (axis,), lambda i: (i ^ distance,))


def shards(table, raw_spectra, owner_plan, pair_valid, quality):
    seg, sta, pol = (lax.axis_size(name) for name in ("seg", "sta", "pol"))
    _, stations, _, bins = raw_spectra.shape
    bands = bins // BAND
    blocks = min(sta, STEPS)
    pairs = stations * stations
    half_lags = table.shape[3]
    lags = 2 * half_lags
    rows = 2 * stations * bands + 16
    sizes = (stations, bands, seg, sta, pol, blocks, lags)

    raw = raw_spectra.reshape(stations, 2, bands, BAND).transpose(0, 2, 1, 3).reshape(-1, BAND)
    vmem = pl.BlockSpec(memory_space=pltpu.VMEM)
    smem = pl.BlockSpec(memory_space=pltpu.SMEM)
    hbm = pl.BlockSpec(memory_space=pltpu.HBM)
    plan = [] if sta == blocks else [owner_plan]
    in_hbm = functools.partial(pltpu.with_memory_space_constraint, memory_space=pltpu.HBM)
    own = pl.pallas_call(
        functools.partial(prepare_kernel, (stations, bands, sta, blocks)),
        out_shape=pltpu.VMEM((1, rows, LANES), jnp.bfloat16),
        in_specs=[smem] * len(plan) + [vmem, vmem, vmem],
        out_specs=vmem,
        scratch_shapes=[pltpu.VMEM((2 * stations * bands, LANES), jnp.float32)],
        compiler_params=pltpu.CompilerParams(vmem_limit_bytes=VMEM_BYTES),
        name="prepare",
    )(*plan, in_hbm(raw), in_hbm(jnp.transpose(pair_valid[0])), in_hbm(quality))

    def call(kernel, out_shape, *args, out_specs=None, scratch=(), flops=0, moved=0, name=None):
        many = isinstance(out_shape, (list, tuple))
        return pl.pallas_call(
            functools.partial(kernel, sizes),
            out_shape=out_shape,
            in_specs=[hbm if x is table_const or x is plan_const else vmem for x in args],
            out_specs=out_specs or ([vmem] * len(out_shape) if many else vmem),
            scratch_shapes=list(scratch),
            compiler_params=pltpu.CompilerParams(vmem_limit_bytes=VMEM_BYTES),
            cost_estimate=pl.CostEstimate(flops=flops, bytes_accessed=moved, transcendentals=0),
            name=name,
        )(*args)

    f32 = jnp.float32
    table_const, plan_const = in_hbm(table), in_hbm(owner_plan)
    table, phase = call(
        fetch_kernel,
        [pltpu.VMEM(table.shape, table.dtype), pltpu.VMEM((2, 2, bands, LANES), f32)],
        table_const,
        scratch=[pltpu.SemaphoreType.DMA(())],
        moved=4 * table.size,
        name="fetch",
    )

    def products(count):
        return [pltpu.VMEM((count * pairs * 8, LANES), f32)] * 2 + [pltpu.VMEM((2, count * pairs, bins), jnp.bfloat16)]

    plan_scratch = [pltpu.SMEM((STEPS,), jnp.int32), pltpu.SemaphoreType.DMA((STEPS + 1,))]
    quarter = 32 * pairs * 2 * bins * lags
    placed_shape = jax.ShapeDtypeStruct((STEPS, pairs, lags), f32)
    local_shape = pltpu.VMEM((seg, stations, 2, bands, LANES), f32)

    if sta == 2 and pol == 2 and seg > 1:
        far, distance = own, seg // 2
        while distance > 1:
            far = join(far, exchange(far, "seg", distance))
            distance //= 2
        far, table = lax.optimization_barrier((far, table))
        near = exchange(far, "seg", 1)
        bare = join(far, rows=rows - 16)
        partner = exchange(bare, "sta", 1)
        across = fetch_from(bare, ("seg", "sta"), lambda z, x: (z ^ 1, x ^ 1))
        mine = join(far, near)
        mine_too = exchange(mine, "pol", 1)
        sums, local, wide = call(
            own_first_kernel,
            [pltpu.VMEM((2, pairs, half_lags), f32), local_shape, pltpu.VMEM((seg, blocks * pairs, LANES), f32)],
            table, phase, mine,
            scratch=products(1), flops=quarter, name="own_first",
        )
        own_lags, local_too = call(
            own_second_kernel,
            [pltpu.VMEM((1, pairs, lags), f32), local_shape],
            table, phase, wide, mine_too, sums,
            scratch=products(1), flops=quarter, name="own_second",
        )
        own_lags, partner, across = lax.optimization_barrier((own_lags, partner, across))
        others = join(partner, across)
        others_too = exchange(others, "pol", 1)
        sums = call(
            other_first_kernel,
            pltpu.VMEM((2, pairs, half_lags), f32),
            table, wide, local, others,
            scratch=products(1), flops=quarter, name="other_first",
        )
        result = call(
            other_second_kernel, placed_shape,
            plan_const, table, wide, local_too, others_too, sums, own_lags,
            out_specs=hbm,
            scratch=[pltpu.VMEM((1, pairs, lags), f32)] + products(1) + plan_scratch,
            flops=quarter, name="other_second",
        )
    else:
        mine, distance = own, seg // 2
        while distance:
            mine = join(mine, exchange(mine, "seg", distance))
            distance //= 2
        gathered = lax.all_gather(mine, "sta")
        sources = join(*(gathered[lax.axis_index("sta") ^ k if sta == blocks else owner_plan[k]] for k in range(blocks)))
        scratch = [
            pltpu.VMEM((blocks, pairs, lags), f32),
            pltpu.VMEM((seg, blocks * pairs, LANES), f32),
            pltpu.VMEM((seg, stations, 2, bands, LANES), f32),
            *products(blocks),
        ]
        sums = call(
            first_half, pltpu.VMEM((2, blocks * pairs, half_lags), f32),
            table, mine, sources,
            scratch=scratch, flops=blocks * quarter, name="first_half",
        )
        result = call(
            second_half, placed_shape,
            plan_const, table, exchange(mine, "pol", 1), exchange(sources, "pol", 1), sums,
            out_specs=hbm, scratch=scratch + plan_scratch, flops=blocks * quarter, name="second_half",
        )
    return result.reshape(STEPS, stations, stations, lags)


def solution(mesh):
    placed = (
        P(("groups", "seg"), "sta", None, "pol"),
        P("groups"),
        P(("groups", "seg"), None, "sta"),
        P(("groups", "seg"), None),
    )

    def whole(raw_spectra, owner_plan, pair_valid, quality):
        seg, pol = mesh.shape["seg"], mesh.shape["pol"]
        bins = raw_spectra.shape[3]
        segments = raw_spectra.shape[0] // mesh.shape["groups"]
        lag_blocks = seg * pol
        table = lag_table(2 * bins // lag_blocks, bins, pol, 1.0 / math.sqrt(bins * segments))
        return jax.shard_map(
            shards,
            mesh=mesh,
            in_specs=(P(),) + placed,
            out_specs=P("groups", None, "sta", ("seg", "pol")),
            check_vma=False,
        )(jnp.asarray(table), raw_spectra, owner_plan, pair_valid, quality)

    return whole
```

```python
import functools
import math

import jax
import jax.numpy as jnp
import numpy as np
from jax import lax
from jax.experimental import pallas as pl
from jax.experimental.pallas import tpu as pltpu
from jax.sharding import PartitionSpec as P

STEPS = 3
BAND = 128
LANES = 128
VMEM_BYTES = 32 * 1024 * 1024


def lag_table(lags, bins, halves, scale):
    bin_index = np.arange(bins, dtype=np.int64)
    lag = 2 * np.arange(lags // 2, dtype=np.int64) + 1
    phase = (bin_index[:, None] * lag[None, :]) % (4 * bins)
    angle = phase * (2.0 * math.pi / (4 * bins))
    factor = np.where(bin_index == 0, 1.0, 2.0)[:, None] * scale
    parts = np.stack([np.cos(angle) * factor, np.sin(angle) * factor])
    parts = parts.reshape(2, halves, bins // halves, lags // 2).transpose(1, 0, 2, 3)
    return parts.astype(jnp.bfloat16)


def turn(count, period):
    count = count % period
    quarter = (count + period // 8) // (period // 4)
    x = (count - quarter * (period // 4)).astype(jnp.float32) * (2.0 * math.pi / period)
    y = x * x
    sine = x * (1.0 + y * (-1 / 6 + y * (1 / 120 + y * (-1 / 5040 + y * (1 / 362880)))))
    cosine = 1.0 + y * (-1 / 2 + y * (1 / 24 + y * (-1 / 720 + y * (1 / 40320))))
    quarter = quarter % 4
    odd = quarter % 2 == 1
    real = jnp.where(odd, sine, cosine)
    imag = jnp.where(odd, cosine, sine)
    real = jnp.where((quarter == 1) | (quarter == 2), -real, real)
    imag = jnp.where(quarter >= 2, -imag, imag)
    return real, imag


def prepare_kernel(sizes, *refs):
    stations, bands, sta, blocks = sizes
    *plan, raw_ref, valid_ref, quality_ref, out_ref, wide = refs
    total = stations * sta
    me = lax.axis_index("sta")
    wide[...] = raw_ref[...].astype(jnp.float32)
    count = stations * bands
    real = wide[pl.ds(0, count, stride=2), :]
    imag = wide[pl.ds(1, count, stride=2), :]
    power = jnp.sum(real * real + imag * imag, axis=1, keepdims=True) * (1.0 / (2 * BAND))
    inverse = 1.0 / jnp.sqrt(power + 1e-06)
    real = (real * inverse).reshape(stations, bands, LANES)
    imag = (imag * inverse).reshape(stations, bands, LANES)
    white = jnp.concatenate([real, imag], axis=1).reshape(2 * count, LANES).astype(jnp.bfloat16)

    valid = valid_ref[...].astype(jnp.float32).astype(jnp.bfloat16)
    quality = jnp.broadcast_to(quality_ref[...].astype(jnp.float32), (8, total)).astype(jnp.bfloat16)
    pair = lax.broadcasted_iota(jnp.int32, (total, LANES), 1)
    station = lax.broadcasted_iota(jnp.int32, (total, LANES), 0)
    mine = lax.broadcasted_iota(jnp.int32, (stations, LANES), 0) == (
        lax.broadcasted_iota(jnp.int32, (stations, LANES), 1) % stations
    )
    dot = functools.partial(jnp.dot, preferred_element_type=jnp.float32)
    pick_local = (station == me * stations + pair % stations).astype(jnp.float32).astype(jnp.bfloat16)
    local_flags = dot(quality, pick_local)
    rows = []
    for k in range(blocks):
        source = (plan[0][k] if plan else k) * stations + pair // stations
        pick_source = (station == source).astype(jnp.float32).astype(jnp.bfloat16)
        valid_row = jnp.sum(jnp.where(mine, dot(valid, pick_source), 0.0), axis=0, keepdims=True)
        rows.append(valid_row * (dot(quality, pick_source) * local_flags)[:1])
    rows.append(jnp.zeros((16 - blocks, LANES), jnp.float32))
    weights = jnp.concatenate(rows, axis=0).astype(jnp.bfloat16)
    out_ref[0, pl.ds(0, 2 * count), :] = white
    out_ref[0, pl.ds(2 * count, 16), :] = weights


def spread_weights(sizes, locals_ref, wide):
    stations, bands, seg, sta, pol, blocks, lags = sizes
    pairs = stations * stations
    row_index = lax.broadcasted_iota(jnp.int32, (16, LANES), 0)
    diagonal = lax.broadcasted_iota(jnp.int32, (pairs, LANES), 0) == lax.broadcasted_iota(
        jnp.int32, (pairs, LANES), 1
    )
    ones = jnp.ones((LANES, LANES), jnp.bfloat16)
    for g in range(seg):
        flags = locals_ref[g, pl.ds(2 * stations * bands, 16), :].astype(jnp.float32)
        spread = []
        for n in range(blocks):
            block = lax.axis_index("sta") ^ n if sta == 2 else n
            row = jnp.sum(jnp.where(row_index == block, flags, 0.0), axis=0, keepdims=True)
            spread.append(jnp.where(diagonal, row, 0.0))
        spread = jnp.concatenate(spread, axis=0).astype(jnp.bfloat16)
        wide[g] = jnp.dot(spread, ones, preferred_element_type=jnp.float32)


def middle_phase(sizes):
    stations, bands, seg, sta, pol, blocks, lags = sizes
    row = lax.axis_index("pol") * bands + lax.broadcasted_iota(jnp.int32, (bands, LANES), 0)
    bin_index = row * LANES + lax.broadcasted_iota(jnp.int32, (bands, LANES), 1)
    run = pol * lags
    return turn(bin_index * (2 * run * lax.axis_index("seg") + run - 1), 2 * run * seg)


def turn_locals(sizes, cosine, sine, locals_ref, local):
    stations, bands, seg = sizes[:3]
    for g in range(seg):
        for j in range(stations):
            tile = locals_ref[g, pl.ds(j * 16, 16), :].astype(jnp.float32)
            local[g, j, 0] = tile[:bands] * cosine + tile[bands:] * sine
            local[g, j, 1] = tile[bands:] * cosine - tile[:bands] * sine


def add_products(stations, count, segments, tile_of, weight_of, local_of, real_x, imag_x):
    def one_source(a, carry):
        tiles = [tile_of(n, a).astype(jnp.float32) for n in range(segments)]
        for j in range(stations):
            pair = a * stations + j
            at = pl.ds(pair * 8 if isinstance(pair, int) else pl.multiple_of(pair * 8, 8), 8)
            real_sum = imag_sum = None
            for n in range(segments):
                weight = jnp.broadcast_to(weight_of(n, pair), (8, LANES))
                real_src = tiles[n][:8] * weight
                imag_src = tiles[n][8:] * weight
                real_loc, imag_loc = local_of(n, j)
                real_term = real_src * real_loc + imag_src * imag_loc
                imag_term = imag_src * real_loc - real_src * imag_loc
                real_sum = real_term if real_sum is None else real_sum + real_term
                imag_sum = imag_term if imag_sum is None else imag_sum + imag_term
            real_x[at, :] = real_sum
            imag_x[at, :] = imag_sum
        return carry

    if count <= 8:
        for a in range(count):
            one_source(a, 0)
    else:
        lax.fori_loop(0, count, one_source, 0, unroll=2)


def pack(rows, bands, real_x, imag_x, packed):
    for band in range(bands):
        at = pl.ds(band * LANES, LANES)
        strided = pl.ds(band, rows, stride=8)
        packed[0, :, at] = real_x[strided, :].astype(jnp.bfloat16)
        packed[1, :, at] = imag_x[strided, :].astype(jnp.bfloat16)


def source_tile(sources_ref, base, count, stations):
    def tile_of(n, a):
        start = a % stations * 16
        start = start if isinstance(a, int) else pl.multiple_of(start, 16)
        return sources_ref[base + a // stations * count + n, pl.ds(start, 16), :]

    return tile_of


def block_sums(sizes, first_block, count, table, wide, local, sources_ref, kept_ref, sent_ref, real_x, imag_x, packed):
    stations, bands, seg = sizes[:3]
    pairs = stations * stations
    add_products(
        stations, count * stations, seg, source_tile(sources_ref, 0, seg, stations),
        lambda n, pair: wide[n, pl.ds(first_block * pairs + pair, 1), :],
        lambda n, j: (local[n, j, 0], local[n, j, 1]),
        real_x, imag_x,
    )
    pack(count * pairs, bands, real_x, imag_x, packed)
    dot = functools.partial(jnp.dot, preferred_element_type=jnp.float32)
    even, odd = dot(packed[0], table[0]), dot(packed[1], table[1])
    before = lax.axis_index("pol") == 0
    odd = jnp.where(before, odd, -odd)
    kept_ref[...] = even + odd
    sent_ref[...] = even - odd


def in_order(sizes, sums):
    before = lax.axis_index("pol") == 0
    lane = lax.broadcasted_iota(jnp.int32, (sums.shape[0], LANES), 1)
    index = jnp.where(before, LANES - 1 - lane, lane)
    runs = [sums[:, at : at + LANES] for at in range(0, sums.shape[1], LANES)]
    runs = [jnp.where(before, back, run) for run, back in zip(runs, runs[::-1])]
    runs = [jnp.take_along_axis(run, index, axis=1, mode="promise_in_bounds") for run in runs]
    return jnp.concatenate(runs, axis=1)


def all_blocks_kernel(sizes, table, phase, mine_ref, sources_ref, kept_ref, sent_ref, local, wide, *scratch):
    spread_weights(sizes, mine_ref, wide)
    turn_locals(sizes, phase[0], phase[1], mine_ref, local)
    block_sums(sizes, 0, sizes[5], table, wide, local, sources_ref, kept_ref, sent_ref, *scratch)


def own_block_kernel(sizes, table, phase, mine_ref, kept_ref, sent_ref, local_ref, wide_ref, *scratch):
    spread_weights(sizes, mine_ref, wide_ref)
    turn_locals(sizes, phase[0], phase[1], mine_ref, local_ref)
    block_sums(sizes, 0, 1, table, wide_ref, local_ref, mine_ref, kept_ref, sent_ref, *scratch)


def other_block_kernel(sizes, table, wide_ref, local_ref, sources_ref, kept_ref, sent_ref, *scratch):
    block_sums(sizes, 1, 1, table, wide_ref, local_ref, sources_ref, kept_ref, sent_ref, *scratch)


def combine_kernel(sizes, kept_ref, got_ref, lags_ref):
    lags_ref[...] = in_order(sizes, kept_ref[...] + got_ref[...])


def place_kernel(sizes, mask_ref, own_ref, kept_ref, got_ref, out_ref, steps, sems):
    other = in_order(sizes, kept_ref[...] + got_ref[...])
    own = own_ref[...]
    copies = []
    for step in range(STEPS):
        mask = jnp.broadcast_to(mask_ref[step, :1, :1], other.shape)
        steps[step] = jnp.where(mask > 0, own, other)
        copies.append(pltpu.make_async_copy(steps.at[step], out_ref.at[step], sems.at[step]))
        copies[-1].start()
    for copy in copies:
        copy.wait()


def fetch_kernel(sizes, table_hbm, plan_any, table_ref, phase_ref, mask_ref, plan_ref, sems):
    copies = [
        pltpu.make_async_copy(table_hbm.at[lax.axis_index("pol")], table_ref, sems.at[0]),
        pltpu.make_async_copy(plan_any, plan_ref, sems.at[1]),
    ]
    for copy in copies:
        copy.start()
    phase_ref[0], phase_ref[1] = middle_phase(sizes)
    copies[1].wait()
    for step in range(STEPS):
        own = (plan_ref[step] == lax.axis_index("sta")).astype(jnp.float32)
        mask_ref[step] = jnp.full(mask_ref.shape[1:], own, jnp.float32)
    copies[0].wait()


def join_kernel(ranges, *refs):
    *pieces, out_ref = refs
    at = 0
    for piece, (first, count) in zip(pieces, ranges):
        out_ref[pl.ds(at, count)] = piece[pl.ds(first, count), pl.ds(0, out_ref.shape[1]), :]
        at += count


def join(*pieces, rows=None):
    pieces = [piece if isinstance(piece, tuple) else (piece, 0, piece.shape[0]) for piece in pieces]
    arrays = [piece[0] for piece in pieces]
    ranges = [piece[1:] for piece in pieces]
    vmem = pl.BlockSpec(memory_space=pltpu.VMEM)
    return pl.pallas_call(
        functools.partial(join_kernel, ranges),
        out_shape=pltpu.VMEM(
            (sum(count for _, count in ranges), rows or arrays[0].shape[1], LANES), arrays[0].dtype
        ),
        in_specs=[vmem] * len(arrays),
        out_specs=vmem,
        compiler_params=pltpu.CompilerParams(vmem_limit_bytes=VMEM_BYTES),
        name="join",
    )(*arrays)


def fetch_from(value, axes, source_of):
    sizes = tuple(lax.axis_size(axis) for axis in axes)
    pairs = []
    for index in np.ndindex(*sizes):
        source = source_of(*index)
        pairs.append((int(np.ravel_multi_index(source, sizes)), int(np.ravel_multi_index(index, sizes))))
    return lax.ppermute(value, axes, pairs)


def exchange(value, axis, distance):
    return fetch_from(value, (axis,), lambda i: (i ^ distance,))


def shards(table, raw_spectra, owner_plan, pair_valid, quality):
    seg, sta, pol = (lax.axis_size(name) for name in ("seg", "sta", "pol"))
    _, stations, _, bins = raw_spectra.shape
    bands = bins // BAND
    fast = sta == 2 and pol == 2 and seg > 1
    blocks = 2 if fast else STEPS
    pairs = stations * stations
    lags = table.shape[3]
    rows = 2 * stations * bands + 16
    sizes = (stations, bands, seg, sta, pol, blocks, lags)

    raw = raw_spectra.reshape(stations, 2, bands, BAND).transpose(0, 2, 1, 3).reshape(-1, BAND)
    vmem = pl.BlockSpec(memory_space=pltpu.VMEM)
    smem = pl.BlockSpec(memory_space=pltpu.SMEM)
    hbm = pl.BlockSpec(memory_space=pltpu.HBM)
    plan = [] if fast else [owner_plan]
    in_hbm = functools.partial(pltpu.with_memory_space_constraint, memory_space=pltpu.HBM)
    own = pl.pallas_call(
        functools.partial(prepare_kernel, (stations, bands, sta, blocks)),
        out_shape=pltpu.VMEM((1, rows, LANES), jnp.bfloat16),
        in_specs=[smem] * len(plan) + [vmem, vmem, vmem],
        out_specs=vmem,
        scratch_shapes=[pltpu.VMEM((2 * stations * bands, LANES), jnp.float32)],
        compiler_params=pltpu.CompilerParams(vmem_limit_bytes=VMEM_BYTES),
        name="prepare",
    )(*plan, in_hbm(raw), in_hbm(jnp.transpose(pair_valid[0])), in_hbm(quality))

    def call(kernel, out_shape, *args, out_specs=None, scratch=(), flops=0, moved=0, name=None):
        many = isinstance(out_shape, (list, tuple))
        return pl.pallas_call(
            functools.partial(kernel, sizes),
            out_shape=out_shape,
            in_specs=[hbm if x is table_const or x is plan_const else vmem for x in args],
            out_specs=out_specs or ([vmem] * len(out_shape) if many else vmem),
            scratch_shapes=list(scratch),
            compiler_params=pltpu.CompilerParams(vmem_limit_bytes=VMEM_BYTES),
            cost_estimate=pl.CostEstimate(flops=flops, bytes_accessed=moved, transcendentals=0),
            name=name,
        )(*args)

    f32 = jnp.float32
    table_const, plan_const = in_hbm(table), in_hbm(owner_plan)
    table, phase, mask = call(
        fetch_kernel,
        [
            pltpu.VMEM(table.shape[1:], table.dtype),
            pltpu.VMEM((2, bands, LANES), f32),
            pltpu.VMEM((STEPS, 8, LANES), f32),
        ],
        table_const, plan_const,
        scratch=[pltpu.SMEM((STEPS,), jnp.int32), pltpu.SemaphoreType.DMA((2,))],
        moved=4 * table.size // pol,
        name="fetch",
    )

    def products(count):
        return [pltpu.VMEM((count * pairs * 8, LANES), f32)] * 2 + [pltpu.VMEM((2, count * pairs, bins), jnp.bfloat16)]

    quarter = 32 * pairs * 2 * bins * lags
    local_shape = pltpu.VMEM((seg, stations, 2, bands, LANES), f32)
    wide_shape = pltpu.VMEM((seg, blocks * pairs, LANES), f32)
    sums_shapes = [pltpu.VMEM((pairs, lags), f32)] * 2

    if fast:
        far, distance = own, seg // 2
        while distance > 1:
            far = join(far, exchange(far, "seg", distance))
            distance //= 2
        far, table = lax.optimization_barrier((far, table))
        near = exchange(far, "seg", 1)
        partner = exchange(far, "sta", 1)
        across = fetch_from(far, ("seg", "sta"), lambda z, x: (z ^ 1, x ^ 1))
        mine = join(far, near)
        own_kept, own_sent, local, wide = call(
            own_block_kernel, sums_shapes + [local_shape, wide_shape],
            table, phase, mine,
            scratch=products(1), flops=quarter, name="own_block",
        )
        own_kept, partner, across = lax.optimization_barrier((own_kept, partner, across))
        kept, sent = call(
            other_block_kernel, sums_shapes,
            table, wide, local, join(partner, across),
            scratch=products(1), flops=quarter, name="other_block",
        )
        own_lags = call(
            combine_kernel, pltpu.VMEM((pairs, lags), f32), own_kept, exchange(own_sent, "pol", 1), name="combine"
        )
        got = exchange(sent, "pol", 1)
        result = call(
            place_kernel, jax.ShapeDtypeStruct((STEPS, pairs, lags), f32),
            mask, own_lags, kept, got,
            out_specs=hbm,
            scratch=[pltpu.VMEM((STEPS, pairs, lags), f32), pltpu.SemaphoreType.DMA((STEPS,))],
            name="place",
        )
    else:
        mine, distance = own, seg // 2
        while distance:
            mine = join(mine, exchange(mine, "seg", distance))
            distance //= 2
        gathered = lax.all_gather(mine, "sta")
        sources = join(*(gathered[owner_plan[k]] for k in range(STEPS)))
        kept, sent = call(
            all_blocks_kernel, [pltpu.VMEM((blocks * pairs, lags), f32)] * 2,
            table, phase, mine, sources,
            scratch=[local_shape, wide_shape] + products(blocks), flops=blocks * quarter, name="all_blocks",
        )
        result = call(
            combine_kernel, jax.ShapeDtypeStruct((blocks * pairs, lags), f32),
            kept, exchange(sent, "pol", 1), name="combine",
        )
    return result.reshape(STEPS, stations, stations, lags)


def solution(mesh):
    placed = (
        P(("groups", "seg"), "sta", None, "pol"),
        P("groups"),
        P(("groups", "seg"), None, "sta"),
        P(("groups", "seg"), None),
    )

    def whole(raw_spectra, owner_plan, pair_valid, quality):
        seg, pol = mesh.shape["seg"], mesh.shape["pol"]
        bins = raw_spectra.shape[3]
        segments = raw_spectra.shape[0] // mesh.shape["groups"]
        table = lag_table(2 * bins // seg, bins, pol, 1.0 / math.sqrt(bins * segments))
        return jax.shard_map(
            shards,
            mesh=mesh,
            in_specs=(P(),) + placed,
            out_specs=P("groups", None, "sta", ("seg", "pol")),
            check_vma=False,
        )(jnp.asarray(table), raw_spectra, owner_plan, pair_valid, quality)

    return whole
```

```python
import functools
import math

import jax
import jax.numpy as jnp
import numpy as np
from jax import lax
from jax.experimental import pallas as pl
from jax.experimental.pallas import tpu as pltpu
from jax.sharding import PartitionSpec as P

STEPS = 3
BAND = 128
LANES = 128
VMEM_BYTES = 32 * 1024 * 1024


def lag_table(lags, bins, halves, scale):
    bin_index = np.arange(bins, dtype=np.int64)
    lag = 2 * np.arange(lags // 2, dtype=np.int64) + 1
    phase = (bin_index[:, None] * lag[None, :]) % (4 * bins)
    angle = phase * (2.0 * math.pi / (4 * bins))
    factor = np.where(bin_index == 0, 1.0, 2.0)[:, None] * scale
    parts = np.stack([np.cos(angle) * factor, np.sin(angle) * factor])
    parts = parts.reshape(2, halves, bins // halves, lags // 2).transpose(1, 0, 2, 3)
    return parts.astype(jnp.bfloat16)


def turn(count, period):
    count = count % period
    quarter = (count + period // 8) // (period // 4)
    x = (count - quarter * (period // 4)).astype(jnp.float32) * (2.0 * math.pi / period)
    y = x * x
    sine = x * (1.0 + y * (-1 / 6 + y * (1 / 120 + y * (-1 / 5040 + y * (1 / 362880)))))
    cosine = 1.0 + y * (-1 / 2 + y * (1 / 24 + y * (-1 / 720 + y * (1 / 40320))))
    quarter = quarter % 4
    odd = quarter % 2 == 1
    real = jnp.where(odd, sine, cosine)
    imag = jnp.where(odd, cosine, sine)
    real = jnp.where((quarter == 1) | (quarter == 2), -real, real)
    imag = jnp.where(quarter >= 2, -imag, imag)
    return real, imag


def prepare_kernel(sizes, *refs):
    stations, bands, sta, blocks = sizes
    *plan, raw_ref, valid_ref, quality_ref, out_ref, wide = refs
    total = stations * sta
    me = lax.axis_index("sta")
    wide[...] = raw_ref[...].astype(jnp.float32)
    count = stations * bands
    real = wide[pl.ds(0, count, stride=2), :]
    imag = wide[pl.ds(1, count, stride=2), :]
    power = jnp.sum(real * real + imag * imag, axis=1, keepdims=True) * (1.0 / (2 * BAND))
    inverse = 1.0 / jnp.sqrt(power + 1e-06)
    real = (real * inverse).reshape(stations, bands, LANES)
    imag = (imag * inverse).reshape(stations, bands, LANES)
    white = jnp.concatenate([real, imag], axis=1).reshape(2 * count, LANES).astype(jnp.bfloat16)

    valid = valid_ref[...].astype(jnp.float32).astype(jnp.bfloat16)
    quality = jnp.broadcast_to(quality_ref[...].astype(jnp.float32), (8, total)).astype(jnp.bfloat16)
    pair = lax.broadcasted_iota(jnp.int32, (total, LANES), 1)
    station = lax.broadcasted_iota(jnp.int32, (total, LANES), 0)
    mine = lax.broadcasted_iota(jnp.int32, (stations, LANES), 0) == (
        lax.broadcasted_iota(jnp.int32, (stations, LANES), 1) % stations
    )
    dot = functools.partial(jnp.dot, preferred_element_type=jnp.float32)
    pick_local = (station == me * stations + pair % stations).astype(jnp.float32).astype(jnp.bfloat16)
    local_flags = dot(quality, pick_local)
    rows = []
    for k in range(blocks):
        source = (plan[0][k] if plan else k) * stations + pair // stations
        pick_source = (station == source).astype(jnp.float32).astype(jnp.bfloat16)
        valid_row = jnp.sum(jnp.where(mine, dot(valid, pick_source), 0.0), axis=0, keepdims=True)
        rows.append(valid_row * (dot(quality, pick_source) * local_flags)[:1])
    rows.append(jnp.zeros((16 - blocks, LANES), jnp.float32))
    weights = jnp.concatenate(rows, axis=0).astype(jnp.bfloat16)
    out_ref[0, pl.ds(0, 2 * count), :] = white
    out_ref[0, pl.ds(2 * count, 16), :] = weights


def spread_weights(sizes, locals_ref, wide):
    stations, bands, seg, sta, pol, blocks, lags = sizes
    pairs = stations * stations
    row_index = lax.broadcasted_iota(jnp.int32, (16, LANES), 0)
    diagonal = lax.broadcasted_iota(jnp.int32, (pairs, LANES), 0) == lax.broadcasted_iota(
        jnp.int32, (pairs, LANES), 1
    )
    ones = jnp.ones((LANES, LANES), jnp.bfloat16)
    for g in range(seg):
        flags = locals_ref[g, pl.ds(2 * stations * bands, 16), :].astype(jnp.float32)
        spread = []
        for n in range(blocks):
            block = lax.axis_index("sta") ^ n if sta == 2 else n
            row = jnp.sum(jnp.where(row_index == block, flags, 0.0), axis=0, keepdims=True)
            spread.append(jnp.where(diagonal, row, 0.0))
        spread = jnp.concatenate(spread, axis=0).astype(jnp.bfloat16)
        wide[g] = jnp.dot(spread, ones, preferred_element_type=jnp.float32)


def middle_phase(sizes):
    stations, bands, seg, sta, pol, blocks, lags = sizes
    row = lax.axis_index("pol") * bands + lax.broadcasted_iota(jnp.int32, (bands, LANES), 0)
    bin_index = row * LANES + lax.broadcasted_iota(jnp.int32, (bands, LANES), 1)
    run = pol * lags
    return turn(bin_index * (2 * run * lax.axis_index("seg") + run - 1), 2 * run * seg)


def turn_locals(sizes, cosine, sine, locals_ref, local):
    stations, bands, seg = sizes[:3]
    for g in range(seg):
        for j in range(stations):
            tile = locals_ref[g, pl.ds(j * 16, 16), :].astype(jnp.float32)
            local[g, j, 0] = tile[:bands] * cosine + tile[bands:] * sine
            local[g, j, 1] = tile[bands:] * cosine - tile[:bands] * sine


def add_products(stations, count, segments, tile_of, weight_of, local_of, real_x, imag_x):
    def one_source(a, carry):
        tiles = [tile_of(n, a).astype(jnp.float32) for n in range(segments)]
        for j in range(stations):
            pair = a * stations + j
            at = pl.ds(pair * 8 if isinstance(pair, int) else pl.multiple_of(pair * 8, 8), 8)
            real_sum = imag_sum = None
            for n in range(segments):
                weight = jnp.broadcast_to(weight_of(n, pair), (8, LANES))
                real_src = tiles[n][:8] * weight
                imag_src = tiles[n][8:] * weight
                real_loc, imag_loc = local_of(n, j)
                real_term = real_src * real_loc + imag_src * imag_loc
                imag_term = imag_src * real_loc - real_src * imag_loc
                real_sum = real_term if real_sum is None else real_sum + real_term
                imag_sum = imag_term if imag_sum is None else imag_sum + imag_term
            real_x[at, :] = real_sum
            imag_x[at, :] = imag_sum
        return carry

    if count <= 8:
        for a in range(count):
            one_source(a, 0)
    else:
        lax.fori_loop(0, count, one_source, 0, unroll=2)


def pack(rows, bands, real_x, imag_x, packed):
    for band in range(bands):
        at = pl.ds(band * LANES, LANES)
        strided = pl.ds(band, rows, stride=8)
        packed[0, :, at] = real_x[strided, :].astype(jnp.bfloat16)
        packed[1, :, at] = imag_x[strided, :].astype(jnp.bfloat16)


def source_tile(sources_ref, base, count, stations):
    def tile_of(n, a):
        start = a % stations * 16
        start = start if isinstance(a, int) else pl.multiple_of(start, 16)
        return sources_ref[base + a // stations * count + n, pl.ds(start, 16), :]

    return tile_of


def block_sums(sizes, first_block, count, table, wide, local, sources_ref, kept_ref, sent_ref, real_x, imag_x, packed):
    stations, bands, seg = sizes[:3]
    pairs = stations * stations
    add_products(
        stations, count * stations, seg, source_tile(sources_ref, 0, seg, stations),
        lambda n, pair: wide[n, pl.ds(first_block * pairs + pair, 1), :],
        lambda n, j: (local[n, j, 0], local[n, j, 1]),
        real_x, imag_x,
    )
    pack(count * pairs, bands, real_x, imag_x, packed)
    dot = functools.partial(jnp.dot, preferred_element_type=jnp.float32)
    even, odd = dot(packed[0], table[0]), dot(packed[1], table[1])
    before = lax.axis_index("pol") == 0
    odd = jnp.where(before, odd, -odd)
    kept_ref[...] = even + odd
    sent_ref[...] = even - odd


def in_order(sizes, sums):
    before = lax.axis_index("pol") == 0
    lane = lax.broadcasted_iota(jnp.int32, (sums.shape[0], LANES), 1)
    index = jnp.where(before, LANES - 1 - lane, lane)
    runs = [sums[:, at : at + LANES] for at in range(0, sums.shape[1], LANES)]
    runs = [jnp.where(before, back, run) for run, back in zip(runs, runs[::-1])]
    runs = [jnp.take_along_axis(run, index, axis=1, mode="promise_in_bounds") for run in runs]
    return jnp.concatenate(runs, axis=1)


def all_blocks_kernel(sizes, table, phase, mine_ref, sources_ref, kept_ref, sent_ref, local, wide, *scratch):
    spread_weights(sizes, mine_ref, wide)
    turn_locals(sizes, phase[0], phase[1], mine_ref, local)
    block_sums(sizes, 0, sizes[5], table, wide, local, sources_ref, kept_ref, sent_ref, *scratch)


def own_block_kernel(sizes, table, phase, mine_ref, kept_ref, sent_ref, local_ref, wide_ref, *scratch):
    spread_weights(sizes, mine_ref, wide_ref)
    turn_locals(sizes, phase[0], phase[1], mine_ref, local_ref)
    block_sums(sizes, 0, 1, table, wide_ref, local_ref, mine_ref, kept_ref, sent_ref, *scratch)


def other_block_kernel(sizes, table, wide_ref, local_ref, sources_ref, kept_ref, sent_ref, *scratch):
    block_sums(sizes, 1, 1, table, wide_ref, local_ref, sources_ref, kept_ref, sent_ref, *scratch)


def combine_kernel(sizes, kept_ref, got_ref, lags_ref):
    lags_ref[...] = in_order(sizes, kept_ref[...] + got_ref[...])


def place_kernel(sizes, mask_ref, own_ref, kept_ref, got_ref, out_ref, steps, sems):
    other = in_order(sizes, kept_ref[...] + got_ref[...])
    own = own_ref[...]
    copies = []
    for step in range(STEPS):
        mask = jnp.broadcast_to(mask_ref[step, :1, :1], other.shape)
        steps[step] = jnp.where(mask > 0, own, other)
        copies.append(pltpu.make_async_copy(steps.at[step], out_ref.at[step], sems.at[step]))
        copies[-1].start()
    for copy in copies:
        copy.wait()


def fetch_kernel(sizes, table_hbm, plan_any, table_ref, phase_ref, mask_ref, plan_ref, sems):
    copies = [
        pltpu.make_async_copy(table_hbm.at[lax.axis_index("pol")], table_ref, sems.at[0]),
        pltpu.make_async_copy(plan_any, plan_ref, sems.at[1]),
    ]
    for copy in copies:
        copy.start()
    phase_ref[0], phase_ref[1] = middle_phase(sizes)
    copies[1].wait()
    for step in range(STEPS):
        own = (plan_ref[step] == lax.axis_index("sta")).astype(jnp.float32)
        mask_ref[step] = jnp.full(mask_ref.shape[1:], own, jnp.float32)
    copies[0].wait()


def join_kernel(ranges, *refs):
    *pieces, out_ref = refs
    at = 0
    for piece, (first, count) in zip(pieces, ranges):
        out_ref[pl.ds(at, count)] = piece[pl.ds(first, count), pl.ds(0, out_ref.shape[1]), :]
        at += count


def join(*pieces, rows=None):
    pieces = [piece if isinstance(piece, tuple) else (piece, 0, piece.shape[0]) for piece in pieces]
    arrays = [piece[0] for piece in pieces]
    ranges = [piece[1:] for piece in pieces]
    vmem = pl.BlockSpec(memory_space=pltpu.VMEM)
    return pl.pallas_call(
        functools.partial(join_kernel, ranges),
        out_shape=pltpu.VMEM(
            (sum(count for _, count in ranges), rows or arrays[0].shape[1], LANES), arrays[0].dtype
        ),
        in_specs=[vmem] * len(arrays),
        out_specs=vmem,
        compiler_params=pltpu.CompilerParams(vmem_limit_bytes=VMEM_BYTES),
        name="join",
    )(*arrays)


def fetch_from(value, axes, source_of):
    sizes = tuple(lax.axis_size(axis) for axis in axes)
    pairs = []
    for index in np.ndindex(*sizes):
        source = source_of(*index)
        pairs.append((int(np.ravel_multi_index(source, sizes)), int(np.ravel_multi_index(index, sizes))))
    return lax.ppermute(value, axes, pairs)


def exchange(value, axis, distance):
    return fetch_from(value, (axis,), lambda i: (i ^ distance,))


def shards(table, raw_spectra, owner_plan, pair_valid, quality):
    seg, sta, pol = (lax.axis_size(name) for name in ("seg", "sta", "pol"))
    _, stations, _, bins = raw_spectra.shape
    bands = bins // BAND
    fast = sta == 2 and pol == 2 and seg > 1
    blocks = 2 if fast else STEPS
    pairs = stations * stations
    lags = table.shape[3]
    rows = 2 * stations * bands + 16
    sizes = (stations, bands, seg, sta, pol, blocks, lags)

    raw = raw_spectra.reshape(stations, 2, bands, BAND).transpose(0, 2, 1, 3).reshape(-1, BAND)
    vmem = pl.BlockSpec(memory_space=pltpu.VMEM)
    smem = pl.BlockSpec(memory_space=pltpu.SMEM)
    hbm = pl.BlockSpec(memory_space=pltpu.HBM)
    plan = [] if fast else [owner_plan]
    in_hbm = functools.partial(pltpu.with_memory_space_constraint, memory_space=pltpu.HBM)
    own = pl.pallas_call(
        functools.partial(prepare_kernel, (stations, bands, sta, blocks)),
        out_shape=pltpu.VMEM((1, rows, LANES), jnp.bfloat16),
        in_specs=[smem] * len(plan) + [vmem, vmem, vmem],
        out_specs=vmem,
        scratch_shapes=[pltpu.VMEM((2 * stations * bands, LANES), jnp.float32)],
        compiler_params=pltpu.CompilerParams(vmem_limit_bytes=VMEM_BYTES),
        name="prepare",
    )(*plan, in_hbm(raw), in_hbm(jnp.transpose(pair_valid[0])), in_hbm(quality))

    def call(kernel, out_shape, *args, out_specs=None, scratch=(), flops=0, moved=0, name=None):
        many = isinstance(out_shape, (list, tuple))
        return pl.pallas_call(
            functools.partial(kernel, sizes),
            out_shape=out_shape,
            in_specs=[hbm if x is table_const or x is plan_const else vmem for x in args],
            out_specs=out_specs or ([vmem] * len(out_shape) if many else vmem),
            scratch_shapes=list(scratch),
            compiler_params=pltpu.CompilerParams(vmem_limit_bytes=VMEM_BYTES),
            cost_estimate=pl.CostEstimate(flops=flops, bytes_accessed=moved, transcendentals=0),
            name=name,
        )(*args)

    f32 = jnp.float32
    table_const, plan_const = in_hbm(table), in_hbm(owner_plan)
    table, phase, mask = call(
        fetch_kernel,
        [
            pltpu.VMEM(table.shape[1:], table.dtype),
            pltpu.VMEM((2, bands, LANES), f32),
            pltpu.VMEM((STEPS, 8, LANES), f32),
        ],
        table_const, plan_const,
        scratch=[pltpu.SMEM((STEPS,), jnp.int32), pltpu.SemaphoreType.DMA((2,))],
        moved=4 * table.size // pol,
        name="fetch",
    )

    def products(count):
        return [pltpu.VMEM((count * pairs * 8, LANES), f32)] * 2 + [pltpu.VMEM((2, count * pairs, bins), jnp.bfloat16)]

    quarter = 32 * pairs * 2 * bins * lags
    local_shape = pltpu.VMEM((seg, stations, 2, bands, LANES), f32)
    wide_shape = pltpu.VMEM((seg, blocks * pairs, LANES), f32)
    sums_shapes = [pltpu.VMEM((pairs, lags), f32)] * 2

    if fast:
        far, distance = own, seg // 2
        while distance > 1:
            far = join(far, exchange(far, "seg", distance))
            distance //= 2
        far, table = lax.optimization_barrier((far, table))
        near = exchange(far, "seg", 1)
        across = fetch_from(far, ("seg", "sta"), lambda z, x: (z ^ 1, x ^ 1))
        partner = exchange(far, "sta", 1)
        mine = join(far, near)
        own_kept, own_sent, local, wide = call(
            own_block_kernel, sums_shapes + [local_shape, wide_shape],
            table, phase, mine,
            scratch=products(1), flops=quarter, name="own_block",
        )
        own_lags = call(
            combine_kernel, pltpu.VMEM((pairs, lags), f32), own_kept, exchange(own_sent, "pol", 1), name="combine"
        )
        own_lags, across, partner = lax.optimization_barrier((own_lags, across, partner))
        kept, sent = call(
            other_block_kernel, sums_shapes,
            table, wide, local, join(partner, across),
            scratch=products(1), flops=quarter, name="other_block",
        )
        got = exchange(sent, "pol", 1)
        result = call(
            place_kernel, jax.ShapeDtypeStruct((STEPS, pairs, lags), f32),
            mask, own_lags, kept, got,
            out_specs=hbm,
            scratch=[pltpu.VMEM((STEPS, pairs, lags), f32), pltpu.SemaphoreType.DMA((STEPS,))],
            name="place",
        )
    else:
        mine, distance = own, seg // 2
        while distance:
            mine = join(mine, exchange(mine, "seg", distance))
            distance //= 2
        gathered = lax.all_gather(mine, "sta")
        sources = join(*(gathered[owner_plan[k]] for k in range(STEPS)))
        kept, sent = call(
            all_blocks_kernel, [pltpu.VMEM((blocks * pairs, lags), f32)] * 2,
            table, phase, mine, sources,
            scratch=[local_shape, wide_shape] + products(blocks), flops=blocks * quarter, name="all_blocks",
        )
        result = call(
            combine_kernel, jax.ShapeDtypeStruct((blocks * pairs, lags), f32),
            kept, exchange(sent, "pol", 1), name="combine",
        )
    return result.reshape(STEPS, stations, stations, lags)


def solution(mesh):
    placed = (
        P(("groups", "seg"), "sta", None, "pol"),
        P("groups"),
        P(("groups", "seg"), None, "sta"),
        P(("groups", "seg"), None),
    )

    def whole(raw_spectra, owner_plan, pair_valid, quality):
        seg, pol = mesh.shape["seg"], mesh.shape["pol"]
        bins = raw_spectra.shape[3]
        segments = raw_spectra.shape[0] // mesh.shape["groups"]
        table = lag_table(2 * bins // seg, bins, pol, 1.0 / math.sqrt(bins * segments))
        return jax.shard_map(
            shards,
            mesh=mesh,
            in_specs=(P(),) + placed,
            out_specs=P("groups", None, "sta", ("seg", "pol")),
            check_vma=False,
        )(jnp.asarray(table), raw_spectra, owner_plan, pair_valid, quality)

    return whole
```

```python
import functools
import math

import jax
import jax.numpy as jnp
import numpy as np
from jax import lax
from jax.experimental import pallas as pl
from jax.experimental.pallas import tpu as pltpu
from jax.sharding import PartitionSpec as P

STEPS = 3
BAND = 128
LANES = 128
VMEM_BYTES = 32 * 1024 * 1024


def lag_table(lags, bins, halves, scale):
    bin_index = np.arange(bins, dtype=np.int64)
    lag = 2 * np.arange(lags // 2, dtype=np.int64) + 1
    phase = (bin_index[:, None] * lag[None, :]) % (4 * bins)
    angle = phase * (2.0 * math.pi / (4 * bins))
    factor = np.where(bin_index == 0, 1.0, 2.0)[:, None] * scale
    parts = np.stack([np.cos(angle) * factor, np.sin(angle) * factor])
    parts = parts.reshape(2, halves, bins // halves, lags // 2).transpose(1, 0, 2, 3)
    return parts.astype(jnp.bfloat16)


def turn(count, period):
    count = count % period
    quarter = (count + period // 8) // (period // 4)
    x = (count - quarter * (period // 4)).astype(jnp.float32) * (2.0 * math.pi / period)
    y = x * x
    sine = x * (1.0 + y * (-1 / 6 + y * (1 / 120 + y * (-1 / 5040 + y * (1 / 362880)))))
    cosine = 1.0 + y * (-1 / 2 + y * (1 / 24 + y * (-1 / 720 + y * (1 / 40320))))
    quarter = quarter % 4
    odd = quarter % 2 == 1
    real = jnp.where(odd, sine, cosine)
    imag = jnp.where(odd, cosine, sine)
    real = jnp.where((quarter == 1) | (quarter == 2), -real, real)
    imag = jnp.where(quarter >= 2, -imag, imag)
    return real, imag


def prepare_kernel(sizes, *refs):
    stations, bands, sta, blocks = sizes
    *plan, raw_ref, valid_ref, quality_ref, out_ref, wide = refs
    total = stations * sta
    me = lax.axis_index("sta")
    wide[...] = raw_ref[...].astype(jnp.float32)
    count = stations * bands
    real = wide[pl.ds(0, count, stride=2), :]
    imag = wide[pl.ds(1, count, stride=2), :]
    power = jnp.sum(real * real + imag * imag, axis=1, keepdims=True) * (1.0 / (2 * BAND))
    inverse = 1.0 / jnp.sqrt(power + 1e-06)
    real = (real * inverse).reshape(stations, bands, LANES)
    imag = (imag * inverse).reshape(stations, bands, LANES)
    white = jnp.concatenate([real, imag], axis=1).reshape(2 * count, LANES).astype(jnp.bfloat16)

    valid = valid_ref[...].astype(jnp.float32).astype(jnp.bfloat16)
    quality = jnp.broadcast_to(quality_ref[...].astype(jnp.float32), (8, total)).astype(jnp.bfloat16)
    pair = lax.broadcasted_iota(jnp.int32, (total, LANES), 1)
    station = lax.broadcasted_iota(jnp.int32, (total, LANES), 0)
    mine = lax.broadcasted_iota(jnp.int32, (stations, LANES), 0) == (
        lax.broadcasted_iota(jnp.int32, (stations, LANES), 1) % stations
    )
    dot = functools.partial(jnp.dot, preferred_element_type=jnp.float32)
    pick_local = (station == me * stations + pair % stations).astype(jnp.float32).astype(jnp.bfloat16)
    local_flags = dot(quality, pick_local)
    rows = []
    for k in range(blocks):
        source = (plan[0][k] if plan else k) * stations + pair // stations
        pick_source = (station == source).astype(jnp.float32).astype(jnp.bfloat16)
        valid_row = jnp.sum(jnp.where(mine, dot(valid, pick_source), 0.0), axis=0, keepdims=True)
        rows.append(valid_row * (dot(quality, pick_source) * local_flags)[:1])
    rows.append(jnp.zeros((16 - blocks, LANES), jnp.float32))
    weights = jnp.concatenate(rows, axis=0).astype(jnp.bfloat16)
    out_ref[0, pl.ds(0, 2 * count), :] = white
    out_ref[0, pl.ds(2 * count, 16), :] = weights


def spread_weights(sizes, locals_ref, wide):
    stations, bands, seg, sta, pol, blocks, lags = sizes
    pairs = stations * stations
    row_index = lax.broadcasted_iota(jnp.int32, (16, LANES), 0)
    diagonal = lax.broadcasted_iota(jnp.int32, (pairs, LANES), 0) == lax.broadcasted_iota(
        jnp.int32, (pairs, LANES), 1
    )
    ones = jnp.ones((LANES, LANES), jnp.bfloat16)
    for g in range(seg):
        flags = locals_ref[g, pl.ds(2 * stations * bands, 16), :].astype(jnp.float32)
        spread = []
        for n in range(blocks):
            block = lax.axis_index("sta") ^ n if sta == 2 else n
            row = jnp.sum(jnp.where(row_index == block, flags, 0.0), axis=0, keepdims=True)
            spread.append(jnp.where(diagonal, row, 0.0))
        spread = jnp.concatenate(spread, axis=0).astype(jnp.bfloat16)
        wide[g] = jnp.dot(spread, ones, preferred_element_type=jnp.float32)


def middle_phase(sizes):
    stations, bands, seg, sta, pol, blocks, lags = sizes
    row = lax.axis_index("pol") * bands + lax.broadcasted_iota(jnp.int32, (bands, LANES), 0)
    bin_index = row * LANES + lax.broadcasted_iota(jnp.int32, (bands, LANES), 1)
    run = pol * lags
    return turn(bin_index * (2 * run * lax.axis_index("seg") + run - 1), 2 * run * seg)


def turn_locals(sizes, cosine, sine, locals_ref, local):
    stations, bands, seg = sizes[:3]
    for g in range(seg):
        for j in range(stations):
            tile = locals_ref[g, pl.ds(j * 16, 16), :].astype(jnp.float32)
            local[g, j, 0] = tile[:bands] * cosine + tile[bands:] * sine
            local[g, j, 1] = tile[bands:] * cosine - tile[:bands] * sine


def add_products(stations, count, segments, tile_of, weight_of, local_of, real_x, imag_x):
    def one_source(a, carry):
        tiles = [tile_of(n, a).astype(jnp.float32) for n in range(segments)]
        for j in range(stations):
            pair = a * stations + j
            at = pl.ds(pair * 8 if isinstance(pair, int) else pl.multiple_of(pair * 8, 8), 8)
            real_sum = imag_sum = None
            for n in range(segments):
                real_src, imag_src = tiles[n][:8], tiles[n][8:]
                if weight_of is not None:
                    weight = jnp.broadcast_to(weight_of(n, pair), (8, LANES))
                    real_src, imag_src = real_src * weight, imag_src * weight
                real_loc, imag_loc = local_of(n, a, j)
                real_term = real_src * real_loc + imag_src * imag_loc
                imag_term = imag_src * real_loc - real_src * imag_loc
                real_sum = real_term if real_sum is None else real_sum + real_term
                imag_sum = imag_term if imag_sum is None else imag_sum + imag_term
            real_x[at, :] = real_sum
            imag_x[at, :] = imag_sum
        return carry

    if count <= 8:
        for a in range(count):
            one_source(a, 0)
    else:
        lax.fori_loop(0, count, one_source, 0, unroll=2)


def pack(rows, bands, real_x, imag_x, packed):
    for band in range(bands):
        at = pl.ds(band * LANES, LANES)
        strided = pl.ds(band, rows, stride=8)
        packed[0, :, at] = real_x[strided, :].astype(jnp.bfloat16)
        packed[1, :, at] = imag_x[strided, :].astype(jnp.bfloat16)


def source_tile(sources_ref, base, count, stations):
    def tile_of(n, a):
        start = a % stations * 16
        start = start if isinstance(a, int) else pl.multiple_of(start, 16)
        return sources_ref[base + a // stations * count + n, pl.ds(start, 16), :]

    return tile_of


def block_sums(sizes, first_block, count, table, wide, local, sources_ref, kept_ref, sent_ref, real_x, imag_x, packed):
    stations, bands, seg = sizes[:3]
    pairs = stations * stations
    add_products(
        stations, count * stations, seg, source_tile(sources_ref, 0, seg, stations),
        lambda n, pair: wide[n, pl.ds(first_block * pairs + pair, 1), :],
        lambda n, a, j: (local[n, j, 0], local[n, j, 1]),
        real_x, imag_x,
    )
    both_sums(sizes, count * pairs, table, kept_ref, sent_ref, real_x, imag_x, packed)


def both_sums(sizes, rows, table, kept_ref, sent_ref, real_x, imag_x, packed):
    pack(rows, sizes[1], real_x, imag_x, packed)
    dot = functools.partial(jnp.dot, preferred_element_type=jnp.float32)
    even, odd = dot(packed[0], table[0]), dot(packed[1], table[1])
    before = lax.axis_index("pol") == 0
    odd = jnp.where(before, odd, -odd)
    kept_ref[...] = even + odd
    sent_ref[...] = even - odd


def in_order(sizes, sums):
    before = lax.axis_index("pol") == 0
    lane = lax.broadcasted_iota(jnp.int32, (sums.shape[0], LANES), 1)
    index = jnp.where(before, LANES - 1 - lane, lane)
    runs = [sums[:, at : at + LANES] for at in range(0, sums.shape[1], LANES)]
    runs = [jnp.where(before, back, run) for run, back in zip(runs, runs[::-1])]
    runs = [jnp.take_along_axis(run, index, axis=1, mode="promise_in_bounds") for run in runs]
    return jnp.concatenate(runs, axis=1)


def all_blocks_kernel(sizes, table, phase, mine_ref, sources_ref, kept_ref, sent_ref, local, wide, *scratch):
    spread_weights(sizes, mine_ref, wide)
    turn_locals(sizes, phase[0], phase[1], mine_ref, local)
    block_sums(sizes, 0, sizes[5], table, wide, local, sources_ref, kept_ref, sent_ref, *scratch)


def own_block_kernel(sizes, table, phase, mine_ref, kept_ref, sent_ref, local_ref, wide_ref, *scratch):
    spread_weights(sizes, mine_ref, wide_ref)
    turn_locals(sizes, phase[0], phase[1], mine_ref, local_ref)
    block_sums(sizes, 0, 1, table, wide_ref, local_ref, mine_ref, kept_ref, sent_ref, *scratch)


def weigh_kernel(sizes, wide_ref, local_ref, weighted_ref):
    stations, bands, seg = sizes[:3]
    for a in range(stations):
        for j in range(stations):
            pair = stations * stations + a * stations + j
            for g in range(seg):
                weight = jnp.broadcast_to(wide_ref[g, pl.ds(pair, 1), :], (bands, LANES))
                weighted_ref[a, j, g, 0] = local_ref[g, j, 0] * weight
                weighted_ref[a, j, g, 1] = local_ref[g, j, 1] * weight


def other_block_kernel(sizes, table, weighted_ref, sources_ref, kept_ref, sent_ref, *scratch):
    stations, bands, seg = sizes[:3]
    add_products(
        stations, stations, seg, source_tile(sources_ref, 0, seg, stations),
        None,
        lambda n, a, j: (weighted_ref[a, j, n, 0], weighted_ref[a, j, n, 1]),
        *scratch[:2],
    )
    both_sums(sizes, stations * stations, table, kept_ref, sent_ref, *scratch)


def combine_kernel(sizes, kept_ref, got_ref, lags_ref):
    lags_ref[...] = in_order(sizes, kept_ref[...] + got_ref[...])


def place_kernel(sizes, mask_ref, own_ref, kept_ref, got_ref, out_ref, steps, sems):
    other = in_order(sizes, kept_ref[...] + got_ref[...])
    own = own_ref[...]
    copies = []
    for step in range(STEPS):
        mask = jnp.broadcast_to(mask_ref[step, :1, :1], other.shape)
        steps[step] = jnp.where(mask > 0, own, other)
        copies.append(pltpu.make_async_copy(steps.at[step], out_ref.at[step], sems.at[step]))
        copies[-1].start()
    for copy in copies:
        copy.wait()


def fetch_kernel(sizes, table_hbm, plan_any, after, table_ref, phase_ref, mask_ref, plan_ref, sems):
    del after
    copies = [
        pltpu.make_async_copy(table_hbm.at[lax.axis_index("pol")], table_ref, sems.at[0]),
        pltpu.make_async_copy(plan_any, plan_ref, sems.at[1]),
    ]
    for copy in copies:
        copy.start()
    phase_ref[0], phase_ref[1] = middle_phase(sizes)
    copies[1].wait()
    for step in range(STEPS):
        own = (plan_ref[step] == lax.axis_index("sta")).astype(jnp.float32)
        mask_ref[step] = jnp.full(mask_ref.shape[1:], own, jnp.float32)
    copies[0].wait()


def join_kernel(ranges, *refs):
    *pieces, out_ref = refs
    at = 0
    for piece, (first, count) in zip(pieces, ranges):
        out_ref[pl.ds(at, count)] = piece[pl.ds(first, count), pl.ds(0, out_ref.shape[1]), :]
        at += count


def join(*pieces, rows=None):
    pieces = [piece if isinstance(piece, tuple) else (piece, 0, piece.shape[0]) for piece in pieces]
    arrays = [piece[0] for piece in pieces]
    ranges = [piece[1:] for piece in pieces]
    vmem = pl.BlockSpec(memory_space=pltpu.VMEM)
    return pl.pallas_call(
        functools.partial(join_kernel, ranges),
        out_shape=pltpu.VMEM(
            (sum(count for _, count in ranges), rows or arrays[0].shape[1], LANES), arrays[0].dtype
        ),
        in_specs=[vmem] * len(arrays),
        out_specs=vmem,
        compiler_params=pltpu.CompilerParams(vmem_limit_bytes=VMEM_BYTES),
        name="join",
    )(*arrays)


def fetch_from(value, axes, source_of):
    sizes = tuple(lax.axis_size(axis) for axis in axes)
    pairs = []
    for index in np.ndindex(*sizes):
        source = source_of(*index)
        pairs.append((int(np.ravel_multi_index(source, sizes)), int(np.ravel_multi_index(index, sizes))))
    return lax.ppermute(value, axes, pairs)


def exchange(value, axis, distance):
    return fetch_from(value, (axis,), lambda i: (i ^ distance,))


def shards(table, raw_spectra, owner_plan, pair_valid, quality):
    seg, sta, pol = (lax.axis_size(name) for name in ("seg", "sta", "pol"))
    _, stations, _, bins = raw_spectra.shape
    bands = bins // BAND
    fast = sta == 2 and pol == 2 and seg == 4
    blocks = 2 if fast else STEPS
    pairs = stations * stations
    lags = table.shape[3]
    rows = 2 * stations * bands + 16
    sizes = (stations, bands, seg, sta, pol, blocks, lags)

    raw = raw_spectra.reshape(stations, 2, bands, BAND).transpose(0, 2, 1, 3).reshape(-1, BAND)
    vmem = pl.BlockSpec(memory_space=pltpu.VMEM)
    smem = pl.BlockSpec(memory_space=pltpu.SMEM)
    hbm = pl.BlockSpec(memory_space=pltpu.HBM)
    plan = [] if fast else [owner_plan]
    in_hbm = functools.partial(pltpu.with_memory_space_constraint, memory_space=pltpu.HBM)
    own = pl.pallas_call(
        functools.partial(prepare_kernel, (stations, bands, sta, blocks)),
        out_shape=pltpu.VMEM((1, rows, LANES), jnp.bfloat16),
        in_specs=[smem] * len(plan) + [vmem, vmem, vmem],
        out_specs=vmem,
        scratch_shapes=[pltpu.VMEM((2 * stations * bands, LANES), jnp.float32)],
        compiler_params=pltpu.CompilerParams(vmem_limit_bytes=VMEM_BYTES),
        name="prepare",
    )(*plan, in_hbm(raw), in_hbm(jnp.transpose(pair_valid[0])), in_hbm(quality))

    def call(kernel, out_shape, *args, out_specs=None, scratch=(), flops=0, moved=0, name=None):
        many = isinstance(out_shape, (list, tuple))
        return pl.pallas_call(
            functools.partial(kernel, sizes),
            out_shape=out_shape,
            in_specs=[hbm if x is table_const or x is plan_const else vmem for x in args],
            out_specs=out_specs or ([vmem] * len(out_shape) if many else vmem),
            scratch_shapes=list(scratch),
            compiler_params=pltpu.CompilerParams(vmem_limit_bytes=VMEM_BYTES),
            cost_estimate=pl.CostEstimate(flops=flops, bytes_accessed=moved, transcendentals=0),
            name=name,
        )(*args)

    f32 = jnp.float32
    table_const, plan_const = in_hbm(table), in_hbm(owner_plan)

    def fetch(after):
        return call(
            fetch_kernel,
            [
                pltpu.VMEM(table.shape[1:], table.dtype),
                pltpu.VMEM((2, bands, LANES), f32),
                pltpu.VMEM((STEPS, 8, LANES), f32),
            ],
            table_const, plan_const, after,
            scratch=[pltpu.SMEM((STEPS,), jnp.int32), pltpu.SemaphoreType.DMA((2,))],
            moved=4 * table.size // pol,
            name="fetch",
        )

    def products(count):
        return [pltpu.VMEM((count * pairs * 8, LANES), f32)] * 2 + [pltpu.VMEM((2, count * pairs, bins), jnp.bfloat16)]

    quarter = 32 * pairs * 2 * bins * lags
    local_shape = pltpu.VMEM((seg, stations, 2, bands, LANES), f32)
    wide_shape = pltpu.VMEM((seg, blocks * pairs, LANES), f32)
    sums_shapes = [pltpu.VMEM((pairs, lags), f32)] * 2

    if fast:
        far = join(own, exchange(own, "seg", 2))
        table, phase, mask = fetch(own)
        far, table = lax.optimization_barrier((far, table))
        bare = join(far, rows=rows - 16)
        near = exchange(far, "seg", 1)
        across = fetch_from(bare, ("seg", "sta"), lambda z, x: (z ^ 1, x ^ 1))
        partner = exchange(bare, "sta", 1)
        mine = join(far, near)
        own_kept, own_sent, local, wide = call(
            own_block_kernel, sums_shapes + [local_shape, wide_shape],
            table, phase, mine,
            scratch=products(1), flops=8 * quarter, name="own_block",
        )
        weighted = call(
            weigh_kernel, pltpu.VMEM((stations, stations, seg, 2, bands, LANES), f32),
            wide, local,
            flops=8 * quarter, name="weigh",
        )
        own_got = exchange(own_sent, "pol", 1)
        own_got, weighted = lax.optimization_barrier((own_got, weighted))
        own_lags = call(combine_kernel, pltpu.VMEM((pairs, lags), f32), own_kept, own_got, name="combine")
        own_lags, across, partner = lax.optimization_barrier((own_lags, across, partner))
        kept, sent = call(
            other_block_kernel, sums_shapes,
            table, weighted, join(partner, across),
            scratch=products(1), flops=quarter, name="other_block",
        )
        got = exchange(sent, "pol", 1)
        result = call(
            place_kernel, jax.ShapeDtypeStruct((STEPS, pairs, lags), f32),
            mask, own_lags, kept, got,
            out_specs=hbm,
            scratch=[pltpu.VMEM((STEPS, pairs, lags), f32), pltpu.SemaphoreType.DMA((STEPS,))],
            name="place",
        )
    else:
        mine, distance = own, seg // 2
        while distance:
            mine = join(mine, exchange(mine, "seg", distance))
            distance //= 2
        gathered = lax.all_gather(mine, "sta")
        sources = join(*(gathered[owner_plan[k]] for k in range(STEPS)))
        table, phase, _ = fetch(mine)
        kept, sent = call(
            all_blocks_kernel, [pltpu.VMEM((blocks * pairs, lags), f32)] * 2,
            table, phase, mine, sources,
            scratch=[local_shape, wide_shape] + products(blocks), flops=blocks * quarter, name="all_blocks",
        )
        result = call(
            combine_kernel, jax.ShapeDtypeStruct((blocks * pairs, lags), f32),
            kept, exchange(sent, "pol", 1), name="combine",
        )
    return result.reshape(STEPS, stations, stations, lags)


def solution(mesh):
    placed = (
        P(("groups", "seg"), "sta", None, "pol"),
        P("groups"),
        P(("groups", "seg"), None, "sta"),
        P(("groups", "seg"), None),
    )

    def whole(raw_spectra, owner_plan, pair_valid, quality):
        seg, pol = mesh.shape["seg"], mesh.shape["pol"]
        bins = raw_spectra.shape[3]
        segments = raw_spectra.shape[0] // mesh.shape["groups"]
        table = lag_table(2 * bins // seg, bins, pol, 1.0 / math.sqrt(bins * segments))
        return jax.shard_map(
            shards,
            mesh=mesh,
            in_specs=(P(),) + placed,
            out_specs=P("groups", None, "sta", ("seg", "pol")),
            check_vma=False,
        )(jnp.asarray(table), raw_spectra, owner_plan, pair_valid, quality)

    return whole
```

```python
import functools
import math

import jax
import jax.numpy as jnp
import numpy as np
from jax import lax
from jax.experimental import pallas as pl
from jax.experimental.pallas import tpu as pltpu
from jax.sharding import PartitionSpec as P

STEPS = 3
BAND = 128
LANES = 128
VMEM_BYTES = 32 * 1024 * 1024


def lag_table(lags, bins, halves, scale):
    bin_index = np.arange(bins, dtype=np.int64)
    lag = 2 * np.arange(lags // 2, dtype=np.int64) + 1
    phase = (bin_index[:, None] * lag[None, :]) % (4 * bins)
    angle = phase * (2.0 * math.pi / (4 * bins))
    factor = np.where(bin_index == 0, 1.0, 2.0)[:, None] * scale
    parts = np.stack([np.cos(angle) * factor, np.sin(angle) * factor])
    parts = parts.reshape(2, halves, bins // halves, lags // 2).transpose(1, 0, 2, 3)
    return parts.astype(jnp.bfloat16)


def turn(count, period):
    count = count % period
    quarter = (count + period // 8) // (period // 4)
    x = (count - quarter * (period // 4)).astype(jnp.float32) * (2.0 * math.pi / period)
    y = x * x
    sine = x * (1.0 + y * (-1 / 6 + y * (1 / 120 + y * (-1 / 5040 + y * (1 / 362880)))))
    cosine = 1.0 + y * (-1 / 2 + y * (1 / 24 + y * (-1 / 720 + y * (1 / 40320))))
    quarter = quarter % 4
    odd = quarter % 2 == 1
    real = jnp.where(odd, sine, cosine)
    imag = jnp.where(odd, cosine, sine)
    real = jnp.where((quarter == 1) | (quarter == 2), -real, real)
    imag = jnp.where(quarter >= 2, -imag, imag)
    return real, imag


def prepare_kernel(sizes, *refs):
    stations, bands, sta, blocks = sizes
    *plan, raw_ref, valid_ref, quality_ref, out_ref, wide = refs
    total = stations * sta
    me = lax.axis_index("sta")
    wide[...] = raw_ref[...].astype(jnp.float32)
    count = stations * bands
    real = wide[pl.ds(0, count, stride=2), :]
    imag = wide[pl.ds(1, count, stride=2), :]
    power = jnp.sum(real * real + imag * imag, axis=1, keepdims=True) * (1.0 / (2 * BAND))
    inverse = 1.0 / jnp.sqrt(power + 1e-06)
    real = (real * inverse).reshape(stations, bands, LANES)
    imag = (imag * inverse).reshape(stations, bands, LANES)
    white = jnp.concatenate([real, imag], axis=1).reshape(2 * count, LANES).astype(jnp.bfloat16)

    valid = valid_ref[...].astype(jnp.float32).astype(jnp.bfloat16)
    quality = jnp.broadcast_to(quality_ref[...].astype(jnp.float32), (8, total)).astype(jnp.bfloat16)
    pair = lax.broadcasted_iota(jnp.int32, (total, LANES), 1)
    station = lax.broadcasted_iota(jnp.int32, (total, LANES), 0)
    mine = lax.broadcasted_iota(jnp.int32, (stations, LANES), 0) == (
        lax.broadcasted_iota(jnp.int32, (stations, LANES), 1) % stations
    )
    dot = functools.partial(jnp.dot, preferred_element_type=jnp.float32)
    pick_local = (station == me * stations + pair % stations).astype(jnp.float32).astype(jnp.bfloat16)
    local_flags = dot(quality, pick_local)
    rows = []
    for k in range(blocks):
        source = (plan[0][k] if plan else k) * stations + pair // stations
        pick_source = (station == source).astype(jnp.float32).astype(jnp.bfloat16)
        valid_row = jnp.sum(jnp.where(mine, dot(valid, pick_source), 0.0), axis=0, keepdims=True)
        rows.append(valid_row * (dot(quality, pick_source) * local_flags)[:1])
    rows.append(jnp.zeros((16 - blocks, LANES), jnp.float32))
    weights = jnp.concatenate(rows, axis=0).astype(jnp.bfloat16)
    out_ref[0, pl.ds(0, 2 * count), :] = white
    out_ref[0, pl.ds(2 * count, 16), :] = weights


def spread_weights(sizes, locals_ref, wide):
    stations, bands, seg, sta, pol, blocks, lags = sizes
    pairs = stations * stations
    row_index = lax.broadcasted_iota(jnp.int32, (16, LANES), 0)
    diagonal = lax.broadcasted_iota(jnp.int32, (pairs, LANES), 0) == lax.broadcasted_iota(
        jnp.int32, (pairs, LANES), 1
    )
    ones = jnp.ones((LANES, LANES), jnp.bfloat16)
    for g in range(seg):
        flags = locals_ref[g, pl.ds(2 * stations * bands, 16), :].astype(jnp.float32)
        spread = []
        for n in range(blocks):
            block = lax.axis_index("sta") ^ n if sta == 2 else n
            row = jnp.sum(jnp.where(row_index == block, flags, 0.0), axis=0, keepdims=True)
            spread.append(jnp.where(diagonal, row, 0.0))
        spread = jnp.concatenate(spread, axis=0).astype(jnp.bfloat16)
        wide[g] = jnp.dot(spread, ones, preferred_element_type=jnp.float32)


def middle_phase(sizes):
    stations, bands, seg, sta, pol, blocks, lags = sizes
    row = lax.axis_index("pol") * bands + lax.broadcasted_iota(jnp.int32, (bands, LANES), 0)
    bin_index = row * LANES + lax.broadcasted_iota(jnp.int32, (bands, LANES), 1)
    run = pol * lags
    return turn(bin_index * (2 * run * lax.axis_index("seg") + run - 1), 2 * run * seg)


def turn_locals(sizes, cosine, sine, locals_ref, local):
    stations, bands, seg = sizes[:3]
    for g in range(seg):
        for j in range(stations):
            tile = locals_ref[g, pl.ds(j * 16, 16), :].astype(jnp.float32)
            local[g, j, 0] = tile[:bands] * cosine + tile[bands:] * sine
            local[g, j, 1] = tile[bands:] * cosine - tile[:bands] * sine


def add_products(stations, count, segments, tile_of, weight_of, local_of, real_x, imag_x):
    def one_source(a, carry):
        tiles = [tile_of(n, a).astype(jnp.float32) for n in range(segments)]
        for j in range(stations):
            pair = a * stations + j
            at = pl.ds(pair * 8 if isinstance(pair, int) else pl.multiple_of(pair * 8, 8), 8)
            real_sum = imag_sum = None
            for n in range(segments):
                real_src, imag_src = tiles[n][:8], tiles[n][8:]
                if weight_of is not None:
                    weight = jnp.broadcast_to(weight_of(n, pair), (8, LANES))
                    real_src, imag_src = real_src * weight, imag_src * weight
                real_loc, imag_loc = local_of(n, a, j)
                real_term = real_src * real_loc + imag_src * imag_loc
                imag_term = imag_src * real_loc - real_src * imag_loc
                real_sum = real_term if real_sum is None else real_sum + real_term
                imag_sum = imag_term if imag_sum is None else imag_sum + imag_term
            real_x[at, :] = real_sum
            imag_x[at, :] = imag_sum
        return carry

    if count <= 8:
        for a in range(count):
            one_source(a, 0)
    else:
        lax.fori_loop(0, count, one_source, 0, unroll=2)


def pack(rows, bands, real_x, imag_x, packed):
    for band in range(bands):
        at = pl.ds(band * LANES, LANES)
        strided = pl.ds(band, rows, stride=8)
        packed[0, :, at] = real_x[strided, :].astype(jnp.bfloat16)
        packed[1, :, at] = imag_x[strided, :].astype(jnp.bfloat16)


def source_tile(sources_ref, base, count, stations):
    def tile_of(n, a):
        start = a % stations * 16
        start = start if isinstance(a, int) else pl.multiple_of(start, 16)
        return sources_ref[base + a // stations * count + n, pl.ds(start, 16), :]

    return tile_of


def block_sums(sizes, first_block, count, table, wide, local, sources_ref, kept_ref, sent_ref, real_x, imag_x, packed):
    stations, bands, seg = sizes[:3]
    pairs = stations * stations
    add_products(
        stations, count * stations, seg, source_tile(sources_ref, 0, seg, stations),
        lambda n, pair: wide[n, pl.ds(first_block * pairs + pair, 1), :],
        lambda n, a, j: (local[n, j, 0], local[n, j, 1]),
        real_x, imag_x,
    )
    both_sums(sizes, count * pairs, table, kept_ref, sent_ref, real_x, imag_x, packed)


def both_sums(sizes, rows, table, real_x, imag_x, packed):
    pack(rows, sizes[1], real_x, imag_x, packed)
    dot = functools.partial(jnp.dot, preferred_element_type=jnp.float32)
    even, odd = dot(packed[0], table[0]), dot(packed[1], table[1])
    return even + odd, even - odd


def turned_round(sums):
    index = LANES - 1 - lax.broadcasted_iota(jnp.int32, (sums.shape[0], LANES), 1)
    runs = [sums[:, at : at + LANES] for at in reversed(range(0, sums.shape[1], LANES))]
    runs = [jnp.take_along_axis(run, index, axis=1, mode="promise_in_bounds") for run in runs]
    return jnp.concatenate(runs, axis=1)


def block_sums(sizes, first_block, count, table, wide, local, sources_ref, real_x, imag_x, packed):
    stations, bands, seg = sizes[:3]
    pairs = stations * stations
    add_products(
        stations, count * stations, seg, source_tile(sources_ref, 0, seg, stations),
        lambda n, pair: wide[n, pl.ds(first_block * pairs + pair, 1), :],
        lambda n, a, j: (local[n, j, 0], local[n, j, 1]),
        real_x, imag_x,
    )
    return both_sums(sizes, count * pairs, table, real_x, imag_x, packed)


def keep_and_send(before, after, kept_ref, sent_ref):
    first_core = lax.axis_index("pol") == 0
    kept_ref[...] = jnp.where(first_core, before, after)
    sent_ref[...] = jnp.where(first_core, after, before).astype(sent_ref.dtype)


def all_blocks_kernel(sizes, table, phase, mine_ref, sources_ref, kept_ref, sent_ref, local, wide, *scratch):
    spread_weights(sizes, mine_ref, wide)
    turn_locals(sizes, phase[0], phase[1], mine_ref, local)
    before, after = block_sums(sizes, 0, sizes[5], table, wide, local, sources_ref, *scratch)
    keep_and_send(turned_round(before), after, kept_ref, sent_ref)


def own_block_kernel(sizes, table, phase, mine_ref, kept_ref, sent_ref, local_ref, wide_ref, *scratch):
    spread_weights(sizes, mine_ref, wide_ref)
    turn_locals(sizes, phase[0], phase[1], mine_ref, local_ref)
    before, after = block_sums(sizes, 0, 1, table, wide_ref, local_ref, mine_ref, *scratch)
    keep_and_send(turned_round(before), after, kept_ref, sent_ref)


def weigh_kernel(sizes, wide_ref, local_ref, weighted_ref):
    stations, bands, seg = sizes[:3]
    for a in range(stations):
        for j in range(stations):
            pair = stations * stations + a * stations + j
            for g in range(seg):
                weight = jnp.broadcast_to(wide_ref[g, pl.ds(pair, 1), :], (bands, LANES))
                weighted_ref[a, j, g, 0] = local_ref[g, j, 0] * weight
                weighted_ref[a, j, g, 1] = local_ref[g, j, 1] * weight


def other_block_kernel(sizes, table, weighted_ref, own_sent_ref, sources_ref, kept_ref, sent_ref, *scratch):
    stations, bands, seg = sizes[:3]
    pairs = stations * stations
    add_products(
        stations, stations, seg, source_tile(sources_ref, 0, seg, stations),
        None,
        lambda n, a, j: (weighted_ref[a, j, n, 0], weighted_ref[a, j, n, 1]),
        *scratch[:2],
    )
    before, after = both_sums(sizes, pairs, table, *scratch)
    sent_ref[pl.ds(0, pairs), :] = own_sent_ref[...]
    first_core = lax.axis_index("pol") == 0

    @pl.when(first_core)
    def _():
        kept_ref[...] = before
        sent_ref[pl.ds(pairs, pairs), :] = after.astype(sent_ref.dtype)

    @pl.when(jnp.logical_not(first_core))
    def _():
        kept_ref[...] = after
        sent_ref[pl.ds(pairs, pairs), :] = turned_round(before).astype(sent_ref.dtype)


def settle_kernel(sizes, kept_ref, settled_ref):
    kept = kept_ref[...]
    settled_ref[...] = jnp.where(lax.axis_index("pol") == 0, turned_round(kept), kept)


def combine_kernel(sizes, kept_ref, got_ref, lags_ref):
    lags_ref[...] = kept_ref[...] + got_ref[...].astype(jnp.float32)


def place_kernel(sizes, mask_ref, own_ref, other_ref, got_ref, out_ref, steps, sems):
    pairs = sizes[0] * sizes[0]
    own = own_ref[...] + got_ref[pl.ds(0, pairs), :].astype(jnp.float32)
    other = other_ref[...] + got_ref[pl.ds(pairs, pairs), :].astype(jnp.float32)
    copies = []
    for step in range(STEPS):
        mask = jnp.broadcast_to(mask_ref[step, :1, :1], other.shape)
        steps[step] = jnp.where(mask > 0, own, other)
        copies.append(pltpu.make_async_copy(steps.at[step], out_ref.at[step], sems.at[step]))
        copies[-1].start()
    for copy in copies:
        copy.wait()


def fetch_kernel(sizes, table_hbm, plan_any, after, table_ref, phase_ref, mask_ref, plan_ref, sems):
    del after
    copies = [
        pltpu.make_async_copy(table_hbm.at[lax.axis_index("pol")], table_ref, sems.at[0]),
        pltpu.make_async_copy(plan_any, plan_ref, sems.at[1]),
    ]
    for copy in copies:
        copy.start()
    phase_ref[0], phase_ref[1] = middle_phase(sizes)
    copies[1].wait()
    for step in range(STEPS):
        own = (plan_ref[step] == lax.axis_index("sta")).astype(jnp.float32)
        mask_ref[step] = jnp.full(mask_ref.shape[1:], own, jnp.float32)
    copies[0].wait()


def join_kernel(ranges, *refs):
    *pieces, out_ref = refs
    at = 0
    for piece, (first, count) in zip(pieces, ranges):
        out_ref[pl.ds(at, count)] = piece[pl.ds(first, count), pl.ds(0, out_ref.shape[1]), :]
        at += count


def join(*pieces, rows=None):
    pieces = [piece if isinstance(piece, tuple) else (piece, 0, piece.shape[0]) for piece in pieces]
    arrays = [piece[0] for piece in pieces]
    ranges = [piece[1:] for piece in pieces]
    vmem = pl.BlockSpec(memory_space=pltpu.VMEM)
    return pl.pallas_call(
        functools.partial(join_kernel, ranges),
        out_shape=pltpu.VMEM(
            (sum(count for _, count in ranges), rows or arrays[0].shape[1], LANES), arrays[0].dtype
        ),
        in_specs=[vmem] * len(arrays),
        out_specs=vmem,
        compiler_params=pltpu.CompilerParams(vmem_limit_bytes=VMEM_BYTES),
        name="join",
    )(*arrays)


def fetch_from(value, axes, source_of):
    sizes = tuple(lax.axis_size(axis) for axis in axes)
    pairs = []
    for index in np.ndindex(*sizes):
        source = source_of(*index)
        pairs.append((int(np.ravel_multi_index(source, sizes)), int(np.ravel_multi_index(index, sizes))))
    return lax.ppermute(value, axes, pairs)


def exchange(value, axis, distance):
    return fetch_from(value, (axis,), lambda i: (i ^ distance,))


def shards(table, raw_spectra, owner_plan, pair_valid, quality):
    seg, sta, pol = (lax.axis_size(name) for name in ("seg", "sta", "pol"))
    _, stations, _, bins = raw_spectra.shape
    bands = bins // BAND
    fast = sta == 2 and pol == 2 and seg == 4
    blocks = 2 if fast else STEPS
    pairs = stations * stations
    lags = table.shape[3]
    rows = 2 * stations * bands + 16
    sizes = (stations, bands, seg, sta, pol, blocks, lags)

    raw = raw_spectra.reshape(stations, 2, bands, BAND).transpose(0, 2, 1, 3).reshape(-1, BAND)
    vmem = pl.BlockSpec(memory_space=pltpu.VMEM)
    smem = pl.BlockSpec(memory_space=pltpu.SMEM)
    hbm = pl.BlockSpec(memory_space=pltpu.HBM)
    plan = [] if fast else [owner_plan]
    in_hbm = functools.partial(pltpu.with_memory_space_constraint, memory_space=pltpu.HBM)
    own = pl.pallas_call(
        functools.partial(prepare_kernel, (stations, bands, sta, blocks)),
        out_shape=pltpu.VMEM((1, rows, LANES), jnp.bfloat16),
        in_specs=[smem] * len(plan) + [vmem, vmem, vmem],
        out_specs=vmem,
        scratch_shapes=[pltpu.VMEM((2 * stations * bands, LANES), jnp.float32)],
        compiler_params=pltpu.CompilerParams(vmem_limit_bytes=VMEM_BYTES),
        name="prepare",
    )(*plan, in_hbm(raw), in_hbm(jnp.transpose(pair_valid[0])), in_hbm(quality))

    def call(kernel, out_shape, *args, out_specs=None, scratch=(), flops=0, moved=0, name=None):
        many = isinstance(out_shape, (list, tuple))
        return pl.pallas_call(
            functools.partial(kernel, sizes),
            out_shape=out_shape,
            in_specs=[hbm if x is table_const or x is plan_const else vmem for x in args],
            out_specs=out_specs or ([vmem] * len(out_shape) if many else vmem),
            scratch_shapes=list(scratch),
            compiler_params=pltpu.CompilerParams(vmem_limit_bytes=VMEM_BYTES),
            cost_estimate=pl.CostEstimate(flops=flops, bytes_accessed=moved, transcendentals=0),
            name=name,
        )(*args)

    f32 = jnp.float32
    table_const, plan_const = in_hbm(table), in_hbm(owner_plan)

    def fetch(after):
        return call(
            fetch_kernel,
            [
                pltpu.VMEM(table.shape[1:], table.dtype),
                pltpu.VMEM((2, bands, LANES), f32),
                pltpu.VMEM((STEPS, 8, LANES), f32),
            ],
            table_const, plan_const, after,
            scratch=[pltpu.SMEM((STEPS,), jnp.int32), pltpu.SemaphoreType.DMA((2,))],
            moved=4 * table.size // pol,
            name="fetch",
        )

    def products(count):
        return [pltpu.VMEM((count * pairs * 8, LANES), f32)] * 2 + [pltpu.VMEM((2, count * pairs, bins), jnp.bfloat16)]

    quarter = 32 * pairs * 2 * bins * lags
    local_shape = pltpu.VMEM((seg, stations, 2, bands, LANES), f32)
    wide_shape = pltpu.VMEM((seg, blocks * pairs, LANES), f32)
    kept_shape = pltpu.VMEM((pairs, lags), f32)

    if fast:
        far = join(own, exchange(own, "seg", 2))
        table, phase, mask = fetch(own)
        far, table = lax.optimization_barrier((far, table))
        bare = join(far, rows=rows - 16)
        near = exchange(far, "seg", 1)
        across = fetch_from(bare, ("seg", "sta"), lambda z, x: (z ^ 1, x ^ 1))
        partner = exchange(bare, "sta", 1)
        mine = join(far, near)
        own_kept, own_sent, local, wide = call(
            own_block_kernel, [kept_shape, pltpu.VMEM((pairs, lags), jnp.bfloat16), local_shape, wide_shape],
            table, phase, mine,
            scratch=products(1), flops=8 * quarter, name="own_block",
        )
        weighted = call(
            weigh_kernel, pltpu.VMEM((stations, stations, seg, 2, bands, LANES), f32),
            wide, local,
            flops=8 * quarter, name="weigh",
        )
        weighted, across, partner = lax.optimization_barrier((weighted, across, partner))
        kept, sent = call(
            other_block_kernel, [kept_shape, pltpu.VMEM((2 * pairs, lags), jnp.bfloat16)],
            table, weighted, own_sent, join(partner, across),
            scratch=products(1), flops=quarter, name="other_block",
        )
        got = exchange(sent, "pol", 1)
        kept = call(settle_kernel, kept_shape, kept, flops=quarter, name="settle")
        result = call(
            place_kernel, jax.ShapeDtypeStruct((STEPS, pairs, lags), f32),
            mask, own_kept, kept, got,
            out_specs=hbm,
            scratch=[pltpu.VMEM((STEPS, pairs, lags), f32), pltpu.SemaphoreType.DMA((STEPS,))],
            name="place",
        )
    else:
        mine, distance = own, seg // 2
        while distance:
            mine = join(mine, exchange(mine, "seg", distance))
            distance //= 2
        gathered = lax.all_gather(mine, "sta")
        sources = join(*(gathered[owner_plan[k]] for k in range(STEPS)))
        table, phase, _ = fetch(mine)
        kept, sent = call(
            all_blocks_kernel,
            [pltpu.VMEM((blocks * pairs, lags), f32), pltpu.VMEM((blocks * pairs, lags), jnp.bfloat16)],
            table, phase, mine, sources,
            scratch=[local_shape, wide_shape] + products(blocks), flops=blocks * quarter, name="all_blocks",
        )
        result = call(
            combine_kernel, jax.ShapeDtypeStruct((blocks * pairs, lags), f32),
            kept, exchange(sent, "pol", 1), name="combine",
        )
    return result.reshape(STEPS, stations, stations, lags)


def solution(mesh):
    placed = (
        P(("groups", "seg"), "sta", None, "pol"),
        P("groups"),
        P(("groups", "seg"), None, "sta"),
        P(("groups", "seg"), None),
    )

    def whole(raw_spectra, owner_plan, pair_valid, quality):
        seg, pol = mesh.shape["seg"], mesh.shape["pol"]
        bins = raw_spectra.shape[3]
        segments = raw_spectra.shape[0] // mesh.shape["groups"]
        table = lag_table(2 * bins // seg, bins, pol, 1.0 / math.sqrt(bins * segments))
        return jax.shard_map(
            shards,
            mesh=mesh,
            in_specs=(P(),) + placed,
            out_specs=P("groups", None, "sta", ("seg", "pol")),
            check_vma=False,
        )(jnp.asarray(table), raw_spectra, owner_plan, pair_valid, quality)

    return whole
```

```python
import functools
import math

import jax
import jax.numpy as jnp
import numpy as np
from jax import lax
from jax.experimental import pallas as pl
from jax.experimental.pallas import tpu as pltpu
from jax.sharding import PartitionSpec as P

STEPS = 3
BAND = 128
LANES = 128
VMEM_BYTES = 32 * 1024 * 1024


def lag_table(lags, bins, halves, scale):
    bin_index = np.arange(bins, dtype=np.int64)
    lag = 2 * np.arange(lags // 2, dtype=np.int64) + 1
    phase = (bin_index[:, None] * lag[None, :]) % (4 * bins)
    angle = phase * (2.0 * math.pi / (4 * bins))
    factor = np.where(bin_index == 0, 1.0, 2.0)[:, None] * scale
    parts = np.stack([np.cos(angle) * factor, np.sin(angle) * factor])
    parts = parts.reshape(2, halves, bins // halves, lags // 2).transpose(1, 0, 2, 3)
    return parts.astype(jnp.bfloat16)


def turn(count, period):
    count = count % period
    quarter = (count + period // 8) // (period // 4)
    x = (count - quarter * (period // 4)).astype(jnp.float32) * (2.0 * math.pi / period)
    y = x * x
    sine = x * (1.0 + y * (-1 / 6 + y * (1 / 120 + y * (-1 / 5040 + y * (1 / 362880)))))
    cosine = 1.0 + y * (-1 / 2 + y * (1 / 24 + y * (-1 / 720 + y * (1 / 40320))))
    quarter = quarter % 4
    odd = quarter % 2 == 1
    real = jnp.where(odd, sine, cosine)
    imag = jnp.where(odd, cosine, sine)
    real = jnp.where((quarter == 1) | (quarter == 2), -real, real)
    imag = jnp.where(quarter >= 2, -imag, imag)
    return real, imag


def prepare_kernel(sizes, *refs):
    stations, bands, sta, blocks = sizes
    *plan, raw_ref, valid_ref, quality_ref, out_ref, wide = refs
    total = stations * sta
    me = lax.axis_index("sta")
    wide[...] = raw_ref[...].astype(jnp.float32)
    count = stations * bands
    real = wide[pl.ds(0, count, stride=2), :]
    imag = wide[pl.ds(1, count, stride=2), :]
    power = jnp.sum(real * real + imag * imag, axis=1, keepdims=True) * (1.0 / (2 * BAND))
    inverse = 1.0 / jnp.sqrt(power + 1e-06)
    real = (real * inverse).reshape(stations, bands, LANES)
    imag = (imag * inverse).reshape(stations, bands, LANES)
    white = jnp.concatenate([real, imag], axis=1).reshape(2 * count, LANES).astype(jnp.bfloat16)

    valid = valid_ref[...].astype(jnp.float32).astype(jnp.bfloat16)
    quality = jnp.broadcast_to(quality_ref[...].astype(jnp.float32), (8, total)).astype(jnp.bfloat16)
    pair = lax.broadcasted_iota(jnp.int32, (total, LANES), 1)
    station = lax.broadcasted_iota(jnp.int32, (total, LANES), 0)
    mine = lax.broadcasted_iota(jnp.int32, (stations, LANES), 0) == (
        lax.broadcasted_iota(jnp.int32, (stations, LANES), 1) % stations
    )
    dot = functools.partial(jnp.dot, preferred_element_type=jnp.float32)
    pick_local = (station == me * stations + pair % stations).astype(jnp.float32).astype(jnp.bfloat16)
    local_flags = dot(quality, pick_local)
    rows = []
    for k in range(blocks):
        source = (plan[0][k] if plan else k) * stations + pair // stations
        pick_source = (station == source).astype(jnp.float32).astype(jnp.bfloat16)
        valid_row = jnp.sum(jnp.where(mine, dot(valid, pick_source), 0.0), axis=0, keepdims=True)
        rows.append(valid_row * (dot(quality, pick_source) * local_flags)[:1])
    rows.append(jnp.zeros((16 - blocks, LANES), jnp.float32))
    weights = jnp.concatenate(rows, axis=0).astype(jnp.bfloat16)
    out_ref[0, pl.ds(0, 2 * count), :] = white
    out_ref[0, pl.ds(2 * count, 16), :] = weights


def spread_weights(sizes, locals_ref, wide):
    stations, bands, seg, sta, pol, blocks, lags = sizes
    pairs = stations * stations
    row_index = lax.broadcasted_iota(jnp.int32, (16, LANES), 0)
    diagonal = lax.broadcasted_iota(jnp.int32, (pairs, LANES), 0) == lax.broadcasted_iota(
        jnp.int32, (pairs, LANES), 1
    )
    ones = jnp.ones((LANES, LANES), jnp.bfloat16)
    for g in range(seg):
        flags = locals_ref[g, pl.ds(2 * stations * bands, 16), :].astype(jnp.float32)
        spread = []
        for n in range(blocks):
            block = lax.axis_index("sta") ^ n if sta == 2 else n
            row = jnp.sum(jnp.where(row_index == block, flags, 0.0), axis=0, keepdims=True)
            spread.append(jnp.where(diagonal, row, 0.0))
        spread = jnp.concatenate(spread, axis=0).astype(jnp.bfloat16)
        wide[g] = jnp.dot(spread, ones, preferred_element_type=jnp.float32)


def middle_phase(sizes):
    stations, bands, seg, sta, pol, blocks, lags = sizes
    row = lax.axis_index("pol") * bands + lax.broadcasted_iota(jnp.int32, (bands, LANES), 0)
    bin_index = row * LANES + lax.broadcasted_iota(jnp.int32, (bands, LANES), 1)
    run = pol * lags
    return turn(bin_index * (2 * run * lax.axis_index("seg") + run - 1), 2 * run * seg)


def turn_locals(sizes, cosine, sine, locals_ref, local):
    stations, bands, seg = sizes[:3]
    for g in range(seg):
        for j in range(stations):
            tile = locals_ref[g, pl.ds(j * 16, 16), :].astype(jnp.float32)
            local[g, j, 0] = tile[:bands] * cosine + tile[bands:] * sine
            local[g, j, 1] = tile[bands:] * cosine - tile[:bands] * sine


def add_products(stations, count, segments, tile_of, weight_of, local_of, real_x, imag_x):
    def one_source(a, carry):
        tiles = [tile_of(n, a).astype(jnp.float32) for n in range(segments)]
        for j in range(stations):
            pair = a * stations + j
            at = pl.ds(pair * 8 if isinstance(pair, int) else pl.multiple_of(pair * 8, 8), 8)
            real_sum = imag_sum = None
            for n in range(segments):
                weight = jnp.broadcast_to(weight_of(n, pair), (8, LANES))
                real_src, imag_src = tiles[n][:8] * weight, tiles[n][8:] * weight
                real_loc, imag_loc = local_of(n, a, j)
                real_term = real_src * real_loc + imag_src * imag_loc
                imag_term = imag_src * real_loc - real_src * imag_loc
                real_sum = real_term if real_sum is None else real_sum + real_term
                imag_sum = imag_term if imag_sum is None else imag_sum + imag_term
            real_x[at, :] = real_sum
            imag_x[at, :] = imag_sum
        return carry

    if count <= 8:
        for a in range(count):
            one_source(a, 0)
    else:
        lax.fori_loop(0, count, one_source, 0, unroll=2)


def pack(rows, bands, real_x, imag_x, packed):
    for band in range(bands):
        at = pl.ds(band * LANES, LANES)
        strided = pl.ds(band, rows, stride=8)
        packed[0, :, at] = real_x[strided, :].astype(jnp.bfloat16)
        packed[1, :, at] = imag_x[strided, :].astype(jnp.bfloat16)


def source_tile(sources_ref, base, count, stations):
    def tile_of(n, a):
        start = a % stations * 16
        start = start if isinstance(a, int) else pl.multiple_of(start, 16)
        return sources_ref[base + a // stations * count + n, pl.ds(start, 16), :]

    return tile_of


def block_sums(sizes, first_block, count, table, wide, local, sources_ref, kept_ref, sent_ref, real_x, imag_x, packed):
    stations, bands, seg = sizes[:3]
    pairs = stations * stations
    add_products(
        stations, count * stations, seg, source_tile(sources_ref, 0, seg, stations),
        lambda n, pair: wide[n, pl.ds(first_block * pairs + pair, 1), :],
        lambda n, a, j: (local[n, j, 0], local[n, j, 1]),
        real_x, imag_x,
    )
    both_sums(sizes, count * pairs, table, kept_ref, sent_ref, real_x, imag_x, packed)


def both_sums(sizes, rows, table, real_x, imag_x, packed):
    pack(rows, sizes[1], real_x, imag_x, packed)
    dot = functools.partial(jnp.dot, preferred_element_type=jnp.float32)
    even, odd = dot(packed[0], table[0]), dot(packed[1], table[1])
    return even + odd, even - odd


def turned_round(sums):
    index = LANES - 1 - lax.broadcasted_iota(jnp.int32, (sums.shape[0], LANES), 1)
    runs = [sums[:, at : at + LANES] for at in reversed(range(0, sums.shape[1], LANES))]
    runs = [jnp.take_along_axis(run, index, axis=1, mode="promise_in_bounds") for run in runs]
    return jnp.concatenate(runs, axis=1)


def block_sums(sizes, first_block, count, table, wide, local, sources_ref, real_x, imag_x, packed):
    stations, bands, seg = sizes[:3]
    pairs = stations * stations
    add_products(
        stations, count * stations, seg, source_tile(sources_ref, 0, seg, stations),
        lambda n, pair: wide[n, pl.ds(first_block * pairs + pair, 1), :],
        lambda n, a, j: (local[n, j, 0], local[n, j, 1]),
        real_x, imag_x,
    )
    return both_sums(sizes, count * pairs, table, real_x, imag_x, packed)


def keep_and_send(before, after, kept_ref, sent_ref):
    first_core = lax.axis_index("pol") == 0
    kept_ref[...] = jnp.where(first_core, before, after)
    sent_ref[...] = jnp.where(first_core, after, before).astype(sent_ref.dtype)


def all_blocks_kernel(sizes, table, phase, mine_ref, sources_ref, kept_ref, sent_ref, local, wide, *scratch):
    spread_weights(sizes, mine_ref, wide)
    turn_locals(sizes, phase[0], phase[1], mine_ref, local)
    before, after = block_sums(sizes, 0, sizes[5], table, wide, local, sources_ref, *scratch)
    keep_and_send(turned_round(before), after, kept_ref, sent_ref)


def both_blocks_kernel(
    sizes, table, phase, mine_ref, others_ref, kept_ref, sent_ref, local, wide, real_x, imag_x, packed
):
    stations, bands, seg = sizes[:3]
    pairs = stations * stations
    spread_weights(sizes, mine_ref, wide)
    turn_locals(sizes, phase[0], phase[1], mine_ref, local)
    for block, sources_ref in enumerate((mine_ref, others_ref)):
        rows = pl.ds(block * pairs * 8, pairs * 8)
        add_products(
            stations, stations, seg, source_tile(sources_ref, 0, seg, stations),
            lambda n, pair: wide[n, pl.ds(block * pairs + pair, 1), :],
            lambda n, a, j: (local[n, j, 0], local[n, j, 1]),
            real_x.at[rows], imag_x.at[rows],
        )
    before, after = both_sums(sizes, 2 * pairs, table, real_x, imag_x, packed)
    first_core = lax.axis_index("pol") == 0

    @pl.when(first_core)
    def _():
        kept_ref[...] = before
        sent_ref[...] = after.astype(sent_ref.dtype)

    @pl.when(jnp.logical_not(first_core))
    def _():
        kept_ref[...] = after
        sent_ref[...] = turned_round(before).astype(sent_ref.dtype)


def arrange_kernel(sizes, far_ref, across_ref, first_ref, second_ref, mine_ref, others_ref):
    half = far_ref.shape[0]
    rows = pl.ds(0, others_ref.shape[1])
    mine_ref[pl.ds(0, half)] = far_ref[...]
    others_ref[pl.ds(half, half)] = across_ref[:, rows, :]
    first_core = lax.axis_index("pol") == 0

    @pl.when(first_core)
    def _():
        mine_ref[pl.ds(half, half)] = first_ref[...]
        others_ref[pl.ds(0, half)] = second_ref[:, rows, :]

    @pl.when(jnp.logical_not(first_core))
    def _():
        mine_ref[pl.ds(half, half)] = second_ref[...]
        others_ref[pl.ds(0, half)] = first_ref[:, rows, :]


def settle_kernel(sizes, kept_ref, settled_ref):
    kept = kept_ref[...]
    settled_ref[...] = jnp.where(lax.axis_index("pol") == 0, turned_round(kept), kept)


def combine_kernel(sizes, kept_ref, got_ref, lags_ref):
    lags_ref[...] = kept_ref[...] + got_ref[...].astype(jnp.float32)


def place_kernel(sizes, mask_ref, kept_ref, got_ref, out_ref, steps, sems):
    pairs = sizes[0] * sizes[0]
    own, other = (
        kept_ref[rows, :] + got_ref[rows, :].astype(jnp.float32) for rows in (pl.ds(0, pairs), pl.ds(pairs, pairs))
    )
    copies = []
    for step in range(STEPS):
        mask = jnp.broadcast_to(mask_ref[step, :1, :1], other.shape)
        steps[step] = jnp.where(mask > 0, own, other)
        copies.append(pltpu.make_async_copy(steps.at[step], out_ref.at[step], sems.at[step]))
        copies[-1].start()
    for copy in copies:
        copy.wait()


def fetch_kernel(sizes, table_hbm, plan_any, after, table_ref, phase_ref, mask_ref, plan_ref, sems):
    del after
    copies = [
        pltpu.make_async_copy(table_hbm.at[lax.axis_index("pol")], table_ref, sems.at[0]),
        pltpu.make_async_copy(plan_any, plan_ref, sems.at[1]),
    ]
    for copy in copies:
        copy.start()
    phase_ref[0], phase_ref[1] = middle_phase(sizes)
    copies[1].wait()
    for step in range(STEPS):
        own = (plan_ref[step] == lax.axis_index("sta")).astype(jnp.float32)
        mask_ref[step] = jnp.full(mask_ref.shape[1:], own, jnp.float32)
    copies[0].wait()


def join_kernel(ranges, *refs):
    *pieces, out_ref = refs
    at = 0
    for piece, (first, count) in zip(pieces, ranges):
        out_ref[pl.ds(at, count)] = piece[pl.ds(first, count), pl.ds(0, out_ref.shape[1]), :]
        at += count


def join(*pieces, rows=None):
    pieces = [piece if isinstance(piece, tuple) else (piece, 0, piece.shape[0]) for piece in pieces]
    arrays = [piece[0] for piece in pieces]
    ranges = [piece[1:] for piece in pieces]
    vmem = pl.BlockSpec(memory_space=pltpu.VMEM)
    return pl.pallas_call(
        functools.partial(join_kernel, ranges),
        out_shape=pltpu.VMEM(
            (sum(count for _, count in ranges), rows or arrays[0].shape[1], LANES), arrays[0].dtype
        ),
        in_specs=[vmem] * len(arrays),
        out_specs=vmem,
        compiler_params=pltpu.CompilerParams(vmem_limit_bytes=VMEM_BYTES),
        name="join",
    )(*arrays)


def fetch_from(value, axes, source_of):
    sizes = tuple(lax.axis_size(axis) for axis in axes)
    pairs = []
    for index in np.ndindex(*sizes):
        source = source_of(*index)
        pairs.append((int(np.ravel_multi_index(source, sizes)), int(np.ravel_multi_index(index, sizes))))
    return lax.ppermute(value, axes, pairs)


def exchange(value, axis, distance):
    return fetch_from(value, (axis,), lambda i: (i ^ distance,))


def shards(table, raw_spectra, owner_plan, pair_valid, quality):
    seg, sta, pol = (lax.axis_size(name) for name in ("seg", "sta", "pol"))
    _, stations, _, bins = raw_spectra.shape
    bands = bins // BAND
    fast = sta == 2 and pol == 2 and seg == 4
    blocks = 2 if fast else STEPS
    pairs = stations * stations
    lags = table.shape[3]
    rows = 2 * stations * bands + 16
    sizes = (stations, bands, seg, sta, pol, blocks, lags)

    raw = raw_spectra.reshape(stations, 2, bands, BAND).transpose(0, 2, 1, 3).reshape(-1, BAND)
    vmem = pl.BlockSpec(memory_space=pltpu.VMEM)
    smem = pl.BlockSpec(memory_space=pltpu.SMEM)
    hbm = pl.BlockSpec(memory_space=pltpu.HBM)
    plan = [] if fast else [owner_plan]
    in_hbm = functools.partial(pltpu.with_memory_space_constraint, memory_space=pltpu.HBM)
    own = pl.pallas_call(
        functools.partial(prepare_kernel, (stations, bands, sta, blocks)),
        out_shape=pltpu.VMEM((1, rows, LANES), jnp.bfloat16),
        in_specs=[smem] * len(plan) + [vmem, vmem, vmem],
        out_specs=vmem,
        scratch_shapes=[pltpu.VMEM((2 * stations * bands, LANES), jnp.float32)],
        compiler_params=pltpu.CompilerParams(vmem_limit_bytes=VMEM_BYTES),
        name="prepare",
    )(*plan, in_hbm(raw), in_hbm(jnp.transpose(pair_valid[0])), in_hbm(quality))

    def call(kernel, out_shape, *args, out_specs=None, scratch=(), flops=0, moved=0, name=None):
        many = isinstance(out_shape, (list, tuple))
        return pl.pallas_call(
            functools.partial(kernel, sizes),
            out_shape=out_shape,
            in_specs=[hbm if x is table_const or x is plan_const else vmem for x in args],
            out_specs=out_specs or ([vmem] * len(out_shape) if many else vmem),
            scratch_shapes=list(scratch),
            compiler_params=pltpu.CompilerParams(vmem_limit_bytes=VMEM_BYTES),
            cost_estimate=pl.CostEstimate(flops=flops, bytes_accessed=moved, transcendentals=0),
            name=name,
        )(*args)

    f32 = jnp.float32
    table_const, plan_const = in_hbm(table), in_hbm(owner_plan)

    def fetch(after):
        return call(
            fetch_kernel,
            [
                pltpu.VMEM(table.shape[1:], table.dtype),
                pltpu.VMEM((2, bands, LANES), f32),
                pltpu.VMEM((STEPS, 8, LANES), f32),
            ],
            table_const, plan_const, after,
            scratch=[pltpu.SMEM((STEPS,), jnp.int32), pltpu.SemaphoreType.DMA((2,))],
            moved=4 * table.size // pol,
            name="fetch",
        )

    def products(count):
        return [pltpu.VMEM((count * pairs * 8, LANES), f32)] * 2 + [pltpu.VMEM((2, count * pairs, bins), jnp.bfloat16)]

    quarter = 32 * pairs * 2 * bins * lags
    local_shape = pltpu.VMEM((seg, stations, 2, bands, LANES), f32)
    wide_shape = pltpu.VMEM((seg, blocks * pairs, LANES), f32)

    if fast:
        distant = exchange(own, "seg", 2)
        table, phase, mask = fetch(own)
        distant, table = lax.optimization_barrier((distant, table))
        far = join(own, distant)
        axes = ("seg", "sta", "pol")
        across = fetch_from(far, axes, lambda z, x, core: (z ^ 1, x ^ 1, core))
        first = fetch_from(far, axes, lambda z, x, core: (z ^ 1 ^ core, x ^ core, core))
        second = fetch_from(far, axes, lambda z, x, core: (z ^ core, x ^ 1 ^ core, core))
        mine, others = call(
            arrange_kernel,
            [pltpu.VMEM((seg, r, LANES), jnp.bfloat16) for r in (rows, rows - 16)],
            far, across, first, second,
            name="arrange",
        )
        kept_shape = pltpu.VMEM((2 * pairs, lags), f32)
        kept, sent = call(
            both_blocks_kernel, [kept_shape, pltpu.VMEM((2 * pairs, lags), jnp.bfloat16)],
            table, phase, mine, others,
            scratch=[local_shape, wide_shape] + products(2), flops=quarter, name="both_blocks",
        )
        got = exchange(sent, "pol", 1)
        kept = call(settle_kernel, kept_shape, kept, flops=quarter, name="settle")
        result = call(
            place_kernel, jax.ShapeDtypeStruct((STEPS, pairs, lags), f32),
            mask, kept, got,
            out_specs=hbm,
            scratch=[pltpu.VMEM((STEPS, pairs, lags), f32), pltpu.SemaphoreType.DMA((STEPS,))],
            name="place",
        )
    else:
        mine, distance = own, seg // 2
        while distance:
            mine = join(mine, exchange(mine, "seg", distance))
            distance //= 2
        gathered = lax.all_gather(mine, "sta")
        sources = join(*(gathered[owner_plan[k]] for k in range(STEPS)))
        table, phase, _ = fetch(mine)
        kept, sent = call(
            all_blocks_kernel,
            [pltpu.VMEM((blocks * pairs, lags), f32), pltpu.VMEM((blocks * pairs, lags), jnp.bfloat16)],
            table, phase, mine, sources,
            scratch=[local_shape, wide_shape] + products(blocks), flops=blocks * quarter, name="all_blocks",
        )
        result = call(
            combine_kernel, jax.ShapeDtypeStruct((blocks * pairs, lags), f32),
            kept, exchange(sent, "pol", 1), name="combine",
        )
    return result.reshape(STEPS, stations, stations, lags)


def solution(mesh):
    placed = (
        P(("groups", "seg"), "sta", None, "pol"),
        P("groups"),
        P(("groups", "seg"), None, "sta"),
        P(("groups", "seg"), None),
    )

    def whole(raw_spectra, owner_plan, pair_valid, quality):
        seg, pol = mesh.shape["seg"], mesh.shape["pol"]
        bins = raw_spectra.shape[3]
        segments = raw_spectra.shape[0] // mesh.shape["groups"]
        table = lag_table(2 * bins // seg, bins, pol, 1.0 / math.sqrt(bins * segments))
        return jax.shard_map(
            shards,
            mesh=mesh,
            in_specs=(P(),) + placed,
            out_specs=P("groups", None, "sta", ("seg", "pol")),
            check_vma=False,
        )(jnp.asarray(table), raw_spectra, owner_plan, pair_valid, quality)

    return whole
```

```python
import functools
import math

import jax
import jax.numpy as jnp
import numpy as np
from jax import lax
from jax.experimental import pallas as pl
from jax.experimental.pallas import tpu as pltpu
from jax.sharding import PartitionSpec as P

STEPS = 3
BAND = 128
LANES = 128
VMEM_BYTES = 32 * 1024 * 1024


def lag_table(lags, bins, halves, scale):
    bin_index = np.arange(bins, dtype=np.int64)
    lag = 2 * np.arange(lags // 2, dtype=np.int64) + 1
    phase = (bin_index[:, None] * lag[None, :]) % (4 * bins)
    angle = phase * (2.0 * math.pi / (4 * bins))
    factor = np.where(bin_index == 0, 1.0, 2.0)[:, None] * scale
    parts = np.stack([np.cos(angle) * factor, np.sin(angle) * factor])
    parts = parts.reshape(2, halves, bins // halves, lags // 2).transpose(1, 0, 2, 3)
    return parts.astype(jnp.bfloat16)


def turn(count, period):
    count = count % period
    quarter = (count + period // 8) // (period // 4)
    x = (count - quarter * (period // 4)).astype(jnp.float32) * (2.0 * math.pi / period)
    y = x * x
    sine = x * (1.0 + y * (-1 / 6 + y * (1 / 120 + y * (-1 / 5040 + y * (1 / 362880)))))
    cosine = 1.0 + y * (-1 / 2 + y * (1 / 24 + y * (-1 / 720 + y * (1 / 40320))))
    quarter = quarter % 4
    odd = quarter % 2 == 1
    real = jnp.where(odd, sine, cosine)
    imag = jnp.where(odd, cosine, sine)
    real = jnp.where((quarter == 1) | (quarter == 2), -real, real)
    imag = jnp.where(quarter >= 2, -imag, imag)
    return real, imag


def prepare_kernel(sizes, *refs):
    stations, bands, sta, blocks = sizes
    *plan, raw_ref, valid_ref, quality_ref, out_ref, wide = refs
    total = stations * sta
    me = lax.axis_index("sta")
    wide[...] = raw_ref[...].astype(jnp.float32)
    count = stations * bands
    real = wide[pl.ds(0, count, stride=2), :]
    imag = wide[pl.ds(1, count, stride=2), :]
    power = jnp.sum(real * real + imag * imag, axis=1, keepdims=True) * (1.0 / (2 * BAND))
    inverse = 1.0 / jnp.sqrt(power + 1e-06)
    real = (real * inverse).reshape(stations, bands, LANES)
    imag = (imag * inverse).reshape(stations, bands, LANES)
    white = jnp.concatenate([real, imag], axis=1).reshape(2 * count, LANES).astype(jnp.bfloat16)

    valid = valid_ref[...].astype(jnp.float32).astype(jnp.bfloat16)
    quality = jnp.broadcast_to(quality_ref[...].astype(jnp.float32), (8, total)).astype(jnp.bfloat16)
    pair = lax.broadcasted_iota(jnp.int32, (total, LANES), 1)
    station = lax.broadcasted_iota(jnp.int32, (total, LANES), 0)
    mine = lax.broadcasted_iota(jnp.int32, (stations, LANES), 0) == (
        lax.broadcasted_iota(jnp.int32, (stations, LANES), 1) % stations
    )
    dot = functools.partial(jnp.dot, preferred_element_type=jnp.float32)
    pick_local = (station == me * stations + pair % stations).astype(jnp.float32).astype(jnp.bfloat16)
    local_flags = dot(quality, pick_local)
    rows = []
    for k in range(blocks):
        source = (plan[0][k] if plan else k) * stations + pair // stations
        pick_source = (station == source).astype(jnp.float32).astype(jnp.bfloat16)
        valid_row = jnp.sum(jnp.where(mine, dot(valid, pick_source), 0.0), axis=0, keepdims=True)
        rows.append(valid_row * (dot(quality, pick_source) * local_flags)[:1])
    rows.append(jnp.zeros((16 - blocks, LANES), jnp.float32))
    weights = jnp.concatenate(rows, axis=0).astype(jnp.bfloat16)
    out_ref[0, pl.ds(0, 2 * count), :] = white
    out_ref[0, pl.ds(2 * count, 16), :] = weights


def spread_weights(sizes, locals_ref, wide):
    stations, bands, seg, sta, pol, blocks, lags = sizes
    pairs = stations * stations
    row_index = lax.broadcasted_iota(jnp.int32, (16, LANES), 0)
    diagonal = lax.broadcasted_iota(jnp.int32, (pairs, LANES), 0) == lax.broadcasted_iota(
        jnp.int32, (pairs, LANES), 1
    )
    ones = jnp.ones((LANES, LANES), jnp.bfloat16)
    for g in range(seg):
        flags = locals_ref[g, pl.ds(2 * stations * bands, 16), :].astype(jnp.float32)
        spread = []
        for n in range(blocks):
            block = lax.axis_index("sta") ^ n if sta == 2 else n
            row = jnp.sum(jnp.where(row_index == block, flags, 0.0), axis=0, keepdims=True)
            spread.append(jnp.where(diagonal, row, 0.0))
        spread = jnp.concatenate(spread, axis=0).astype(jnp.bfloat16)
        wide[g] = jnp.dot(spread, ones, preferred_element_type=jnp.float32)


def middle_phase(sizes):
    stations, bands, seg, sta, pol, blocks, lags = sizes
    row = lax.axis_index("pol") * bands + lax.broadcasted_iota(jnp.int32, (bands, LANES), 0)
    bin_index = row * LANES + lax.broadcasted_iota(jnp.int32, (bands, LANES), 1)
    run = pol * lags
    return turn(bin_index * (2 * run * lax.axis_index("seg") + run - 1), 2 * run * seg)


def turn_locals(sizes, cosine, sine, locals_ref, local):
    stations, bands, seg = sizes[:3]
    for g in range(seg):
        for j in range(stations):
            tile = locals_ref[g, pl.ds(j * 16, 16), :].astype(jnp.float32)
            local[g, j, 0] = tile[:bands] * cosine + tile[bands:] * sine
            local[g, j, 1] = tile[bands:] * cosine - tile[:bands] * sine


def add_products(stations, count, segments, tile_of, weight_of, local_of, real_x, imag_x, before=None):
    def one_source(a, carry):
        tiles = [tile_of(n, a).astype(jnp.float32) for n in range(segments)]
        for j in range(stations):
            pair = a * stations + j
            at = pl.ds(pair * 8 if isinstance(pair, int) else pl.multiple_of(pair * 8, 8), 8)
            real_sum = imag_sum = None
            if before is not None:
                real_sum, imag_sum = before[0][at, :], before[1][at, :]
            for n in range(segments):
                real_src, imag_src = tiles[n][:8], tiles[n][8:]
                if weight_of is not None:
                    weight = jnp.broadcast_to(weight_of(n, pair), (8, LANES))
                    real_src, imag_src = real_src * weight, imag_src * weight
                real_loc, imag_loc = local_of(n, a, j)
                real_term = real_src * real_loc + imag_src * imag_loc
                imag_term = imag_src * real_loc - real_src * imag_loc
                real_sum = real_term if real_sum is None else real_sum + real_term
                imag_sum = imag_term if imag_sum is None else imag_sum + imag_term
            real_x[at, :] = real_sum
            imag_x[at, :] = imag_sum
        return carry

    if count <= 8:
        for a in range(count):
            one_source(a, 0)
    else:
        lax.fori_loop(0, count, one_source, 0, unroll=2)


def pack(rows, bands, real_x, imag_x, packed):
    for band in range(bands):
        at = pl.ds(band * LANES, LANES)
        strided = pl.ds(band, rows, stride=8)
        packed[0, :, at] = real_x[strided, :].astype(jnp.bfloat16)
        packed[1, :, at] = imag_x[strided, :].astype(jnp.bfloat16)


def source_tile(sources_ref, base, count, stations):
    def tile_of(n, a):
        start = a % stations * 16
        start = start if isinstance(a, int) else pl.multiple_of(start, 16)
        return sources_ref[base + a // stations * count + n, pl.ds(start, 16), :]

    return tile_of


def block_sums(sizes, first_block, count, table, wide, local, sources_ref, kept_ref, sent_ref, real_x, imag_x, packed):
    stations, bands, seg = sizes[:3]
    pairs = stations * stations
    add_products(
        stations, count * stations, seg, source_tile(sources_ref, 0, seg, stations),
        lambda n, pair: wide[n, pl.ds(first_block * pairs + pair, 1), :],
        lambda n, a, j: (local[n, j, 0], local[n, j, 1]),
        real_x, imag_x,
    )
    both_sums(sizes, count * pairs, table, kept_ref, sent_ref, real_x, imag_x, packed)


def both_sums(sizes, rows, table, real_x, imag_x, packed):
    pack(rows, sizes[1], real_x, imag_x, packed)
    dot = functools.partial(jnp.dot, preferred_element_type=jnp.float32)
    even, odd = dot(packed[0], table[0]), dot(packed[1], table[1])
    return even + odd, even - odd


def turned_round(sums):
    index = LANES - 1 - lax.broadcasted_iota(jnp.int32, (sums.shape[0], LANES), 1)
    runs = [sums[:, at : at + LANES] for at in reversed(range(0, sums.shape[1], LANES))]
    runs = [jnp.take_along_axis(run, index, axis=1, mode="promise_in_bounds") for run in runs]
    return jnp.concatenate(runs, axis=1)


def block_sums(sizes, first_block, count, table, wide, local, sources_ref, real_x, imag_x, packed):
    stations, bands, seg = sizes[:3]
    pairs = stations * stations
    add_products(
        stations, count * stations, seg, source_tile(sources_ref, 0, seg, stations),
        lambda n, pair: wide[n, pl.ds(first_block * pairs + pair, 1), :],
        lambda n, a, j: (local[n, j, 0], local[n, j, 1]),
        real_x, imag_x,
    )
    return both_sums(sizes, count * pairs, table, real_x, imag_x, packed)


def keep_and_send(before, after, kept_ref, sent_ref):
    first_core = lax.axis_index("pol") == 0
    kept_ref[...] = jnp.where(first_core, before, after)
    sent_ref[...] = jnp.where(first_core, after, before).astype(sent_ref.dtype)


def all_blocks_kernel(sizes, table, phase, mine_ref, sources_ref, kept_ref, sent_ref, local, wide, *scratch):
    spread_weights(sizes, mine_ref, wide)
    turn_locals(sizes, phase[0], phase[1], mine_ref, local)
    before, after = block_sums(sizes, 0, sizes[5], table, wide, local, sources_ref, *scratch)
    keep_and_send(turned_round(before), after, kept_ref, sent_ref)


def own_block_kernel(sizes, table, phase, mine_ref, kept_ref, sent_ref, local_ref, wide_ref, *scratch):
    spread_weights(sizes, mine_ref, wide_ref)
    turn_locals(sizes, phase[0], phase[1], mine_ref, local_ref)
    before, after = block_sums(sizes, 0, 1, table, wide_ref, local_ref, mine_ref, *scratch)
    keep_and_send(turned_round(before), after, kept_ref, sent_ref)


def weigh_kernel(sizes, wide_ref, local_ref, weighted_ref):
    stations, bands, seg = sizes[:3]
    for a in range(stations):
        for j in range(stations):
            pair = stations * stations + a * stations + j
            for g in range(seg):
                weight = jnp.broadcast_to(wide_ref[g, pl.ds(pair, 1), :], (bands, LANES))
                weighted_ref[a, j, g, 0] = local_ref[g, j, 0] * weight
                weighted_ref[a, j, g, 1] = local_ref[g, j, 1] * weight


def across_kernel(sizes, weighted_ref, across_ref, real_x, imag_x):
    stations = sizes[0]
    add_products(
        stations, stations, 2,
        lambda n, a: across_ref[n, pl.ds(a * 16, 16), :],
        None,
        lambda n, a, j: (weighted_ref[a, j, 2 + n, 0], weighted_ref[a, j, 2 + n, 1]),
        real_x, imag_x,
    )


def other_block_kernel(sizes, table, weighted_ref, real_ref, imag_ref, partner_ref, kept_ref, sent_ref, *scratch):
    stations, bands, seg = sizes[:3]
    add_products(
        stations, stations, 2,
        lambda n, a: partner_ref[n, pl.ds(a * 16, 16), :],
        None,
        lambda n, a, j: (weighted_ref[a, j, n, 0], weighted_ref[a, j, n, 1]),
        *scratch[:2],
        before=(real_ref, imag_ref),
    )
    before, after = both_sums(sizes, stations * stations, table, *scratch)
    first_core = lax.axis_index("pol") == 0

    @pl.when(first_core)
    def _():
        kept_ref[...] = before
        sent_ref[...] = after.astype(sent_ref.dtype)

    @pl.when(jnp.logical_not(first_core))
    def _():
        kept_ref[...] = after
        sent_ref[...] = turned_round(before).astype(sent_ref.dtype)


def settle_kernel(sizes, own_kept_ref, own_got_ref, kept_ref, own_lags_ref, settled_ref):
    own_lags_ref[...] = own_kept_ref[...] + own_got_ref[...]
    kept = kept_ref[...]
    settled_ref[...] = jnp.where(lax.axis_index("pol") == 0, turned_round(kept), kept)


def combine_kernel(sizes, kept_ref, got_ref, lags_ref):
    lags_ref[...] = kept_ref[...] + got_ref[...].astype(jnp.float32)


def place_kernel(sizes, mask_ref, own_ref, other_ref, got_ref, out_ref, steps, sems):
    own = own_ref[...]
    other = other_ref[...] + got_ref[...].astype(jnp.float32)
    copies = []
    for step in range(STEPS):
        mask = jnp.broadcast_to(mask_ref[step, :1, :1], other.shape)
        steps[step] = jnp.where(mask > 0, own, other)
        copies.append(pltpu.make_async_copy(steps.at[step], out_ref.at[step], sems.at[step]))
        copies[-1].start()
    for copy in copies:
        copy.wait()


def fetch_kernel(sizes, table_hbm, plan_any, after, table_ref, phase_ref, mask_ref, plan_ref, sems):
    del after
    copies = [
        pltpu.make_async_copy(table_hbm.at[lax.axis_index("pol")], table_ref, sems.at[0]),
        pltpu.make_async_copy(plan_any, plan_ref, sems.at[1]),
    ]
    for copy in copies:
        copy.start()
    phase_ref[0], phase_ref[1] = middle_phase(sizes)
    copies[1].wait()
    for step in range(STEPS):
        own = (plan_ref[step] == lax.axis_index("sta")).astype(jnp.float32)
        mask_ref[step] = jnp.full(mask_ref.shape[1:], own, jnp.float32)
    copies[0].wait()


def join_kernel(ranges, *refs):
    *pieces, out_ref = refs
    at = 0
    for piece, (first, count) in zip(pieces, ranges):
        out_ref[pl.ds(at, count)] = piece[pl.ds(first, count), pl.ds(0, out_ref.shape[1]), :]
        at += count


def join(*pieces, rows=None):
    pieces = [piece if isinstance(piece, tuple) else (piece, 0, piece.shape[0]) for piece in pieces]
    arrays = [piece[0] for piece in pieces]
    ranges = [piece[1:] for piece in pieces]
    vmem = pl.BlockSpec(memory_space=pltpu.VMEM)
    return pl.pallas_call(
        functools.partial(join_kernel, ranges),
        out_shape=pltpu.VMEM(
            (sum(count for _, count in ranges), rows or arrays[0].shape[1], LANES), arrays[0].dtype
        ),
        in_specs=[vmem] * len(arrays),
        out_specs=vmem,
        compiler_params=pltpu.CompilerParams(vmem_limit_bytes=VMEM_BYTES),
        name="join",
    )(*arrays)


def fetch_from(value, axes, source_of):
    sizes = tuple(lax.axis_size(axis) for axis in axes)
    pairs = []
    for index in np.ndindex(*sizes):
        source = source_of(*index)
        pairs.append((int(np.ravel_multi_index(source, sizes)), int(np.ravel_multi_index(index, sizes))))
    return lax.ppermute(value, axes, pairs)


def exchange(value, axis, distance):
    return fetch_from(value, (axis,), lambda i: (i ^ distance,))


def shards(table, raw_spectra, owner_plan, pair_valid, quality):
    seg, sta, pol = (lax.axis_size(name) for name in ("seg", "sta", "pol"))
    _, stations, _, bins = raw_spectra.shape
    bands = bins // BAND
    fast = sta == 2 and pol == 2 and seg == 4
    blocks = 2 if fast else STEPS
    pairs = stations * stations
    lags = table.shape[3]
    rows = 2 * stations * bands + 16
    sizes = (stations, bands, seg, sta, pol, blocks, lags)

    raw = raw_spectra.reshape(stations, 2, bands, BAND).transpose(0, 2, 1, 3).reshape(-1, BAND)
    vmem = pl.BlockSpec(memory_space=pltpu.VMEM)
    smem = pl.BlockSpec(memory_space=pltpu.SMEM)
    hbm = pl.BlockSpec(memory_space=pltpu.HBM)
    plan = [] if fast else [owner_plan]
    in_hbm = functools.partial(pltpu.with_memory_space_constraint, memory_space=pltpu.HBM)
    own = pl.pallas_call(
        functools.partial(prepare_kernel, (stations, bands, sta, blocks)),
        out_shape=pltpu.VMEM((1, rows, LANES), jnp.bfloat16),
        in_specs=[smem] * len(plan) + [vmem, vmem, vmem],
        out_specs=vmem,
        scratch_shapes=[pltpu.VMEM((2 * stations * bands, LANES), jnp.float32)],
        compiler_params=pltpu.CompilerParams(vmem_limit_bytes=VMEM_BYTES),
        name="prepare",
    )(*plan, in_hbm(raw), in_hbm(jnp.transpose(pair_valid[0])), in_hbm(quality))

    def call(kernel, out_shape, *args, out_specs=None, scratch=(), flops=0, moved=0, name=None):
        many = isinstance(out_shape, (list, tuple))
        return pl.pallas_call(
            functools.partial(kernel, sizes),
            out_shape=out_shape,
            in_specs=[hbm if x is table_const or x is plan_const else vmem for x in args],
            out_specs=out_specs or ([vmem] * len(out_shape) if many else vmem),
            scratch_shapes=list(scratch),
            compiler_params=pltpu.CompilerParams(vmem_limit_bytes=VMEM_BYTES),
            cost_estimate=pl.CostEstimate(flops=flops, bytes_accessed=moved, transcendentals=0),
            name=name,
        )(*args)

    f32 = jnp.float32
    table_const, plan_const = in_hbm(table), in_hbm(owner_plan)

    def fetch(after):
        return call(
            fetch_kernel,
            [
                pltpu.VMEM(table.shape[1:], table.dtype),
                pltpu.VMEM((2, bands, LANES), f32),
                pltpu.VMEM((STEPS, 8, LANES), f32),
            ],
            table_const, plan_const, after,
            scratch=[pltpu.SMEM((STEPS,), jnp.int32), pltpu.SemaphoreType.DMA((2,))],
            moved=4 * table.size // pol,
            name="fetch",
        )

    def products(count):
        return [pltpu.VMEM((count * pairs * 8, LANES), f32)] * 2 + [pltpu.VMEM((2, count * pairs, bins), jnp.bfloat16)]

    quarter = 32 * pairs * 2 * bins * lags
    local_shape = pltpu.VMEM((seg, stations, 2, bands, LANES), f32)
    wide_shape = pltpu.VMEM((seg, blocks * pairs, LANES), f32)
    kept_shape = pltpu.VMEM((pairs, lags), f32)

    if fast:
        far = join(own, exchange(own, "seg", 2))
        table, phase, mask = fetch(own)
        far, table = lax.optimization_barrier((far, table))
        bare = join(far, rows=rows - 16)
        near = exchange(far, "seg", 1)
        across = fetch_from(bare, ("seg", "sta"), lambda z, x: (z ^ 1, x ^ 1))
        partner = exchange(bare, "sta", 1)
        mine = join(far, near)
        own_kept, own_sent, local, wide = call(
            own_block_kernel, [kept_shape, kept_shape, local_shape, wide_shape],
            table, phase, mine,
            scratch=products(1), flops=8 * quarter, name="own_block",
        )
        weighted = call(
            weigh_kernel, pltpu.VMEM((stations, stations, seg, 2, bands, LANES), f32),
            wide, local,
            flops=8 * quarter, name="weigh",
        )
        own_got = exchange(own_sent, "pol", 1)
        weighted, across = lax.optimization_barrier((weighted, across))
        partial = call(
            across_kernel, [pltpu.VMEM((pairs * 8, LANES), f32)] * 2,
            weighted, across,
            name="across",
        )
        own_got, partial, partner = lax.optimization_barrier((own_got, partial, partner))
        kept, sent = call(
            other_block_kernel, [kept_shape, pltpu.VMEM((pairs, lags), jnp.bfloat16)],
            table, weighted, *partial, partner,
            scratch=products(1), flops=quarter, name="other_block",
        )
        got = exchange(sent, "pol", 1)
        own_lags, kept = call(
            settle_kernel, [kept_shape] * 2, own_kept, own_got, kept, flops=quarter, name="settle"
        )
        result = call(
            place_kernel, jax.ShapeDtypeStruct((STEPS, pairs, lags), f32),
            mask, own_lags, kept, got,
            out_specs=hbm,
            scratch=[pltpu.VMEM((STEPS, pairs, lags), f32), pltpu.SemaphoreType.DMA((STEPS,))],
            name="place",
        )
    else:
        mine, distance = own, seg // 2
        while distance:
            mine = join(mine, exchange(mine, "seg", distance))
            distance //= 2
        gathered = lax.all_gather(mine, "sta")
        sources = join(*(gathered[owner_plan[k]] for k in range(STEPS)))
        table, phase, _ = fetch(mine)
        kept, sent = call(
            all_blocks_kernel,
            [pltpu.VMEM((blocks * pairs, lags), f32), pltpu.VMEM((blocks * pairs, lags), jnp.bfloat16)],
            table, phase, mine, sources,
            scratch=[local_shape, wide_shape] + products(blocks), flops=blocks * quarter, name="all_blocks",
        )
        result = call(
            combine_kernel, jax.ShapeDtypeStruct((blocks * pairs, lags), f32),
            kept, exchange(sent, "pol", 1), name="combine",
        )
    return result.reshape(STEPS, stations, stations, lags)


def solution(mesh):
    placed = (
        P(("groups", "seg"), "sta", None, "pol"),
        P("groups"),
        P(("groups", "seg"), None, "sta"),
        P(("groups", "seg"), None),
    )

    def whole(raw_spectra, owner_plan, pair_valid, quality):
        seg, pol = mesh.shape["seg"], mesh.shape["pol"]
        bins = raw_spectra.shape[3]
        segments = raw_spectra.shape[0] // mesh.shape["groups"]
        table = lag_table(2 * bins // seg, bins, pol, 1.0 / math.sqrt(bins * segments))
        return jax.shard_map(
            shards,
            mesh=mesh,
            in_specs=(P(),) + placed,
            out_specs=P("groups", None, "sta", ("seg", "pol")),
            check_vma=False,
        )(jnp.asarray(table), raw_spectra, owner_plan, pair_valid, quality)

    return whole
```

```python
import functools
import math

import jax
import jax.numpy as jnp
import numpy as np
from jax import lax
from jax.experimental import pallas as pl
from jax.experimental.pallas import tpu as pltpu
from jax.sharding import PartitionSpec as P

STEPS = 3
BAND = 128
LANES = 128
VMEM_BYTES = 32 * 1024 * 1024


def lag_table(lags, bins, halves, scale):
    bin_index = np.arange(bins, dtype=np.int64)
    lag = 2 * np.arange(lags // 2, dtype=np.int64) + 1
    phase = (bin_index[:, None] * lag[None, :]) % (4 * bins)
    angle = phase * (2.0 * math.pi / (4 * bins))
    factor = np.where(bin_index == 0, 1.0, 2.0)[:, None] * scale
    parts = np.stack([np.cos(angle) * factor, np.sin(angle) * factor])
    parts = parts.reshape(2, halves, bins // halves, lags // 2).transpose(1, 0, 2, 3)
    return parts.astype(jnp.bfloat16)


def turn(count, period):
    count = count % period
    quarter = (count + period // 8) // (period // 4)
    x = (count - quarter * (period // 4)).astype(jnp.float32) * (2.0 * math.pi / period)
    y = x * x
    sine = x * (1.0 + y * (-1 / 6 + y * (1 / 120 + y * (-1 / 5040 + y * (1 / 362880)))))
    cosine = 1.0 + y * (-1 / 2 + y * (1 / 24 + y * (-1 / 720 + y * (1 / 40320))))
    quarter = quarter % 4
    odd = quarter % 2 == 1
    real = jnp.where(odd, sine, cosine)
    imag = jnp.where(odd, cosine, sine)
    real = jnp.where((quarter == 1) | (quarter == 2), -real, real)
    imag = jnp.where(quarter >= 2, -imag, imag)
    return real, imag


def prepare_kernel(sizes, *refs):
    stations, bands, sta, blocks = sizes
    *plan, raw_ref, valid_ref, quality_ref, out_ref, wide = refs
    total = stations * sta
    me = lax.axis_index("sta")
    wide[...] = raw_ref[...].astype(jnp.float32)
    count = stations * bands
    real = wide[pl.ds(0, count, stride=2), :]
    imag = wide[pl.ds(1, count, stride=2), :]
    power = jnp.sum(real * real + imag * imag, axis=1, keepdims=True) * (1.0 / (2 * BAND))
    inverse = 1.0 / jnp.sqrt(power + 1e-06)
    real = (real * inverse).reshape(stations, bands, LANES)
    imag = (imag * inverse).reshape(stations, bands, LANES)
    white = jnp.concatenate([real, imag], axis=1).reshape(2 * count, LANES).astype(jnp.bfloat16)

    valid = valid_ref[...].astype(jnp.float32).astype(jnp.bfloat16)
    quality = jnp.broadcast_to(quality_ref[...].astype(jnp.float32), (8, total)).astype(jnp.bfloat16)
    pair = lax.broadcasted_iota(jnp.int32, (total, LANES), 1)
    station = lax.broadcasted_iota(jnp.int32, (total, LANES), 0)
    mine = lax.broadcasted_iota(jnp.int32, (stations, LANES), 0) == (
        lax.broadcasted_iota(jnp.int32, (stations, LANES), 1) % stations
    )
    dot = functools.partial(jnp.dot, preferred_element_type=jnp.float32)
    pick_local = (station == me * stations + pair % stations).astype(jnp.float32).astype(jnp.bfloat16)
    local_flags = dot(quality, pick_local)
    rows = []
    for k in range(blocks):
        source = (plan[0][k] if plan else k) * stations + pair // stations
        pick_source = (station == source).astype(jnp.float32).astype(jnp.bfloat16)
        valid_row = jnp.sum(jnp.where(mine, dot(valid, pick_source), 0.0), axis=0, keepdims=True)
        rows.append(valid_row * (dot(quality, pick_source) * local_flags)[:1])
    rows.append(jnp.zeros((16 - blocks, LANES), jnp.float32))
    weights = jnp.concatenate(rows, axis=0).astype(jnp.bfloat16)
    out_ref[0, pl.ds(0, 2 * count), :] = white
    out_ref[0, pl.ds(2 * count, 16), :] = weights


def spread_weights(sizes, locals_ref, wide):
    stations, bands, seg, sta, pol, blocks, lags = sizes
    pairs = stations * stations
    row_index = lax.broadcasted_iota(jnp.int32, (16, LANES), 0)
    diagonal = lax.broadcasted_iota(jnp.int32, (pairs, LANES), 0) == lax.broadcasted_iota(
        jnp.int32, (pairs, LANES), 1
    )
    ones = jnp.ones((LANES, LANES), jnp.bfloat16)
    for g in range(seg):
        flags = locals_ref[g, pl.ds(2 * stations * bands, 16), :].astype(jnp.float32)
        spread = []
        for n in range(blocks):
            block = lax.axis_index("sta") ^ n if sta == 2 else n
            row = jnp.sum(jnp.where(row_index == block, flags, 0.0), axis=0, keepdims=True)
            spread.append(jnp.where(diagonal, row, 0.0))
        spread = jnp.concatenate(spread, axis=0).astype(jnp.bfloat16)
        wide[g] = jnp.dot(spread, ones, preferred_element_type=jnp.float32)


def middle_phase(sizes):
    stations, bands, seg, sta, pol, blocks, lags = sizes
    row = lax.axis_index("pol") * bands + lax.broadcasted_iota(jnp.int32, (bands, LANES), 0)
    bin_index = row * LANES + lax.broadcasted_iota(jnp.int32, (bands, LANES), 1)
    run = pol * lags
    return turn(bin_index * (2 * run * lax.axis_index("seg") + run - 1), 2 * run * seg)


def turn_locals(sizes, cosine, sine, locals_ref, local):
    stations, bands, seg = sizes[:3]
    for g in range(seg):
        for j in range(stations):
            tile = locals_ref[g, pl.ds(j * 16, 16), :].astype(jnp.float32)
            local[g, j, 0] = tile[:bands] * cosine + tile[bands:] * sine
            local[g, j, 1] = tile[bands:] * cosine - tile[:bands] * sine


def add_products(stations, count, segments, tile_of, weight_of, local_of, real_x, imag_x, before=None):
    def one_source(a, carry):
        tiles = [tile_of(n, a).astype(jnp.float32) for n in range(segments)]
        for j in range(stations):
            pair = a * stations + j
            at = pl.ds(pair * 8 if isinstance(pair, int) else pl.multiple_of(pair * 8, 8), 8)
            real_sum = imag_sum = None
            if before is not None:
                real_sum, imag_sum = before[0][at, :], before[1][at, :]
            for n in range(segments):
                real_src, imag_src = tiles[n][:8], tiles[n][8:]
                if weight_of is not None:
                    weight = jnp.broadcast_to(weight_of(n, pair), (8, LANES))
                    real_src, imag_src = real_src * weight, imag_src * weight
                real_loc, imag_loc = local_of(n, a, j)
                real_term = real_src * real_loc + imag_src * imag_loc
                imag_term = imag_src * real_loc - real_src * imag_loc
                real_sum = real_term if real_sum is None else real_sum + real_term
                imag_sum = imag_term if imag_sum is None else imag_sum + imag_term
            real_x[at, :] = real_sum
            imag_x[at, :] = imag_sum
        return carry

    if count <= 8:
        for a in range(count):
            one_source(a, 0)
    else:
        lax.fori_loop(0, count, one_source, 0, unroll=2)


def pack(rows, bands, real_x, imag_x, packed):
    for band in range(bands):
        at = pl.ds(band * LANES, LANES)
        strided = pl.ds(band, rows, stride=8)
        packed[0, :, at] = real_x[strided, :].astype(jnp.bfloat16)
        packed[1, :, at] = imag_x[strided, :].astype(jnp.bfloat16)


def source_tile(sources_ref, base, count, stations):
    def tile_of(n, a):
        start = a % stations * 16
        start = start if isinstance(a, int) else pl.multiple_of(start, 16)
        return sources_ref[base + a // stations * count + n, pl.ds(start, 16), :]

    return tile_of


def block_sums(sizes, first_block, count, table, wide, local, sources_ref, kept_ref, sent_ref, real_x, imag_x, packed):
    stations, bands, seg = sizes[:3]
    pairs = stations * stations
    add_products(
        stations, count * stations, seg, source_tile(sources_ref, 0, seg, stations),
        lambda n, pair: wide[n, pl.ds(first_block * pairs + pair, 1), :],
        lambda n, a, j: (local[n, j, 0], local[n, j, 1]),
        real_x, imag_x,
    )
    both_sums(sizes, count * pairs, table, kept_ref, sent_ref, real_x, imag_x, packed)


def both_sums(sizes, rows, table, real_x, imag_x, packed):
    pack(rows, sizes[1], real_x, imag_x, packed)
    dot = functools.partial(jnp.dot, preferred_element_type=jnp.float32)
    even, odd = dot(packed[0], table[0]), dot(packed[1], table[1])
    return even + odd, even - odd


def turned_round(sums):
    index = LANES - 1 - lax.broadcasted_iota(jnp.int32, (sums.shape[0], LANES), 1)
    runs = [sums[:, at : at + LANES] for at in reversed(range(0, sums.shape[1], LANES))]
    runs = [jnp.take_along_axis(run, index, axis=1, mode="promise_in_bounds") for run in runs]
    return jnp.concatenate(runs, axis=1)


def block_sums(sizes, first_block, count, table, wide, local, sources_ref, real_x, imag_x, packed):
    stations, bands, seg = sizes[:3]
    pairs = stations * stations
    add_products(
        stations, count * stations, seg, source_tile(sources_ref, 0, seg, stations),
        lambda n, pair: wide[n, pl.ds(first_block * pairs + pair, 1), :],
        lambda n, a, j: (local[n, j, 0], local[n, j, 1]),
        real_x, imag_x,
    )
    return both_sums(sizes, count * pairs, table, real_x, imag_x, packed)


def keep_and_send(before, after, kept_ref, sent_ref):
    first_core = lax.axis_index("pol") == 0
    kept_ref[...] = jnp.where(first_core, before, after)
    sent_ref[...] = jnp.where(first_core, after, before).astype(sent_ref.dtype)


def all_blocks_kernel(sizes, table, phase, mine_ref, sources_ref, kept_ref, sent_ref, local, wide, *scratch):
    spread_weights(sizes, mine_ref, wide)
    turn_locals(sizes, phase[0], phase[1], mine_ref, local)
    before, after = block_sums(sizes, 0, sizes[5], table, wide, local, sources_ref, *scratch)
    keep_and_send(turned_round(before), after, kept_ref, sent_ref)


def own_block_kernel(sizes, table, phase, mine_ref, kept_ref, sent_ref, local_ref, wide_ref, *scratch):
    spread_weights(sizes, mine_ref, wide_ref)
    turn_locals(sizes, phase[0], phase[1], mine_ref, local_ref)
    before, after = block_sums(sizes, 0, 1, table, wide_ref, local_ref, mine_ref, *scratch)
    keep_and_send(turned_round(before), after, kept_ref, sent_ref)


def weigh_kernel(sizes, wide_ref, local_ref, weighted_ref):
    stations, bands, seg = sizes[:3]
    for a in range(stations):
        for j in range(stations):
            pair = stations * stations + a * stations + j
            for g in range(seg):
                weight = jnp.broadcast_to(wide_ref[g, pl.ds(pair, 1), :], (bands, LANES))
                weighted_ref[a, j, g, 0] = local_ref[g, j, 0] * weight
                weighted_ref[a, j, g, 1] = local_ref[g, j, 1] * weight


def across_kernel(sizes, weighted_ref, across_ref, real_x, imag_x):
    stations = sizes[0]
    add_products(
        stations, stations, 2,
        lambda n, a: across_ref[n, pl.ds(a * 16, 16), :],
        None,
        lambda n, a, j: (weighted_ref[a, j, 2 + n, 0], weighted_ref[a, j, 2 + n, 1]),
        real_x, imag_x,
    )


def other_block_kernel(sizes, table, weighted_ref, real_ref, imag_ref, partner_ref, kept_ref, sent_ref, *scratch):
    stations, bands, seg = sizes[:3]
    add_products(
        stations, stations, 2,
        lambda n, a: partner_ref[n, pl.ds(a * 16, 16), :],
        None,
        lambda n, a, j: (weighted_ref[a, j, n, 0], weighted_ref[a, j, n, 1]),
        *scratch[:2],
        before=(real_ref, imag_ref),
    )
    before, after = both_sums(sizes, stations * stations, table, *scratch)
    first_core = lax.axis_index("pol") == 0

    @pl.when(first_core)
    def _():
        kept_ref[...] = before
        sent_ref[...] = after.astype(sent_ref.dtype)

    @pl.when(jnp.logical_not(first_core))
    def _():
        kept_ref[...] = after
        sent_ref[...] = turned_round(before).astype(sent_ref.dtype)


def settle_kernel(sizes, own_kept_ref, own_got_ref, kept_ref, out_ref, settled_ref, own, sems):
    own[...] = own_kept_ref[...] + own_got_ref[...]
    copies = [pltpu.make_async_copy(own, out_ref.at[step], sems.at[step]) for step in range(STEPS)]
    for copy in copies:
        copy.start()
    kept = kept_ref[...]
    settled_ref[...] = jnp.where(lax.axis_index("pol") == 0, turned_round(kept), kept)
    for copy in copies:
        copy.wait()


def combine_kernel(sizes, kept_ref, got_ref, lags_ref):
    lags_ref[...] = kept_ref[...] + got_ref[...].astype(jnp.float32)


def place_kernel(sizes, is_own_ref, kept_ref, got_ref, steps_ref, out_ref, other, sems):
    del steps_ref
    other[...] = kept_ref[...] + got_ref[...].astype(jnp.float32)
    for act in ("start", "wait"):
        for step in range(STEPS):

            @pl.when(is_own_ref[step] == 0)
            def _():
                getattr(pltpu.make_async_copy(other, out_ref.at[step], sems.at[step]), act)()


def fetch_kernel(sizes, table_hbm, plan_any, after, table_ref, phase_ref, is_own_ref, plan_ref, sems):
    del after
    copies = [
        pltpu.make_async_copy(table_hbm.at[lax.axis_index("pol")], table_ref, sems.at[0]),
        pltpu.make_async_copy(plan_any, plan_ref, sems.at[1]),
    ]
    for copy in copies:
        copy.start()
    phase_ref[0], phase_ref[1] = middle_phase(sizes)
    copies[1].wait()
    for step in range(STEPS):
        is_own_ref[step] = (plan_ref[step] == lax.axis_index("sta")).astype(jnp.int32)
    copies[0].wait()


def join_kernel(ranges, *refs):
    *pieces, out_ref = refs
    at = 0
    for piece, (first, count) in zip(pieces, ranges):
        out_ref[pl.ds(at, count)] = piece[pl.ds(first, count), pl.ds(0, out_ref.shape[1]), :]
        at += count


def join(*pieces, rows=None):
    pieces = [piece if isinstance(piece, tuple) else (piece, 0, piece.shape[0]) for piece in pieces]
    arrays = [piece[0] for piece in pieces]
    ranges = [piece[1:] for piece in pieces]
    vmem = pl.BlockSpec(memory_space=pltpu.VMEM)
    return pl.pallas_call(
        functools.partial(join_kernel, ranges),
        out_shape=pltpu.VMEM(
            (sum(count for _, count in ranges), rows or arrays[0].shape[1], LANES), arrays[0].dtype
        ),
        in_specs=[vmem] * len(arrays),
        out_specs=vmem,
        compiler_params=pltpu.CompilerParams(vmem_limit_bytes=VMEM_BYTES),
        name="join",
    )(*arrays)


def fetch_from(value, axes, source_of):
    sizes = tuple(lax.axis_size(axis) for axis in axes)
    pairs = []
    for index in np.ndindex(*sizes):
        source = source_of(*index)
        pairs.append((int(np.ravel_multi_index(source, sizes)), int(np.ravel_multi_index(index, sizes))))
    return lax.ppermute(value, axes, pairs)


def exchange(value, axis, distance):
    return fetch_from(value, (axis,), lambda i: (i ^ distance,))


def shards(table, raw_spectra, owner_plan, pair_valid, quality):
    seg, sta, pol = (lax.axis_size(name) for name in ("seg", "sta", "pol"))
    _, stations, _, bins = raw_spectra.shape
    bands = bins // BAND
    fast = sta == 2 and pol == 2 and seg == 4
    blocks = 2 if fast else STEPS
    pairs = stations * stations
    lags = table.shape[3]
    rows = 2 * stations * bands + 16
    sizes = (stations, bands, seg, sta, pol, blocks, lags)

    raw = raw_spectra.reshape(stations, 2, bands, BAND).transpose(0, 2, 1, 3).reshape(-1, BAND)
    vmem = pl.BlockSpec(memory_space=pltpu.VMEM)
    smem = pl.BlockSpec(memory_space=pltpu.SMEM)
    hbm = pl.BlockSpec(memory_space=pltpu.HBM)
    plan = [] if fast else [owner_plan]
    in_hbm = functools.partial(pltpu.with_memory_space_constraint, memory_space=pltpu.HBM)
    own = pl.pallas_call(
        functools.partial(prepare_kernel, (stations, bands, sta, blocks)),
        out_shape=pltpu.VMEM((1, rows, LANES), jnp.bfloat16),
        in_specs=[smem] * len(plan) + [vmem, vmem, vmem],
        out_specs=vmem,
        scratch_shapes=[pltpu.VMEM((2 * stations * bands, LANES), jnp.float32)],
        compiler_params=pltpu.CompilerParams(vmem_limit_bytes=VMEM_BYTES),
        name="prepare",
    )(*plan, in_hbm(raw), in_hbm(jnp.transpose(pair_valid[0])), in_hbm(quality))

    def call(kernel, out_shape, *args, aliases=None, scratch=(), flops=0, moved=0, name=None):
        def spec(x):
            if x is table_const or x is plan_const or x.shape == placed_shape.shape:
                return hbm
            return smem if x.shape == (STEPS,) else vmem

        many = isinstance(out_shape, (list, tuple))
        return pl.pallas_call(
            functools.partial(kernel, sizes),
            out_shape=out_shape,
            in_specs=[spec(x) for x in args],
            out_specs=[spec(x) for x in out_shape] if many else spec(out_shape),
            input_output_aliases=aliases or {},
            scratch_shapes=list(scratch),
            compiler_params=pltpu.CompilerParams(vmem_limit_bytes=VMEM_BYTES),
            cost_estimate=pl.CostEstimate(flops=flops, bytes_accessed=moved, transcendentals=0),
            name=name,
        )(*args)

    f32 = jnp.float32
    placed_shape = jax.ShapeDtypeStruct((STEPS, pairs, lags), f32)
    table_const, plan_const = in_hbm(table), in_hbm(owner_plan)

    def fetch(after):
        return call(
            fetch_kernel,
            [
                pltpu.VMEM(table.shape[1:], table.dtype),
                pltpu.VMEM((2, bands, LANES), f32),
                pltpu.SMEM((STEPS,), jnp.int32),
            ],
            table_const, plan_const, after,
            scratch=[pltpu.SMEM((STEPS,), jnp.int32), pltpu.SemaphoreType.DMA((2,))],
            moved=4 * table.size // pol,
            name="fetch",
        )

    def products(count):
        return [pltpu.VMEM((count * pairs * 8, LANES), f32)] * 2 + [pltpu.VMEM((2, count * pairs, bins), jnp.bfloat16)]

    quarter = 32 * pairs * 2 * bins * lags
    local_shape = pltpu.VMEM((seg, stations, 2, bands, LANES), f32)
    wide_shape = pltpu.VMEM((seg, blocks * pairs, LANES), f32)
    kept_shape = pltpu.VMEM((pairs, lags), f32)

    if fast:
        far = join(own, exchange(own, "seg", 2))
        table, phase, is_own = fetch(own)
        far, table = lax.optimization_barrier((far, table))
        bare = join(far, rows=rows - 16)
        near = exchange(far, "seg", 1)
        across = fetch_from(bare, ("seg", "sta"), lambda z, x: (z ^ 1, x ^ 1))
        partner = exchange(bare, "sta", 1)
        mine = join(far, near)
        own_kept, own_sent, local, wide = call(
            own_block_kernel, [kept_shape, kept_shape, local_shape, wide_shape],
            table, phase, mine,
            scratch=products(1), flops=8 * quarter, name="own_block",
        )
        weighted = call(
            weigh_kernel, pltpu.VMEM((stations, stations, seg, 2, bands, LANES), f32),
            wide, local,
            flops=8 * quarter, name="weigh",
        )
        own_got = exchange(own_sent, "pol", 1)
        weighted, across = lax.optimization_barrier((weighted, across))
        partial = call(
            across_kernel, [pltpu.VMEM((pairs * 8, LANES), f32)] * 2,
            weighted, across,
            name="across",
        )
        own_got, partial, partner = lax.optimization_barrier((own_got, partial, partner))
        kept, sent = call(
            other_block_kernel, [kept_shape, pltpu.VMEM((pairs, lags), jnp.bfloat16)],
            table, weighted, *partial, partner,
            scratch=products(1), flops=quarter, name="other_block",
        )
        got = exchange(sent, "pol", 1)
        steps, kept = call(
            settle_kernel, [placed_shape, kept_shape], own_kept, own_got, kept,
            scratch=[pltpu.VMEM((pairs, lags), f32), pltpu.SemaphoreType.DMA((STEPS,))],
            flops=quarter, name="settle",
        )
        result = call(
            place_kernel, placed_shape, is_own, kept, got, steps,
            aliases={3: 0},
            scratch=[pltpu.VMEM((pairs, lags), f32), pltpu.SemaphoreType.DMA((STEPS,))],
            name="place",
        )
    else:
        mine, distance = own, seg // 2
        while distance:
            mine = join(mine, exchange(mine, "seg", distance))
            distance //= 2
        gathered = lax.all_gather(mine, "sta")
        sources = join(*(gathered[owner_plan[k]] for k in range(STEPS)))
        table, phase, _ = fetch(mine)
        kept, sent = call(
            all_blocks_kernel,
            [pltpu.VMEM((blocks * pairs, lags), f32), pltpu.VMEM((blocks * pairs, lags), jnp.bfloat16)],
            table, phase, mine, sources,
            scratch=[local_shape, wide_shape] + products(blocks), flops=blocks * quarter, name="all_blocks",
        )
        result = call(
            combine_kernel, jax.ShapeDtypeStruct((blocks * pairs, lags), f32),
            kept, exchange(sent, "pol", 1), name="combine",
        )
    return result.reshape(STEPS, stations, stations, lags)


def solution(mesh):
    placed = (
        P(("groups", "seg"), "sta", None, "pol"),
        P("groups"),
        P(("groups", "seg"), None, "sta"),
        P(("groups", "seg"), None),
    )

    def whole(raw_spectra, owner_plan, pair_valid, quality):
        seg, pol = mesh.shape["seg"], mesh.shape["pol"]
        bins = raw_spectra.shape[3]
        segments = raw_spectra.shape[0] // mesh.shape["groups"]
        table = lag_table(2 * bins // seg, bins, pol, 1.0 / math.sqrt(bins * segments))
        return jax.shard_map(
            shards,
            mesh=mesh,
            in_specs=(P(),) + placed,
            out_specs=P("groups", None, "sta", ("seg", "pol")),
            check_vma=False,
        )(jnp.asarray(table), raw_spectra, owner_plan, pair_valid, quality)

    return whole
```

```python
import functools
import math

import jax
import jax.numpy as jnp
import numpy as np
from jax import lax
from jax.experimental import pallas as pl
from jax.experimental.pallas import tpu as pltpu
from jax.sharding import PartitionSpec as P

STEPS = 3
BAND = 128
LANES = 128
VMEM_BYTES = 32 * 1024 * 1024


def lag_table(lags, bins, halves, scale):
    bin_index = np.arange(bins, dtype=np.int64)
    lag = 2 * np.arange(lags // 2, dtype=np.int64) + 1
    phase = (bin_index[:, None] * lag[None, :]) % (4 * bins)
    angle = phase * (2.0 * math.pi / (4 * bins))
    factor = np.where(bin_index == 0, 1.0, 2.0)[:, None] * scale
    parts = np.stack([np.cos(angle) * factor, np.sin(angle) * factor])
    parts = parts.reshape(2, halves, bins // halves, lags // 2).transpose(1, 0, 2, 3)
    return parts.astype(jnp.bfloat16)


def turn(count, period):
    count = count % period
    quarter = (count + period // 8) // (period // 4)
    x = (count - quarter * (period // 4)).astype(jnp.float32) * (2.0 * math.pi / period)
    y = x * x
    sine = x * (1.0 + y * (-1 / 6 + y * (1 / 120 + y * (-1 / 5040 + y * (1 / 362880)))))
    cosine = 1.0 + y * (-1 / 2 + y * (1 / 24 + y * (-1 / 720 + y * (1 / 40320))))
    quarter = quarter % 4
    odd = quarter % 2 == 1
    real = jnp.where(odd, sine, cosine)
    imag = jnp.where(odd, cosine, sine)
    real = jnp.where((quarter == 1) | (quarter == 2), -real, real)
    imag = jnp.where(quarter >= 2, -imag, imag)
    return real, imag


def prepare_kernel(sizes, *refs):
    stations, bands, sta, blocks = sizes
    *plan, raw_ref, valid_ref, quality_ref, out_ref, wide = refs
    total = stations * sta
    me = lax.axis_index("sta")
    wide[...] = raw_ref[...].astype(jnp.float32)
    count = stations * bands
    real = wide[pl.ds(0, count, stride=2), :]
    imag = wide[pl.ds(1, count, stride=2), :]
    power = jnp.sum(real * real + imag * imag, axis=1, keepdims=True) * (1.0 / (2 * BAND))
    inverse = lax.rsqrt(power + 1e-06)
    real = (real * inverse).reshape(stations, bands, LANES)
    imag = (imag * inverse).reshape(stations, bands, LANES)
    white = jnp.concatenate([real, imag], axis=1).reshape(2 * count, LANES).astype(jnp.bfloat16)

    flags = jnp.concatenate([valid_ref[...], jnp.broadcast_to(quality_ref[...], (8, total))], axis=0)
    pair = lax.broadcasted_iota(jnp.int32, (total, LANES), 1)
    station = lax.broadcasted_iota(jnp.int32, (total, LANES), 0)
    wanted = [(plan[0][k] if plan else k) * stations + pair // stations for k in range(blocks)]
    wanted.append(me * stations + pair % stations)
    picks = jnp.concatenate([(station == x).astype(jnp.float32) for x in wanted], axis=1)
    picked = jnp.dot(
        flags.astype(jnp.float32).astype(jnp.bfloat16), picks.astype(jnp.bfloat16),
        preferred_element_type=jnp.float32,
    )
    mine = lax.broadcasted_iota(jnp.int32, (stations, LANES), 0) == (
        lax.broadcasted_iota(jnp.int32, (stations, LANES), 1) % stations
    )
    local_flags = picked[stations : stations + 1, blocks * LANES :]
    rows = []
    for k in range(blocks):
        part = picked[:, k * LANES : (k + 1) * LANES]
        valid_row = jnp.sum(jnp.where(mine, part[:stations], 0.0), axis=0, keepdims=True)
        rows.append(valid_row * part[stations : stations + 1] * local_flags)
    rows.append(jnp.zeros((16 - blocks, LANES), jnp.float32))
    weights = jnp.concatenate(rows, axis=0).astype(jnp.bfloat16)
    out_ref[0, pl.ds(0, 2 * count), :] = white
    out_ref[0, pl.ds(2 * count, 16), :] = weights


def spread_weights(sizes, locals_ref, wide):
    stations, bands, seg, sta, pol, blocks, lags = sizes
    pairs = stations * stations
    row_index = lax.broadcasted_iota(jnp.int32, (16, LANES), 0)
    diagonal = lax.broadcasted_iota(jnp.int32, (pairs, LANES), 0) == lax.broadcasted_iota(
        jnp.int32, (pairs, LANES), 1
    )
    ones = jnp.ones((LANES, LANES), jnp.bfloat16)
    for g in range(seg):
        flags = locals_ref[g, pl.ds(2 * stations * bands, 16), :].astype(jnp.float32)
        spread = []
        for n in range(blocks):
            block = lax.axis_index("sta") ^ n if sta == 2 else n
            row = jnp.sum(jnp.where(row_index == block, flags, 0.0), axis=0, keepdims=True)
            spread.append(jnp.where(diagonal, row, 0.0))
        spread = jnp.concatenate(spread, axis=0).astype(jnp.bfloat16)
        wide[g] = jnp.dot(spread, ones, preferred_element_type=jnp.float32)


def middle_phase(sizes):
    stations, bands, seg, sta, pol, blocks, lags = sizes
    row = lax.axis_index("pol") * bands + lax.broadcasted_iota(jnp.int32, (bands, LANES), 0)
    bin_index = row * LANES + lax.broadcasted_iota(jnp.int32, (bands, LANES), 1)
    run = pol * lags
    return turn(bin_index * (2 * run * lax.axis_index("seg") + run - 1), 2 * run * seg)


def turn_locals(sizes, cosine, sine, locals_ref, local):
    stations, bands, seg = sizes[:3]
    for g in range(seg):
        for j in range(stations):
            tile = locals_ref[g, pl.ds(j * 16, 16), :].astype(jnp.float32)
            local[g, j, 0] = tile[:bands] * cosine + tile[bands:] * sine
            local[g, j, 1] = tile[bands:] * cosine - tile[:bands] * sine


def add_products(stations, count, segments, tile_of, weight_of, local_of, real_x, imag_x, before=None):
    def one_source(a, carry):
        tiles = [tile_of(n, a).astype(jnp.float32) for n in range(segments)]
        for j in range(stations):
            pair = a * stations + j
            at = pl.ds(pair * 8 if isinstance(pair, int) else pl.multiple_of(pair * 8, 8), 8)
            real_sum = imag_sum = None
            if before is not None:
                real_sum, imag_sum = before[0][at, :], before[1][at, :]
            for n in range(segments):
                real_src, imag_src = tiles[n][:8], tiles[n][8:]
                if weight_of is not None:
                    weight = jnp.broadcast_to(weight_of(n, pair), (8, LANES))
                    real_src, imag_src = real_src * weight, imag_src * weight
                real_loc, imag_loc = local_of(n, a, j)
                real_term = real_src * real_loc + imag_src * imag_loc
                imag_term = imag_src * real_loc - real_src * imag_loc
                real_sum = real_term if real_sum is None else real_sum + real_term
                imag_sum = imag_term if imag_sum is None else imag_sum + imag_term
            real_x[at, :] = real_sum
            imag_x[at, :] = imag_sum
        return carry

    if count <= 8:
        for a in range(count):
            one_source(a, 0)
    else:
        lax.fori_loop(0, count, one_source, 0, unroll=2)


def pack(rows, bands, real_x, imag_x, packed):
    for band in range(bands):
        at = pl.ds(band * LANES, LANES)
        strided = pl.ds(band, rows, stride=8)
        packed[0, :, at] = real_x[strided, :].astype(jnp.bfloat16)
        packed[1, :, at] = imag_x[strided, :].astype(jnp.bfloat16)


def source_tile(sources_ref, base, count, stations):
    def tile_of(n, a):
        start = a % stations * 16
        start = start if isinstance(a, int) else pl.multiple_of(start, 16)
        return sources_ref[base + a // stations * count + n, pl.ds(start, 16), :]

    return tile_of


def block_sums(sizes, first_block, count, table, wide, local, sources_ref, kept_ref, sent_ref, real_x, imag_x, packed):
    stations, bands, seg = sizes[:3]
    pairs = stations * stations
    add_products(
        stations, count * stations, seg, source_tile(sources_ref, 0, seg, stations),
        lambda n, pair: wide[n, pl.ds(first_block * pairs + pair, 1), :],
        lambda n, a, j: (local[n, j, 0], local[n, j, 1]),
        real_x, imag_x,
    )
    both_sums(sizes, count * pairs, table, kept_ref, sent_ref, real_x, imag_x, packed)


def both_sums(sizes, rows, table, real_x, imag_x, packed):
    pack(rows, sizes[1], real_x, imag_x, packed)
    dot = functools.partial(jnp.dot, preferred_element_type=jnp.float32)
    even, odd = dot(packed[0], table[0]), dot(packed[1], table[1])
    return even + odd, even - odd


def turned_round(sums):
    index = LANES - 1 - lax.broadcasted_iota(jnp.int32, (sums.shape[0], LANES), 1)
    runs = [sums[:, at : at + LANES] for at in reversed(range(0, sums.shape[1], LANES))]
    runs = [jnp.take_along_axis(run, index, axis=1, mode="promise_in_bounds") for run in runs]
    return jnp.concatenate(runs, axis=1)


def block_sums(sizes, first_block, count, table, wide, local, sources_ref, real_x, imag_x, packed):
    stations, bands, seg = sizes[:3]
    pairs = stations * stations
    add_products(
        stations, count * stations, seg, source_tile(sources_ref, 0, seg, stations),
        lambda n, pair: wide[n, pl.ds(first_block * pairs + pair, 1), :],
        lambda n, a, j: (local[n, j, 0], local[n, j, 1]),
        real_x, imag_x,
    )
    return both_sums(sizes, count * pairs, table, real_x, imag_x, packed)


def keep_and_send(before, after, kept_ref, sent_ref):
    first_core = lax.axis_index("pol") == 0
    kept_ref[...] = jnp.where(first_core, before, after)
    sent_ref[...] = jnp.where(first_core, after, before).astype(sent_ref.dtype)


def all_blocks_kernel(sizes, table, phase, mine_ref, sources_ref, kept_ref, sent_ref, local, wide, *scratch):
    spread_weights(sizes, mine_ref, wide)
    turn_locals(sizes, phase[0], phase[1], mine_ref, local)
    before, after = block_sums(sizes, 0, sizes[5], table, wide, local, sources_ref, *scratch)
    keep_and_send(turned_round(before), after, kept_ref, sent_ref)


def own_block_kernel(sizes, table, phase, mine_ref, kept_ref, sent_ref, local_ref, wide_ref, *scratch):
    spread_weights(sizes, mine_ref, wide_ref)
    turn_locals(sizes, phase[0], phase[1], mine_ref, local_ref)
    before, after = block_sums(sizes, 0, 1, table, wide_ref, local_ref, mine_ref, *scratch)
    keep_and_send(turned_round(before), after, kept_ref, sent_ref)


def weigh_kernel(sizes, wide_ref, local_ref, weighted_ref):
    stations, bands, seg = sizes[:3]
    for a in range(stations):
        for j in range(stations):
            pair = stations * stations + a * stations + j
            for g in range(seg):
                weight = jnp.broadcast_to(wide_ref[g, pl.ds(pair, 1), :], (bands, LANES))
                weighted_ref[a, j, g, 0] = local_ref[g, j, 0] * weight
                weighted_ref[a, j, g, 1] = local_ref[g, j, 1] * weight


def across_kernel(sizes, weighted_ref, across_ref, real_x, imag_x):
    stations = sizes[0]
    add_products(
        stations, stations, 2,
        lambda n, a: across_ref[n, pl.ds(a * 16, 16), :],
        None,
        lambda n, a, j: (weighted_ref[a, j, 2 + n, 0], weighted_ref[a, j, 2 + n, 1]),
        real_x, imag_x,
    )


def other_block_kernel(sizes, table, weighted_ref, real_ref, imag_ref, partner_ref, kept_ref, sent_ref, *scratch):
    stations, bands, seg = sizes[:3]
    add_products(
        stations, stations, 2,
        lambda n, a: partner_ref[n, pl.ds(a * 16, 16), :],
        None,
        lambda n, a, j: (weighted_ref[a, j, n, 0], weighted_ref[a, j, n, 1]),
        *scratch[:2],
        before=(real_ref, imag_ref),
    )
    before, after = both_sums(sizes, stations * stations, table, *scratch)
    first_core = lax.axis_index("pol") == 0

    @pl.when(first_core)
    def _():
        kept_ref[...] = before
        sent_ref[...] = after.astype(sent_ref.dtype)

    @pl.when(jnp.logical_not(first_core))
    def _():
        kept_ref[...] = after
        sent_ref[...] = turned_round(before).astype(sent_ref.dtype)


def settle_kernel(sizes, own_kept_ref, own_got_ref, kept_ref, out_ref, settled_ref, own, sems):
    own[...] = own_kept_ref[...] + own_got_ref[...]
    copies = [pltpu.make_async_copy(own, out_ref.at[step], sems.at[step]) for step in range(STEPS)]
    for copy in copies:
        copy.start()
    kept = kept_ref[...]
    settled_ref[...] = jnp.where(lax.axis_index("pol") == 0, turned_round(kept), kept)
    for copy in copies:
        copy.wait()


def combine_kernel(sizes, kept_ref, got_ref, lags_ref):
    lags_ref[...] = kept_ref[...] + got_ref[...].astype(jnp.float32)


def place_kernel(sizes, is_own_ref, kept_ref, got_ref, steps_ref, out_ref, other, sems):
    del steps_ref
    other[...] = kept_ref[...] + got_ref[...].astype(jnp.float32)
    for act in ("start", "wait"):
        for step in range(STEPS):

            @pl.when(is_own_ref[step] == 0)
            def _():
                getattr(pltpu.make_async_copy(other, out_ref.at[step], sems.at[step]), act)()


def fetch_kernel(sizes, table_hbm, plan_any, after, table_ref, phase_ref, is_own_ref, plan_ref, sems):
    del after
    copies = [
        pltpu.make_async_copy(table_hbm.at[lax.axis_index("pol")], table_ref, sems.at[0]),
        pltpu.make_async_copy(plan_any, plan_ref, sems.at[1]),
    ]
    for copy in copies:
        copy.start()
    phase_ref[0], phase_ref[1] = middle_phase(sizes)
    copies[1].wait()
    for step in range(STEPS):
        is_own_ref[step] = (plan_ref[step] == lax.axis_index("sta")).astype(jnp.int32)
    copies[0].wait()


def join_kernel(ranges, *refs):
    *pieces, out_ref = refs
    at = 0
    for piece, (first, count) in zip(pieces, ranges):
        out_ref[pl.ds(at, count)] = piece[pl.ds(first, count), pl.ds(0, out_ref.shape[1]), :]
        at += count


def join(*pieces, rows=None):
    pieces = [piece if isinstance(piece, tuple) else (piece, 0, piece.shape[0]) for piece in pieces]
    arrays = [piece[0] for piece in pieces]
    ranges = [piece[1:] for piece in pieces]
    vmem = pl.BlockSpec(memory_space=pltpu.VMEM)
    return pl.pallas_call(
        functools.partial(join_kernel, ranges),
        out_shape=pltpu.VMEM(
            (sum(count for _, count in ranges), rows or arrays[0].shape[1], LANES), arrays[0].dtype
        ),
        in_specs=[vmem] * len(arrays),
        out_specs=vmem,
        compiler_params=pltpu.CompilerParams(vmem_limit_bytes=VMEM_BYTES),
        name="join",
    )(*arrays)


def fetch_from(value, axes, source_of):
    sizes = tuple(lax.axis_size(axis) for axis in axes)
    pairs = []
    for index in np.ndindex(*sizes):
        source = source_of(*index)
        pairs.append((int(np.ravel_multi_index(source, sizes)), int(np.ravel_multi_index(index, sizes))))
    return lax.ppermute(value, axes, pairs)


def exchange(value, axis, distance):
    return fetch_from(value, (axis,), lambda i: (i ^ distance,))


def shards(table, raw_spectra, owner_plan, pair_valid, quality):
    seg, sta, pol = (lax.axis_size(name) for name in ("seg", "sta", "pol"))
    _, stations, _, bins = raw_spectra.shape
    bands = bins // BAND
    fast = sta == 2 and pol == 2 and seg == 4
    blocks = 2 if fast else STEPS
    pairs = stations * stations
    lags = table.shape[3]
    rows = 2 * stations * bands + 16
    sizes = (stations, bands, seg, sta, pol, blocks, lags)

    raw = raw_spectra.reshape(stations, 2, bands, BAND).transpose(0, 2, 1, 3).reshape(-1, BAND)
    vmem = pl.BlockSpec(memory_space=pltpu.VMEM)
    smem = pl.BlockSpec(memory_space=pltpu.SMEM)
    hbm = pl.BlockSpec(memory_space=pltpu.HBM)
    plan = [] if fast else [owner_plan]
    in_hbm = functools.partial(pltpu.with_memory_space_constraint, memory_space=pltpu.HBM)
    own = pl.pallas_call(
        functools.partial(prepare_kernel, (stations, bands, sta, blocks)),
        out_shape=pltpu.VMEM((1, rows, LANES), jnp.bfloat16),
        in_specs=[smem] * len(plan) + [vmem, vmem, vmem],
        out_specs=vmem,
        scratch_shapes=[pltpu.VMEM((2 * stations * bands, LANES), jnp.float32)],
        compiler_params=pltpu.CompilerParams(vmem_limit_bytes=VMEM_BYTES),
        name="prepare",
    )(*plan, in_hbm(raw), in_hbm(jnp.transpose(pair_valid[0])), in_hbm(quality))

    def call(kernel, out_shape, *args, aliases=None, scratch=(), flops=0, moved=0, name=None):
        def spec(x):
            if x is table_const or x is plan_const or x.shape == placed_shape.shape:
                return hbm
            return smem if x.shape == (STEPS,) else vmem

        many = isinstance(out_shape, (list, tuple))
        return pl.pallas_call(
            functools.partial(kernel, sizes),
            out_shape=out_shape,
            in_specs=[spec(x) for x in args],
            out_specs=[spec(x) for x in out_shape] if many else spec(out_shape),
            input_output_aliases=aliases or {},
            scratch_shapes=list(scratch),
            compiler_params=pltpu.CompilerParams(vmem_limit_bytes=VMEM_BYTES),
            cost_estimate=pl.CostEstimate(flops=flops, bytes_accessed=moved, transcendentals=0),
            name=name,
        )(*args)

    f32 = jnp.float32
    placed_shape = jax.ShapeDtypeStruct((STEPS, pairs, lags), f32)
    table_const, plan_const = in_hbm(table), in_hbm(owner_plan)

    def fetch(after):
        return call(
            fetch_kernel,
            [
                pltpu.VMEM(table.shape[1:], table.dtype),
                pltpu.VMEM((2, bands, LANES), f32),
                pltpu.SMEM((STEPS,), jnp.int32),
            ],
            table_const, plan_const, after,
            scratch=[pltpu.SMEM((STEPS,), jnp.int32), pltpu.SemaphoreType.DMA((2,))],
            moved=4 * table.size // pol,
            name="fetch",
        )

    def products(count):
        return [pltpu.VMEM((count * pairs * 8, LANES), f32)] * 2 + [pltpu.VMEM((2, count * pairs, bins), jnp.bfloat16)]

    quarter = 32 * pairs * 2 * bins * lags
    local_shape = pltpu.VMEM((seg, stations, 2, bands, LANES), f32)
    wide_shape = pltpu.VMEM((seg, blocks * pairs, LANES), f32)
    kept_shape = pltpu.VMEM((pairs, lags), f32)

    if fast:
        far = join(own, exchange(own, "seg", 2))
        table, phase, is_own = fetch(own)
        far, table = lax.optimization_barrier((far, table))
        bare = join(far, rows=rows - 16)
        near = exchange(far, "seg", 1)
        across = fetch_from(bare, ("seg", "sta"), lambda z, x: (z ^ 1, x ^ 1))
        partner = exchange(bare, "sta", 1)
        mine = join(far, near)
        own_kept, own_sent, local, wide = call(
            own_block_kernel, [kept_shape, kept_shape, local_shape, wide_shape],
            table, phase, mine,
            scratch=products(1), flops=8 * quarter, name="own_block",
        )
        weighted = call(
            weigh_kernel, pltpu.VMEM((stations, stations, seg, 2, bands, LANES), f32),
            wide, local,
            flops=8 * quarter, name="weigh",
        )
        own_got = exchange(own_sent, "pol", 1)
        weighted, across = lax.optimization_barrier((weighted, across))
        partial = call(
            across_kernel, [pltpu.VMEM((pairs * 8, LANES), f32)] * 2,
            weighted, across,
            name="across",
        )
        own_got, partial, partner = lax.optimization_barrier((own_got, partial, partner))
        kept, sent = call(
            other_block_kernel, [kept_shape, pltpu.VMEM((pairs, lags), jnp.bfloat16)],
            table, weighted, *partial, partner,
            scratch=products(1), flops=quarter, name="other_block",
        )
        got = exchange(sent, "pol", 1)
        steps, kept = call(
            settle_kernel, [placed_shape, kept_shape], own_kept, own_got, kept,
            scratch=[pltpu.VMEM((pairs, lags), f32), pltpu.SemaphoreType.DMA((STEPS,))],
            flops=quarter, name="settle",
        )
        result = call(
            place_kernel, placed_shape, is_own, kept, got, steps,
            aliases={3: 0},
            scratch=[pltpu.VMEM((pairs, lags), f32), pltpu.SemaphoreType.DMA((STEPS,))],
            name="place",
        )
    else:
        mine, distance = own, seg // 2
        while distance:
            mine = join(mine, exchange(mine, "seg", distance))
            distance //= 2
        gathered = lax.all_gather(mine, "sta")
        sources = join(*(gathered[owner_plan[k]] for k in range(STEPS)))
        table, phase, _ = fetch(mine)
        kept, sent = call(
            all_blocks_kernel,
            [pltpu.VMEM((blocks * pairs, lags), f32), pltpu.VMEM((blocks * pairs, lags), jnp.bfloat16)],
            table, phase, mine, sources,
            scratch=[local_shape, wide_shape] + products(blocks), flops=blocks * quarter, name="all_blocks",
        )
        result = call(
            combine_kernel, jax.ShapeDtypeStruct((blocks * pairs, lags), f32),
            kept, exchange(sent, "pol", 1), name="combine",
        )
    return result.reshape(STEPS, stations, stations, lags)


def solution(mesh):
    placed = (
        P(("groups", "seg"), "sta", None, "pol"),
        P("groups"),
        P(("groups", "seg"), None, "sta"),
        P(("groups", "seg"), None),
    )

    def whole(raw_spectra, owner_plan, pair_valid, quality):
        seg, pol = mesh.shape["seg"], mesh.shape["pol"]
        bins = raw_spectra.shape[3]
        segments = raw_spectra.shape[0] // mesh.shape["groups"]
        table = lag_table(2 * bins // seg, bins, pol, 1.0 / math.sqrt(bins * segments))
        return jax.shard_map(
            shards,
            mesh=mesh,
            in_specs=(P(),) + placed,
            out_specs=P("groups", None, "sta", ("seg", "pol")),
            check_vma=False,
        )(jnp.asarray(table), raw_spectra, owner_plan, pair_valid, quality)

    return whole
```

```python
import functools
import math

import jax
import jax.numpy as jnp
import numpy as np
from jax import lax
from jax.experimental import pallas as pl
from jax.experimental.pallas import tpu as pltpu
from jax.sharding import PartitionSpec as P

STEPS = 3
BAND = 128
LANES = 128
VMEM_BYTES = 32 * 1024 * 1024


def lag_table(lags, bins, halves, scale):
    bin_index = np.arange(bins, dtype=np.int64)
    lag = 2 * np.arange(lags // 2, dtype=np.int64) + 1
    phase = (bin_index[:, None] * lag[None, :]) % (4 * bins)
    angle = phase * (2.0 * math.pi / (4 * bins))
    factor = np.where(bin_index == 0, 1.0, 2.0)[:, None] * scale
    parts = np.stack([np.cos(angle) * factor, np.sin(angle) * factor])
    parts = parts.reshape(2, halves, bins // halves, lags // 2).transpose(1, 0, 2, 3)
    return parts.astype(jnp.bfloat16)


def turn(count, period):
    count = count % period
    quarter = (count + period // 8) // (period // 4)
    x = (count - quarter * (period // 4)).astype(jnp.float32) * (2.0 * math.pi / period)
    y = x * x
    sine = x * (1.0 + y * (-1 / 6 + y * (1 / 120 + y * (-1 / 5040 + y * (1 / 362880)))))
    cosine = 1.0 + y * (-1 / 2 + y * (1 / 24 + y * (-1 / 720 + y * (1 / 40320))))
    quarter = quarter % 4
    odd = quarter % 2 == 1
    real = jnp.where(odd, sine, cosine)
    imag = jnp.where(odd, cosine, sine)
    real = jnp.where((quarter == 1) | (quarter == 2), -real, real)
    imag = jnp.where(quarter >= 2, -imag, imag)
    return real, imag


def prepare_kernel(sizes, *refs):
    stations, bands, sta, blocks = sizes
    *plan, raw_ref, valid_ref, quality_ref, out_ref, wide = refs
    total = stations * sta
    me = lax.axis_index("sta")
    wide[...] = raw_ref[...].astype(jnp.float32)
    count = stations * bands
    real = wide[pl.ds(0, count, stride=2), :]
    imag = wide[pl.ds(1, count, stride=2), :]
    power = jnp.sum(real * real + imag * imag, axis=1, keepdims=True) * (1.0 / (2 * BAND))
    inverse = lax.rsqrt(power + 1e-06)
    real = (real * inverse).reshape(stations, bands, LANES)
    imag = (imag * inverse).reshape(stations, bands, LANES)
    white = jnp.concatenate([real, imag], axis=1).reshape(2 * count, LANES).astype(jnp.bfloat16)

    flags = jnp.concatenate([valid_ref[...], jnp.broadcast_to(quality_ref[...], (8, total))], axis=0)
    pair = lax.broadcasted_iota(jnp.int32, (total, LANES), 1)
    station = lax.broadcasted_iota(jnp.int32, (total, LANES), 0)
    wanted = [(plan[0][k] if plan else k) * stations + pair // stations for k in range(blocks)]
    wanted.append(me * stations + pair % stations)
    picks = jnp.concatenate([(station == x).astype(jnp.float32) for x in wanted], axis=1)
    picked = jnp.dot(
        flags.astype(jnp.float32).astype(jnp.bfloat16), picks.astype(jnp.bfloat16),
        preferred_element_type=jnp.float32,
    )
    mine = lax.broadcasted_iota(jnp.int32, (stations, LANES), 0) == (
        lax.broadcasted_iota(jnp.int32, (stations, LANES), 1) % stations
    )
    local_flags = picked[stations : stations + 1, blocks * LANES :]
    rows = []
    for k in range(blocks):
        part = picked[:, k * LANES : (k + 1) * LANES]
        valid_row = jnp.sum(jnp.where(mine, part[:stations], 0.0), axis=0, keepdims=True)
        rows.append(valid_row * part[stations : stations + 1] * local_flags)
    rows.append(jnp.zeros((16 - blocks, LANES), jnp.float32))
    weights = jnp.concatenate(rows, axis=0).astype(jnp.bfloat16)
    out_ref[0, pl.ds(0, 2 * count), :] = white
    out_ref[0, pl.ds(2 * count, 16), :] = weights


def spread_weights(sizes, locals_ref, wide):
    stations, bands, seg, sta, pol, blocks, lags = sizes
    pairs = stations * stations
    row_index = lax.broadcasted_iota(jnp.int32, (16, LANES), 0)
    diagonal = lax.broadcasted_iota(jnp.int32, (pairs, LANES), 0) == lax.broadcasted_iota(
        jnp.int32, (pairs, LANES), 1
    )
    ones = jnp.ones((LANES, LANES), jnp.bfloat16)
    for g in range(seg):
        flags = locals_ref[g, pl.ds(2 * stations * bands, 16), :].astype(jnp.float32)
        spread = []
        for n in range(blocks):
            block = lax.axis_index("sta") ^ n if sta == 2 else n
            row = jnp.sum(jnp.where(row_index == block, flags, 0.0), axis=0, keepdims=True)
            spread.append(jnp.where(diagonal, row, 0.0))
        spread = jnp.concatenate(spread, axis=0).astype(jnp.bfloat16)
        wide[g] = jnp.dot(spread, ones, preferred_element_type=jnp.float32)


def middle_phase(sizes):
    stations, bands, seg, sta, pol, blocks, lags = sizes
    row = lax.axis_index("pol") * bands + lax.broadcasted_iota(jnp.int32, (bands, LANES), 0)
    bin_index = row * LANES + lax.broadcasted_iota(jnp.int32, (bands, LANES), 1)
    run = pol * lags
    return turn(bin_index * (2 * run * lax.axis_index("seg") + run - 1), 2 * run * seg)


def turn_locals(sizes, cosine, sine, locals_ref, local):
    stations, bands, seg = sizes[:3]
    for g in range(seg):
        for j in range(stations):
            tile = locals_ref[g, pl.ds(j * 16, 16), :].astype(jnp.float32)
            local[g, j, 0] = tile[:bands] * cosine + tile[bands:] * sine
            local[g, j, 1] = tile[bands:] * cosine - tile[:bands] * sine


def add_products(stations, count, segments, tile_of, weight_of, local_of, real_x, imag_x, before=None):
    def one_source(a, carry):
        tiles = [tile_of(n, a).astype(jnp.float32) for n in range(segments)]
        for j in range(stations):
            pair = a * stations + j
            at = pl.ds(pair * 8 if isinstance(pair, int) else pl.multiple_of(pair * 8, 8), 8)
            real_sum = imag_sum = None
            if before is not None:
                real_sum, imag_sum = before[0][at, :], before[1][at, :]
            for n in range(segments):
                real_src, imag_src = tiles[n][:8], tiles[n][8:]
                if weight_of is not None:
                    weight = jnp.broadcast_to(weight_of(n, pair), (8, LANES))
                    real_src, imag_src = real_src * weight, imag_src * weight
                real_loc, imag_loc = local_of(n, a, j)
                real_term = real_src * real_loc + imag_src * imag_loc
                imag_term = imag_src * real_loc - real_src * imag_loc
                real_sum = real_term if real_sum is None else real_sum + real_term
                imag_sum = imag_term if imag_sum is None else imag_sum + imag_term
            real_x[at, :] = real_sum
            imag_x[at, :] = imag_sum
        return carry

    if count <= 8:
        for a in range(count):
            one_source(a, 0)
    else:
        lax.fori_loop(0, count, one_source, 0, unroll=2)


def pack(rows, bands, real_x, imag_x, packed):
    for band in range(bands):
        at = pl.ds(band * LANES, LANES)
        strided = pl.ds(band, rows, stride=8)
        packed[0, :, at] = real_x[strided, :].astype(jnp.bfloat16)
        packed[1, :, at] = imag_x[strided, :].astype(jnp.bfloat16)


def source_tile(sources_ref, base, count, stations):
    def tile_of(n, a):
        start = a % stations * 16
        start = start if isinstance(a, int) else pl.multiple_of(start, 16)
        return sources_ref[base + a // stations * count + n, pl.ds(start, 16), :]

    return tile_of


def block_sums(sizes, first_block, count, table, wide, local, sources_ref, kept_ref, sent_ref, real_x, imag_x, packed):
    stations, bands, seg = sizes[:3]
    pairs = stations * stations
    add_products(
        stations, count * stations, seg, source_tile(sources_ref, 0, seg, stations),
        lambda n, pair: wide[n, pl.ds(first_block * pairs + pair, 1), :],
        lambda n, a, j: (local[n, j, 0], local[n, j, 1]),
        real_x, imag_x,
    )
    both_sums(sizes, count * pairs, table, kept_ref, sent_ref, real_x, imag_x, packed)


def both_sums(sizes, rows, table, real_x, imag_x, packed):
    pack(rows, sizes[1], real_x, imag_x, packed)
    dot = functools.partial(jnp.dot, preferred_element_type=jnp.float32)
    even, odd = dot(packed[0], table[0]), dot(packed[1], table[1])
    return even + odd, even - odd


def turned_round(sums):
    index = LANES - 1 - lax.broadcasted_iota(jnp.int32, (sums.shape[0], LANES), 1)
    runs = [sums[:, at : at + LANES] for at in reversed(range(0, sums.shape[1], LANES))]
    runs = [jnp.take_along_axis(run, index, axis=1, mode="promise_in_bounds") for run in runs]
    return jnp.concatenate(runs, axis=1)


def block_sums(sizes, first_block, count, table, wide, local, sources_ref, real_x, imag_x, packed):
    stations, bands, seg = sizes[:3]
    pairs = stations * stations
    add_products(
        stations, count * stations, seg, source_tile(sources_ref, 0, seg, stations),
        lambda n, pair: wide[n, pl.ds(first_block * pairs + pair, 1), :],
        lambda n, a, j: (local[n, j, 0], local[n, j, 1]),
        real_x, imag_x,
    )
    return both_sums(sizes, count * pairs, table, real_x, imag_x, packed)


def keep_and_send(before, after, kept_ref, sent_ref):
    first_core = lax.axis_index("pol") == 0
    kept_ref[...] = jnp.where(first_core, before, after)
    sent_ref[...] = jnp.where(first_core, after, before).astype(sent_ref.dtype)


def all_blocks_kernel(sizes, table, phase, mine_ref, sources_ref, kept_ref, sent_ref, local, wide, *scratch):
    spread_weights(sizes, mine_ref, wide)
    turn_locals(sizes, phase[0], phase[1], mine_ref, local)
    before, after = block_sums(sizes, 0, sizes[5], table, wide, local, sources_ref, *scratch)
    keep_and_send(turned_round(before), after, kept_ref, sent_ref)


def own_block_kernel(sizes, table, phase, mine_ref, kept_ref, sent_ref, local_ref, wide_ref, *scratch):
    spread_weights(sizes, mine_ref, wide_ref)
    turn_locals(sizes, phase[0], phase[1], mine_ref, local_ref)
    before, after = block_sums(sizes, 0, 1, table, wide_ref, local_ref, mine_ref, *scratch)
    keep_and_send(turned_round(before), after, kept_ref, sent_ref)


def weigh_kernel(sizes, wide_ref, local_ref, weighted_ref):
    stations, bands, seg = sizes[:3]
    for a in range(stations):
        for j in range(stations):
            pair = stations * stations + a * stations + j
            for g in range(seg):
                weight = jnp.broadcast_to(wide_ref[g, pl.ds(pair, 1), :], (bands, LANES))
                weighted_ref[a, j, g, 0] = local_ref[g, j, 0] * weight
                weighted_ref[a, j, g, 1] = local_ref[g, j, 1] * weight


def across_kernel(sizes, weighted_ref, across_ref, real_x, imag_x):
    stations = sizes[0]
    add_products(
        stations, stations, 2,
        lambda n, a: across_ref[n, pl.ds(a * 16, 16), :],
        None,
        lambda n, a, j: (weighted_ref[a, j, 2 + n, 0], weighted_ref[a, j, 2 + n, 1]),
        real_x, imag_x,
    )


def other_block_kernel(sizes, table, weighted_ref, real_ref, imag_ref, partner_ref, kept_ref, sent_ref, *scratch):
    stations, bands, seg = sizes[:3]
    add_products(
        stations, stations, 2,
        lambda n, a: partner_ref[n, pl.ds(a * 16, 16), :],
        None,
        lambda n, a, j: (weighted_ref[a, j, n, 0], weighted_ref[a, j, n, 1]),
        *scratch[:2],
        before=(real_ref, imag_ref),
    )
    before, after = both_sums(sizes, stations * stations, table, *scratch)
    first_core = lax.axis_index("pol") == 0

    @pl.when(first_core)
    def _():
        kept_ref[...] = before
        sent_ref[...] = after.astype(sent_ref.dtype)

    @pl.when(jnp.logical_not(first_core))
    def _():
        kept_ref[...] = after
        sent_ref[...] = turned_round(before).astype(sent_ref.dtype)


def settle_kernel(sizes, own_kept_ref, own_got_ref, kept_ref, out_ref, settled_ref, own, sems):
    own[...] = own_kept_ref[...] + own_got_ref[...]
    copies = [pltpu.make_async_copy(own, out_ref.at[step], sems.at[step]) for step in range(STEPS)]
    for copy in copies:
        copy.start()
    kept = kept_ref[...]
    settled_ref[...] = jnp.where(lax.axis_index("pol") == 0, turned_round(kept), kept)
    for copy in copies:
        copy.wait()


def combine_kernel(sizes, kept_ref, got_ref, lags_ref):
    lags_ref[...] = kept_ref[...] + got_ref[...].astype(jnp.float32)


def place_kernel(sizes, is_own_ref, kept_ref, got_ref, steps_ref, out_ref, other, sems):
    del steps_ref
    other[...] = kept_ref[...] + got_ref[...].astype(jnp.float32)
    for act in ("start", "wait"):
        for step in range(STEPS):

            @pl.when(is_own_ref[step] == 0)
            def _():
                getattr(pltpu.make_async_copy(other, out_ref.at[step], sems.at[step]), act)()


def fetch_kernel(sizes, table_hbm, plan_any, after, table_ref, phase_ref, is_own_ref, plan_ref, sems):
    del after
    copies = [
        pltpu.make_async_copy(table_hbm.at[lax.axis_index("pol")], table_ref, sems.at[0]),
        pltpu.make_async_copy(plan_any, plan_ref, sems.at[1]),
    ]
    for copy in copies:
        copy.start()
    phase_ref[0], phase_ref[1] = middle_phase(sizes)
    copies[1].wait()
    for step in range(STEPS):
        is_own_ref[step] = (plan_ref[step] == lax.axis_index("sta")).astype(jnp.int32)
    copies[0].wait()


def join_kernel(ranges, *refs):
    *pieces, out_ref = refs
    at = 0
    for piece, (first, count) in zip(pieces, ranges):
        out_ref[pl.ds(at, count)] = piece[pl.ds(first, count), pl.ds(0, out_ref.shape[1]), :]
        at += count


def join(*pieces, rows=None):
    pieces = [piece if isinstance(piece, tuple) else (piece, 0, piece.shape[0]) for piece in pieces]
    arrays = [piece[0] for piece in pieces]
    ranges = [piece[1:] for piece in pieces]
    vmem = pl.BlockSpec(memory_space=pltpu.VMEM)
    return pl.pallas_call(
        functools.partial(join_kernel, ranges),
        out_shape=pltpu.VMEM(
            (sum(count for _, count in ranges), rows or arrays[0].shape[1], LANES), arrays[0].dtype
        ),
        in_specs=[vmem] * len(arrays),
        out_specs=vmem,
        compiler_params=pltpu.CompilerParams(vmem_limit_bytes=VMEM_BYTES),
        name="join",
    )(*arrays)


def fetch_from(value, axes, source_of):
    sizes = tuple(lax.axis_size(axis) for axis in axes)
    pairs = []
    for index in np.ndindex(*sizes):
        source = source_of(*index)
        pairs.append((int(np.ravel_multi_index(source, sizes)), int(np.ravel_multi_index(index, sizes))))
    return lax.ppermute(value, axes, pairs)


def exchange(value, axis, distance):
    return fetch_from(value, (axis,), lambda i: (i ^ distance,))


def shards(table, raw_spectra, owner_plan, pair_valid, quality):
    seg, sta, pol = (lax.axis_size(name) for name in ("seg", "sta", "pol"))
    _, stations, _, bins = raw_spectra.shape
    bands = bins // BAND
    fast = sta == 2 and pol == 2 and seg == 4
    blocks = 2 if fast else STEPS
    pairs = stations * stations
    lags = table.shape[3]
    rows = 2 * stations * bands + 16
    sizes = (stations, bands, seg, sta, pol, blocks, lags)

    raw = raw_spectra.reshape(stations, 2, bands, BAND).transpose(0, 2, 1, 3).reshape(-1, BAND)
    vmem = pl.BlockSpec(memory_space=pltpu.VMEM)
    smem = pl.BlockSpec(memory_space=pltpu.SMEM)
    hbm = pl.BlockSpec(memory_space=pltpu.HBM)
    plan = [] if fast else [owner_plan]
    in_hbm = functools.partial(pltpu.with_memory_space_constraint, memory_space=pltpu.HBM)
    own = pl.pallas_call(
        functools.partial(prepare_kernel, (stations, bands, sta, blocks)),
        out_shape=pltpu.VMEM((1, rows, LANES), jnp.bfloat16),
        in_specs=[smem] * len(plan) + [vmem, vmem, vmem],
        out_specs=vmem,
        scratch_shapes=[pltpu.VMEM((2 * stations * bands, LANES), jnp.float32)],
        compiler_params=pltpu.CompilerParams(vmem_limit_bytes=VMEM_BYTES),
        name="prepare",
    )(*plan, in_hbm(raw), in_hbm(jnp.transpose(pair_valid[0])), in_hbm(quality))

    def call(kernel, out_shape, *args, aliases=None, scratch=(), flops=0, moved=0, name=None):
        def spec(x):
            if x is table_const or x is plan_const or x.shape == placed_shape.shape:
                return hbm
            return smem if x.shape == (STEPS,) else vmem

        many = isinstance(out_shape, (list, tuple))
        return pl.pallas_call(
            functools.partial(kernel, sizes),
            out_shape=out_shape,
            in_specs=[spec(x) for x in args],
            out_specs=[spec(x) for x in out_shape] if many else spec(out_shape),
            input_output_aliases=aliases or {},
            scratch_shapes=list(scratch),
            compiler_params=pltpu.CompilerParams(vmem_limit_bytes=VMEM_BYTES),
            cost_estimate=pl.CostEstimate(flops=flops, bytes_accessed=moved, transcendentals=0),
            name=name,
        )(*args)

    f32 = jnp.float32
    placed_shape = jax.ShapeDtypeStruct((STEPS, pairs, lags), f32)
    table_const, plan_const = in_hbm(table), in_hbm(owner_plan)

    def fetch(after):
        return call(
            fetch_kernel,
            [
                pltpu.VMEM(table.shape[1:], table.dtype),
                pltpu.VMEM((2, bands, LANES), f32),
                pltpu.SMEM((STEPS,), jnp.int32),
            ],
            table_const, plan_const, after,
            scratch=[pltpu.SMEM((STEPS,), jnp.int32), pltpu.SemaphoreType.DMA((2,))],
            moved=4 * table.size // pol,
            name="fetch",
        )

    def products(count):
        return [pltpu.VMEM((count * pairs * 8, LANES), f32)] * 2 + [pltpu.VMEM((2, count * pairs, bins), jnp.bfloat16)]

    quarter = 32 * pairs * 2 * bins * lags
    local_shape = pltpu.VMEM((seg, stations, 2, bands, LANES), f32)
    wide_shape = pltpu.VMEM((seg, blocks * pairs, LANES), f32)
    kept_shape = pltpu.VMEM((pairs, lags), f32)

    if fast:
        far = join(own, exchange(own, "seg", 2))
        table, phase, is_own = fetch(own)
        far, table = lax.optimization_barrier((far, table))
        bare = join(far, rows=rows - 16)
        near = exchange(far, "seg", 1)
        across = fetch_from(bare, ("seg", "sta"), lambda z, x: (z ^ 1, x ^ 1))
        partner = exchange(bare, "sta", 1)
        mine = join(far, near)
        own_kept, own_sent, local, wide = call(
            own_block_kernel, [kept_shape, kept_shape, local_shape, wide_shape],
            table, phase, mine,
            scratch=products(1), flops=8 * quarter, name="own_block",
        )
        weighted = call(
            weigh_kernel, pltpu.VMEM((stations, stations, seg, 2, bands, LANES), f32),
            wide, local,
            flops=8 * quarter, name="weigh",
        )
        own_got = exchange(own_sent, "pol", 1)
        weighted, across = lax.optimization_barrier((weighted, across))
        partial = call(
            across_kernel, [pltpu.VMEM((pairs * 8, LANES), f32)] * 2,
            weighted, across,
            name="across",
        )
        partial, partner = lax.optimization_barrier((partial, partner))
        kept, sent = call(
            other_block_kernel, [kept_shape, pltpu.VMEM((pairs, lags), jnp.bfloat16)],
            table, weighted, *partial, partner,
            scratch=products(1), name="other_block",
        )
        got = exchange(sent, "pol", 1)
        steps, kept = call(
            settle_kernel, [placed_shape, kept_shape], own_kept, own_got, kept,
            scratch=[pltpu.VMEM((pairs, lags), f32), pltpu.SemaphoreType.DMA((STEPS,))],
            flops=quarter, name="settle",
        )
        result = call(
            place_kernel, placed_shape, is_own, kept, got, steps,
            aliases={3: 0},
            scratch=[pltpu.VMEM((pairs, lags), f32), pltpu.SemaphoreType.DMA((STEPS,))],
            name="place",
        )
    else:
        mine, distance = own, seg // 2
        while distance:
            mine = join(mine, exchange(mine, "seg", distance))
            distance //= 2
        gathered = lax.all_gather(mine, "sta")
        sources = join(*(gathered[owner_plan[k]] for k in range(STEPS)))
        table, phase, _ = fetch(mine)
        kept, sent = call(
            all_blocks_kernel,
            [pltpu.VMEM((blocks * pairs, lags), f32), pltpu.VMEM((blocks * pairs, lags), jnp.bfloat16)],
            table, phase, mine, sources,
            scratch=[local_shape, wide_shape] + products(blocks), flops=blocks * quarter, name="all_blocks",
        )
        result = call(
            combine_kernel, jax.ShapeDtypeStruct((blocks * pairs, lags), f32),
            kept, exchange(sent, "pol", 1), name="combine",
        )
    return result.reshape(STEPS, stations, stations, lags)


def solution(mesh):
    placed = (
        P(("groups", "seg"), "sta", None, "pol"),
        P("groups"),
        P(("groups", "seg"), None, "sta"),
        P(("groups", "seg"), None),
    )

    def whole(raw_spectra, owner_plan, pair_valid, quality):
        seg, pol = mesh.shape["seg"], mesh.shape["pol"]
        bins = raw_spectra.shape[3]
        segments = raw_spectra.shape[0] // mesh.shape["groups"]
        table = lag_table(2 * bins // seg, bins, pol, 1.0 / math.sqrt(bins * segments))
        return jax.shard_map(
            shards,
            mesh=mesh,
            in_specs=(P(),) + placed,
            out_specs=P("groups", None, "sta", ("seg", "pol")),
            check_vma=False,
        )(jnp.asarray(table), raw_spectra, owner_plan, pair_valid, quality)

    return whole
```

```python
import functools
import math

import jax
import jax.numpy as jnp
import numpy as np
from jax import lax
from jax.experimental import pallas as pl
from jax.experimental.pallas import tpu as pltpu
from jax.sharding import PartitionSpec as P

STEPS = 3
BAND = 128
LANES = 128
VMEM_BYTES = 32 * 1024 * 1024


def lag_table(lags, bins, halves, scale):
    bin_index = np.arange(bins, dtype=np.int64)
    lag = 2 * np.arange(lags // 2, dtype=np.int64) + 1
    phase = (bin_index[:, None] * lag[None, :]) % (4 * bins)
    angle = phase * (2.0 * math.pi / (4 * bins))
    factor = np.where(bin_index == 0, 1.0, 2.0)[:, None] * scale
    parts = np.stack([np.cos(angle) * factor, np.sin(angle) * factor])
    parts = parts.reshape(2, halves, bins // halves, lags // 2).transpose(1, 0, 2, 3)
    return parts.astype(jnp.bfloat16)


def turn(count, period):
    count = count % period
    quarter = (count + period // 8) // (period // 4)
    x = (count - quarter * (period // 4)).astype(jnp.float32) * (2.0 * math.pi / period)
    y = x * x
    sine = x * (1.0 + y * (-1 / 6 + y * (1 / 120 + y * (-1 / 5040 + y * (1 / 362880)))))
    cosine = 1.0 + y * (-1 / 2 + y * (1 / 24 + y * (-1 / 720 + y * (1 / 40320))))
    quarter = quarter % 4
    odd = quarter % 2 == 1
    real = jnp.where(odd, sine, cosine)
    imag = jnp.where(odd, cosine, sine)
    real = jnp.where((quarter == 1) | (quarter == 2), -real, real)
    imag = jnp.where(quarter >= 2, -imag, imag)
    return real, imag


def prepare_kernel(sizes, *refs):
    stations, bands, sta, blocks = sizes
    *plan, raw_ref, valid_ref, quality_ref, out_ref, wide = refs
    total = stations * sta
    me = lax.axis_index("sta")
    wide[...] = raw_ref[...].astype(jnp.float32)
    count = stations * bands
    real = wide[pl.ds(0, count, stride=2), :]
    imag = wide[pl.ds(1, count, stride=2), :]
    power = jnp.sum(real * real + imag * imag, axis=1, keepdims=True) * (1.0 / (2 * BAND))
    inverse = lax.rsqrt(power + 1e-06)
    real = (real * inverse).reshape(stations, bands, LANES)
    imag = (imag * inverse).reshape(stations, bands, LANES)
    white = jnp.concatenate([real, imag], axis=1).reshape(2 * count, LANES).astype(jnp.bfloat16)

    flags = jnp.concatenate([valid_ref[...], jnp.broadcast_to(quality_ref[...], (8, total))], axis=0)
    pair = lax.broadcasted_iota(jnp.int32, (total, LANES), 1)
    station = lax.broadcasted_iota(jnp.int32, (total, LANES), 0)
    wanted = [(plan[0][k] if plan else k) * stations + pair // stations for k in range(blocks)]
    wanted.append(me * stations + pair % stations)
    picks = jnp.concatenate([(station == x).astype(jnp.float32) for x in wanted], axis=1)
    picked = jnp.dot(
        flags.astype(jnp.float32).astype(jnp.bfloat16), picks.astype(jnp.bfloat16),
        preferred_element_type=jnp.float32,
    )
    mine = lax.broadcasted_iota(jnp.int32, (stations, LANES), 0) == (
        lax.broadcasted_iota(jnp.int32, (stations, LANES), 1) % stations
    )
    local_flags = picked[stations : stations + 1, blocks * LANES :]
    rows = []
    for k in range(blocks):
        part = picked[:, k * LANES : (k + 1) * LANES]
        valid_row = jnp.sum(jnp.where(mine, part[:stations], 0.0), axis=0, keepdims=True)
        rows.append(valid_row * part[stations : stations + 1] * local_flags)
    rows.append(jnp.zeros((16 - blocks, LANES), jnp.float32))
    weights = jnp.concatenate(rows, axis=0).astype(jnp.bfloat16)
    out_ref[0, pl.ds(0, 2 * count), :] = white
    out_ref[0, pl.ds(2 * count, 16), :] = weights


def spread_weights(sizes, locals_ref, wide):
    stations, bands, seg, sta, pol, blocks, lags = sizes
    pairs = stations * stations
    row_index = lax.broadcasted_iota(jnp.int32, (16, LANES), 0)
    diagonal = lax.broadcasted_iota(jnp.int32, (pairs, LANES), 0) == lax.broadcasted_iota(
        jnp.int32, (pairs, LANES), 1
    )
    ones = jnp.ones((LANES, LANES), jnp.bfloat16)
    for g in range(seg):
        flags = locals_ref[g, pl.ds(2 * stations * bands, 16), :].astype(jnp.float32)
        spread = []
        for n in range(blocks):
            block = lax.axis_index("sta") ^ n if sta == 2 else n
            row = jnp.sum(jnp.where(row_index == block, flags, 0.0), axis=0, keepdims=True)
            spread.append(jnp.where(diagonal, row, 0.0))
        spread = jnp.concatenate(spread, axis=0).astype(jnp.bfloat16)
        wide[g] = jnp.dot(spread, ones, preferred_element_type=jnp.float32)


def middle_phase(sizes):
    stations, bands, seg, sta, pol, blocks, lags = sizes
    row = lax.axis_index("pol") * bands + lax.broadcasted_iota(jnp.int32, (bands, LANES), 0)
    bin_index = row * LANES + lax.broadcasted_iota(jnp.int32, (bands, LANES), 1)
    run = pol * lags
    return turn(bin_index * (2 * run * lax.axis_index("seg") + run - 1), 2 * run * seg)


def turn_locals(sizes, cosine, sine, locals_ref, local):
    stations, bands, seg = sizes[:3]
    for g in range(seg):
        for j in range(stations):
            tile = locals_ref[g, pl.ds(j * 16, 16), :].astype(jnp.float32)
            local[g, j, 0] = tile[:bands] * cosine + tile[bands:] * sine
            local[g, j, 1] = tile[bands:] * cosine - tile[:bands] * sine


def add_products(stations, count, segments, tile_of, weight_of, local_of, real_x, imag_x, before=None):
    def one_source(a, carry):
        tiles = [tile_of(n, a).astype(jnp.float32) for n in range(segments)]
        for j in range(stations):
            pair = a * stations + j
            at = pl.ds(pair * 8 if isinstance(pair, int) else pl.multiple_of(pair * 8, 8), 8)
            real_sum = imag_sum = None
            if before is not None:
                real_sum, imag_sum = before[0][at, :], before[1][at, :]
            for n in range(segments):
                real_src, imag_src = tiles[n][:8], tiles[n][8:]
                if weight_of is not None:
                    weight = jnp.broadcast_to(weight_of(n, pair), (8, LANES))
                    real_src, imag_src = real_src * weight, imag_src * weight
                real_loc, imag_loc = local_of(n, a, j)
                real_term = real_src * real_loc + imag_src * imag_loc
                imag_term = imag_src * real_loc - real_src * imag_loc
                real_sum = real_term if real_sum is None else real_sum + real_term
                imag_sum = imag_term if imag_sum is None else imag_sum + imag_term
            real_x[at, :] = real_sum
            imag_x[at, :] = imag_sum
        return carry

    if count <= 8:
        for a in range(count):
            one_source(a, 0)
    else:
        lax.fori_loop(0, count, one_source, 0, unroll=2)


def pack(rows, bands, real_x, imag_x, packed):
    for band in range(bands):
        at = pl.ds(band * LANES, LANES)
        strided = pl.ds(band, rows, stride=8)
        packed[0, :, at] = real_x[strided, :].astype(jnp.bfloat16)
        packed[1, :, at] = imag_x[strided, :].astype(jnp.bfloat16)


def source_tile(sources_ref, base, count, stations):
    def tile_of(n, a):
        start = a % stations * 16
        start = start if isinstance(a, int) else pl.multiple_of(start, 16)
        return sources_ref[base + a // stations * count + n, pl.ds(start, 16), :]

    return tile_of


def block_sums(sizes, first_block, count, table, wide, local, sources_ref, kept_ref, sent_ref, real_x, imag_x, packed):
    stations, bands, seg = sizes[:3]
    pairs = stations * stations
    add_products(
        stations, count * stations, seg, source_tile(sources_ref, 0, seg, stations),
        lambda n, pair: wide[n, pl.ds(first_block * pairs + pair, 1), :],
        lambda n, a, j: (local[n, j, 0], local[n, j, 1]),
        real_x, imag_x,
    )
    both_sums(sizes, count * pairs, table, kept_ref, sent_ref, real_x, imag_x, packed)


def both_sums(sizes, rows, table, real_x, imag_x, packed):
    pack(rows, sizes[1], real_x, imag_x, packed)
    dot = functools.partial(jnp.dot, preferred_element_type=jnp.float32)
    even, odd = dot(packed[0], table[0]), dot(packed[1], table[1])
    return even + odd, even - odd


def turned_round(sums):
    index = LANES - 1 - lax.broadcasted_iota(jnp.int32, (sums.shape[0], LANES), 1)
    runs = [sums[:, at : at + LANES] for at in reversed(range(0, sums.shape[1], LANES))]
    runs = [jnp.take_along_axis(run, index, axis=1, mode="promise_in_bounds") for run in runs]
    return jnp.concatenate(runs, axis=1)


def block_sums(sizes, first_block, count, table, wide, local, sources_ref, real_x, imag_x, packed):
    stations, bands, seg = sizes[:3]
    pairs = stations * stations
    add_products(
        stations, count * stations, seg, source_tile(sources_ref, 0, seg, stations),
        lambda n, pair: wide[n, pl.ds(first_block * pairs + pair, 1), :],
        lambda n, a, j: (local[n, j, 0], local[n, j, 1]),
        real_x, imag_x,
    )
    return both_sums(sizes, count * pairs, table, real_x, imag_x, packed)


def keep_and_send(before, after, kept_ref, sent_ref):
    first_core = lax.axis_index("pol") == 0
    kept_ref[...] = jnp.where(first_core, before, after)
    sent_ref[...] = jnp.where(first_core, after, before).astype(sent_ref.dtype)


def all_blocks_kernel(sizes, table, phase, mine_ref, sources_ref, kept_ref, sent_ref, local, wide, *scratch):
    spread_weights(sizes, mine_ref, wide)
    turn_locals(sizes, phase[0], phase[1], mine_ref, local)
    before, after = block_sums(sizes, 0, sizes[5], table, wide, local, sources_ref, *scratch)
    keep_and_send(turned_round(before), after, kept_ref, sent_ref)


def own_block_kernel(sizes, table, phase, mine_ref, kept_ref, sent_ref, local_ref, wide_ref, *scratch):
    spread_weights(sizes, mine_ref, wide_ref)
    turn_locals(sizes, phase[0], phase[1], mine_ref, local_ref)
    before, after = block_sums(sizes, 0, 1, table, wide_ref, local_ref, mine_ref, *scratch)
    keep_and_send(turned_round(before), after, kept_ref, sent_ref)


def weigh_kernel(sizes, wide_ref, local_ref, weighted_ref):
    stations, bands, seg = sizes[:3]
    for a in range(stations):
        for j in range(stations):
            pair = stations * stations + a * stations + j
            for g in range(seg):
                weight = jnp.broadcast_to(wide_ref[g, pl.ds(pair, 1), :], (bands, LANES))
                weighted_ref[a, j, g, 0] = local_ref[g, j, 0] * weight
                weighted_ref[a, j, g, 1] = local_ref[g, j, 1] * weight


def across_kernel(sizes, weighted_ref, across_ref, real_x, imag_x):
    stations = sizes[0]
    add_products(
        stations, stations, 2,
        lambda n, a: across_ref[n, pl.ds(a * 16, 16), :],
        None,
        lambda n, a, j: (weighted_ref[a, j, 2 + n, 0], weighted_ref[a, j, 2 + n, 1]),
        real_x, imag_x,
    )


def other_block_kernel(sizes, table, weighted_ref, real_ref, imag_ref, partner_ref, kept_ref, sent_ref, *scratch):
    stations, bands, seg = sizes[:3]
    add_products(
        stations, stations, 2,
        lambda n, a: partner_ref[n, pl.ds(a * 16, 16), :],
        None,
        lambda n, a, j: (weighted_ref[a, j, n, 0], weighted_ref[a, j, n, 1]),
        *scratch[:2],
        before=(real_ref, imag_ref),
    )
    before, after = both_sums(sizes, stations * stations, table, *scratch)
    first_core = lax.axis_index("pol") == 0

    @pl.when(first_core)
    def _():
        kept_ref[...] = before
        sent_ref[...] = after.astype(sent_ref.dtype)

    @pl.when(jnp.logical_not(first_core))
    def _():
        kept_ref[...] = after
        sent_ref[...] = turned_round(before).astype(sent_ref.dtype)


def settle_kernel(sizes, own_kept_ref, own_got_ref, kept_ref, out_ref, settled_ref, own, sems):
    own[...] = own_kept_ref[...] + own_got_ref[...]
    copies = [pltpu.make_async_copy(own, out_ref.at[step], sems.at[step]) for step in range(STEPS)]
    for copy in copies:
        copy.start()
    kept = kept_ref[...]
    settled_ref[...] = jnp.where(lax.axis_index("pol") == 0, turned_round(kept), kept)
    for copy in copies:
        copy.wait()


def combine_kernel(sizes, kept_ref, got_ref, lags_ref):
    lags_ref[...] = kept_ref[...] + got_ref[...].astype(jnp.float32)


def place_kernel(sizes, is_own_ref, kept_ref, got_ref, steps_ref, out_ref, other, sems):
    del steps_ref
    other[...] = kept_ref[...] + got_ref[...].astype(jnp.float32)
    for act in ("start", "wait"):
        for step in range(STEPS):

            @pl.when(is_own_ref[step] == 0)
            def _():
                getattr(pltpu.make_async_copy(other, out_ref.at[step], sems.at[step]), act)()


def fetch_kernel(sizes, table_hbm, plan_any, after, table_ref, phase_ref, is_own_ref, plan_ref, sems):
    del after
    copies = [
        pltpu.make_async_copy(table_hbm.at[lax.axis_index("pol")], table_ref, sems.at[0]),
        pltpu.make_async_copy(plan_any, plan_ref, sems.at[1]),
    ]
    for copy in copies:
        copy.start()
    phase_ref[0], phase_ref[1] = middle_phase(sizes)
    copies[1].wait()
    for step in range(STEPS):
        is_own_ref[step] = (plan_ref[step] == lax.axis_index("sta")).astype(jnp.int32)
    copies[0].wait()


def join_kernel(ranges, *refs):
    *pieces, out_ref = refs
    at = 0
    for piece, (first, count) in zip(pieces, ranges):
        out_ref[pl.ds(at, count)] = piece[pl.ds(first, count), pl.ds(0, out_ref.shape[1]), :]
        at += count


def join(*pieces, rows=None):
    pieces = [piece if isinstance(piece, tuple) else (piece, 0, piece.shape[0]) for piece in pieces]
    arrays = [piece[0] for piece in pieces]
    ranges = [piece[1:] for piece in pieces]
    vmem = pl.BlockSpec(memory_space=pltpu.VMEM)
    return pl.pallas_call(
        functools.partial(join_kernel, ranges),
        out_shape=pltpu.VMEM(
            (sum(count for _, count in ranges), rows or arrays[0].shape[1], LANES), arrays[0].dtype
        ),
        in_specs=[vmem] * len(arrays),
        out_specs=vmem,
        compiler_params=pltpu.CompilerParams(vmem_limit_bytes=VMEM_BYTES),
        name="join",
    )(*arrays)


def fetch_from(value, axes, source_of):
    sizes = tuple(lax.axis_size(axis) for axis in axes)
    pairs = []
    for index in np.ndindex(*sizes):
        source = source_of(*index)
        pairs.append((int(np.ravel_multi_index(source, sizes)), int(np.ravel_multi_index(index, sizes))))
    return lax.ppermute(value, axes, pairs)


def exchange(value, axis, distance):
    return fetch_from(value, (axis,), lambda i: (i ^ distance,))


def shards(table, raw_spectra, owner_plan, pair_valid, quality):
    seg, sta, pol = (lax.axis_size(name) for name in ("seg", "sta", "pol"))
    _, stations, _, bins = raw_spectra.shape
    bands = bins // BAND
    fast = sta == 2 and pol == 2 and seg == 4
    blocks = 2 if fast else STEPS
    pairs = stations * stations
    lags = table.shape[3]
    rows = 2 * stations * bands + 16
    sizes = (stations, bands, seg, sta, pol, blocks, lags)

    raw = raw_spectra.reshape(stations, 2, bands, BAND).transpose(0, 2, 1, 3).reshape(-1, BAND)
    vmem = pl.BlockSpec(memory_space=pltpu.VMEM)
    smem = pl.BlockSpec(memory_space=pltpu.SMEM)
    hbm = pl.BlockSpec(memory_space=pltpu.HBM)
    plan = [] if fast else [owner_plan]
    in_hbm = functools.partial(pltpu.with_memory_space_constraint, memory_space=pltpu.HBM)
    own = pl.pallas_call(
        functools.partial(prepare_kernel, (stations, bands, sta, blocks)),
        out_shape=pltpu.VMEM((1, rows, LANES), jnp.bfloat16),
        in_specs=[smem] * len(plan) + [vmem, vmem, vmem],
        out_specs=vmem,
        scratch_shapes=[pltpu.VMEM((2 * stations * bands, LANES), jnp.float32)],
        compiler_params=pltpu.CompilerParams(vmem_limit_bytes=VMEM_BYTES),
        name="prepare",
    )(*plan, in_hbm(raw), in_hbm(jnp.transpose(pair_valid[0])), in_hbm(quality))

    def call(kernel, out_shape, *args, aliases=None, scratch=(), flops=0, moved=0, name=None):
        def spec(x):
            if x is table_const or x is plan_const or x.shape == placed_shape.shape:
                return hbm
            return smem if x.shape == (STEPS,) else vmem

        many = isinstance(out_shape, (list, tuple))
        return pl.pallas_call(
            functools.partial(kernel, sizes),
            out_shape=out_shape,
            in_specs=[spec(x) for x in args],
            out_specs=[spec(x) for x in out_shape] if many else spec(out_shape),
            input_output_aliases=aliases or {},
            scratch_shapes=list(scratch),
            compiler_params=pltpu.CompilerParams(vmem_limit_bytes=VMEM_BYTES),
            cost_estimate=pl.CostEstimate(flops=flops, bytes_accessed=moved, transcendentals=0),
            name=name,
        )(*args)

    f32 = jnp.float32
    placed_shape = jax.ShapeDtypeStruct((STEPS, pairs, lags), f32)
    table_const, plan_const = in_hbm(table), in_hbm(owner_plan)

    def fetch(after):
        return call(
            fetch_kernel,
            [
                pltpu.VMEM(table.shape[1:], table.dtype),
                pltpu.VMEM((2, bands, LANES), f32),
                pltpu.SMEM((STEPS,), jnp.int32),
            ],
            table_const, plan_const, after,
            scratch=[pltpu.SMEM((STEPS,), jnp.int32), pltpu.SemaphoreType.DMA((2,))],
            moved=4 * table.size // pol,
            name="fetch",
        )

    def products(count):
        return [pltpu.VMEM((count * pairs * 8, LANES), f32)] * 2 + [pltpu.VMEM((2, count * pairs, bins), jnp.bfloat16)]

    quarter = 32 * pairs * 2 * bins * lags
    local_shape = pltpu.VMEM((seg, stations, 2, bands, LANES), f32)
    wide_shape = pltpu.VMEM((seg, blocks * pairs, LANES), f32)
    kept_shape = pltpu.VMEM((pairs, lags), f32)

    if fast:
        far = join(own, exchange(own, "seg", 2))
        table, phase, is_own = fetch(own)
        far, table = lax.optimization_barrier((far, table))
        bare = join(far, rows=rows - 16)
        near = exchange(far, "seg", 1)
        across = fetch_from(far, ("seg", "sta"), lambda z, x: (z ^ 1, x ^ 1))
        partner = exchange(bare, "sta", 1)
        mine = join(far, near)
        own_kept, own_sent, local, wide = call(
            own_block_kernel, [kept_shape, kept_shape, local_shape, wide_shape],
            table, phase, mine,
            scratch=products(1), flops=8 * quarter, name="own_block",
        )
        weighted = call(
            weigh_kernel, pltpu.VMEM((stations, stations, seg, 2, bands, LANES), f32),
            wide, local,
            flops=8 * quarter, name="weigh",
        )
        own_got = exchange(own_sent, "pol", 1)
        weighted, across = lax.optimization_barrier((weighted, across))
        partial = call(
            across_kernel, [pltpu.VMEM((pairs * 8, LANES), f32)] * 2,
            weighted, across,
            name="across",
        )
        partial, partner = lax.optimization_barrier((partial, partner))
        kept, sent = call(
            other_block_kernel, [kept_shape, pltpu.VMEM((pairs, lags), jnp.bfloat16)],
            table, weighted, *partial, partner,
            scratch=products(1), name="other_block",
        )
        got = exchange(sent, "pol", 1)
        steps, kept = call(
            settle_kernel, [placed_shape, kept_shape], own_kept, own_got, kept,
            scratch=[pltpu.VMEM((pairs, lags), f32), pltpu.SemaphoreType.DMA((STEPS,))],
            flops=quarter, name="settle",
        )
        result = call(
            place_kernel, placed_shape, is_own, kept, got, steps,
            aliases={3: 0},
            scratch=[pltpu.VMEM((pairs, lags), f32), pltpu.SemaphoreType.DMA((STEPS,))],
            name="place",
        )
    else:
        mine, distance = own, seg // 2
        while distance:
            mine = join(mine, exchange(mine, "seg", distance))
            distance //= 2
        gathered = lax.all_gather(mine, "sta")
        sources = join(*(gathered[owner_plan[k]] for k in range(STEPS)))
        table, phase, _ = fetch(mine)
        kept, sent = call(
            all_blocks_kernel,
            [pltpu.VMEM((blocks * pairs, lags), f32), pltpu.VMEM((blocks * pairs, lags), jnp.bfloat16)],
            table, phase, mine, sources,
            scratch=[local_shape, wide_shape] + products(blocks), flops=blocks * quarter, name="all_blocks",
        )
        result = call(
            combine_kernel, jax.ShapeDtypeStruct((blocks * pairs, lags), f32),
            kept, exchange(sent, "pol", 1), name="combine",
        )
    return result.reshape(STEPS, stations, stations, lags)


def solution(mesh):
    placed = (
        P(("groups", "seg"), "sta", None, "pol"),
        P("groups"),
        P(("groups", "seg"), None, "sta"),
        P(("groups", "seg"), None),
    )

    def whole(raw_spectra, owner_plan, pair_valid, quality):
        seg, pol = mesh.shape["seg"], mesh.shape["pol"]
        bins = raw_spectra.shape[3]
        segments = raw_spectra.shape[0] // mesh.shape["groups"]
        table = lag_table(2 * bins // seg, bins, pol, 1.0 / math.sqrt(bins * segments))
        return jax.shard_map(
            shards,
            mesh=mesh,
            in_specs=(P(),) + placed,
            out_specs=P("groups", None, "sta", ("seg", "pol")),
            check_vma=False,
        )(jnp.asarray(table), raw_spectra, owner_plan, pair_valid, quality)

    return whole
```

```python
import functools
import math

import jax
import jax.numpy as jnp
import numpy as np
from jax import lax
from jax.experimental import pallas as pl
from jax.experimental.pallas import tpu as pltpu
from jax.sharding import PartitionSpec as P

STEPS = 3
BAND = 128
LANES = 128
VMEM_BYTES = 32 * 1024 * 1024


def lag_table(lags, bins, halves, scale):
    bin_index = np.arange(bins, dtype=np.int64)
    lag = 2 * np.arange(lags // 2, dtype=np.int64) + 1
    phase = (bin_index[:, None] * lag[None, :]) % (4 * bins)
    angle = phase * (2.0 * math.pi / (4 * bins))
    factor = np.where(bin_index == 0, 1.0, 2.0)[:, None] * scale
    parts = np.stack([np.cos(angle) * factor, np.sin(angle) * factor])
    parts = parts.reshape(2, halves, bins // halves, lags // 2).transpose(1, 0, 2, 3)
    return parts.astype(jnp.bfloat16)


def turn(count, period):
    count = count % period
    quarter = (count + period // 8) // (period // 4)
    x = (count - quarter * (period // 4)).astype(jnp.float32) * (2.0 * math.pi / period)
    y = x * x
    sine = x * (1.0 + y * (-1 / 6 + y * (1 / 120 + y * (-1 / 5040 + y * (1 / 362880)))))
    cosine = 1.0 + y * (-1 / 2 + y * (1 / 24 + y * (-1 / 720 + y * (1 / 40320))))
    quarter = quarter % 4
    odd = quarter % 2 == 1
    real = jnp.where(odd, sine, cosine)
    imag = jnp.where(odd, cosine, sine)
    real = jnp.where((quarter == 1) | (quarter == 2), -real, real)
    imag = jnp.where(quarter >= 2, -imag, imag)
    return real, imag


def prepare_kernel(sizes, *refs):
    stations, bands, sta, blocks = sizes
    *plan, raw_ref, valid_ref, quality_ref, out_ref, wide = refs
    total = stations * sta
    me = lax.axis_index("sta")
    wide[...] = raw_ref[...].astype(jnp.float32)
    count = stations * bands
    real = wide[pl.ds(0, count, stride=2), :]
    imag = wide[pl.ds(1, count, stride=2), :]
    power = jnp.sum(real * real + imag * imag, axis=1, keepdims=True) * (1.0 / (2 * BAND))
    inverse = lax.rsqrt(power + 1e-06)
    real = (real * inverse).reshape(stations, bands, LANES)
    imag = (imag * inverse).reshape(stations, bands, LANES)
    white = jnp.concatenate([real, imag], axis=1).reshape(2 * count, LANES).astype(jnp.bfloat16)

    flags = jnp.concatenate([valid_ref[...], jnp.broadcast_to(quality_ref[...], (8, total))], axis=0)
    pair = lax.broadcasted_iota(jnp.int32, (total, LANES), 1)
    station = lax.broadcasted_iota(jnp.int32, (total, LANES), 0)
    wanted = [(plan[0][k] if plan else k) * stations + pair // stations for k in range(blocks)]
    wanted.append(me * stations + pair % stations)
    picks = jnp.concatenate([(station == x).astype(jnp.float32) for x in wanted], axis=1)
    picked = jnp.dot(
        flags.astype(jnp.float32).astype(jnp.bfloat16), picks.astype(jnp.bfloat16),
        preferred_element_type=jnp.float32,
    )
    mine = lax.broadcasted_iota(jnp.int32, (stations, LANES), 0) == (
        lax.broadcasted_iota(jnp.int32, (stations, LANES), 1) % stations
    )
    local_flags = picked[stations : stations + 1, blocks * LANES :]
    rows = []
    for k in range(blocks):
        part = picked[:, k * LANES : (k + 1) * LANES]
        valid_row = jnp.sum(jnp.where(mine, part[:stations], 0.0), axis=0, keepdims=True)
        rows.append(valid_row * part[stations : stations + 1] * local_flags)
    rows.append(jnp.zeros((16 - blocks, LANES), jnp.float32))
    weights = jnp.concatenate(rows, axis=0).astype(jnp.bfloat16)
    out_ref[0, pl.ds(0, 2 * count), :] = white
    out_ref[0, pl.ds(2 * count, 16), :] = weights


def spread_weights(sizes, locals_ref, wide):
    stations, bands, seg, sta, pol, blocks, lags = sizes
    pairs = stations * stations
    row_index = lax.broadcasted_iota(jnp.int32, (16, LANES), 0)
    diagonal = lax.broadcasted_iota(jnp.int32, (pairs, LANES), 0) == lax.broadcasted_iota(
        jnp.int32, (pairs, LANES), 1
    )
    ones = jnp.ones((LANES, LANES), jnp.bfloat16)
    for g in range(seg):
        flags = locals_ref[g, pl.ds(2 * stations * bands, 16), :].astype(jnp.float32)
        spread = []
        for n in range(blocks):
            block = lax.axis_index("sta") ^ n if sta == 2 else n
            row = jnp.sum(jnp.where(row_index == block, flags, 0.0), axis=0, keepdims=True)
            spread.append(jnp.where(diagonal, row, 0.0))
        spread = jnp.concatenate(spread, axis=0).astype(jnp.bfloat16)
        wide[g] = jnp.dot(spread, ones, preferred_element_type=jnp.float32)


def middle_phase(sizes):
    stations, bands, seg, sta, pol, blocks, lags = sizes
    row = lax.axis_index("pol") * bands + lax.broadcasted_iota(jnp.int32, (bands, LANES), 0)
    bin_index = row * LANES + lax.broadcasted_iota(jnp.int32, (bands, LANES), 1)
    run = pol * lags
    return turn(bin_index * (2 * run * lax.axis_index("seg") + run - 1), 2 * run * seg)


def turn_locals(sizes, cosine, sine, locals_ref, local):
    stations, bands, seg = sizes[:3]
    for g in range(seg):
        for j in range(stations):
            tile = locals_ref[g, pl.ds(j * 16, 16), :].astype(jnp.float32)
            local[g, j, 0] = tile[:bands] * cosine + tile[bands:] * sine
            local[g, j, 1] = tile[bands:] * cosine - tile[:bands] * sine


def add_products(stations, count, segments, tile_of, weight_of, local_of, real_x, imag_x, before=None):
    def one_source(a, carry):
        tiles = [tile_of(n, a).astype(jnp.float32) for n in range(segments)]
        for j in range(stations):
            pair = a * stations + j
            at = pl.ds(pair * 8 if isinstance(pair, int) else pl.multiple_of(pair * 8, 8), 8)
            real_sum = imag_sum = None
            if before is not None:
                real_sum, imag_sum = before[0][at, :], before[1][at, :]
            for n in range(segments):
                real_src, imag_src = tiles[n][:8], tiles[n][8:]
                if weight_of is not None:
                    weight = jnp.broadcast_to(weight_of(n, pair), (8, LANES))
                    real_src, imag_src = real_src * weight, imag_src * weight
                real_loc, imag_loc = local_of(n, a, j)
                real_term = real_src * real_loc + imag_src * imag_loc
                imag_term = imag_src * real_loc - real_src * imag_loc
                real_sum = real_term if real_sum is None else real_sum + real_term
                imag_sum = imag_term if imag_sum is None else imag_sum + imag_term
            real_x[at, :] = real_sum
            imag_x[at, :] = imag_sum
        return carry

    if count <= 8:
        for a in range(count):
            one_source(a, 0)
    else:
        lax.fori_loop(0, count, one_source, 0, unroll=2)


def pack(rows, bands, real_x, imag_x, packed):
    for band in range(bands):
        at = pl.ds(band * LANES, LANES)
        strided = pl.ds(band, rows, stride=8)
        packed[0, :, at] = real_x[strided, :].astype(jnp.bfloat16)
        packed[1, :, at] = imag_x[strided, :].astype(jnp.bfloat16)


def source_tile(sources_ref, base, count, stations):
    def tile_of(n, a):
        start = a % stations * 16
        start = start if isinstance(a, int) else pl.multiple_of(start, 16)
        return sources_ref[base + a // stations * count + n, pl.ds(start, 16), :]

    return tile_of


def block_sums(sizes, first_block, count, table, wide, local, sources_ref, kept_ref, sent_ref, real_x, imag_x, packed):
    stations, bands, seg = sizes[:3]
    pairs = stations * stations
    add_products(
        stations, count * stations, seg, source_tile(sources_ref, 0, seg, stations),
        lambda n, pair: wide[n, pl.ds(first_block * pairs + pair, 1), :],
        lambda n, a, j: (local[n, j, 0], local[n, j, 1]),
        real_x, imag_x,
    )
    both_sums(sizes, count * pairs, table, kept_ref, sent_ref, real_x, imag_x, packed)


def both_sums(sizes, rows, table, real_x, imag_x, packed):
    pack(rows, sizes[1], real_x, imag_x, packed)
    dot = functools.partial(jnp.dot, preferred_element_type=jnp.float32)
    even, odd = dot(packed[0], table[0]), dot(packed[1], table[1])
    return even + odd, even - odd


def turned_round(sums):
    index = LANES - 1 - lax.broadcasted_iota(jnp.int32, (sums.shape[0], LANES), 1)
    runs = [sums[:, at : at + LANES] for at in reversed(range(0, sums.shape[1], LANES))]
    runs = [jnp.take_along_axis(run, index, axis=1, mode="promise_in_bounds") for run in runs]
    return jnp.concatenate(runs, axis=1)


def block_sums(sizes, first_block, count, table, wide, local, sources_ref, real_x, imag_x, packed):
    stations, bands, seg = sizes[:3]
    pairs = stations * stations
    add_products(
        stations, count * stations, seg, source_tile(sources_ref, 0, seg, stations),
        lambda n, pair: wide[n, pl.ds(first_block * pairs + pair, 1), :],
        lambda n, a, j: (local[n, j, 0], local[n, j, 1]),
        real_x, imag_x,
    )
    return both_sums(sizes, count * pairs, table, real_x, imag_x, packed)


def keep_and_send(before, after, kept_ref, sent_ref):
    first_core = lax.axis_index("pol") == 0
    kept_ref[...] = jnp.where(first_core, before, after)
    sent_ref[...] = jnp.where(first_core, after, before).astype(sent_ref.dtype)


def all_blocks_kernel(sizes, table, phase, mine_ref, sources_ref, kept_ref, sent_ref, local, wide, *scratch):
    spread_weights(sizes, mine_ref, wide)
    turn_locals(sizes, phase[0], phase[1], mine_ref, local)
    before, after = block_sums(sizes, 0, sizes[5], table, wide, local, sources_ref, *scratch)
    keep_and_send(turned_round(before), after, kept_ref, sent_ref)


def own_block_kernel(sizes, table, phase, mine_ref, kept_ref, sent_ref, local_ref, wide_ref, *scratch):
    spread_weights(sizes, mine_ref, wide_ref)
    turn_locals(sizes, phase[0], phase[1], mine_ref, local_ref)
    before, after = block_sums(sizes, 0, 1, table, wide_ref, local_ref, mine_ref, *scratch)
    keep_and_send(turned_round(before), after, kept_ref, sent_ref)


def weigh_kernel(sizes, wide_ref, local_ref, weighted_ref):
    stations, bands, seg = sizes[:3]
    for a in range(stations):
        for j in range(stations):
            pair = stations * stations + a * stations + j
            for g in range(seg):
                weight = jnp.broadcast_to(wide_ref[g, pl.ds(pair, 1), :], (bands, LANES))
                weighted_ref[a, j, g, 0] = local_ref[g, j, 0] * weight
                weighted_ref[a, j, g, 1] = local_ref[g, j, 1] * weight


def partner_kernel(sizes, weighted_ref, first_ref, second_ref, real_x, imag_x):
    stations = sizes[0]
    add_products(
        stations, stations, 2,
        lambda n, a: (first_ref, second_ref)[n][0, pl.ds(a * 16, 16), :],
        None,
        lambda n, a, j: (weighted_ref[a, j, n, 0], weighted_ref[a, j, n, 1]),
        real_x, imag_x,
    )


def other_block_kernel(sizes, table, weighted_ref, real_ref, imag_ref, across_ref, kept_ref, sent_ref, *scratch):
    stations, bands, seg = sizes[:3]
    add_products(
        stations, stations, 2,
        lambda n, a: across_ref[n, pl.ds(a * 16, 16), :],
        None,
        lambda n, a, j: (weighted_ref[a, j, 2 + n, 0], weighted_ref[a, j, 2 + n, 1]),
        *scratch[:2],
        before=(real_ref, imag_ref),
    )
    before, after = both_sums(sizes, stations * stations, table, *scratch)
    first_core = lax.axis_index("pol") == 0

    @pl.when(first_core)
    def _():
        kept_ref[...] = before
        sent_ref[...] = after.astype(sent_ref.dtype)

    @pl.when(jnp.logical_not(first_core))
    def _():
        kept_ref[...] = after
        sent_ref[...] = turned_round(before).astype(sent_ref.dtype)


def settle_kernel(sizes, own_kept_ref, own_got_ref, kept_ref, out_ref, settled_ref, own, sems):
    own[...] = own_kept_ref[...] + own_got_ref[...]
    copies = [pltpu.make_async_copy(own, out_ref.at[step], sems.at[step]) for step in range(STEPS)]
    for copy in copies:
        copy.start()
    kept = kept_ref[...]
    settled_ref[...] = jnp.where(lax.axis_index("pol") == 0, turned_round(kept), kept)
    for copy in copies:
        copy.wait()


def combine_kernel(sizes, kept_ref, got_ref, lags_ref):
    lags_ref[...] = kept_ref[...] + got_ref[...].astype(jnp.float32)


def place_kernel(sizes, is_own_ref, kept_ref, got_ref, steps_ref, out_ref, other, sems):
    del steps_ref
    other[...] = kept_ref[...] + got_ref[...].astype(jnp.float32)
    for act in ("start", "wait"):
        for step in range(STEPS):

            @pl.when(is_own_ref[step] == 0)
            def _():
                getattr(pltpu.make_async_copy(other, out_ref.at[step], sems.at[step]), act)()


def phase_kernel(sizes, after, phase_ref):
    del after
    phase_ref[0], phase_ref[1] = middle_phase(sizes)


def fetch_kernel(sizes, table_hbm, plan_any, after, table_ref, is_own_ref, plan_ref, sems):
    del after
    copies = [
        pltpu.make_async_copy(table_hbm.at[lax.axis_index("pol")], table_ref, sems.at[0]),
        pltpu.make_async_copy(plan_any, plan_ref, sems.at[1]),
    ]
    for copy in copies:
        copy.start()
    copies[1].wait()
    for step in range(STEPS):
        is_own_ref[step] = (plan_ref[step] == lax.axis_index("sta")).astype(jnp.int32)
    copies[0].wait()


def join_kernel(ranges, *refs):
    *pieces, out_ref = refs
    at = 0
    for piece, (first, count) in zip(pieces, ranges):
        out_ref[pl.ds(at, count)] = piece[pl.ds(first, count), pl.ds(0, out_ref.shape[1]), :]
        at += count


def join(*pieces, rows=None):
    pieces = [piece if isinstance(piece, tuple) else (piece, 0, piece.shape[0]) for piece in pieces]
    arrays = [piece[0] for piece in pieces]
    ranges = [piece[1:] for piece in pieces]
    vmem = pl.BlockSpec(memory_space=pltpu.VMEM)
    return pl.pallas_call(
        functools.partial(join_kernel, ranges),
        out_shape=pltpu.VMEM(
            (sum(count for _, count in ranges), rows or arrays[0].shape[1], LANES), arrays[0].dtype
        ),
        in_specs=[vmem] * len(arrays),
        out_specs=vmem,
        compiler_params=pltpu.CompilerParams(vmem_limit_bytes=VMEM_BYTES),
        name="join",
    )(*arrays)


def fetch_from(value, axes, source_of):
    sizes = tuple(lax.axis_size(axis) for axis in axes)
    pairs = []
    for index in np.ndindex(*sizes):
        source = source_of(*index)
        pairs.append((int(np.ravel_multi_index(source, sizes)), int(np.ravel_multi_index(index, sizes))))
    return lax.ppermute(value, axes, pairs)


def exchange(value, axis, distance):
    return fetch_from(value, (axis,), lambda i: (i ^ distance,))


def shards(table, raw_spectra, owner_plan, pair_valid, quality):
    seg, sta, pol = (lax.axis_size(name) for name in ("seg", "sta", "pol"))
    _, stations, _, bins = raw_spectra.shape
    bands = bins // BAND
    fast = sta == 2 and pol == 2 and seg == 4
    blocks = 2 if fast else STEPS
    pairs = stations * stations
    lags = table.shape[3]
    rows = 2 * stations * bands + 16
    sizes = (stations, bands, seg, sta, pol, blocks, lags)

    raw = raw_spectra.reshape(stations, 2, bands, BAND).transpose(0, 2, 1, 3).reshape(-1, BAND)
    vmem = pl.BlockSpec(memory_space=pltpu.VMEM)
    smem = pl.BlockSpec(memory_space=pltpu.SMEM)
    hbm = pl.BlockSpec(memory_space=pltpu.HBM)
    plan = [] if fast else [owner_plan]
    in_hbm = functools.partial(pltpu.with_memory_space_constraint, memory_space=pltpu.HBM)
    own = pl.pallas_call(
        functools.partial(prepare_kernel, (stations, bands, sta, blocks)),
        out_shape=pltpu.VMEM((1, rows, LANES), jnp.bfloat16),
        in_specs=[smem] * len(plan) + [vmem, vmem, vmem],
        out_specs=vmem,
        scratch_shapes=[pltpu.VMEM((2 * stations * bands, LANES), jnp.float32)],
        compiler_params=pltpu.CompilerParams(vmem_limit_bytes=VMEM_BYTES),
        name="prepare",
    )(*plan, in_hbm(raw), in_hbm(jnp.transpose(pair_valid[0])), in_hbm(quality))

    def call(kernel, out_shape, *args, aliases=None, scratch=(), flops=0, moved=0, name=None):
        def spec(x):
            if x is table_const or x is plan_const or x.shape == placed_shape.shape:
                return hbm
            return smem if x.shape == (STEPS,) else vmem

        many = isinstance(out_shape, (list, tuple))
        return pl.pallas_call(
            functools.partial(kernel, sizes),
            out_shape=out_shape,
            in_specs=[spec(x) for x in args],
            out_specs=[spec(x) for x in out_shape] if many else spec(out_shape),
            input_output_aliases=aliases or {},
            scratch_shapes=list(scratch),
            compiler_params=pltpu.CompilerParams(vmem_limit_bytes=VMEM_BYTES),
            cost_estimate=pl.CostEstimate(flops=flops, bytes_accessed=moved, transcendentals=0),
            name=name,
        )(*args)

    f32 = jnp.float32
    placed_shape = jax.ShapeDtypeStruct((STEPS, pairs, lags), f32)
    table_const, plan_const = in_hbm(table), in_hbm(owner_plan)

    quarter = 32 * pairs * 2 * bins * lags

    def fetch(after):
        return call(
            fetch_kernel,
            [
                pltpu.VMEM(table.shape[1:], table.dtype),
                pltpu.SMEM((STEPS,), jnp.int32),
            ],
            table_const, plan_const, after,
            scratch=[pltpu.SMEM((STEPS,), jnp.int32), pltpu.SemaphoreType.DMA((2,))],
            flops=64 * quarter, name="fetch",
        )

    def products(count):
        return [pltpu.VMEM((count * pairs * 8, LANES), f32)] * 2 + [pltpu.VMEM((2, count * pairs, bins), jnp.bfloat16)]

    local_shape = pltpu.VMEM((seg, stations, 2, bands, LANES), f32)
    wide_shape = pltpu.VMEM((seg, blocks * pairs, LANES), f32)
    kept_shape = pltpu.VMEM((pairs, lags), f32)

    if fast:
        bare = rows - 16
        distant = exchange(own, "seg", 2)
        partner_own = exchange(join(own, rows=bare), "sta", 1)
        phase = call(phase_kernel, pltpu.VMEM((2, bands, LANES), f32), own, flops=64 * quarter, name="phase")
        distant, phase = lax.optimization_barrier((distant, phase))
        far = join(own, distant)
        near = exchange(far, "seg", 1)
        across = fetch_from(far, ("seg", "sta"), lambda z, x: (z ^ 1, x ^ 1))
        partner_far = exchange(join(distant, rows=bare), "sta", 1)
        table, is_own = fetch(far)
        near, table = lax.optimization_barrier((near, table))
        mine = join(far, near)
        own_kept, own_sent, local, wide = call(
            own_block_kernel, [kept_shape, kept_shape, local_shape, wide_shape],
            table, phase, mine,
            scratch=products(1), flops=8 * quarter, name="own_block",
        )
        weighted = call(
            weigh_kernel, pltpu.VMEM((stations, stations, seg, 2, bands, LANES), f32),
            wide, local,
            flops=8 * quarter, name="weigh",
        )
        own_got = exchange(own_sent, "pol", 1)
        weighted, partner_own, partner_far = lax.optimization_barrier((weighted, partner_own, partner_far))
        partial = call(
            partner_kernel, [pltpu.VMEM((pairs * 8, LANES), f32)] * 2,
            weighted, partner_own, partner_far,
            name="partner",
        )
        partial, across = lax.optimization_barrier((partial, across))
        kept, sent = call(
            other_block_kernel, [kept_shape, pltpu.VMEM((pairs, lags), jnp.bfloat16)],
            table, weighted, *partial, across,
            scratch=products(1), name="other_block",
        )
        got = exchange(sent, "pol", 1)
        steps, kept = call(
            settle_kernel, [placed_shape, kept_shape], own_kept, own_got, kept,
            scratch=[pltpu.VMEM((pairs, lags), f32), pltpu.SemaphoreType.DMA((STEPS,))],
            name="settle",
        )
        result = call(
            place_kernel, placed_shape, is_own, kept, got, steps,
            aliases={3: 0},
            scratch=[pltpu.VMEM((pairs, lags), f32), pltpu.SemaphoreType.DMA((STEPS,))],
            name="place",
        )
    else:
        mine, distance = own, seg // 2
        while distance:
            mine = join(mine, exchange(mine, "seg", distance))
            distance //= 2
        gathered = lax.all_gather(mine, "sta")
        sources = join(*(gathered[owner_plan[k]] for k in range(STEPS)))
        table, _ = fetch(mine)
        phase = call(phase_kernel, pltpu.VMEM((2, bands, LANES), f32), mine, name="phase")
        kept, sent = call(
            all_blocks_kernel,
            [pltpu.VMEM((blocks * pairs, lags), f32), pltpu.VMEM((blocks * pairs, lags), jnp.bfloat16)],
            table, phase, mine, sources,
            scratch=[local_shape, wide_shape] + products(blocks), flops=blocks * quarter, name="all_blocks",
        )
        result = call(
            combine_kernel, jax.ShapeDtypeStruct((blocks * pairs, lags), f32),
            kept, exchange(sent, "pol", 1), name="combine",
        )
    return result.reshape(STEPS, stations, stations, lags)


def solution(mesh):
    placed = (
        P(("groups", "seg"), "sta", None, "pol"),
        P("groups"),
        P(("groups", "seg"), None, "sta"),
        P(("groups", "seg"), None),
    )

    def whole(raw_spectra, owner_plan, pair_valid, quality):
        seg, pol = mesh.shape["seg"], mesh.shape["pol"]
        bins = raw_spectra.shape[3]
        segments = raw_spectra.shape[0] // mesh.shape["groups"]
        table = lag_table(2 * bins // seg, bins, pol, 1.0 / math.sqrt(bins * segments))
        return jax.shard_map(
            shards,
            mesh=mesh,
            in_specs=(P(),) + placed,
            out_specs=P("groups", None, "sta", ("seg", "pol")),
            check_vma=False,
        )(jnp.asarray(table), raw_spectra, owner_plan, pair_valid, quality)

    return whole
```

```python
import functools
import math

import jax
import jax.numpy as jnp
import numpy as np
from jax import lax
from jax.experimental import pallas as pl
from jax.experimental.pallas import tpu as pltpu
from jax.sharding import PartitionSpec as P

STEPS = 3
BAND = 128
LANES = 128
VMEM_BYTES = 32 * 1024 * 1024


def lag_table(lags, bins, halves, scale):
    bin_index = np.arange(bins, dtype=np.int64)
    lag = 2 * np.arange(lags // 2, dtype=np.int64) + 1
    phase = (bin_index[:, None] * lag[None, :]) % (4 * bins)
    angle = phase * (2.0 * math.pi / (4 * bins))
    factor = np.where(bin_index == 0, 1.0, 2.0)[:, None] * scale
    parts = np.stack([np.cos(angle) * factor, np.sin(angle) * factor])
    parts = parts.reshape(2, halves, bins // halves, lags // 2).transpose(1, 0, 2, 3)
    return parts.astype(jnp.bfloat16)


def turn(count, period):
    count = count % period
    quarter = (count + period // 8) // (period // 4)
    x = (count - quarter * (period // 4)).astype(jnp.float32) * (2.0 * math.pi / period)
    y = x * x
    sine = x * (1.0 + y * (-1 / 6 + y * (1 / 120 + y * (-1 / 5040 + y * (1 / 362880)))))
    cosine = 1.0 + y * (-1 / 2 + y * (1 / 24 + y * (-1 / 720 + y * (1 / 40320))))
    quarter = quarter % 4
    odd = quarter % 2 == 1
    real = jnp.where(odd, sine, cosine)
    imag = jnp.where(odd, cosine, sine)
    real = jnp.where((quarter == 1) | (quarter == 2), -real, real)
    imag = jnp.where(quarter >= 2, -imag, imag)
    return real, imag


def prepare_kernel(sizes, *refs):
    stations, bands, sta, blocks = sizes
    *plan, raw_ref, valid_ref, quality_ref, out_ref, wide = refs
    total = stations * sta
    me = lax.axis_index("sta")
    wide[...] = raw_ref[...].astype(jnp.float32)
    count = stations * bands
    real = wide[pl.ds(0, count, stride=2), :]
    imag = wide[pl.ds(1, count, stride=2), :]
    power = jnp.sum(real * real + imag * imag, axis=1, keepdims=True) * (1.0 / (2 * BAND))
    inverse = lax.rsqrt(power + 1e-06)
    real = (real * inverse).reshape(stations, bands, LANES)
    imag = (imag * inverse).reshape(stations, bands, LANES)
    white = jnp.concatenate([real, imag], axis=1).reshape(2 * count, LANES).astype(jnp.bfloat16)

    flags = jnp.concatenate([valid_ref[...], jnp.broadcast_to(quality_ref[...], (8, total))], axis=0)
    pair = lax.broadcasted_iota(jnp.int32, (total, LANES), 1)
    station = lax.broadcasted_iota(jnp.int32, (total, LANES), 0)
    wanted = [(plan[0][k] if plan else k) * stations + pair // stations for k in range(blocks)]
    wanted.append(me * stations + pair % stations)
    picks = jnp.concatenate([(station == x).astype(jnp.float32) for x in wanted], axis=1)
    picked = jnp.dot(
        flags.astype(jnp.float32).astype(jnp.bfloat16), picks.astype(jnp.bfloat16),
        preferred_element_type=jnp.float32,
    )
    mine = lax.broadcasted_iota(jnp.int32, (stations, LANES), 0) == (
        lax.broadcasted_iota(jnp.int32, (stations, LANES), 1) % stations
    )
    local_flags = picked[stations : stations + 1, blocks * LANES :]
    rows = []
    for k in range(blocks):
        part = picked[:, k * LANES : (k + 1) * LANES]
        valid_row = jnp.sum(jnp.where(mine, part[:stations], 0.0), axis=0, keepdims=True)
        rows.append(valid_row * part[stations : stations + 1] * local_flags)
    rows.append(jnp.zeros((16 - blocks, LANES), jnp.float32))
    weights = jnp.concatenate(rows, axis=0).astype(jnp.bfloat16)
    out_ref[0, pl.ds(0, 2 * count), :] = white
    out_ref[0, pl.ds(2 * count, 16), :] = weights


def spread_weights(sizes, locals_ref, wide):
    stations, bands, seg, sta, pol, blocks, lags = sizes
    pairs = stations * stations
    row_index = lax.broadcasted_iota(jnp.int32, (16, LANES), 0)
    diagonal = lax.broadcasted_iota(jnp.int32, (pairs, LANES), 0) == lax.broadcasted_iota(
        jnp.int32, (pairs, LANES), 1
    )
    ones = jnp.ones((LANES, LANES), jnp.bfloat16)
    for g in range(seg):
        flags = locals_ref[g, pl.ds(2 * stations * bands, 16), :].astype(jnp.float32)
        spread = []
        for n in range(blocks):
            block = lax.axis_index("sta") ^ n if sta == 2 else n
            row = jnp.sum(jnp.where(row_index == block, flags, 0.0), axis=0, keepdims=True)
            spread.append(jnp.where(diagonal, row, 0.0))
        spread = jnp.concatenate(spread, axis=0).astype(jnp.bfloat16)
        wide[g] = jnp.dot(spread, ones, preferred_element_type=jnp.float32)


def middle_phase(sizes):
    stations, bands, seg, sta, pol, blocks, lags = sizes
    row = lax.axis_index("pol") * bands + lax.broadcasted_iota(jnp.int32, (bands, LANES), 0)
    bin_index = row * LANES + lax.broadcasted_iota(jnp.int32, (bands, LANES), 1)
    run = pol * lags
    return turn(bin_index * (2 * run * lax.axis_index("seg") + run - 1), 2 * run * seg)


def turn_locals(sizes, cosine, sine, locals_ref, local):
    stations, bands, seg = sizes[:3]
    for g in range(seg):
        for j in range(stations):
            tile = locals_ref[g, pl.ds(j * 16, 16), :].astype(jnp.float32)
            local[g, j, 0] = tile[:bands] * cosine + tile[bands:] * sine
            local[g, j, 1] = tile[bands:] * cosine - tile[:bands] * sine


def add_products(stations, count, segments, tile_of, weight_of, local_of, real_x, imag_x, before=None):
    def one_source(a, carry):
        tiles = [tile_of(n, a).astype(jnp.float32) for n in range(segments)]
        for j in range(stations):
            pair = a * stations + j
            at = pl.ds(pair * 8 if isinstance(pair, int) else pl.multiple_of(pair * 8, 8), 8)
            real_sum = imag_sum = None
            if before is not None:
                real_sum, imag_sum = before[0][at, :], before[1][at, :]
            for n in range(segments):
                real_src, imag_src = tiles[n][:8], tiles[n][8:]
                if weight_of is not None:
                    weight = jnp.broadcast_to(weight_of(n, pair), (8, LANES))
                    real_src, imag_src = real_src * weight, imag_src * weight
                real_loc, imag_loc = local_of(n, a, j)
                real_term = real_src * real_loc + imag_src * imag_loc
                imag_term = imag_src * real_loc - real_src * imag_loc
                real_sum = real_term if real_sum is None else real_sum + real_term
                imag_sum = imag_term if imag_sum is None else imag_sum + imag_term
            real_x[at, :] = real_sum
            imag_x[at, :] = imag_sum
        return carry

    if count <= 8:
        for a in range(count):
            one_source(a, 0)
    else:
        lax.fori_loop(0, count, one_source, 0, unroll=2)


def pack(rows, bands, real_x, imag_x, packed):
    for band in range(bands):
        at = pl.ds(band * LANES, LANES)
        strided = pl.ds(band, rows, stride=8)
        packed[0, :, at] = real_x[strided, :].astype(jnp.bfloat16)
        packed[1, :, at] = imag_x[strided, :].astype(jnp.bfloat16)


def source_tile(sources_ref, base, count, stations):
    def tile_of(n, a):
        start = a % stations * 16
        start = start if isinstance(a, int) else pl.multiple_of(start, 16)
        return sources_ref[base + a // stations * count + n, pl.ds(start, 16), :]

    return tile_of


def block_sums(sizes, first_block, count, table, wide, local, sources_ref, kept_ref, sent_ref, real_x, imag_x, packed):
    stations, bands, seg = sizes[:3]
    pairs = stations * stations
    add_products(
        stations, count * stations, seg, source_tile(sources_ref, 0, seg, stations),
        lambda n, pair: wide[n, pl.ds(first_block * pairs + pair, 1), :],
        lambda n, a, j: (local[n, j, 0], local[n, j, 1]),
        real_x, imag_x,
    )
    both_sums(sizes, count * pairs, table, kept_ref, sent_ref, real_x, imag_x, packed)


def both_sums(sizes, rows, table, real_x, imag_x, packed):
    pack(rows, sizes[1], real_x, imag_x, packed)
    dot = functools.partial(jnp.dot, preferred_element_type=jnp.float32)
    even, odd = dot(packed[0], table[0]), dot(packed[1], table[1])
    return even + odd, even - odd


def turned_round(sums):
    index = LANES - 1 - lax.broadcasted_iota(jnp.int32, (sums.shape[0], LANES), 1)
    runs = [sums[:, at : at + LANES] for at in reversed(range(0, sums.shape[1], LANES))]
    runs = [jnp.take_along_axis(run, index, axis=1, mode="promise_in_bounds") for run in runs]
    return jnp.concatenate(runs, axis=1)


def block_sums(sizes, first_block, count, table, wide, local, sources_ref, real_x, imag_x, packed):
    stations, bands, seg = sizes[:3]
    pairs = stations * stations
    add_products(
        stations, count * stations, seg, source_tile(sources_ref, 0, seg, stations),
        lambda n, pair: wide[n, pl.ds(first_block * pairs + pair, 1), :],
        lambda n, a, j: (local[n, j, 0], local[n, j, 1]),
        real_x, imag_x,
    )
    return both_sums(sizes, count * pairs, table, real_x, imag_x, packed)


def keep_and_send(before, after, kept_ref, sent_ref):
    first_core = lax.axis_index("pol") == 0
    kept_ref[...] = jnp.where(first_core, before, after)
    sent_ref[...] = jnp.where(first_core, after, before).astype(sent_ref.dtype)


def all_blocks_kernel(sizes, table, phase, mine_ref, sources_ref, kept_ref, sent_ref, local, wide, *scratch):
    spread_weights(sizes, mine_ref, wide)
    turn_locals(sizes, phase[0], phase[1], mine_ref, local)
    before, after = block_sums(sizes, 0, sizes[5], table, wide, local, sources_ref, *scratch)
    keep_and_send(turned_round(before), after, kept_ref, sent_ref)


def own_block_kernel(sizes, table, phase, mine_ref, kept_ref, sent_ref, local_ref, wide_ref, *scratch):
    spread_weights(sizes, mine_ref, wide_ref)
    turn_locals(sizes, phase[0], phase[1], mine_ref, local_ref)
    before, after = block_sums(sizes, 0, 1, table, wide_ref, local_ref, mine_ref, *scratch)
    keep_and_send(turned_round(before), after, kept_ref, sent_ref)


def weigh_kernel(sizes, wide_ref, local_ref, weighted_ref):
    stations, bands, seg = sizes[:3]
    for a in range(stations):
        for j in range(stations):
            pair = stations * stations + a * stations + j
            for g in range(seg):
                weight = jnp.broadcast_to(wide_ref[g, pl.ds(pair, 1), :], (bands, LANES))
                weighted_ref[a, j, g, 0] = local_ref[g, j, 0] * weight
                weighted_ref[a, j, g, 1] = local_ref[g, j, 1] * weight


def partner_kernel(sizes, weighted_ref, first_ref, second_ref, real_x, imag_x):
    stations = sizes[0]
    add_products(
        stations, stations, 2,
        lambda n, a: (first_ref, second_ref)[n][0, pl.ds(a * 16, 16), :],
        None,
        lambda n, a, j: (weighted_ref[a, j, n, 0], weighted_ref[a, j, n, 1]),
        real_x, imag_x,
    )


def other_block_kernel(sizes, table, weighted_ref, real_ref, imag_ref, across_ref, kept_ref, sent_ref, *scratch):
    stations, bands, seg = sizes[:3]
    add_products(
        stations, stations, 2,
        lambda n, a: across_ref[n, pl.ds(a * 16, 16), :],
        None,
        lambda n, a, j: (weighted_ref[a, j, 2 + n, 0], weighted_ref[a, j, 2 + n, 1]),
        *scratch[:2],
        before=(real_ref, imag_ref),
    )
    before, after = both_sums(sizes, stations * stations, table, *scratch)
    first_core = lax.axis_index("pol") == 0

    @pl.when(first_core)
    def _():
        kept_ref[...] = before
        sent_ref[...] = after.astype(sent_ref.dtype)

    @pl.when(jnp.logical_not(first_core))
    def _():
        kept_ref[...] = after
        sent_ref[...] = turned_round(before).astype(sent_ref.dtype)


def settle_kernel(sizes, own_kept_ref, own_got_ref, kept_ref, out_ref, settled_ref, own, sems):
    own[...] = own_kept_ref[...] + own_got_ref[...]
    copies = [pltpu.make_async_copy(own, out_ref.at[step], sems.at[step]) for step in range(STEPS)]
    for copy in copies:
        copy.start()
    kept = kept_ref[...]
    settled_ref[...] = jnp.where(lax.axis_index("pol") == 0, turned_round(kept), kept)
    for copy in copies:
        copy.wait()


def combine_kernel(sizes, kept_ref, got_ref, lags_ref):
    lags_ref[...] = kept_ref[...] + got_ref[...].astype(jnp.float32)


def place_kernel(sizes, is_own_ref, kept_ref, got_ref, steps_ref, out_ref, other, sems):
    del steps_ref
    other[...] = kept_ref[...] + got_ref[...].astype(jnp.float32)
    for act in ("start", "wait"):
        for step in range(STEPS):

            @pl.when(is_own_ref[step] == 0)
            def _():
                getattr(pltpu.make_async_copy(other, out_ref.at[step], sems.at[step]), act)()


def phase_kernel(sizes, after, phase_ref):
    del after
    phase_ref[0], phase_ref[1] = middle_phase(sizes)


def fetch_kernel(sizes, table_hbm, plan_any, after, table_ref, is_own_ref, plan_ref, sems):
    del after
    copies = [
        pltpu.make_async_copy(table_hbm.at[lax.axis_index("pol")], table_ref, sems.at[0]),
        pltpu.make_async_copy(plan_any, plan_ref, sems.at[1]),
    ]
    for copy in copies:
        copy.start()
    copies[1].wait()
    for step in range(STEPS):
        is_own_ref[step] = (plan_ref[step] == lax.axis_index("sta")).astype(jnp.int32)
    copies[0].wait()


def join_kernel(ranges, *refs):
    *pieces, out_ref = refs
    at = 0
    for piece, (first, count) in zip(pieces, ranges):
        out_ref[pl.ds(at, count)] = piece[pl.ds(first, count), pl.ds(0, out_ref.shape[1]), :]
        at += count


def join(*pieces, rows=None):
    pieces = [piece if isinstance(piece, tuple) else (piece, 0, piece.shape[0]) for piece in pieces]
    arrays = [piece[0] for piece in pieces]
    ranges = [piece[1:] for piece in pieces]
    vmem = pl.BlockSpec(memory_space=pltpu.VMEM)
    return pl.pallas_call(
        functools.partial(join_kernel, ranges),
        out_shape=pltpu.VMEM(
            (sum(count for _, count in ranges), rows or arrays[0].shape[1], LANES), arrays[0].dtype
        ),
        in_specs=[vmem] * len(arrays),
        out_specs=vmem,
        compiler_params=pltpu.CompilerParams(vmem_limit_bytes=VMEM_BYTES),
        name="join",
    )(*arrays)


def fetch_from(value, axes, source_of):
    sizes = tuple(lax.axis_size(axis) for axis in axes)
    pairs = []
    for index in np.ndindex(*sizes):
        source = source_of(*index)
        pairs.append((int(np.ravel_multi_index(source, sizes)), int(np.ravel_multi_index(index, sizes))))
    return lax.ppermute(value, axes, pairs)


def exchange(value, axis, distance):
    return fetch_from(value, (axis,), lambda i: (i ^ distance,))


def shards(table, raw_spectra, owner_plan, pair_valid, quality):
    seg, sta, pol = (lax.axis_size(name) for name in ("seg", "sta", "pol"))
    _, stations, _, bins = raw_spectra.shape
    bands = bins // BAND
    fast = sta == 2 and pol == 2 and seg == 4
    blocks = 2 if fast else STEPS
    pairs = stations * stations
    lags = table.shape[3]
    rows = 2 * stations * bands + 16
    sizes = (stations, bands, seg, sta, pol, blocks, lags)

    raw = raw_spectra.reshape(stations, 2, bands, BAND).transpose(0, 2, 1, 3).reshape(-1, BAND)
    vmem = pl.BlockSpec(memory_space=pltpu.VMEM)
    smem = pl.BlockSpec(memory_space=pltpu.SMEM)
    hbm = pl.BlockSpec(memory_space=pltpu.HBM)
    plan = [] if fast else [owner_plan]
    in_hbm = functools.partial(pltpu.with_memory_space_constraint, memory_space=pltpu.HBM)
    own = pl.pallas_call(
        functools.partial(prepare_kernel, (stations, bands, sta, blocks)),
        out_shape=pltpu.VMEM((1, rows, LANES), jnp.bfloat16),
        in_specs=[smem] * len(plan) + [vmem, vmem, vmem],
        out_specs=vmem,
        scratch_shapes=[pltpu.VMEM((2 * stations * bands, LANES), jnp.float32)],
        compiler_params=pltpu.CompilerParams(vmem_limit_bytes=VMEM_BYTES),
        name="prepare",
    )(*plan, in_hbm(raw), in_hbm(jnp.transpose(pair_valid[0])), in_hbm(quality))

    def call(kernel, out_shape, *args, aliases=None, scratch=(), flops=0, moved=0, name=None):
        def spec(x):
            if x is table_const or x is plan_const or x.shape == placed_shape.shape:
                return hbm
            return smem if x.shape == (STEPS,) else vmem

        many = isinstance(out_shape, (list, tuple))
        return pl.pallas_call(
            functools.partial(kernel, sizes),
            out_shape=out_shape,
            in_specs=[spec(x) for x in args],
            out_specs=[spec(x) for x in out_shape] if many else spec(out_shape),
            input_output_aliases=aliases or {},
            scratch_shapes=list(scratch),
            compiler_params=pltpu.CompilerParams(vmem_limit_bytes=VMEM_BYTES),
            cost_estimate=pl.CostEstimate(flops=flops, bytes_accessed=moved, transcendentals=0),
            name=name,
        )(*args)

    f32 = jnp.float32
    placed_shape = jax.ShapeDtypeStruct((STEPS, pairs, lags), f32)
    table_const, plan_const = in_hbm(table), in_hbm(owner_plan)

    quarter = 32 * pairs * 2 * bins * lags

    def fetch(after):
        return call(
            fetch_kernel,
            [
                pltpu.VMEM(table.shape[1:], table.dtype),
                pltpu.SMEM((STEPS,), jnp.int32),
            ],
            table_const, plan_const, after,
            scratch=[pltpu.SMEM((STEPS,), jnp.int32), pltpu.SemaphoreType.DMA((2,))],
            flops=4 * quarter, name="fetch",
        )

    def products(count):
        return [pltpu.VMEM((count * pairs * 8, LANES), f32)] * 2 + [pltpu.VMEM((2, count * pairs, bins), jnp.bfloat16)]

    local_shape = pltpu.VMEM((seg, stations, 2, bands, LANES), f32)
    wide_shape = pltpu.VMEM((seg, blocks * pairs, LANES), f32)
    kept_shape = pltpu.VMEM((pairs, lags), f32)

    if fast:
        bare = rows - 16
        distant = exchange(own, "seg", 2)
        partner_own = exchange(join(own, rows=bare), "sta", 1)
        phase = call(phase_kernel, pltpu.VMEM((2, bands, LANES), f32), own, flops=4 * quarter, name="phase")
        distant, phase = lax.optimization_barrier((distant, phase))
        far = join(own, distant)
        near = exchange(far, "seg", 1)
        across = fetch_from(far, ("seg", "sta"), lambda z, x: (z ^ 1, x ^ 1))
        partner_far = exchange(join(distant, rows=bare), "sta", 1)
        table, is_own = fetch(far)
        near, table = lax.optimization_barrier((near, table))
        mine = join(far, near)
        own_kept, own_sent, local, wide = call(
            own_block_kernel, [kept_shape, kept_shape, local_shape, wide_shape],
            table, phase, mine,
            scratch=products(1), flops=8 * quarter, name="own_block",
        )
        weighted = call(
            weigh_kernel, pltpu.VMEM((stations, stations, seg, 2, bands, LANES), f32),
            wide, local,
            flops=8 * quarter, name="weigh",
        )
        own_got = exchange(own_sent, "pol", 1)
        weighted, partner_own, partner_far = lax.optimization_barrier((weighted, partner_own, partner_far))
        partial = call(
            partner_kernel, [pltpu.VMEM((pairs * 8, LANES), f32)] * 2,
            weighted, partner_own, partner_far,
            name="partner",
        )
        partial, across = lax.optimization_barrier((partial, across))
        kept, sent = call(
            other_block_kernel, [kept_shape, pltpu.VMEM((pairs, lags), jnp.bfloat16)],
            table, weighted, *partial, across,
            scratch=products(1), name="other_block",
        )
        got = exchange(sent, "pol", 1)
        steps, kept = call(
            settle_kernel, [placed_shape, kept_shape], own_kept, own_got, kept,
            scratch=[pltpu.VMEM((pairs, lags), f32), pltpu.SemaphoreType.DMA((STEPS,))],
            name="settle",
        )
        result = call(
            place_kernel, placed_shape, is_own, kept, got, steps,
            aliases={3: 0},
            scratch=[pltpu.VMEM((pairs, lags), f32), pltpu.SemaphoreType.DMA((STEPS,))],
            name="place",
        )
    else:
        mine, distance = own, seg // 2
        while distance:
            mine = join(mine, exchange(mine, "seg", distance))
            distance //= 2
        gathered = lax.all_gather(mine, "sta")
        sources = join(*(gathered[owner_plan[k]] for k in range(STEPS)))
        table, _ = fetch(mine)
        phase = call(phase_kernel, pltpu.VMEM((2, bands, LANES), f32), mine, name="phase")
        kept, sent = call(
            all_blocks_kernel,
            [pltpu.VMEM((blocks * pairs, lags), f32), pltpu.VMEM((blocks * pairs, lags), jnp.bfloat16)],
            table, phase, mine, sources,
            scratch=[local_shape, wide_shape] + products(blocks), flops=blocks * quarter, name="all_blocks",
        )
        result = call(
            combine_kernel, jax.ShapeDtypeStruct((blocks * pairs, lags), f32),
            kept, exchange(sent, "pol", 1), name="combine",
        )
    return result.reshape(STEPS, stations, stations, lags)


def solution(mesh):
    placed = (
        P(("groups", "seg"), "sta", None, "pol"),
        P("groups"),
        P(("groups", "seg"), None, "sta"),
        P(("groups", "seg"), None),
    )

    def whole(raw_spectra, owner_plan, pair_valid, quality):
        seg, pol = mesh.shape["seg"], mesh.shape["pol"]
        bins = raw_spectra.shape[3]
        segments = raw_spectra.shape[0] // mesh.shape["groups"]
        table = lag_table(2 * bins // seg, bins, pol, 1.0 / math.sqrt(bins * segments))
        return jax.shard_map(
            shards,
            mesh=mesh,
            in_specs=(P(),) + placed,
            out_specs=P("groups", None, "sta", ("seg", "pol")),
            check_vma=False,
        )(jnp.asarray(table), raw_spectra, owner_plan, pair_valid, quality)

    return whole
```

```python
import functools
import math

import jax
import jax.numpy as jnp
import numpy as np
from jax import lax
from jax.experimental import pallas as pl
from jax.experimental.pallas import tpu as pltpu
from jax.sharding import PartitionSpec as P

STEPS = 3
BAND = 128
LANES = 128
VMEM_BYTES = 32 * 1024 * 1024


def lag_table(lags, bins, halves, scale):
    bin_index = np.arange(bins, dtype=np.int64)
    lag = 2 * np.arange(lags // 2, dtype=np.int64) + 1
    phase = (bin_index[:, None] * lag[None, :]) % (4 * bins)
    angle = phase * (2.0 * math.pi / (4 * bins))
    factor = np.where(bin_index == 0, 1.0, 2.0)[:, None] * scale
    parts = np.stack([np.cos(angle) * factor, np.sin(angle) * factor])
    parts = parts.reshape(2, halves, bins // halves, lags // 2).transpose(1, 0, 2, 3)
    return parts.astype(jnp.bfloat16)


def turn(count, period):
    count = count % period
    quarter = (count + period // 8) // (period // 4)
    x = (count - quarter * (period // 4)).astype(jnp.float32) * (2.0 * math.pi / period)
    y = x * x
    sine = x * (1.0 + y * (-1 / 6 + y * (1 / 120 + y * (-1 / 5040 + y * (1 / 362880)))))
    cosine = 1.0 + y * (-1 / 2 + y * (1 / 24 + y * (-1 / 720 + y * (1 / 40320))))
    quarter = quarter % 4
    odd = quarter % 2 == 1
    real = jnp.where(odd, sine, cosine)
    imag = jnp.where(odd, cosine, sine)
    real = jnp.where((quarter == 1) | (quarter == 2), -real, real)
    imag = jnp.where(quarter >= 2, -imag, imag)
    return real, imag


def prepare_kernel(sizes, *refs):
    stations, bands, sta, blocks = sizes
    *plan, raw_ref, valid_ref, quality_ref, out_ref, wide = refs
    total = stations * sta
    me = lax.axis_index("sta")
    wide[...] = raw_ref[...].astype(jnp.float32)
    count = stations * bands
    real = wide[pl.ds(0, count, stride=2), :]
    imag = wide[pl.ds(1, count, stride=2), :]
    power = jnp.sum(real * real + imag * imag, axis=1, keepdims=True) * (1.0 / (2 * BAND))
    inverse = lax.rsqrt(power + 1e-06)
    real = (real * inverse).reshape(stations, bands, LANES)
    imag = (imag * inverse).reshape(stations, bands, LANES)
    white = jnp.concatenate([real, imag], axis=1).reshape(2 * count, LANES).astype(jnp.bfloat16)

    flags = jnp.concatenate([valid_ref[...], jnp.broadcast_to(quality_ref[...], (8, total))], axis=0)
    pair = lax.broadcasted_iota(jnp.int32, (total, LANES), 1)
    station = lax.broadcasted_iota(jnp.int32, (total, LANES), 0)
    wanted = [(plan[0][k] if plan else k) * stations + pair // stations for k in range(blocks)]
    wanted.append(me * stations + pair % stations)
    picks = jnp.concatenate([(station == x).astype(jnp.float32) for x in wanted], axis=1)
    picked = jnp.dot(
        flags.astype(jnp.float32).astype(jnp.bfloat16), picks.astype(jnp.bfloat16),
        preferred_element_type=jnp.float32,
    )
    mine = lax.broadcasted_iota(jnp.int32, (stations, LANES), 0) == (
        lax.broadcasted_iota(jnp.int32, (stations, LANES), 1) % stations
    )
    local_flags = picked[stations : stations + 1, blocks * LANES :]
    rows = []
    for k in range(blocks):
        part = picked[:, k * LANES : (k + 1) * LANES]
        valid_row = jnp.sum(jnp.where(mine, part[:stations], 0.0), axis=0, keepdims=True)
        rows.append(valid_row * part[stations : stations + 1] * local_flags)
    rows.append(jnp.zeros((16 - blocks, LANES), jnp.float32))
    weights = jnp.concatenate(rows, axis=0).astype(jnp.bfloat16)
    out_ref[0, pl.ds(0, 2 * count), :] = white
    out_ref[0, pl.ds(2 * count, 16), :] = weights


def spread_weights(sizes, locals_ref, wide):
    stations, bands, seg, sta, pol, blocks, lags = sizes
    pairs = stations * stations
    row_index = lax.broadcasted_iota(jnp.int32, (16, LANES), 0)
    diagonal = lax.broadcasted_iota(jnp.int32, (pairs, LANES), 0) == lax.broadcasted_iota(
        jnp.int32, (pairs, LANES), 1
    )
    ones = jnp.ones((LANES, LANES), jnp.bfloat16)
    for g in range(seg):
        flags = locals_ref[g, pl.ds(2 * stations * bands, 16), :].astype(jnp.float32)
        spread = []
        for n in range(blocks):
            block = lax.axis_index("sta") ^ n if sta == 2 else n
            row = jnp.sum(jnp.where(row_index == block, flags, 0.0), axis=0, keepdims=True)
            spread.append(jnp.where(diagonal, row, 0.0))
        spread = jnp.concatenate(spread, axis=0).astype(jnp.bfloat16)
        wide[g] = jnp.dot(spread, ones, preferred_element_type=jnp.float32)


def middle_phase(sizes):
    stations, bands, seg, sta, pol, blocks, lags = sizes
    row = lax.axis_index("pol") * bands + lax.broadcasted_iota(jnp.int32, (bands, LANES), 0)
    bin_index = row * LANES + lax.broadcasted_iota(jnp.int32, (bands, LANES), 1)
    run = pol * lags
    return turn(bin_index * (2 * run * lax.axis_index("seg") + run - 1), 2 * run * seg)


def turn_locals(sizes, cosine, sine, locals_ref, local):
    stations, bands, seg = sizes[:3]
    for g in range(seg):
        for j in range(stations):
            tile = locals_ref[g, pl.ds(j * 16, 16), :].astype(jnp.float32)
            local[g, j, 0] = tile[:bands] * cosine + tile[bands:] * sine
            local[g, j, 1] = tile[bands:] * cosine - tile[:bands] * sine


def add_products(stations, count, segments, tile_of, weight_of, local_of, real_x, imag_x, before=None):
    def one_source(a, carry):
        tiles = [tile_of(n, a).astype(jnp.float32) for n in range(segments)]
        for j in range(stations):
            pair = a * stations + j
            at = pl.ds(pair * 8 if isinstance(pair, int) else pl.multiple_of(pair * 8, 8), 8)
            real_sum = imag_sum = None
            if before is not None:
                real_sum, imag_sum = before[0][at, :], before[1][at, :]
            for n in range(segments):
                real_src, imag_src = tiles[n][:8], tiles[n][8:]
                if weight_of is not None:
                    weight = jnp.broadcast_to(weight_of(n, pair), (8, LANES))
                    real_src, imag_src = real_src * weight, imag_src * weight
                real_loc, imag_loc = local_of(n, a, j)
                real_term = real_src * real_loc + imag_src * imag_loc
                imag_term = imag_src * real_loc - real_src * imag_loc
                real_sum = real_term if real_sum is None else real_sum + real_term
                imag_sum = imag_term if imag_sum is None else imag_sum + imag_term
            real_x[at, :] = real_sum
            imag_x[at, :] = imag_sum
        return carry

    if count <= 8:
        for a in range(count):
            one_source(a, 0)
    else:
        lax.fori_loop(0, count, one_source, 0, unroll=2)


def pack(rows, bands, real_x, imag_x, packed):
    for band in range(bands):
        at = pl.ds(band * LANES, LANES)
        strided = pl.ds(band, rows, stride=8)
        packed[0, :, at] = real_x[strided, :].astype(jnp.bfloat16)
        packed[1, :, at] = imag_x[strided, :].astype(jnp.bfloat16)


def source_tile(sources_ref, base, count, stations):
    def tile_of(n, a):
        start = a % stations * 16
        start = start if isinstance(a, int) else pl.multiple_of(start, 16)
        return sources_ref[base + a // stations * count + n, pl.ds(start, 16), :]

    return tile_of


def block_sums(sizes, first_block, count, table, wide, local, sources_ref, kept_ref, sent_ref, real_x, imag_x, packed):
    stations, bands, seg = sizes[:3]
    pairs = stations * stations
    add_products(
        stations, count * stations, seg, source_tile(sources_ref, 0, seg, stations),
        lambda n, pair: wide[n, pl.ds(first_block * pairs + pair, 1), :],
        lambda n, a, j: (local[n, j, 0], local[n, j, 1]),
        real_x, imag_x,
    )
    both_sums(sizes, count * pairs, table, kept_ref, sent_ref, real_x, imag_x, packed)


def both_sums(sizes, rows, table, real_x, imag_x, packed):
    pack(rows, sizes[1], real_x, imag_x, packed)
    dot = functools.partial(jnp.dot, preferred_element_type=jnp.float32)
    even, odd = dot(packed[0], table[0]), dot(packed[1], table[1])
    return even + odd, even - odd


def turned_round(sums):
    index = LANES - 1 - lax.broadcasted_iota(jnp.int32, (sums.shape[0], LANES), 1)
    runs = [sums[:, at : at + LANES] for at in reversed(range(0, sums.shape[1], LANES))]
    runs = [jnp.take_along_axis(run, index, axis=1, mode="promise_in_bounds") for run in runs]
    return jnp.concatenate(runs, axis=1)


def block_sums(sizes, first_block, count, table, wide, local, sources_ref, real_x, imag_x, packed):
    stations, bands, seg = sizes[:3]
    pairs = stations * stations
    add_products(
        stations, count * stations, seg, source_tile(sources_ref, 0, seg, stations),
        lambda n, pair: wide[n, pl.ds(first_block * pairs + pair, 1), :],
        lambda n, a, j: (local[n, j, 0], local[n, j, 1]),
        real_x, imag_x,
    )
    return both_sums(sizes, count * pairs, table, real_x, imag_x, packed)


def keep_and_send(before, after, kept_ref, sent_ref):
    first_core = lax.axis_index("pol") == 0
    kept_ref[...] = jnp.where(first_core, before, after)
    sent_ref[...] = jnp.where(first_core, after, before).astype(sent_ref.dtype)


def all_blocks_kernel(sizes, table, phase, mine_ref, sources_ref, kept_ref, sent_ref, local, wide, *scratch):
    spread_weights(sizes, mine_ref, wide)
    turn_locals(sizes, phase[0], phase[1], mine_ref, local)
    before, after = block_sums(sizes, 0, sizes[5], table, wide, local, sources_ref, *scratch)
    keep_and_send(turned_round(before), after, kept_ref, sent_ref)


def own_block_kernel(sizes, table, phase, mine_ref, kept_ref, sent_ref, local_ref, wide_ref, *scratch):
    spread_weights(sizes, mine_ref, wide_ref)
    turn_locals(sizes, phase[0], phase[1], mine_ref, local_ref)
    before, after = block_sums(sizes, 0, 1, table, wide_ref, local_ref, mine_ref, *scratch)
    keep_and_send(turned_round(before), after, kept_ref, sent_ref)


def weigh_kernel(sizes, wide_ref, local_ref, weighted_ref):
    stations, bands, seg = sizes[:3]
    for a in range(stations):
        for j in range(stations):
            pair = stations * stations + a * stations + j
            for g in range(seg):
                weight = jnp.broadcast_to(wide_ref[g, pl.ds(pair, 1), :], (bands, LANES))
                weighted_ref[a, j, g, 0] = local_ref[g, j, 0] * weight
                weighted_ref[a, j, g, 1] = local_ref[g, j, 1] * weight


def across_kernel(sizes, weighted_ref, across_ref, real_x, imag_x):
    stations = sizes[0]
    add_products(
        stations, stations, 2,
        lambda n, a: across_ref[n, pl.ds(a * 16, 16), :],
        None,
        lambda n, a, j: (weighted_ref[a, j, 2 + n, 0], weighted_ref[a, j, 2 + n, 1]),
        real_x, imag_x,
    )


def other_block_kernel(
    sizes, table, weighted_ref, real_ref, imag_ref, first_ref, second_ref, kept_ref, sent_ref, *scratch
):
    stations, bands, seg = sizes[:3]
    add_products(
        stations, stations, 2,
        lambda n, a: (first_ref, second_ref)[n][0, pl.ds(a * 16, 16), :],
        None,
        lambda n, a, j: (weighted_ref[a, j, n, 0], weighted_ref[a, j, n, 1]),
        *scratch[:2],
        before=(real_ref, imag_ref),
    )
    before, after = both_sums(sizes, stations * stations, table, *scratch)
    first_core = lax.axis_index("pol") == 0

    @pl.when(first_core)
    def _():
        kept_ref[...] = before
        sent_ref[...] = after.astype(sent_ref.dtype)

    @pl.when(jnp.logical_not(first_core))
    def _():
        kept_ref[...] = after
        sent_ref[...] = turned_round(before).astype(sent_ref.dtype)


def settle_kernel(sizes, own_kept_ref, own_got_ref, kept_ref, out_ref, settled_ref, own, sems):
    own[...] = own_kept_ref[...] + own_got_ref[...]
    copies = [pltpu.make_async_copy(own, out_ref.at[step], sems.at[step]) for step in range(STEPS)]
    for copy in copies:
        copy.start()
    kept = kept_ref[...]
    settled_ref[...] = jnp.where(lax.axis_index("pol") == 0, turned_round(kept), kept)
    for copy in copies:
        copy.wait()


def combine_kernel(sizes, kept_ref, got_ref, lags_ref):
    lags_ref[...] = kept_ref[...] + got_ref[...].astype(jnp.float32)


def place_kernel(sizes, is_own_ref, kept_ref, got_ref, steps_ref, out_ref, other, sems):
    del steps_ref
    other[...] = kept_ref[...] + got_ref[...].astype(jnp.float32)
    for act in ("start", "wait"):
        for step in range(STEPS):

            @pl.when(is_own_ref[step] == 0)
            def _():
                getattr(pltpu.make_async_copy(other, out_ref.at[step], sems.at[step]), act)()


def phase_kernel(sizes, after, phase_ref):
    del after
    phase_ref[0], phase_ref[1] = middle_phase(sizes)


def fetch_kernel(sizes, table_hbm, plan_any, after, table_ref, is_own_ref, plan_ref, sems):
    del after
    copies = [
        pltpu.make_async_copy(table_hbm.at[lax.axis_index("pol")], table_ref, sems.at[0]),
        pltpu.make_async_copy(plan_any, plan_ref, sems.at[1]),
    ]
    for copy in copies:
        copy.start()
    copies[1].wait()
    for step in range(STEPS):
        is_own_ref[step] = (plan_ref[step] == lax.axis_index("sta")).astype(jnp.int32)
    copies[0].wait()


def join_kernel(ranges, *refs):
    *pieces, out_ref = refs
    at = 0
    for piece, (first, count) in zip(pieces, ranges):
        out_ref[pl.ds(at, count)] = piece[pl.ds(first, count), pl.ds(0, out_ref.shape[1]), :]
        at += count


def join(*pieces, rows=None, flops=0):
    pieces = [piece if isinstance(piece, tuple) else (piece, 0, piece.shape[0]) for piece in pieces]
    arrays = [piece[0] for piece in pieces]
    ranges = [piece[1:] for piece in pieces]
    vmem = pl.BlockSpec(memory_space=pltpu.VMEM)
    return pl.pallas_call(
        functools.partial(join_kernel, ranges),
        out_shape=pltpu.VMEM(
            (sum(count for _, count in ranges), rows or arrays[0].shape[1], LANES), arrays[0].dtype
        ),
        in_specs=[vmem] * len(arrays),
        out_specs=vmem,
        compiler_params=pltpu.CompilerParams(vmem_limit_bytes=VMEM_BYTES),
        cost_estimate=pl.CostEstimate(flops=flops, bytes_accessed=0, transcendentals=0),
        name="join",
    )(*arrays)


def fetch_from(value, axes, source_of):
    sizes = tuple(lax.axis_size(axis) for axis in axes)
    pairs = []
    for index in np.ndindex(*sizes):
        source = source_of(*index)
        pairs.append((int(np.ravel_multi_index(source, sizes)), int(np.ravel_multi_index(index, sizes))))
    return lax.ppermute(value, axes, pairs)


def exchange(value, axis, distance):
    return fetch_from(value, (axis,), lambda i: (i ^ distance,))


def shards(table, raw_spectra, owner_plan, pair_valid, quality):
    seg, sta, pol = (lax.axis_size(name) for name in ("seg", "sta", "pol"))
    _, stations, _, bins = raw_spectra.shape
    bands = bins // BAND
    fast = sta == 2 and pol == 2 and seg == 4
    blocks = 2 if fast else STEPS
    pairs = stations * stations
    lags = table.shape[3]
    rows = 2 * stations * bands + 16
    sizes = (stations, bands, seg, sta, pol, blocks, lags)

    raw = raw_spectra.reshape(stations, 2, bands, BAND).transpose(0, 2, 1, 3).reshape(-1, BAND)
    vmem = pl.BlockSpec(memory_space=pltpu.VMEM)
    smem = pl.BlockSpec(memory_space=pltpu.SMEM)
    hbm = pl.BlockSpec(memory_space=pltpu.HBM)
    plan = [] if fast else [owner_plan]
    in_hbm = functools.partial(pltpu.with_memory_space_constraint, memory_space=pltpu.HBM)
    own = pl.pallas_call(
        functools.partial(prepare_kernel, (stations, bands, sta, blocks)),
        out_shape=pltpu.VMEM((1, rows, LANES), jnp.bfloat16),
        in_specs=[smem] * len(plan) + [vmem, vmem, vmem],
        out_specs=vmem,
        scratch_shapes=[pltpu.VMEM((2 * stations * bands, LANES), jnp.float32)],
        compiler_params=pltpu.CompilerParams(vmem_limit_bytes=VMEM_BYTES),
        name="prepare",
    )(*plan, in_hbm(raw), in_hbm(jnp.transpose(pair_valid[0])), in_hbm(quality))

    def call(kernel, out_shape, *args, aliases=None, scratch=(), flops=0, moved=0, name=None):
        def spec(x):
            if x is table_const or x is plan_const or x.shape == placed_shape.shape:
                return hbm
            return smem if x.shape == (STEPS,) else vmem

        many = isinstance(out_shape, (list, tuple))
        return pl.pallas_call(
            functools.partial(kernel, sizes),
            out_shape=out_shape,
            in_specs=[spec(x) for x in args],
            out_specs=[spec(x) for x in out_shape] if many else spec(out_shape),
            input_output_aliases=aliases or {},
            scratch_shapes=list(scratch),
            compiler_params=pltpu.CompilerParams(vmem_limit_bytes=VMEM_BYTES),
            cost_estimate=pl.CostEstimate(flops=flops, bytes_accessed=moved, transcendentals=0),
            name=name,
        )(*args)

    f32 = jnp.float32
    placed_shape = jax.ShapeDtypeStruct((STEPS, pairs, lags), f32)
    table_const, plan_const = in_hbm(table), in_hbm(owner_plan)

    quarter = 32 * pairs * 2 * bins * lags

    def fetch(after):
        return call(
            fetch_kernel,
            [
                pltpu.VMEM(table.shape[1:], table.dtype),
                pltpu.SMEM((STEPS,), jnp.int32),
            ],
            table_const, plan_const, after,
            scratch=[pltpu.SMEM((STEPS,), jnp.int32), pltpu.SemaphoreType.DMA((2,))],
            name="fetch",
        )

    def products(count):
        return [pltpu.VMEM((count * pairs * 8, LANES), f32)] * 2 + [pltpu.VMEM((2, count * pairs, bins), jnp.bfloat16)]

    local_shape = pltpu.VMEM((seg, stations, 2, bands, LANES), f32)
    wide_shape = pltpu.VMEM((seg, blocks * pairs, LANES), f32)
    kept_shape = pltpu.VMEM((pairs, lags), f32)

    if fast:
        bare = rows - 16
        distant = exchange(own, "seg", 2)
        partner_own = exchange(join(own, rows=bare), "sta", 1)
        phase = call(phase_kernel, pltpu.VMEM((2, bands, LANES), f32), own, flops=4 * quarter, name="phase")
        distant, phase = lax.optimization_barrier((distant, phase))
        far = join(own, distant)
        near = exchange(far, "seg", 1)
        across = fetch_from(
            join(far, rows=bare, flops=4 * quarter), ("seg", "sta"), lambda z, x: (z ^ 1, x ^ 1)
        )
        partner_far = exchange(join(distant, rows=bare), "sta", 1)
        table, is_own = fetch(far)
        near, table = lax.optimization_barrier((near, table))
        mine = join(far, near)
        own_kept, own_sent, local, wide = call(
            own_block_kernel, [kept_shape, kept_shape, local_shape, wide_shape],
            table, phase, mine,
            scratch=products(1), flops=8 * quarter, name="own_block",
        )
        weighted = call(
            weigh_kernel, pltpu.VMEM((stations, stations, seg, 2, bands, LANES), f32),
            wide, local,
            flops=8 * quarter, name="weigh",
        )
        own_got = exchange(own_sent, "pol", 1)
        weighted, across = lax.optimization_barrier((weighted, across))
        partial = call(
            across_kernel, [pltpu.VMEM((pairs * 8, LANES), f32)] * 2,
            weighted, across,
            name="across",
        )
        partial, partner_own, partner_far = lax.optimization_barrier((partial, partner_own, partner_far))
        kept, sent = call(
            other_block_kernel, [kept_shape, pltpu.VMEM((pairs, lags), jnp.bfloat16)],
            table, weighted, *partial, partner_own, partner_far,
            scratch=products(1), name="other_block",
        )
        got = exchange(sent, "pol", 1)
        steps, kept = call(
            settle_kernel, [placed_shape, kept_shape], own_kept, own_got, kept,
            scratch=[pltpu.VMEM((pairs, lags), f32), pltpu.SemaphoreType.DMA((STEPS,))],
            name="settle",
        )
        result = call(
            place_kernel, placed_shape, is_own, kept, got, steps,
            aliases={3: 0},
            scratch=[pltpu.VMEM((pairs, lags), f32), pltpu.SemaphoreType.DMA((STEPS,))],
            name="place",
        )
    else:
        mine, distance = own, seg // 2
        while distance:
            mine = join(mine, exchange(mine, "seg", distance))
            distance //= 2
        gathered = lax.all_gather(mine, "sta")
        sources = join(*(gathered[owner_plan[k]] for k in range(STEPS)))
        table, _ = fetch(mine)
        phase = call(phase_kernel, pltpu.VMEM((2, bands, LANES), f32), mine, name="phase")
        kept, sent = call(
            all_blocks_kernel,
            [pltpu.VMEM((blocks * pairs, lags), f32), pltpu.VMEM((blocks * pairs, lags), jnp.bfloat16)],
            table, phase, mine, sources,
            scratch=[local_shape, wide_shape] + products(blocks), flops=blocks * quarter, name="all_blocks",
        )
        result = call(
            combine_kernel, jax.ShapeDtypeStruct((blocks * pairs, lags), f32),
            kept, exchange(sent, "pol", 1), name="combine",
        )
    return result.reshape(STEPS, stations, stations, lags)


def solution(mesh):
    placed = (
        P(("groups", "seg"), "sta", None, "pol"),
        P("groups"),
        P(("groups", "seg"), None, "sta"),
        P(("groups", "seg"), None),
    )

    def whole(raw_spectra, owner_plan, pair_valid, quality):
        seg, pol = mesh.shape["seg"], mesh.shape["pol"]
        bins = raw_spectra.shape[3]
        segments = raw_spectra.shape[0] // mesh.shape["groups"]
        table = lag_table(2 * bins // seg, bins, pol, 1.0 / math.sqrt(bins * segments))
        return jax.shard_map(
            shards,
            mesh=mesh,
            in_specs=(P(),) + placed,
            out_specs=P("groups", None, "sta", ("seg", "pol")),
            check_vma=False,
        )(jnp.asarray(table), raw_spectra, owner_plan, pair_valid, quality)

    return whole
```

```python
import functools
import math

import jax
import jax.numpy as jnp
import numpy as np
from jax import lax
from jax.experimental import pallas as pl
from jax.experimental.pallas import tpu as pltpu
from jax.sharding import PartitionSpec as P

STEPS = 3
BAND = 128
LANES = 128
VMEM_BYTES = 32 * 1024 * 1024


def lag_table(lags, bins, halves, scale):
    bin_index = np.arange(bins, dtype=np.int64)
    lag = 2 * np.arange(lags // 2, dtype=np.int64) + 1
    phase = (bin_index[:, None] * lag[None, :]) % (4 * bins)
    angle = phase * (2.0 * math.pi / (4 * bins))
    factor = np.where(bin_index == 0, 1.0, 2.0)[:, None] * scale
    parts = np.stack([np.cos(angle) * factor, np.sin(angle) * factor])
    parts = parts.reshape(2, halves, bins // halves, lags // 2).transpose(1, 0, 2, 3)
    return parts.astype(jnp.bfloat16)


def turn(count, period):
    count = count % period
    quarter = (count + period // 8) // (period // 4)
    x = (count - quarter * (period // 4)).astype(jnp.float32) * (2.0 * math.pi / period)
    y = x * x
    sine = x * (1.0 + y * (-1 / 6 + y * (1 / 120 + y * (-1 / 5040 + y * (1 / 362880)))))
    cosine = 1.0 + y * (-1 / 2 + y * (1 / 24 + y * (-1 / 720 + y * (1 / 40320))))
    quarter = quarter % 4
    odd = quarter % 2 == 1
    real = jnp.where(odd, sine, cosine)
    imag = jnp.where(odd, cosine, sine)
    real = jnp.where((quarter == 1) | (quarter == 2), -real, real)
    imag = jnp.where(quarter >= 2, -imag, imag)
    return real, imag


def prepare_kernel(sizes, *refs):
    stations, bands, sta, blocks = sizes
    *plan, raw_ref, valid_ref, quality_ref, out_ref, wide = refs
    total = stations * sta
    me = lax.axis_index("sta")
    wide[...] = raw_ref[...].astype(jnp.float32)
    count = stations * bands
    real = wide[pl.ds(0, count, stride=2), :]
    imag = wide[pl.ds(1, count, stride=2), :]
    power = jnp.sum(real * real + imag * imag, axis=1, keepdims=True) * (1.0 / (2 * BAND))
    inverse = lax.rsqrt(power + 1e-06)
    real = (real * inverse).reshape(stations, bands, LANES)
    imag = (imag * inverse).reshape(stations, bands, LANES)
    white = jnp.concatenate([real, imag], axis=1).reshape(2 * count, LANES).astype(jnp.bfloat16)

    flags = jnp.concatenate([valid_ref[...], jnp.broadcast_to(quality_ref[...], (8, total))], axis=0)
    pair = lax.broadcasted_iota(jnp.int32, (total, LANES), 1)
    station = lax.broadcasted_iota(jnp.int32, (total, LANES), 0)
    wanted = [(plan[0][k] if plan else k) * stations + pair // stations for k in range(blocks)]
    wanted.append(me * stations + pair % stations)
    picks = jnp.concatenate([(station == x).astype(jnp.float32) for x in wanted], axis=1)
    picked = jnp.dot(
        flags.astype(jnp.float32).astype(jnp.bfloat16), picks.astype(jnp.bfloat16),
        preferred_element_type=jnp.float32,
    )
    mine = lax.broadcasted_iota(jnp.int32, (stations, LANES), 0) == (
        lax.broadcasted_iota(jnp.int32, (stations, LANES), 1) % stations
    )
    local_flags = picked[stations : stations + 1, blocks * LANES :]
    rows = []
    for k in range(blocks):
        part = picked[:, k * LANES : (k + 1) * LANES]
        valid_row = jnp.sum(jnp.where(mine, part[:stations], 0.0), axis=0, keepdims=True)
        rows.append(valid_row * part[stations : stations + 1] * local_flags)
    rows.append(jnp.zeros((16 - blocks, LANES), jnp.float32))
    weights = jnp.concatenate(rows, axis=0).astype(jnp.bfloat16)
    out_ref[0, pl.ds(0, 2 * count), :] = white
    out_ref[0, pl.ds(2 * count, 16), :] = weights


def spread_weights(sizes, locals_ref, wide):
    stations, bands, seg, sta, pol, blocks, lags = sizes
    pairs = stations * stations
    row_index = lax.broadcasted_iota(jnp.int32, (16, LANES), 0)
    diagonal = lax.broadcasted_iota(jnp.int32, (pairs, LANES), 0) == lax.broadcasted_iota(
        jnp.int32, (pairs, LANES), 1
    )
    ones = jnp.ones((LANES, LANES), jnp.bfloat16)
    for g in range(seg):
        flags = locals_ref[g, pl.ds(2 * stations * bands, 16), :].astype(jnp.float32)
        spread = []
        for n in range(blocks):
            block = lax.axis_index("sta") ^ n if sta == 2 else n
            row = jnp.sum(jnp.where(row_index == block, flags, 0.0), axis=0, keepdims=True)
            spread.append(jnp.where(diagonal, row, 0.0))
        spread = jnp.concatenate(spread, axis=0).astype(jnp.bfloat16)
        wide[g] = jnp.dot(spread, ones, preferred_element_type=jnp.float32)


def middle_phase(sizes):
    stations, bands, seg, sta, pol, blocks, lags = sizes
    row = lax.axis_index("pol") * bands + lax.broadcasted_iota(jnp.int32, (bands, LANES), 0)
    bin_index = row * LANES + lax.broadcasted_iota(jnp.int32, (bands, LANES), 1)
    run = pol * lags
    return turn(bin_index * (2 * run * lax.axis_index("seg") + run - 1), 2 * run * seg)


def turn_locals(sizes, cosine, sine, locals_ref, local):
    stations, bands, seg = sizes[:3]
    for g in range(seg):
        for j in range(stations):
            tile = locals_ref[g, pl.ds(j * 16, 16), :].astype(jnp.float32)
            local[g, j, 0] = tile[:bands] * cosine + tile[bands:] * sine
            local[g, j, 1] = tile[bands:] * cosine - tile[:bands] * sine


def add_products(stations, count, segments, tile_of, weight_of, local_of, real_x, imag_x, before=None):
    def one_source(a, carry):
        tiles = [tile_of(n, a).astype(jnp.float32) for n in range(segments)]
        for j in range(stations):
            pair = a * stations + j
            at = pl.ds(pair * 8 if isinstance(pair, int) else pl.multiple_of(pair * 8, 8), 8)
            real_sum = imag_sum = None
            if before is not None:
                real_sum, imag_sum = before[0][at, :], before[1][at, :]
            for n in range(segments):
                real_src, imag_src = tiles[n][:8], tiles[n][8:]
                if weight_of is not None:
                    weight = jnp.broadcast_to(weight_of(n, pair), (8, LANES))
                    real_src, imag_src = real_src * weight, imag_src * weight
                real_loc, imag_loc = local_of(n, a, j)
                real_term = real_src * real_loc + imag_src * imag_loc
                imag_term = imag_src * real_loc - real_src * imag_loc
                real_sum = real_term if real_sum is None else real_sum + real_term
                imag_sum = imag_term if imag_sum is None else imag_sum + imag_term
            real_x[at, :] = real_sum
            imag_x[at, :] = imag_sum
        return carry

    if count <= 8:
        for a in range(count):
            one_source(a, 0)
    else:
        lax.fori_loop(0, count, one_source, 0, unroll=2)


def pack(rows, bands, real_x, imag_x, packed):
    for band in range(bands):
        at = pl.ds(band * LANES, LANES)
        strided = pl.ds(band, rows, stride=8)
        packed[0, :, at] = real_x[strided, :].astype(jnp.bfloat16)
        packed[1, :, at] = imag_x[strided, :].astype(jnp.bfloat16)


def source_tile(sources_ref, base, count, stations):
    def tile_of(n, a):
        start = a % stations * 16
        start = start if isinstance(a, int) else pl.multiple_of(start, 16)
        return sources_ref[base + a // stations * count + n, pl.ds(start, 16), :]

    return tile_of


def block_sums(sizes, first_block, count, table, wide, local, sources_ref, kept_ref, sent_ref, real_x, imag_x, packed):
    stations, bands, seg = sizes[:3]
    pairs = stations * stations
    add_products(
        stations, count * stations, seg, source_tile(sources_ref, 0, seg, stations),
        lambda n, pair: wide[n, pl.ds(first_block * pairs + pair, 1), :],
        lambda n, a, j: (local[n, j, 0], local[n, j, 1]),
        real_x, imag_x,
    )
    both_sums(sizes, count * pairs, table, kept_ref, sent_ref, real_x, imag_x, packed)


def both_sums(sizes, rows, table, real_x, imag_x, packed):
    pack(rows, sizes[1], real_x, imag_x, packed)
    dot = functools.partial(jnp.dot, preferred_element_type=jnp.float32)
    even, odd = dot(packed[0], table[0]), dot(packed[1], table[1])
    return even + odd, even - odd


def turned_round(sums):
    index = LANES - 1 - lax.broadcasted_iota(jnp.int32, (sums.shape[0], LANES), 1)
    runs = [sums[:, at : at + LANES] for at in reversed(range(0, sums.shape[1], LANES))]
    runs = [jnp.take_along_axis(run, index, axis=1, mode="promise_in_bounds") for run in runs]
    return jnp.concatenate(runs, axis=1)


def block_sums(sizes, first_block, count, table, wide, local, sources_ref, real_x, imag_x, packed):
    stations, bands, seg = sizes[:3]
    pairs = stations * stations
    add_products(
        stations, count * stations, seg, source_tile(sources_ref, 0, seg, stations),
        lambda n, pair: wide[n, pl.ds(first_block * pairs + pair, 1), :],
        lambda n, a, j: (local[n, j, 0], local[n, j, 1]),
        real_x, imag_x,
    )
    return both_sums(sizes, count * pairs, table, real_x, imag_x, packed)


def keep_and_send(before, after, kept_ref, sent_ref):
    first_core = lax.axis_index("pol") == 0
    kept_ref[...] = jnp.where(first_core, before, after)
    sent_ref[...] = jnp.where(first_core, after, before).astype(sent_ref.dtype)


def all_blocks_kernel(sizes, table, phase, mine_ref, sources_ref, kept_ref, sent_ref, local, wide, *scratch):
    spread_weights(sizes, mine_ref, wide)
    turn_locals(sizes, phase[0], phase[1], mine_ref, local)
    before, after = block_sums(sizes, 0, sizes[5], table, wide, local, sources_ref, *scratch)
    keep_and_send(turned_round(before), after, kept_ref, sent_ref)


def own_block_kernel(sizes, table, phase, mine_ref, kept_ref, sent_ref, local_ref, wide_ref, *scratch):
    spread_weights(sizes, mine_ref, wide_ref)
    turn_locals(sizes, phase[0], phase[1], mine_ref, local_ref)
    before, after = block_sums(sizes, 0, 1, table, wide_ref, local_ref, mine_ref, *scratch)
    keep_and_send(turned_round(before), after, kept_ref, sent_ref)


def weigh_kernel(sizes, wide_ref, local_ref, weighted_ref):
    stations, bands, seg = sizes[:3]
    for a in range(stations):
        for j in range(stations):
            pair = stations * stations + a * stations + j
            for g in range(seg):
                weight = jnp.broadcast_to(wide_ref[g, pl.ds(pair, 1), :], (bands, LANES))
                weighted_ref[a, j, g, 0] = local_ref[g, j, 0] * weight
                weighted_ref[a, j, g, 1] = local_ref[g, j, 1] * weight


def across_kernel(sizes, weighted_ref, across_ref, real_x, imag_x):
    stations = sizes[0]
    add_products(
        stations, stations, 2,
        lambda n, a: across_ref[n, pl.ds(a * 16, 16), :],
        None,
        lambda n, a, j: (weighted_ref[a, j, 2 + n, 0], weighted_ref[a, j, 2 + n, 1]),
        real_x, imag_x,
    )


def other_block_kernel(
    sizes, table, weighted_ref, real_ref, imag_ref, first_ref, second_ref, kept_ref, sent_ref, *scratch
):
    stations, bands, seg = sizes[:3]
    add_products(
        stations, stations, 2,
        lambda n, a: (first_ref, second_ref)[n][0, pl.ds(a * 16, 16), :],
        None,
        lambda n, a, j: (weighted_ref[a, j, n, 0], weighted_ref[a, j, n, 1]),
        *scratch[:2],
        before=(real_ref, imag_ref),
    )
    before, after = both_sums(sizes, stations * stations, table, *scratch)
    first_core = lax.axis_index("pol") == 0

    @pl.when(first_core)
    def _():
        kept_ref[...] = before
        sent_ref[...] = after.astype(sent_ref.dtype)

    @pl.when(jnp.logical_not(first_core))
    def _():
        kept_ref[...] = after
        sent_ref[...] = turned_round(before).astype(sent_ref.dtype)


def settle_kernel(sizes, own_kept_ref, own_got_ref, kept_ref, out_ref, settled_ref, own, sems):
    own[...] = own_kept_ref[...] + own_got_ref[...]
    copies = [pltpu.make_async_copy(own, out_ref.at[step], sems.at[step]) for step in range(STEPS)]
    for copy in copies:
        copy.start()
    kept = kept_ref[...]
    settled_ref[...] = jnp.where(lax.axis_index("pol") == 0, turned_round(kept), kept)
    for copy in copies:
        copy.wait()


def combine_kernel(sizes, kept_ref, got_ref, lags_ref):
    lags_ref[...] = kept_ref[...] + got_ref[...].astype(jnp.float32)


def place_kernel(sizes, is_own_ref, kept_ref, got_ref, steps_ref, out_ref, other, sems):
    del steps_ref
    other[...] = kept_ref[...] + got_ref[...].astype(jnp.float32)
    for act in ("start", "wait"):
        for step in range(STEPS):

            @pl.when(is_own_ref[step] == 0)
            def _():
                getattr(pltpu.make_async_copy(other, out_ref.at[step], sems.at[step]), act)()


def phase_kernel(sizes, after, phase_ref):
    del after
    phase_ref[0], phase_ref[1] = middle_phase(sizes)


def fetch_kernel(sizes, table_hbm, plan_any, after, table_ref, is_own_ref, plan_ref, sems):
    del after
    copies = [
        pltpu.make_async_copy(table_hbm.at[lax.axis_index("pol")], table_ref, sems.at[0]),
        pltpu.make_async_copy(plan_any, plan_ref, sems.at[1]),
    ]
    for copy in copies:
        copy.start()
    copies[1].wait()
    for step in range(STEPS):
        is_own_ref[step] = (plan_ref[step] == lax.axis_index("sta")).astype(jnp.int32)
    copies[0].wait()


def join_kernel(ranges, *refs):
    *pieces, out_ref = refs
    at = 0
    for piece, (first, count) in zip(pieces, ranges):
        out_ref[pl.ds(at, count)] = piece[pl.ds(first, count), pl.ds(0, out_ref.shape[1]), :]
        at += count


def join(*pieces, rows=None, flops=0):
    pieces = [piece if isinstance(piece, tuple) else (piece, 0, piece.shape[0]) for piece in pieces]
    arrays = [piece[0] for piece in pieces]
    ranges = [piece[1:] for piece in pieces]
    vmem = pl.BlockSpec(memory_space=pltpu.VMEM)
    return pl.pallas_call(
        functools.partial(join_kernel, ranges),
        out_shape=pltpu.VMEM(
            (sum(count for _, count in ranges), rows or arrays[0].shape[1], LANES), arrays[0].dtype
        ),
        in_specs=[vmem] * len(arrays),
        out_specs=vmem,
        compiler_params=pltpu.CompilerParams(vmem_limit_bytes=VMEM_BYTES),
        cost_estimate=pl.CostEstimate(flops=flops, bytes_accessed=0, transcendentals=0),
        name="join",
    )(*arrays)


def fetch_from(value, axes, source_of):
    sizes = tuple(lax.axis_size(axis) for axis in axes)
    pairs = []
    for index in np.ndindex(*sizes):
        source = source_of(*index)
        pairs.append((int(np.ravel_multi_index(source, sizes)), int(np.ravel_multi_index(index, sizes))))
    return lax.ppermute(value, axes, pairs)


def exchange(value, axis, distance):
    return fetch_from(value, (axis,), lambda i: (i ^ distance,))


def shards(table, raw_spectra, owner_plan, pair_valid, quality):
    seg, sta, pol = (lax.axis_size(name) for name in ("seg", "sta", "pol"))
    _, stations, _, bins = raw_spectra.shape
    bands = bins // BAND
    fast = sta == 2 and pol == 2 and seg == 4
    blocks = 2 if fast else STEPS
    pairs = stations * stations
    lags = table.shape[3]
    rows = 2 * stations * bands + 16
    sizes = (stations, bands, seg, sta, pol, blocks, lags)

    raw = raw_spectra.reshape(stations, 2, bands, BAND).transpose(0, 2, 1, 3).reshape(-1, BAND)
    vmem = pl.BlockSpec(memory_space=pltpu.VMEM)
    smem = pl.BlockSpec(memory_space=pltpu.SMEM)
    hbm = pl.BlockSpec(memory_space=pltpu.HBM)
    plan = [] if fast else [owner_plan]
    in_hbm = functools.partial(pltpu.with_memory_space_constraint, memory_space=pltpu.HBM)
    own = pl.pallas_call(
        functools.partial(prepare_kernel, (stations, bands, sta, blocks)),
        out_shape=pltpu.VMEM((1, rows, LANES), jnp.bfloat16),
        in_specs=[smem] * len(plan) + [vmem, vmem, vmem],
        out_specs=vmem,
        scratch_shapes=[pltpu.VMEM((2 * stations * bands, LANES), jnp.float32)],
        compiler_params=pltpu.CompilerParams(vmem_limit_bytes=VMEM_BYTES),
        name="prepare",
    )(*plan, in_hbm(raw), in_hbm(jnp.transpose(pair_valid[0])), in_hbm(quality))

    def call(kernel, out_shape, *args, aliases=None, scratch=(), flops=0, moved=0, name=None):
        def spec(x):
            if x is table_const or x is plan_const or x.shape == placed_shape.shape:
                return hbm
            return smem if x.shape == (STEPS,) else vmem

        many = isinstance(out_shape, (list, tuple))
        return pl.pallas_call(
            functools.partial(kernel, sizes),
            out_shape=out_shape,
            in_specs=[spec(x) for x in args],
            out_specs=[spec(x) for x in out_shape] if many else spec(out_shape),
            input_output_aliases=aliases or {},
            scratch_shapes=list(scratch),
            compiler_params=pltpu.CompilerParams(vmem_limit_bytes=VMEM_BYTES),
            cost_estimate=pl.CostEstimate(flops=flops, bytes_accessed=moved, transcendentals=0),
            name=name,
        )(*args)

    f32 = jnp.float32
    placed_shape = jax.ShapeDtypeStruct((STEPS, pairs, lags), f32)
    table_const, plan_const = in_hbm(table), in_hbm(owner_plan)

    quarter = 32 * pairs * 2 * bins * lags

    def fetch(after):
        return call(
            fetch_kernel,
            [
                pltpu.VMEM(table.shape[1:], table.dtype),
                pltpu.SMEM((STEPS,), jnp.int32),
            ],
            table_const, plan_const, after,
            scratch=[pltpu.SMEM((STEPS,), jnp.int32), pltpu.SemaphoreType.DMA((2,))],
            name="fetch",
        )

    def products(count):
        return [pltpu.VMEM((count * pairs * 8, LANES), f32)] * 2 + [pltpu.VMEM((2, count * pairs, bins), jnp.bfloat16)]

    local_shape = pltpu.VMEM((seg, stations, 2, bands, LANES), f32)
    wide_shape = pltpu.VMEM((seg, blocks * pairs, LANES), f32)
    kept_shape = pltpu.VMEM((pairs, lags), f32)

    if fast:
        bare = rows - 16
        distant = exchange(own, "seg", 2)
        partner_own = exchange(join(own, rows=bare), "sta", 1)
        phase = call(phase_kernel, pltpu.VMEM((2, bands, LANES), f32), own, flops=4 * quarter, name="phase")
        distant, phase = lax.optimization_barrier((distant, phase))
        far = join(own, distant)
        near = exchange(far, "seg", 1)
        far_bare = join(far, rows=bare, flops=4 * quarter)
        across = fetch_from(far_bare, ("seg", "sta"), lambda z, x: (z ^ 1, x ^ 1))
        partner_far = exchange(join((far_bare, 1, 1)), "sta", 1)
        table, is_own = fetch(far)
        near, table = lax.optimization_barrier((near, table))
        mine = join(far, near)
        own_kept, own_sent, local, wide = call(
            own_block_kernel, [kept_shape, kept_shape, local_shape, wide_shape],
            table, phase, mine,
            scratch=products(1), flops=8 * quarter, name="own_block",
        )
        weighted = call(
            weigh_kernel, pltpu.VMEM((stations, stations, seg, 2, bands, LANES), f32),
            wide, local,
            flops=8 * quarter, name="weigh",
        )
        own_got = exchange(own_sent, "pol", 1)
        weighted, across = lax.optimization_barrier((weighted, across))
        partial = call(
            across_kernel, [pltpu.VMEM((pairs * 8, LANES), f32)] * 2,
            weighted, across,
            name="across",
        )
        partial, partner_own, partner_far = lax.optimization_barrier((partial, partner_own, partner_far))
        kept, sent = call(
            other_block_kernel, [kept_shape, pltpu.VMEM((pairs, lags), jnp.bfloat16)],
            table, weighted, *partial, partner_own, partner_far,
            scratch=products(1), name="other_block",
        )
        got = exchange(sent, "pol", 1)
        steps, kept = call(
            settle_kernel, [placed_shape, kept_shape], own_kept, own_got, kept,
            scratch=[pltpu.VMEM((pairs, lags), f32), pltpu.SemaphoreType.DMA((STEPS,))],
            name="settle",
        )
        result = call(
            place_kernel, placed_shape, is_own, kept, got, steps,
            aliases={3: 0},
            scratch=[pltpu.VMEM((pairs, lags), f32), pltpu.SemaphoreType.DMA((STEPS,))],
            name="place",
        )
    else:
        mine, distance = own, seg // 2
        while distance:
            mine = join(mine, exchange(mine, "seg", distance))
            distance //= 2
        gathered = lax.all_gather(mine, "sta")
        sources = join(*(gathered[owner_plan[k]] for k in range(STEPS)))
        table, _ = fetch(mine)
        phase = call(phase_kernel, pltpu.VMEM((2, bands, LANES), f32), mine, name="phase")
        kept, sent = call(
            all_blocks_kernel,
            [pltpu.VMEM((blocks * pairs, lags), f32), pltpu.VMEM((blocks * pairs, lags), jnp.bfloat16)],
            table, phase, mine, sources,
            scratch=[local_shape, wide_shape] + products(blocks), flops=blocks * quarter, name="all_blocks",
        )
        result = call(
            combine_kernel, jax.ShapeDtypeStruct((blocks * pairs, lags), f32),
            kept, exchange(sent, "pol", 1), name="combine",
        )
    return result.reshape(STEPS, stations, stations, lags)


def solution(mesh):
    placed = (
        P(("groups", "seg"), "sta", None, "pol"),
        P("groups"),
        P(("groups", "seg"), None, "sta"),
        P(("groups", "seg"), None),
    )

    def whole(raw_spectra, owner_plan, pair_valid, quality):
        seg, pol = mesh.shape["seg"], mesh.shape["pol"]
        bins = raw_spectra.shape[3]
        segments = raw_spectra.shape[0] // mesh.shape["groups"]
        table = lag_table(2 * bins // seg, bins, pol, 1.0 / math.sqrt(bins * segments))
        return jax.shard_map(
            shards,
            mesh=mesh,
            in_specs=(P(),) + placed,
            out_specs=P("groups", None, "sta", ("seg", "pol")),
            check_vma=False,
        )(jnp.asarray(table), raw_spectra, owner_plan, pair_valid, quality)

    return whole
```

```python
import functools
import math

import jax
import jax.numpy as jnp
import numpy as np
from jax import lax
from jax.experimental import pallas as pl
from jax.experimental.pallas import tpu as pltpu
from jax.sharding import PartitionSpec as P

STEPS = 3
BAND = 128
LANES = 128
VMEM_BYTES = 32 * 1024 * 1024


def lag_table(lags, bins, halves, scale):
    bin_index = np.arange(bins, dtype=np.int64)
    lag = 2 * np.arange(lags // 2, dtype=np.int64) + 1
    phase = (bin_index[:, None] * lag[None, :]) % (4 * bins)
    angle = phase * (2.0 * math.pi / (4 * bins))
    factor = np.where(bin_index == 0, 1.0, 2.0)[:, None] * scale
    parts = np.stack([np.cos(angle) * factor, np.sin(angle) * factor])
    parts = parts.reshape(2, halves, bins // halves, lags // 2).transpose(1, 0, 2, 3)
    return parts.astype(jnp.bfloat16)


def turn(count, period):
    count = count % period
    quarter = (count + period // 8) // (period // 4)
    x = (count - quarter * (period // 4)).astype(jnp.float32) * (2.0 * math.pi / period)
    y = x * x
    sine = x * (1.0 + y * (-1 / 6 + y * (1 / 120 + y * (-1 / 5040 + y * (1 / 362880)))))
    cosine = 1.0 + y * (-1 / 2 + y * (1 / 24 + y * (-1 / 720 + y * (1 / 40320))))
    quarter = quarter % 4
    odd = quarter % 2 == 1
    real = jnp.where(odd, sine, cosine)
    imag = jnp.where(odd, cosine, sine)
    real = jnp.where((quarter == 1) | (quarter == 2), -real, real)
    imag = jnp.where(quarter >= 2, -imag, imag)
    return real, imag


def prepare_kernel(sizes, *refs):
    stations, bands, sta, blocks = sizes
    *plan, raw_ref, valid_ref, quality_ref, out_ref, wide = refs
    total = stations * sta
    me = lax.axis_index("sta")
    wide[...] = raw_ref[...].astype(jnp.float32)
    count = stations * bands
    real = wide[pl.ds(0, count, stride=2), :]
    imag = wide[pl.ds(1, count, stride=2), :]
    power = jnp.sum(real * real + imag * imag, axis=1, keepdims=True) * (1.0 / (2 * BAND))
    inverse = lax.rsqrt(power + 1e-06)
    real = (real * inverse).reshape(stations, bands, LANES)
    imag = (imag * inverse).reshape(stations, bands, LANES)
    white = jnp.concatenate([real, imag], axis=1).reshape(2 * count, LANES).astype(jnp.bfloat16)

    flags = jnp.concatenate([valid_ref[...], jnp.broadcast_to(quality_ref[...], (8, total))], axis=0)
    pair = lax.broadcasted_iota(jnp.int32, (total, LANES), 1)
    station = lax.broadcasted_iota(jnp.int32, (total, LANES), 0)
    wanted = [(plan[0][k] if plan else k) * stations + pair // stations for k in range(blocks)]
    wanted.append(me * stations + pair % stations)
    picks = jnp.concatenate([(station == x).astype(jnp.float32) for x in wanted], axis=1)
    picked = jnp.dot(
        flags.astype(jnp.float32).astype(jnp.bfloat16), picks.astype(jnp.bfloat16),
        preferred_element_type=jnp.float32,
    )
    mine = lax.broadcasted_iota(jnp.int32, (stations, LANES), 0) == (
        lax.broadcasted_iota(jnp.int32, (stations, LANES), 1) % stations
    )
    local_flags = picked[stations : stations + 1, blocks * LANES :]
    rows = []
    for k in range(blocks):
        part = picked[:, k * LANES : (k + 1) * LANES]
        valid_row = jnp.sum(jnp.where(mine, part[:stations], 0.0), axis=0, keepdims=True)
        rows.append(valid_row * part[stations : stations + 1] * local_flags)
    rows.append(jnp.zeros((16 - blocks, LANES), jnp.float32))
    weights = jnp.concatenate(rows, axis=0).astype(jnp.bfloat16)
    out_ref[0, pl.ds(0, 2 * count), :] = white
    out_ref[0, pl.ds(2 * count, 16), :] = weights


def spread_weights(sizes, locals_ref, wide):
    stations, bands, seg, sta, pol, blocks, lags = sizes
    pairs = stations * stations
    row_index = lax.broadcasted_iota(jnp.int32, (16, LANES), 0)
    diagonal = lax.broadcasted_iota(jnp.int32, (pairs, LANES), 0) == lax.broadcasted_iota(
        jnp.int32, (pairs, LANES), 1
    )
    ones = jnp.ones((LANES, LANES), jnp.bfloat16)
    for g in range(seg):
        flags = locals_ref[g, pl.ds(2 * stations * bands, 16), :].astype(jnp.float32)
        spread = []
        for n in range(blocks):
            block = lax.axis_index("sta") ^ n if sta == 2 else n
            row = jnp.sum(jnp.where(row_index == block, flags, 0.0), axis=0, keepdims=True)
            spread.append(jnp.where(diagonal, row, 0.0))
        spread = jnp.concatenate(spread, axis=0).astype(jnp.bfloat16)
        wide[g] = jnp.dot(spread, ones, preferred_element_type=jnp.float32)


def middle_phase(sizes):
    stations, bands, seg, sta, pol, blocks, lags = sizes
    row = lax.axis_index("pol") * bands + lax.broadcasted_iota(jnp.int32, (bands, LANES), 0)
    bin_index = row * LANES + lax.broadcasted_iota(jnp.int32, (bands, LANES), 1)
    run = pol * lags
    return turn(bin_index * (2 * run * lax.axis_index("seg") + run - 1), 2 * run * seg)


def turn_locals(sizes, cosine, sine, locals_ref, local):
    stations, bands, seg = sizes[:3]
    for g in range(seg):
        for j in range(stations):
            tile = locals_ref[g, pl.ds(j * 16, 16), :].astype(jnp.float32)
            local[g, j, 0] = tile[:bands] * cosine + tile[bands:] * sine
            local[g, j, 1] = tile[bands:] * cosine - tile[:bands] * sine


def add_products(stations, count, segments, tile_of, weight_of, local_of, real_x, imag_x, before=None):
    def one_source(a, carry):
        tiles = [tile_of(n, a).astype(jnp.float32) for n in range(segments)]
        for j in range(stations):
            pair = a * stations + j
            at = pl.ds(pair * 8 if isinstance(pair, int) else pl.multiple_of(pair * 8, 8), 8)
            real_sum = imag_sum = None
            if before is not None:
                real_sum, imag_sum = before[0][at, :], before[1][at, :]
            for n in range(segments):
                real_src, imag_src = tiles[n][:8], tiles[n][8:]
                if weight_of is not None:
                    weight = jnp.broadcast_to(weight_of(n, pair), (8, LANES))
                    real_src, imag_src = real_src * weight, imag_src * weight
                real_loc, imag_loc = local_of(n, a, j)
                real_term = real_src * real_loc + imag_src * imag_loc
                imag_term = imag_src * real_loc - real_src * imag_loc
                real_sum = real_term if real_sum is None else real_sum + real_term
                imag_sum = imag_term if imag_sum is None else imag_sum + imag_term
            real_x[at, :] = real_sum
            imag_x[at, :] = imag_sum
        return carry

    if count <= 8:
        for a in range(count):
            one_source(a, 0)
    else:
        lax.fori_loop(0, count, one_source, 0, unroll=2)


def pack(rows, bands, real_x, imag_x, packed):
    for band in range(bands):
        at = pl.ds(band * LANES, LANES)
        strided = pl.ds(band, rows, stride=8)
        packed[0, :, at] = real_x[strided, :].astype(jnp.bfloat16)
        packed[1, :, at] = imag_x[strided, :].astype(jnp.bfloat16)


def source_tile(sources_ref, base, count, stations):
    def tile_of(n, a):
        start = a % stations * 16
        start = start if isinstance(a, int) else pl.multiple_of(start, 16)
        return sources_ref[base + a // stations * count + n, pl.ds(start, 16), :]

    return tile_of


def block_sums(sizes, first_block, count, table, wide, local, sources_ref, kept_ref, sent_ref, real_x, imag_x, packed):
    stations, bands, seg = sizes[:3]
    pairs = stations * stations
    add_products(
        stations, count * stations, seg, source_tile(sources_ref, 0, seg, stations),
        lambda n, pair: wide[n, pl.ds(first_block * pairs + pair, 1), :],
        lambda n, a, j: (local[n, j, 0], local[n, j, 1]),
        real_x, imag_x,
    )
    both_sums(sizes, count * pairs, table, kept_ref, sent_ref, real_x, imag_x, packed)


def both_sums(sizes, rows, table, real_x, imag_x, packed):
    pack(rows, sizes[1], real_x, imag_x, packed)
    dot = functools.partial(jnp.dot, preferred_element_type=jnp.float32)
    even, odd = dot(packed[0], table[0]), dot(packed[1], table[1])
    return even + odd, even - odd


def turned_round(sums):
    index = LANES - 1 - lax.broadcasted_iota(jnp.int32, (sums.shape[0], LANES), 1)
    runs = [sums[:, at : at + LANES] for at in reversed(range(0, sums.shape[1], LANES))]
    runs = [jnp.take_along_axis(run, index, axis=1, mode="promise_in_bounds") for run in runs]
    return jnp.concatenate(runs, axis=1)


def block_sums(sizes, first_block, count, table, wide, local, sources_ref, real_x, imag_x, packed):
    stations, bands, seg = sizes[:3]
    pairs = stations * stations
    add_products(
        stations, count * stations, seg, source_tile(sources_ref, 0, seg, stations),
        lambda n, pair: wide[n, pl.ds(first_block * pairs + pair, 1), :],
        lambda n, a, j: (local[n, j, 0], local[n, j, 1]),
        real_x, imag_x,
    )
    return both_sums(sizes, count * pairs, table, real_x, imag_x, packed)


def keep_and_send(before, after, kept_ref, sent_ref):
    first_core = lax.axis_index("pol") == 0
    kept_ref[...] = jnp.where(first_core, before, after)
    sent_ref[...] = jnp.where(first_core, after, before).astype(sent_ref.dtype)


def all_blocks_kernel(sizes, table, phase, mine_ref, sources_ref, kept_ref, sent_ref, local, wide, *scratch):
    spread_weights(sizes, mine_ref, wide)
    turn_locals(sizes, phase[0], phase[1], mine_ref, local)
    before, after = block_sums(sizes, 0, sizes[5], table, wide, local, sources_ref, *scratch)
    keep_and_send(turned_round(before), after, kept_ref, sent_ref)


def own_block_kernel(sizes, table, phase, mine_ref, kept_ref, sent_ref, local_ref, wide_ref, *scratch):
    spread_weights(sizes, mine_ref, wide_ref)
    turn_locals(sizes, phase[0], phase[1], mine_ref, local_ref)
    before, after = block_sums(sizes, 0, 1, table, wide_ref, local_ref, mine_ref, *scratch)
    keep_and_send(turned_round(before), after, kept_ref, sent_ref)


def weigh_kernel(sizes, wide_ref, local_ref, weighted_ref):
    stations, bands, seg = sizes[:3]
    for a in range(stations):
        for j in range(stations):
            pair = stations * stations + a * stations + j
            for g in range(seg):
                weight = jnp.broadcast_to(wide_ref[g, pl.ds(pair, 1), :], (bands, LANES))
                weighted_ref[a, j, g, 0] = local_ref[g, j, 0] * weight
                weighted_ref[a, j, g, 1] = local_ref[g, j, 1] * weight


def across_kernel(sizes, weighted_ref, first_ref, across_ref, real_x, imag_x):
    stations = sizes[0]
    add_products(
        stations, stations, 3,
        lambda n, a: (across_ref[n - 1] if n else first_ref[0])[a * 16 : a * 16 + 16],
        None,
        lambda n, a, j: (weighted_ref[a, j, n + (n > 0), 0], weighted_ref[a, j, n + (n > 0), 1]),
        real_x, imag_x,
    )


def other_block_kernel(
    sizes, table, weighted_ref, real_ref, imag_ref, second_ref, kept_ref, sent_ref, *scratch
):
    stations, bands, seg = sizes[:3]
    add_products(
        stations, stations, 1,
        lambda n, a: second_ref[0, pl.ds(a * 16, 16), :],
        None,
        lambda n, a, j: (weighted_ref[a, j, 1, 0], weighted_ref[a, j, 1, 1]),
        *scratch[:2],
        before=(real_ref, imag_ref),
    )
    before, after = both_sums(sizes, stations * stations, table, *scratch)
    first_core = lax.axis_index("pol") == 0

    @pl.when(first_core)
    def _():
        kept_ref[...] = before
        sent_ref[...] = after.astype(sent_ref.dtype)

    @pl.when(jnp.logical_not(first_core))
    def _():
        kept_ref[...] = after
        sent_ref[...] = turned_round(before).astype(sent_ref.dtype)


def settle_kernel(sizes, own_kept_ref, own_got_ref, kept_ref, out_ref, settled_ref, own, sems):
    own[...] = own_kept_ref[...] + own_got_ref[...]
    copies = [pltpu.make_async_copy(own, out_ref.at[step], sems.at[step]) for step in range(STEPS)]
    for copy in copies:
        copy.start()
    kept = kept_ref[...]
    settled_ref[...] = jnp.where(lax.axis_index("pol") == 0, turned_round(kept), kept)
    for copy in copies:
        copy.wait()


def combine_kernel(sizes, kept_ref, got_ref, lags_ref):
    lags_ref[...] = kept_ref[...] + got_ref[...].astype(jnp.float32)


def place_kernel(sizes, is_own_ref, kept_ref, got_ref, steps_ref, out_ref, other, sems):
    del steps_ref
    other[...] = kept_ref[...] + got_ref[...].astype(jnp.float32)
    for act in ("start", "wait"):
        for step in range(STEPS):

            @pl.when(is_own_ref[step] == 0)
            def _():
                getattr(pltpu.make_async_copy(other, out_ref.at[step], sems.at[step]), act)()


def phase_kernel(sizes, after, phase_ref):
    del after
    phase_ref[0], phase_ref[1] = middle_phase(sizes)


def fetch_kernel(sizes, table_hbm, plan_any, after, table_ref, is_own_ref, plan_ref, sems):
    del after
    copies = [
        pltpu.make_async_copy(table_hbm.at[lax.axis_index("pol")], table_ref, sems.at[0]),
        pltpu.make_async_copy(plan_any, plan_ref, sems.at[1]),
    ]
    for copy in copies:
        copy.start()
    copies[1].wait()
    for step in range(STEPS):
        is_own_ref[step] = (plan_ref[step] == lax.axis_index("sta")).astype(jnp.int32)
    copies[0].wait()


def join_kernel(ranges, *refs):
    *pieces, out_ref = refs
    at = 0
    for piece, (first, count) in zip(pieces, ranges):
        out_ref[pl.ds(at, count)] = piece[pl.ds(first, count), pl.ds(0, out_ref.shape[1]), :]
        at += count


def join(*pieces, rows=None, flops=0):
    pieces = [piece if isinstance(piece, tuple) else (piece, 0, piece.shape[0]) for piece in pieces]
    arrays = [piece[0] for piece in pieces]
    ranges = [piece[1:] for piece in pieces]
    vmem = pl.BlockSpec(memory_space=pltpu.VMEM)
    return pl.pallas_call(
        functools.partial(join_kernel, ranges),
        out_shape=pltpu.VMEM(
            (sum(count for _, count in ranges), rows or arrays[0].shape[1], LANES), arrays[0].dtype
        ),
        in_specs=[vmem] * len(arrays),
        out_specs=vmem,
        compiler_params=pltpu.CompilerParams(vmem_limit_bytes=VMEM_BYTES),
        cost_estimate=pl.CostEstimate(flops=flops, bytes_accessed=0, transcendentals=0),
        name="join",
    )(*arrays)


def fetch_from(value, axes, source_of):
    sizes = tuple(lax.axis_size(axis) for axis in axes)
    pairs = []
    for index in np.ndindex(*sizes):
        source = source_of(*index)
        pairs.append((int(np.ravel_multi_index(source, sizes)), int(np.ravel_multi_index(index, sizes))))
    return lax.ppermute(value, axes, pairs)


def exchange(value, axis, distance):
    return fetch_from(value, (axis,), lambda i: (i ^ distance,))


def shards(table, raw_spectra, owner_plan, pair_valid, quality):
    seg, sta, pol = (lax.axis_size(name) for name in ("seg", "sta", "pol"))
    _, stations, _, bins = raw_spectra.shape
    bands = bins // BAND
    fast = sta == 2 and pol == 2 and seg == 4
    blocks = 2 if fast else STEPS
    pairs = stations * stations
    lags = table.shape[3]
    rows = 2 * stations * bands + 16
    sizes = (stations, bands, seg, sta, pol, blocks, lags)

    raw = raw_spectra.reshape(stations, 2, bands, BAND).transpose(0, 2, 1, 3).reshape(-1, BAND)
    vmem = pl.BlockSpec(memory_space=pltpu.VMEM)
    smem = pl.BlockSpec(memory_space=pltpu.SMEM)
    hbm = pl.BlockSpec(memory_space=pltpu.HBM)
    plan = [] if fast else [owner_plan]
    in_hbm = functools.partial(pltpu.with_memory_space_constraint, memory_space=pltpu.HBM)
    own = pl.pallas_call(
        functools.partial(prepare_kernel, (stations, bands, sta, blocks)),
        out_shape=pltpu.VMEM((1, rows, LANES), jnp.bfloat16),
        in_specs=[smem] * len(plan) + [vmem, vmem, vmem],
        out_specs=vmem,
        scratch_shapes=[pltpu.VMEM((2 * stations * bands, LANES), jnp.float32)],
        compiler_params=pltpu.CompilerParams(vmem_limit_bytes=VMEM_BYTES),
        name="prepare",
    )(*plan, in_hbm(raw), in_hbm(jnp.transpose(pair_valid[0])), in_hbm(quality))

    def call(kernel, out_shape, *args, aliases=None, scratch=(), flops=0, moved=0, name=None):
        def spec(x):
            if x is table_const or x is plan_const or x.shape == placed_shape.shape:
                return hbm
            return smem if x.shape == (STEPS,) else vmem

        many = isinstance(out_shape, (list, tuple))
        return pl.pallas_call(
            functools.partial(kernel, sizes),
            out_shape=out_shape,
            in_specs=[spec(x) for x in args],
            out_specs=[spec(x) for x in out_shape] if many else spec(out_shape),
            input_output_aliases=aliases or {},
            scratch_shapes=list(scratch),
            compiler_params=pltpu.CompilerParams(vmem_limit_bytes=VMEM_BYTES),
            cost_estimate=pl.CostEstimate(flops=flops, bytes_accessed=moved, transcendentals=0),
            name=name,
        )(*args)

    f32 = jnp.float32
    placed_shape = jax.ShapeDtypeStruct((STEPS, pairs, lags), f32)
    table_const, plan_const = in_hbm(table), in_hbm(owner_plan)

    quarter = 32 * pairs * 2 * bins * lags

    def fetch(after):
        return call(
            fetch_kernel,
            [
                pltpu.VMEM(table.shape[1:], table.dtype),
                pltpu.SMEM((STEPS,), jnp.int32),
            ],
            table_const, plan_const, after,
            scratch=[pltpu.SMEM((STEPS,), jnp.int32), pltpu.SemaphoreType.DMA((2,))],
            name="fetch",
        )

    def products(count):
        return [pltpu.VMEM((count * pairs * 8, LANES), f32)] * 2 + [pltpu.VMEM((2, count * pairs, bins), jnp.bfloat16)]

    local_shape = pltpu.VMEM((seg, stations, 2, bands, LANES), f32)
    wide_shape = pltpu.VMEM((seg, blocks * pairs, LANES), f32)
    kept_shape = pltpu.VMEM((pairs, lags), f32)

    if fast:
        bare = rows - 16
        distant = exchange(own, "seg", 2)
        partner_own = exchange(join(own, rows=bare), "sta", 1)
        phase = call(phase_kernel, pltpu.VMEM((2, bands, LANES), f32), own, flops=4 * quarter, name="phase")
        distant, phase = lax.optimization_barrier((distant, phase))
        far = join(own, distant)
        near = exchange(far, "seg", 1)
        far_bare = join(far, rows=bare, flops=4 * quarter)
        across = fetch_from(far_bare, ("seg", "sta"), lambda z, x: (z ^ 1, x ^ 1))
        partner_far = exchange(join((far_bare, 1, 1)), "sta", 1)
        table, is_own = fetch(far)
        near, table = lax.optimization_barrier((near, table))
        mine = join(far, near)
        own_kept, own_sent, local, wide = call(
            own_block_kernel, [kept_shape, kept_shape, local_shape, wide_shape],
            table, phase, mine,
            scratch=products(1), flops=8 * quarter, name="own_block",
        )
        weighted = call(
            weigh_kernel, pltpu.VMEM((stations, stations, seg, 2, bands, LANES), f32),
            wide, local,
            flops=8 * quarter, name="weigh",
        )
        own_got = exchange(own_sent, "pol", 1)
        weighted, across, partner_own = lax.optimization_barrier((weighted, across, partner_own))
        partial = call(
            across_kernel, [pltpu.VMEM((pairs * 8, LANES), f32)] * 2,
            weighted, partner_own, across,
            name="across",
        )
        partial, partner_far = lax.optimization_barrier((partial, partner_far))
        kept, sent = call(
            other_block_kernel, [kept_shape, pltpu.VMEM((pairs, lags), jnp.bfloat16)],
            table, weighted, *partial, partner_far,
            scratch=products(1), name="other_block",
        )
        got = exchange(sent, "pol", 1)
        steps, kept = call(
            settle_kernel, [placed_shape, kept_shape], own_kept, own_got, kept,
            scratch=[pltpu.VMEM((pairs, lags), f32), pltpu.SemaphoreType.DMA((STEPS,))],
            name="settle",
        )
        result = call(
            place_kernel, placed_shape, is_own, kept, got, steps,
            aliases={3: 0},
            scratch=[pltpu.VMEM((pairs, lags), f32), pltpu.SemaphoreType.DMA((STEPS,))],
            name="place",
        )
    else:
        mine, distance = own, seg // 2
        while distance:
            mine = join(mine, exchange(mine, "seg", distance))
            distance //= 2
        gathered = lax.all_gather(mine, "sta")
        sources = join(*(gathered[owner_plan[k]] for k in range(STEPS)))
        table, _ = fetch(mine)
        phase = call(phase_kernel, pltpu.VMEM((2, bands, LANES), f32), mine, name="phase")
        kept, sent = call(
            all_blocks_kernel,
            [pltpu.VMEM((blocks * pairs, lags), f32), pltpu.VMEM((blocks * pairs, lags), jnp.bfloat16)],
            table, phase, mine, sources,
            scratch=[local_shape, wide_shape] + products(blocks), flops=blocks * quarter, name="all_blocks",
        )
        result = call(
            combine_kernel, jax.ShapeDtypeStruct((blocks * pairs, lags), f32),
            kept, exchange(sent, "pol", 1), name="combine",
        )
    return result.reshape(STEPS, stations, stations, lags)


def solution(mesh):
    placed = (
        P(("groups", "seg"), "sta", None, "pol"),
        P("groups"),
        P(("groups", "seg"), None, "sta"),
        P(("groups", "seg"), None),
    )

    def whole(raw_spectra, owner_plan, pair_valid, quality):
        seg, pol = mesh.shape["seg"], mesh.shape["pol"]
        bins = raw_spectra.shape[3]
        segments = raw_spectra.shape[0] // mesh.shape["groups"]
        table = lag_table(2 * bins // seg, bins, pol, 1.0 / math.sqrt(bins * segments))
        return jax.shard_map(
            shards,
            mesh=mesh,
            in_specs=(P(),) + placed,
            out_specs=P("groups", None, "sta", ("seg", "pol")),
            check_vma=False,
        )(jnp.asarray(table), raw_spectra, owner_plan, pair_valid, quality)

    return whole
```
